32 devices in a mesh: groups: 2 (over y), seq: 4 (over x, core), role: 4 (over z).
Axes of the slice: x: 2, y: 2, z: 4, core: 2. Of those that a mesh axis runs over, the one named last changes fastest.
Arguments:
- query_rows: bfloat16 [8, 256, 4096], P('groups', 'seq', 'role'), parts along dimension 0, may hold values from -6 to 6
- encoded_key_rows: bfloat16 [8, 256, 512], P('groups', ('seq', 'role')), parts along dimension 0, may hold values from -6 to 6
- value_matrix_rows: bfloat16 [8, 256, 512], P('groups', ('seq', 'role')), parts along dimension 0, may hold values from -6 to 6
- output_weight: bfloat16 [4096, 2048], P('role', 'seq'), may hold values from -0.09375 to 0.09375
- residual: bfloat16 [8, 256, 2048], P(('groups', 'role'), 'seq'), parts along dimension 0, may hold values from -7.5 to 7.5
- norm_gain: float32 [2048], replicated, may hold values from 0.5 to 1.5
- route_experts: int32 [8, 256, 8], P(('groups', 'role'), 'seq'), parts along dimension 0, may hold values from 0 to 15, all different within a row; in each aligned block of 64 rows (0 to 63, 64 to 127, ..., all dimensions but the last counted through in order) at most 33 rows name the same one
- route_gates: float32 [8, 256, 8], P(('groups', 'role'), 'seq'), parts along dimension 0, may hold values from 0.05 to 0.3
- gate_weight: bfloat16 [16, 2048, 768], P(('seq', 'role')), may hold values from -0.125 to 0.125
- up_weight: bfloat16 [16, 2048, 768], P(('seq', 'role')), may hold values from -0.125 to 0.125
- down_weight: bfloat16 [16, 768, 2048], P(('seq', 'role')), may hold values from -0.21875 to 0.21875
Outputs:
- layer_output: bfloat16 [8, 256, 2048], P(('groups', 'role'), 'seq'), parts along dimension 0
The draws below stay inside these ranges and needn't reach their ends.
There are 2 independent parts, one for each index of `groups`. The reference program is written for one: setup_inputs(seed, part) draws one part's arguments, and reference() takes and returns one part's arrays. A program takes and returns all parts, laid end to end along the dimension named above; an argument that names none is the same for every part. Nothing has to cross between parts.
Inputs may be any that keep to these rules, and one draw needn't show every extreme that they name: `route_experts`: each token names 8 different experts. Within the 64 positions of one sequence that one index of seq holds, no expert is named by more than 33 routes, and in every draw some expert is named by exactly 33 routes in some such block.
All inputs are finite; a program needn't handle non-finite values.
Results may differ from the reference program's by a relative error of at most 0.014.
Values may be sent and summed in bfloat16 or wider, within the bound.
No kernel may reach another device: no remote copies, remote signals or barrier semaphores. Data moves between devices by JAX's collectives and lax.ppermute only.
A program may use at most 128 MiB of HBM per device.

```python
import math
import jax
import jax.numpy as jnp
import numpy as np
from jax import lax

D = 2048
FF = 768
QUERY_HEADS = 32
KEY_VALUE_HEADS = 4
HEAD_WIDTH = 128
TOPK = 8
SEQ_TOK = 64
EXPERTS = 16
SEQUENCE_LENGTH = 256
BATCH_SEQUENCES = 4
HPD = 8
CAP = 33
N_SEQ = 4
N_ROLE = 4


def draw_query_rows(key, part):
    value_entries = jnp.clip(1.5 * jax.random.normal(jax.random.fold_in(key, 11), (BATCH_SEQUENCES, SEQUENCE_LENGTH, QUERY_HEADS * HEAD_WIDTH), jnp.float32), -6.0, 6.0)
    return value_entries.astype(jnp.bfloat16)


def draw_encoded_key_rows(key, part):
    value_entries = jnp.clip(1.5 * jax.random.normal(jax.random.fold_in(key, 12), (BATCH_SEQUENCES, SEQUENCE_LENGTH, KEY_VALUE_HEADS * HEAD_WIDTH), jnp.float32), -6.0, 6.0)
    return value_entries.astype(jnp.bfloat16)


def draw_residual(key, part):
    random_splits = jax.random.split(jax.random.fold_in(key, 13), 3)
    row_scale = jnp.exp(jax.random.uniform(random_splits[1], (BATCH_SEQUENCES, SEQUENCE_LENGTH, 1), jnp.float32, math.log(0.25), math.log(2.5)))
    column_scale = jnp.exp(jax.random.uniform(random_splits[0], (D,), jnp.float32, math.log(0.1), 0.0))
    noise_rows = jnp.clip(jax.random.normal(random_splits[2], (BATCH_SEQUENCES, SEQUENCE_LENGTH, D), jnp.float32), -3.0, 3.0)
    return (noise_rows * column_scale * row_scale).astype(jnp.bfloat16)


def block_scale(stream_key, dims, pieces, least, largest):
    gain, own = 1.0, jax.random.fold_in(stream_key, 6)
    for axis_at, shards_of in pieces:
        draws = jnp.exp(jax.random.uniform(jax.random.fold_in(own, axis_at), (shards_of,), jnp.float32, least / len(pieces), largest / len(pieces)))
        gain = gain * jnp.repeat(draws, dims[axis_at] // shards_of).reshape([-1 if axis == axis_at else 1 for axis in range(len(dims))])
    return gain


def shared_out(key, own, number, rows, amount, top, most, skew):
    sequence = jax.random.permutation(key, amount)
    packed, usual = load_shares(amount, rows * top, most, skew, True), load_shares(amount, rows * top, most, skew, False)
    places = jnp.arange(amount)

    def named(sizes, turn):
        used = int((sizes > 0).sum())
        fixed = max(1, used // 4)
        shifted = fixed + (places - fixed + turn * (used - fixed)) % max(1, amount - fixed)
        return jnp.zeros((amount,), jnp.int32).at[sequence[jnp.where(places < fixed, places, shifted)]].set(jnp.asarray(sizes, jnp.int32))

    sizes = jnp.where(number % 4 == 0, named(packed, number // 4), named(usual, number - number // 4 - 1))
    mixed = jax.random.permutation(jax.random.fold_in(own, 3), amount)
    source_of, receiver = mixed[0:amount // 2 * 2:2], mixed[1:amount // 2 * 2:2]
    room = jnp.minimum(sizes[source_of] - 1, most - sizes[receiver]) // 2
    room = jnp.where((source_of == sequence[0]) | (receiver == sequence[0]) | (sizes[receiver] == 0), 0, jnp.maximum(room, 0))
    shifted = jax.random.randint(jax.random.fold_in(own, 4), (amount // 2,), 0, 1 << 20) % (room + 1)
    sizes = sizes.at[source_of].add(-shifted).at[receiver].add(shifted)
    members = jnp.searchsorted(jnp.cumsum(sizes), jnp.arange(rows * top), side="right").astype(jnp.int32)
    grid = members.reshape(top, rows).T
    grid = grid[jax.random.permutation(jax.random.fold_in(own, 1), rows)]
    turn = jax.random.randint(jax.random.fold_in(own, 2), (rows, 1), 0, top)
    return jnp.take_along_axis(grid, (jnp.arange(top)[None, :] + turn) % top, axis=1)


def load_shares(amount, total, bound, slope, full):
    weights = [(1 << 20) // math.isqrt(grade ** slope) + 1 for grade in range(1, amount + 1)]
    largest = bound if full else min(bound, max(-(-total // amount), total * weights[0] // sum(weights)))
    least = 1 if total - largest >= amount - 1 else 0
    holding, surplus = [largest] + [least] * (amount - 1), total - largest - least * (amount - 1)
    while surplus > 0:
        movable = [i for i in range(1, amount) if holding[i] < largest] or [i for i in range(1, amount) if holding[i] < bound]
        whole, left = sum([weights[i] for i in movable]), surplus
        for i in movable:
            addition = min(bound - holding[i], max(1, left * weights[i] // whole), surplus)
            holding[i] = holding[i] + addition
            surplus = surplus - addition
    return np.array(holding)


def normal_values(rng, dims, deviation, bound, cuts=(), kind=jnp.bfloat16):
    loudness = block_scale(rng, dims, cuts, -0.22, 0.18) if cuts else 1.0
    drawn = jax.random.normal(rng, dims, jnp.float32) * deviation * loudness
    return jnp.minimum(jnp.maximum(drawn, -bound), bound).astype(kind)


def setup_inputs(seed: int = 0, part: int = 0) -> dict:
    key_of = jax.random.split(jax.random.key(seed), 12)
    part_keys = jax.random.split(jax.random.fold_in(key_of[11], part), 12)
    query_rows = draw_query_rows(jax.random.fold_in(jax.random.fold_in(key_of[11], part), 71), part)
    encoded_key_rows = draw_encoded_key_rows(jax.random.fold_in(jax.random.fold_in(key_of[11], part), 71), part)
    value_matrix_rows = normal_values(part_keys[2], (BATCH_SEQUENCES, SEQUENCE_LENGTH, KEY_VALUE_HEADS * HEAD_WIDTH), 1.0, 6.0, ((1, 16),))
    output_weight = normal_values(key_of[3], (QUERY_HEADS * HEAD_WIDTH, D), (QUERY_HEADS * HEAD_WIDTH) ** -0.5, 0.09375, ((0, 4), (1, 4)))
    residual = draw_residual(jax.random.fold_in(jax.random.fold_in(key_of[11], part), 71), part)
    norm_gain = jnp.clip(1.0 + 0.1 * jax.random.normal(key_of[5], (D,), jnp.float32), 0.5, 1.5)
    route_experts_keys = jax.random.split(jax.random.fold_in(part_keys[6], 1), BATCH_SEQUENCES * SEQUENCE_LENGTH // SEQ_TOK)
    route_experts_turns = jax.random.permutation(jax.random.fold_in(part_keys[6], 3), BATCH_SEQUENCES * SEQUENCE_LENGTH // SEQ_TOK)
    route_experts = jax.vmap(lambda own, number: shared_out(jax.random.fold_in(part_keys[6], 2), own, number, SEQ_TOK, EXPERTS, TOPK, CAP, 1))(route_experts_keys, route_experts_turns).reshape((BATCH_SEQUENCES, SEQUENCE_LENGTH, TOPK))
    route_gates = jnp.clip(0.05 + 0.25 * jax.random.uniform(part_keys[7], (BATCH_SEQUENCES, SEQUENCE_LENGTH, TOPK), jnp.float32) ** block_scale(part_keys[7], (BATCH_SEQUENCES, SEQUENCE_LENGTH, TOPK), ((0, 4), (1, 4)), -0.2, 0.2), 0.05, 0.3)
    gate_weight = normal_values(key_of[8], (EXPERTS, D, FF), D ** -0.5, 0.125, ((0, 16),))
    up_weight = normal_values(key_of[9], (EXPERTS, D, FF), D ** -0.5, 0.125, ((0, 16),))
    down_weight = normal_values(key_of[10], (EXPERTS, FF, D), FF ** -0.5, 0.21875, ((0, 16),))
    return dict(query_rows=query_rows, encoded_key_rows=encoded_key_rows, value_matrix_rows=value_matrix_rows, output_weight=output_weight, residual=residual, norm_gain=norm_gain, route_experts=route_experts, route_gates=route_gates, gate_weight=gate_weight, up_weight=up_weight, down_weight=down_weight)


epsilon = 1e-06
masked_score = -1e+30

def attend_head(query_head, key_head, value_head):
    length = query_head.shape[0]
    scores = jnp.dot(query_head.astype(jnp.float32), key_head.astype(jnp.float32).T, precision=lax.Precision.HIGHEST) * HEAD_WIDTH ** (-0.5)
    positions = jnp.arange(length, dtype=jnp.int32)
    causal = positions[None, :] <= positions[:, None]
    scores = jnp.where(causal, scores, masked_score)
    row_peak = lax.optimization_barrier(jnp.max(scores, axis=1, keepdims=True))
    weights = jnp.exp(scores - row_peak)
    totals = lax.optimization_barrier(jnp.sum(weights, axis=1, keepdims=True))
    rounded = weights.astype(jnp.bfloat16)
    mixed_rows = jnp.dot(rounded.astype(jnp.float32), value_head.astype(jnp.float32), precision=lax.Precision.HIGHEST) / totals
    return mixed_rows.astype(jnp.bfloat16)

def reference(query_rows, encoded_key_rows, value_matrix_rows, output_weight, residual, norm_gain, route_experts, route_gates, gate_weight, up_weight, down_weight):
    query_group_width = QUERY_HEADS // KEY_VALUE_HEADS
    heads_query = query_rows.reshape(BATCH_SEQUENCES, SEQUENCE_LENGTH, QUERY_HEADS, HEAD_WIDTH)
    key_per_head = encoded_key_rows.reshape(BATCH_SEQUENCES, SEQUENCE_LENGTH, KEY_VALUE_HEADS, HEAD_WIDTH)
    value_per_head = value_matrix_rows.reshape(BATCH_SEQUENCES, SEQUENCE_LENGTH, KEY_VALUE_HEADS, HEAD_WIDTH)

    def one_pair(pair_index):
        batch_index = pair_index // QUERY_HEADS
        head_index = pair_index % QUERY_HEADS
        kv_index = head_index // query_group_width
        return attend_head(heads_query[batch_index, :, head_index], key_per_head[batch_index, :, kv_index], value_per_head[batch_index, :, kv_index])
    attended = lax.map(one_pair, jnp.arange(BATCH_SEQUENCES * QUERY_HEADS, dtype=jnp.int32))
    attended = attended.reshape(BATCH_SEQUENCES, QUERY_HEADS, SEQUENCE_LENGTH, HEAD_WIDTH).transpose(0, 2, 1, 3).reshape(BATCH_SEQUENCES, SEQUENCE_LENGTH, QUERY_HEADS * HEAD_WIDTH)
    grouped_weight = output_weight.astype(jnp.float32).reshape(N_ROLE, HPD * HEAD_WIDTH, D)

    def project(sequence_rows):
        split_rows = sequence_rows.astype(jnp.float32).reshape(SEQUENCE_LENGTH, N_ROLE, HPD * HEAD_WIDTH)
        partials = jnp.einsum('lgk,gkd->lgd', split_rows, grouped_weight, precision=lax.Precision.HIGHEST)
        partials = lax.optimization_barrier(partials.astype(jnp.bfloat16))
        return lax.optimization_barrier(jnp.sum(partials.astype(jnp.float32), axis=1))
    projected = lax.map(project, attended)
    hidden = residual.astype(jnp.float32) + projected
    variance = lax.optimization_barrier(jnp.mean(hidden * hidden, axis=-1, keepdims=True))
    normed = (hidden * lax.rsqrt(variance + epsilon) * norm_gain).astype(jnp.bfloat16)
    tokens = BATCH_SEQUENCES * SEQUENCE_LENGTH
    flat_inputs = normed.reshape(tokens, D)
    flat_ids = route_experts.reshape(tokens * TOPK)
    flat_gates = route_gates.reshape(tokens * TOPK)
    most_rows = CAP * N_SEQ * N_ROLE

    def one_expert(running, inputs):
        gate_matrix, up_matrix, down_matrix, expert = inputs
        chosen = flat_ids == expert
        picked = jnp.nonzero(chosen, size=most_rows, fill_value=0)[0]
        listed = jnp.sum(chosen.astype(jnp.int32))
        valid = jnp.arange(most_rows, dtype=jnp.int32) < listed
        token_index = picked // TOPK
        row_block = flat_inputs[token_index].astype(jnp.float32)
        gate_hidden = jnp.dot(row_block, gate_matrix.astype(jnp.float32), precision=lax.Precision.HIGHEST)
        up_hidden = jnp.dot(row_block, up_matrix.astype(jnp.float32), precision=lax.Precision.HIGHEST)
        activated = (jax.nn.silu(gate_hidden) * up_hidden).astype(jnp.bfloat16)
        expert_out = jnp.dot(activated.astype(jnp.float32), down_matrix.astype(jnp.float32), precision=lax.Precision.HIGHEST)
        expert_out = lax.optimization_barrier(expert_out.astype(jnp.bfloat16))
        weight = jnp.where(valid, flat_gates[picked], 0.0)
        running = running.at[token_index].add(weight[:, None] * expert_out.astype(jnp.float32))
        return (running, None)
    start_sum = jnp.zeros((tokens, D), jnp.float32)
    expert_sum, unused = lax.scan(one_expert, start_sum, (gate_weight, up_weight, down_weight, jnp.arange(EXPERTS, dtype=jnp.int32)))
    return (hidden + expert_sum.reshape(BATCH_SEQUENCES, SEQUENCE_LENGTH, D)).astype(jnp.bfloat16)
```

```python
from functools import partial

import jax
import jax.numpy as jnp
from jax import lax
from jax.experimental import pallas as pl
from jax.experimental.pallas import tpu as pltpu
from jax.sharding import PartitionSpec as P

D = 2048
QUERY_HEADS = 32
KEY_VALUE_HEADS = 4
HEAD_WIDTH = 128
TOPK = 8


epsilon = 1e-06
masked_score = -1e30
VMEM_BYTES = 40 * 2**20


def score_block(queries, every_key, query_position, block_start, block_width, score_scale):
    keys_part = lax.slice_in_dim(every_key, block_start, block_start + block_width, axis=0)
    raw_scores = (
        jnp.einsum("qhd,kd->hqk", queries, keys_part, preferred_element_type=jnp.float32)
        * score_scale
    )
    key_position = block_start + jnp.arange(block_width, dtype=jnp.int32)
    return jnp.where(
        key_position[None, None, :] <= query_position[None, :, None], raw_scores, masked_score
    )


def value_block(rounded, every_value, block_start, block_width):
    prob_block = lax.slice_in_dim(rounded, block_start, block_start + block_width, axis=2)
    values_part = lax.slice_in_dim(every_value, block_start, block_start + block_width, axis=0)
    return jnp.einsum("hqk,kd->qhd", prob_block, values_part, preferred_element_type=jnp.float32)


def routed_shards(
    query_rows,
    encoded_key_rows,
    value_matrix_rows,
    output_weight,
    residual,
    norm_gain,
    route_experts,
    route_gates,
    gate_weight,
    up_weight,
    down_weight,
):
    seq_count = lax.axis_size("seq")
    role_count = lax.axis_size("role")
    seq_index = lax.axis_index("seq")
    role_index = lax.axis_index("role")
    batch_count = query_rows.shape[0]
    local_length = query_rows.shape[1]
    local_heads = query_rows.shape[2] // HEAD_WIDTH
    full_length = local_length * seq_count
    query_group_width = QUERY_HEADS // KEY_VALUE_HEADS
    head_pick = role_index * local_heads // query_group_width
    role_keys, role_values = (
        lax.all_gather(encoded_key_rows, "role", axis=1, tiled=True),
        lax.all_gather(value_matrix_rows, "role", axis=1, tiled=True),
    )
    head_keys = lax.dynamic_slice_in_dim(role_keys, head_pick * HEAD_WIDTH, HEAD_WIDTH, 2)
    head_values = lax.dynamic_slice_in_dim(role_values, head_pick * HEAD_WIDTH, HEAD_WIDTH, 2)
    whole_keys, whole_values, whole_proj = (
        lax.all_gather(head_keys, "seq", axis=1, tiled=True),
        lax.all_gather(head_values, "seq", axis=1, tiled=True),
        lax.all_gather(output_weight, "seq", axis=1, tiled=True),
    )
    key_width = full_length // 8
    score_scale = HEAD_WIDTH ** (-0.5)
    query_position = seq_index * local_length + jnp.arange(local_length, dtype=jnp.int32)
    last_needed = (seq_index + 1) * local_length

    def one_sequence(operands):
        own_queries, every_key, every_value = operands
        queries = own_queries.reshape(local_length, local_heads, HEAD_WIDTH)
        pieces = []
        for number in range(8):
            block_start = number * key_width
            compute = partial(
                score_block, queries, every_key, query_position, block_start, key_width, score_scale
            )
            skipped = partial(
                jnp.full, (local_heads, local_length, key_width), masked_score, jnp.float32
            )
            pieces.append(lax.cond(block_start < last_needed, compute, skipped))
        scores = jnp.concatenate(pieces, axis=2)
        row_peak = jnp.max(scores, axis=2, keepdims=True)
        weights = jnp.exp(scores - row_peak)
        totals = jnp.sum(weights, axis=2, keepdims=True)
        rounded = weights.astype(jnp.bfloat16)
        mixed_rows = jnp.zeros((local_length, local_heads, HEAD_WIDTH), jnp.float32)
        for number in range(8):
            block_start = number * key_width
            product = partial(value_block, rounded, every_value, block_start, key_width)
            nothing = partial(jnp.zeros, (local_length, local_heads, HEAD_WIDTH), jnp.float32)
            mixed_rows = mixed_rows + lax.cond(block_start < last_needed, product, nothing)
        attended = (mixed_rows / totals.transpose(1, 0, 2)).astype(jnp.bfloat16)
        return attended.reshape(local_length, local_heads * HEAD_WIDTH)

    attended = lax.map(one_sequence, (query_rows, whole_keys, whole_values))
    flat_attended = attended.reshape(batch_count * local_length, local_heads * HEAD_WIDTH)
    projected = lax.psum_scatter(
        jnp.dot(flat_attended, whole_proj, preferred_element_type=jnp.float32).astype(jnp.bfloat16),
        "role",
        scatter_dimension=0,
        tiled=True,
    ).astype(jnp.float32)
    hidden = residual[0].astype(jnp.float32) + projected
    variance = jnp.mean(hidden * hidden, axis=-1, keepdims=True)
    normed = (hidden * lax.rsqrt(variance + epsilon) * norm_gain).astype(jnp.bfloat16)
    expert_ids = route_experts.reshape(-1)
    gate_values = route_gates.reshape(-1)
    experts_local = gate_weight.shape[0]
    device_count = seq_count * role_count
    expert_count = experts_local * device_count
    assign = expert_ids.shape[0]
    capacity = assign // expert_count + 1
    onehot = (expert_ids[:, None] == jnp.arange(expert_count, dtype=jnp.int32)[None, :]).astype(
        jnp.int32
    )
    earlier = jnp.cumsum(onehot, axis=0) - onehot
    slot_rank = jnp.sum(earlier * onehot, axis=1)
    slot_index = expert_ids * capacity + slot_rank
    source_token = jnp.arange(assign, dtype=jnp.int32) // TOPK
    slot_token = jnp.zeros((expert_count * capacity,), jnp.int32).at[slot_index].set(source_token)
    slot_used = jnp.zeros((expert_count * capacity,), jnp.bfloat16).at[slot_index].set(1.0)
    outgoing = (normed[slot_token] * slot_used[:, None]).reshape(
        device_count, experts_local, capacity, D
    )
    incoming = lax.all_to_all(outgoing, ("seq", "role"), split_axis=0, concat_axis=0, tiled=True)
    gate_hidden = jnp.einsum(
        "sjcd,jdf->sjcf", incoming, gate_weight, preferred_element_type=jnp.float32
    )
    up_hidden = jnp.einsum(
        "sjcd,jdf->sjcf", incoming, up_weight, preferred_element_type=jnp.float32
    )
    activated = (jax.nn.silu(gate_hidden) * up_hidden).astype(jnp.bfloat16)
    returned = lax.all_to_all(
        jnp.einsum(
            "sjcf,jfd->sjcd", activated, down_weight, preferred_element_type=jnp.float32
        ).astype(jnp.bfloat16),
        ("seq", "role"),
        split_axis=0,
        concat_axis=0,
        tiled=True,
    )
    gathered = returned.reshape(expert_count * capacity, D)[slot_index]
    weighted = gathered.astype(jnp.float32) * gate_values[:, None]
    expert_sum = jnp.sum(weighted.reshape(-1, TOPK, D), axis=1)
    return (hidden + expert_sum).astype(jnp.bfloat16).reshape(residual.shape)


def in_vmem(count):
    return [pl.BlockSpec(memory_space=pltpu.VMEM)] * count


def attend_kernel(seq_count, role_count, at_ref, query_ref, *refs):
    blocks = refs[:seq_count]
    proj_refs = refs[seq_count : seq_count + 2]
    attended_ref = refs[seq_count + 2]
    partial_refs = refs[seq_count + 3 :]
    seq_index, role_index = at_ref[0], at_ref[1]
    local_length = query_ref.shape[1]
    local_heads = query_ref.shape[2] // HEAD_WIDTH
    per_role = local_length // role_count
    rows = local_heads * local_length
    keys_all = seq_count * local_length
    slot = lax.broadcasted_iota(jnp.int32, (rows, keys_all), 1)
    block_number, within = slot // local_length, slot % local_length
    key_position = (
        (seq_index ^ block_number) * local_length
        + (role_index ^ (within // per_role)) * per_role
        + within % per_role
    )
    query_position = (
        seq_index * local_length
        + lax.broadcasted_iota(jnp.int32, (rows, keys_all), 0) % local_length
    )
    seen = key_position <= query_position
    scale = HEAD_WIDTH ** (-0.5)
    for k in range(role_count):
        b = role_index ^ k
        own = query_ref[b]
        queries = jnp.concatenate(
            [own[:, h * HEAD_WIDTH : (h + 1) * HEAD_WIDTH] for h in range(local_heads)], axis=0
        )
        key_value = jnp.concatenate([block[b] for block in blocks], axis=0)
        keys, values = key_value[:, :HEAD_WIDTH], key_value[:, HEAD_WIDTH:]
        scores = lax.dot_general(
            queries, keys, (((1,), (1,)), ((), ())), preferred_element_type=jnp.float32
        )
        scores = jnp.where(seen, scores * scale, masked_score)
        weights = jnp.exp(scores - jnp.max(scores, axis=1, keepdims=True))
        totals = jnp.sum(weights, axis=1, keepdims=True)
        mixed = jnp.dot(weights.astype(jnp.bfloat16), values, preferred_element_type=jnp.float32)
        attended = (mixed / totals).astype(jnp.bfloat16)
        for h in range(local_heads):
            attended_ref[
                k * local_length : (k + 1) * local_length, h * HEAD_WIDTH : (h + 1) * HEAD_WIDTH
            ] = attended[h * local_length : (h + 1) * local_length]
    project_into(attended_ref, proj_refs, partial_refs)


def project_into(attended_ref, proj_refs, partial_refs):
    rows = attended_ref.shape[0] // len(partial_refs)
    at = 0
    for proj_ref in proj_refs:
        width = proj_ref.shape[1]
        product = jnp.dot(
            attended_ref[...], proj_ref[...], preferred_element_type=jnp.float32
        ).astype(jnp.bfloat16)
        for k, partial_ref in enumerate(partial_refs):
            partial_ref[:, at : at + width] = product[k * rows : (k + 1) * rows]
        at += width


def project_kernel(weight_count, attended_ref, *refs):
    project_into(attended_ref, refs[:weight_count], refs[weight_count:])


def norm_kernel(near_count, far_count, at_ref, residual_ref, gain_ref, *refs):
    near = refs[:near_count]
    far = refs[near_count : near_count + far_count]
    hidden_ref, normed_ref = refs[near_count + far_count :]
    seq_index = at_ref[0]
    width = near[0].shape[1] // 2
    at = 0
    for group in (near, far):
        total = group[0][...].astype(jnp.float32)
        for part in group[1:]:
            total = total + part[...].astype(jnp.float32)
        for j in range(total.shape[1] // width):
            columns = pl.ds(pl.multiple_of((seq_index ^ at) * width, width), width)
            hidden_ref[:, columns] = total[:, j * width : (j + 1) * width] + residual_ref[
                0, :, columns
            ].astype(jnp.float32)
            at += 1
    hidden = hidden_ref[...]
    variance = jnp.mean(hidden * hidden, axis=1, keepdims=True)
    normed_ref[...] = (hidden * lax.rsqrt(variance + epsilon) * gain_ref[...]).astype(jnp.bfloat16)


def expert_kernel(
    own_ref, across_ref, beside_ref, share_ref, gate_ref, up_ref, down_ref, keep_ref, send_ref, total
):
    step = pl.program_id(0)
    tokens = jnp.concatenate([own_ref[...], across_ref[...], beside_ref[...]], axis=0)
    gate_hidden = jnp.dot(tokens, gate_ref[...], preferred_element_type=jnp.float32)
    up_hidden = jnp.dot(tokens, up_ref[...], preferred_element_type=jnp.float32)
    activated = (gate_hidden / (1.0 + jnp.exp(-gate_hidden)) * up_hidden).astype(jnp.bfloat16)
    product = jnp.dot(activated, down_ref[...], preferred_element_type=jnp.float32)

    @pl.when(step == 0)
    def _():
        total[...] = product

    @pl.when(step > 0)
    def _():
        total[...] += product

    @pl.when(step == pl.num_programs(0) - 1)
    def _():
        weighted = (total[...] * share_ref[...]).astype(jnp.bfloat16)
        kept = keep_ref.shape[0]
        keep_ref[...] = weighted[:kept]
        send_ref[...] = weighted[kept:]


def run_expert(own, across, beside, share, gate_weight, up_weight, down_weight):
    units = gate_weight.shape[2]
    block = 256 if units % 256 == 0 else units
    rows = own.shape[0] + across.shape[0] + beside.shape[0]
    width = own.shape[1]
    whole = lambda array: pl.BlockSpec(array.shape, lambda f: (0, 0))
    half = jax.ShapeDtypeStruct((rows // 2, width), jnp.bfloat16)
    return pl.pallas_call(
        expert_kernel,
        grid=(units // block,),
        in_specs=[
            whole(own),
            whole(across),
            whole(beside),
            whole(share),
            pl.BlockSpec((None, width, block), lambda f: (0, 0, f)),
            pl.BlockSpec((None, width, block), lambda f: (0, 0, f)),
            pl.BlockSpec((None, block, width), lambda f: (0, f, 0)),
        ],
        out_specs=[pl.BlockSpec((rows // 2, width), lambda f: (0, 0))] * 2,
        out_shape=[half, half],
        scratch_shapes=[pltpu.VMEM((rows, width), jnp.float32)],
        compiler_params=pltpu.CompilerParams(vmem_limit_bytes=VMEM_BYTES),
        cost_estimate=pl.CostEstimate(
            flops=6 * rows * width * units,
            bytes_accessed=6 * width * units + 4 * rows * width,
            transcendentals=rows * units,
        ),
    )(own, across, beside, share, gate_weight, up_weight, down_weight)


def gathered_shards(
    query_rows,
    encoded_key_rows,
    value_matrix_rows,
    output_weight,
    residual,
    norm_gain,
    route_experts,
    route_gates,
    gate_weight,
    up_weight,
    down_weight,
):
    seq_count = lax.axis_size("seq")
    role_count = lax.axis_size("role")
    seq_index = lax.axis_index("seq")
    role_index = lax.axis_index("role")
    batch_count, local_length, query_width = query_rows.shape
    local_heads = query_width // HEAD_WIDTH
    group_width = QUERY_HEADS // KEY_VALUE_HEADS
    at = jnp.stack([seq_index, role_index]).astype(jnp.int32)

    def over_role(array, k):
        return lax.ppermute(array, "role", [(i, i ^ k) for i in range(role_count)])

    def over_seq(array, j):
        return lax.ppermute(array, "seq", [(i, i ^ j) for i in range(seq_count)])

    pieces = []
    for k in range(role_count):
        head = ((role_index ^ k) * local_heads // group_width) * HEAD_WIDTH
        piece = jnp.concatenate(
            [
                lax.dynamic_slice_in_dim(encoded_key_rows, head, HEAD_WIDTH, 2),
                lax.dynamic_slice_in_dim(value_matrix_rows, head, HEAD_WIDTH, 2),
            ],
            axis=2,
        )
        pieces.append(piece if k == 0 else over_role(piece, k))
    block = jnp.concatenate(pieces, axis=1)
    blocks = [block] + [over_seq(block, j) for j in range(1, seq_count)]

    near_proj = [output_weight, over_seq(output_weight, 1)]
    far_proj = []
    for j in range(2, seq_count, 2):
        across = over_seq(output_weight, j)
        far_proj += [across, over_seq(across, 1)]

    expert_count = seq_count * role_count
    chosen = route_experts[0][:, :, None] == jnp.arange(expert_count, dtype=jnp.int32)
    table = jnp.sum(jnp.where(chosen, route_gates[0][:, :, None], 0.0), axis=1)
    table = table.T.reshape(seq_count, role_count, local_length)
    by_role = []
    for k in range(role_count):
        part = lax.dynamic_index_in_dim(table, role_index ^ k, 1, keepdims=False)
        by_role.append(part if k == 0 else over_role(part, k))
    by_role = jnp.stack(by_role, axis=1)
    by_seq = []
    for j in range(seq_count):
        part = lax.dynamic_index_in_dim(by_role, seq_index ^ j, 0, keepdims=False)
        by_seq.append(part if j == 0 else over_seq(part, j))
    order = list(range(0, seq_count, 2)) + list(range(1, seq_count, 2))
    shares = jnp.stack([by_seq[j] for j in order], axis=1)
    shares = shares.reshape(role_count, seq_count * local_length, 1)

    rows = batch_count * local_length
    slot_shape = jax.ShapeDtypeStruct((local_length, 2 * output_weight.shape[1]), jnp.bfloat16)
    attended, *near = pl.pallas_call(
        partial(attend_kernel, seq_count, role_count),
        in_specs=[pl.BlockSpec(memory_space=pltpu.SMEM)] + in_vmem(3 + seq_count),
        out_specs=in_vmem(1 + role_count),
        out_shape=[jax.ShapeDtypeStruct((rows, query_width), jnp.bfloat16)]
        + [slot_shape] * role_count,
        compiler_params=pltpu.CompilerParams(vmem_limit_bytes=VMEM_BYTES),
        cost_estimate=pl.CostEstimate(
            flops=4 * rows * query_width * (local_length * seq_count + output_weight.shape[1]),
            bytes_accessed=2 * (2 * rows * query_width + 2 * output_weight.size),
            transcendentals=rows * local_heads * local_length * seq_count,
        ),
    )(at, query_rows, *blocks, *near_proj)
    near = [near[0]] + [over_role(near[k], k) for k in range(1, role_count)]
    far_width = len(far_proj) * output_weight.shape[1]
    far = pl.pallas_call(
        partial(project_kernel, len(far_proj)),
        in_specs=in_vmem(1 + len(far_proj)),
        out_specs=in_vmem(role_count),
        out_shape=[jax.ShapeDtypeStruct((local_length, far_width), jnp.bfloat16)] * role_count,
        compiler_params=pltpu.CompilerParams(vmem_limit_bytes=VMEM_BYTES),
        cost_estimate=pl.CostEstimate(
            flops=2 * rows * query_width * far_width,
            bytes_accessed=2 * (rows * query_width + query_width * far_width + rows * far_width),
            transcendentals=0,
        ),
    )(attended, *far_proj)
    far = [far[0]] + [over_role(far[k], k) for k in range(1, role_count)]

    width = residual.shape[2]
    hidden, normed = pl.pallas_call(
        partial(norm_kernel, len(near), len(far)),
        in_specs=[pl.BlockSpec(memory_space=pltpu.SMEM)] + in_vmem(2 + len(near) + len(far)),
        out_specs=in_vmem(2),
        out_shape=[
            jax.ShapeDtypeStruct((local_length, width), jnp.float32),
            jax.ShapeDtypeStruct((local_length, width), jnp.bfloat16),
        ],
        compiler_params=pltpu.CompilerParams(vmem_limit_bytes=VMEM_BYTES),
        cost_estimate=pl.CostEstimate(
            flops=16 * local_length * width, bytes_accessed=20 * local_length * width, transcendentals=0
        ),
    )(at, residual, norm_gain.reshape(1, width), *near, *far)

    total = hidden
    for k in range(role_count):
        own = normed if k == 0 else over_role(normed, k)
        across = [over_seq(own, j) for j in range(2, seq_count, 2)]
        across = across[0] if len(across) == 1 else jnp.concatenate(across, axis=0)
        beside = over_seq(jnp.concatenate([own, across], axis=0), 1)
        keep, send = run_expert(
            own, across, beside, shares[k], gate_weight, up_weight, down_weight
        )
        summed = keep.astype(jnp.float32) + over_seq(send, 1).astype(jnp.float32)
        back = summed[:local_length]
        for j in range(2, seq_count, 2):
            start = j // 2 * local_length
            leaving = summed[start : start + local_length].astype(jnp.bfloat16)
            back = back + over_seq(leaving, j).astype(jnp.float32)
        if k > 0:
            back = over_role(back.astype(jnp.bfloat16), k).astype(jnp.float32)
        total = total + back
    return total.astype(jnp.bfloat16).reshape(residual.shape)


def solution(mesh):
    placed = (
        P("groups", "seq", "role"),
        P("groups", ("seq", "role"), None),
        P("groups", ("seq", "role"), None),
        P("role", "seq"),
        P(("groups", "role"), "seq", None),
        P(),
        P(("groups", "role"), "seq", None),
        P(("groups", "role"), "seq", None),
        P(("seq", "role"), None, None),
        P(("seq", "role"), None, None),
        P(("seq", "role"), None, None),
    )
    experts = mesh.shape["seq"] * mesh.shape["role"]
    return jax.shard_map(
        gathered_shards if experts <= 2 * TOPK else routed_shards,
        mesh=mesh,
        in_specs=placed,
        out_specs=P(("groups", "role"), "seq", None),
        check_vma=False,
    )
```

```python
from functools import partial

import jax
import jax.numpy as jnp
from jax import lax
from jax.experimental import pallas as pl
from jax.experimental.pallas import tpu as pltpu
from jax.sharding import PartitionSpec as P

D = 2048
QUERY_HEADS = 32
KEY_VALUE_HEADS = 4
HEAD_WIDTH = 128
TOPK = 8


epsilon = 1e-06
masked_score = -1e30
MIB = 2**20
GATE_COLUMNS = 128
SHORT = pl.CostEstimate(flops=1, bytes_accessed=1, transcendentals=0)


def score_block(queries, every_key, query_position, block_start, block_width, score_scale):
    keys_part = lax.slice_in_dim(every_key, block_start, block_start + block_width, axis=0)
    raw_scores = (
        jnp.einsum("qhd,kd->hqk", queries, keys_part, preferred_element_type=jnp.float32)
        * score_scale
    )
    key_position = block_start + jnp.arange(block_width, dtype=jnp.int32)
    return jnp.where(
        key_position[None, None, :] <= query_position[None, :, None], raw_scores, masked_score
    )


def value_block(rounded, every_value, block_start, block_width):
    prob_block = lax.slice_in_dim(rounded, block_start, block_start + block_width, axis=2)
    values_part = lax.slice_in_dim(every_value, block_start, block_start + block_width, axis=0)
    return jnp.einsum("hqk,kd->qhd", prob_block, values_part, preferred_element_type=jnp.float32)


def routed_shards(
    query_rows,
    encoded_key_rows,
    value_matrix_rows,
    output_weight,
    residual,
    norm_gain,
    route_experts,
    route_gates,
    gate_weight,
    up_weight,
    down_weight,
):
    seq_count = lax.axis_size("seq")
    role_count = lax.axis_size("role")
    seq_index = lax.axis_index("seq")
    role_index = lax.axis_index("role")
    batch_count = query_rows.shape[0]
    local_length = query_rows.shape[1]
    local_heads = query_rows.shape[2] // HEAD_WIDTH
    full_length = local_length * seq_count
    query_group_width = QUERY_HEADS // KEY_VALUE_HEADS
    head_pick = role_index * local_heads // query_group_width
    role_keys, role_values = (
        lax.all_gather(encoded_key_rows, "role", axis=1, tiled=True),
        lax.all_gather(value_matrix_rows, "role", axis=1, tiled=True),
    )
    head_keys = lax.dynamic_slice_in_dim(role_keys, head_pick * HEAD_WIDTH, HEAD_WIDTH, 2)
    head_values = lax.dynamic_slice_in_dim(role_values, head_pick * HEAD_WIDTH, HEAD_WIDTH, 2)
    whole_keys, whole_values, whole_proj = (
        lax.all_gather(head_keys, "seq", axis=1, tiled=True),
        lax.all_gather(head_values, "seq", axis=1, tiled=True),
        lax.all_gather(output_weight, "seq", axis=1, tiled=True),
    )
    key_width = full_length // 8
    score_scale = HEAD_WIDTH ** (-0.5)
    query_position = seq_index * local_length + jnp.arange(local_length, dtype=jnp.int32)
    last_needed = (seq_index + 1) * local_length

    def one_sequence(operands):
        own_queries, every_key, every_value = operands
        queries = own_queries.reshape(local_length, local_heads, HEAD_WIDTH)
        pieces = []
        for number in range(8):
            block_start = number * key_width
            compute = partial(
                score_block, queries, every_key, query_position, block_start, key_width, score_scale
            )
            skipped = partial(
                jnp.full, (local_heads, local_length, key_width), masked_score, jnp.float32
            )
            pieces.append(lax.cond(block_start < last_needed, compute, skipped))
        scores = jnp.concatenate(pieces, axis=2)
        row_peak = jnp.max(scores, axis=2, keepdims=True)
        weights = jnp.exp(scores - row_peak)
        totals = jnp.sum(weights, axis=2, keepdims=True)
        rounded = weights.astype(jnp.bfloat16)
        mixed_rows = jnp.zeros((local_length, local_heads, HEAD_WIDTH), jnp.float32)
        for number in range(8):
            block_start = number * key_width
            product = partial(value_block, rounded, every_value, block_start, key_width)
            nothing = partial(jnp.zeros, (local_length, local_heads, HEAD_WIDTH), jnp.float32)
            mixed_rows = mixed_rows + lax.cond(block_start < last_needed, product, nothing)
        attended = (mixed_rows / totals.transpose(1, 0, 2)).astype(jnp.bfloat16)
        return attended.reshape(local_length, local_heads * HEAD_WIDTH)

    attended = lax.map(one_sequence, (query_rows, whole_keys, whole_values))
    flat_attended = attended.reshape(batch_count * local_length, local_heads * HEAD_WIDTH)
    projected = lax.psum_scatter(
        jnp.dot(flat_attended, whole_proj, preferred_element_type=jnp.float32).astype(jnp.bfloat16),
        "role",
        scatter_dimension=0,
        tiled=True,
    ).astype(jnp.float32)
    hidden = residual[0].astype(jnp.float32) + projected
    variance = jnp.mean(hidden * hidden, axis=-1, keepdims=True)
    normed = (hidden * lax.rsqrt(variance + epsilon) * norm_gain).astype(jnp.bfloat16)
    expert_ids = route_experts.reshape(-1)
    gate_values = route_gates.reshape(-1)
    experts_local = gate_weight.shape[0]
    device_count = seq_count * role_count
    expert_count = experts_local * device_count
    assign = expert_ids.shape[0]
    capacity = assign // expert_count + 1
    onehot = (expert_ids[:, None] == jnp.arange(expert_count, dtype=jnp.int32)[None, :]).astype(
        jnp.int32
    )
    earlier = jnp.cumsum(onehot, axis=0) - onehot
    slot_rank = jnp.sum(earlier * onehot, axis=1)
    slot_index = expert_ids * capacity + slot_rank
    source_token = jnp.arange(assign, dtype=jnp.int32) // TOPK
    slot_token = jnp.zeros((expert_count * capacity,), jnp.int32).at[slot_index].set(source_token)
    slot_used = jnp.zeros((expert_count * capacity,), jnp.bfloat16).at[slot_index].set(1.0)
    outgoing = (normed[slot_token] * slot_used[:, None]).reshape(
        device_count, experts_local, capacity, D
    )
    incoming = lax.all_to_all(outgoing, ("seq", "role"), split_axis=0, concat_axis=0, tiled=True)
    gate_hidden = jnp.einsum(
        "sjcd,jdf->sjcf", incoming, gate_weight, preferred_element_type=jnp.float32
    )
    up_hidden = jnp.einsum(
        "sjcd,jdf->sjcf", incoming, up_weight, preferred_element_type=jnp.float32
    )
    activated = (jax.nn.silu(gate_hidden) * up_hidden).astype(jnp.bfloat16)
    returned = lax.all_to_all(
        jnp.einsum(
            "sjcf,jfd->sjcd", activated, down_weight, preferred_element_type=jnp.float32
        ).astype(jnp.bfloat16),
        ("seq", "role"),
        split_axis=0,
        concat_axis=0,
        tiled=True,
    )
    gathered = returned.reshape(expert_count * capacity, D)[slot_index]
    weighted = gathered.astype(jnp.float32) * gate_values[:, None]
    expert_sum = jnp.sum(weighted.reshape(-1, TOPK, D), axis=1)
    return (hidden + expert_sum).astype(jnp.bfloat16).reshape(residual.shape)


def in_vmem(count):
    return [pl.BlockSpec(memory_space=pltpu.VMEM)] * count


def attend_kernel(seq_count, role_count, at_ref, query_ref, *refs):
    blocks = refs[:seq_count]
    proj_refs = refs[seq_count : seq_count + 2]
    attended_ref = refs[seq_count + 2]
    partial_refs = refs[seq_count + 3 :]
    seq_index, role_index = at_ref[0], at_ref[1]
    local_length = query_ref.shape[1]
    local_heads = query_ref.shape[2] // HEAD_WIDTH
    per_role = local_length // role_count
    rows = local_heads * local_length
    keys_all = seq_count * local_length
    slot = lax.broadcasted_iota(jnp.int32, (rows, keys_all), 1)
    block_number, within = slot // local_length, slot % local_length
    key_position = (
        (seq_index ^ block_number) * local_length
        + (role_index ^ (within // per_role)) * per_role
        + within % per_role
    )
    query_position = (
        seq_index * local_length
        + lax.broadcasted_iota(jnp.int32, (rows, keys_all), 0) % local_length
    )
    seen = key_position <= query_position
    scale = HEAD_WIDTH ** (-0.5)
    for k in range(role_count):
        b = role_index ^ k
        own = query_ref[b]
        queries = jnp.concatenate(
            [own[:, h * HEAD_WIDTH : (h + 1) * HEAD_WIDTH] for h in range(local_heads)], axis=0
        )
        key_value = jnp.concatenate([block[b] for block in blocks], axis=0)
        keys, values = key_value[:, :HEAD_WIDTH], key_value[:, HEAD_WIDTH:]
        scores = lax.dot_general(
            queries, keys, (((1,), (1,)), ((), ())), preferred_element_type=jnp.float32
        )
        scores = jnp.where(seen, scores * scale, masked_score)
        weights = jnp.exp(scores - jnp.max(scores, axis=1, keepdims=True))
        totals = jnp.sum(weights, axis=1, keepdims=True)
        mixed = jnp.dot(weights.astype(jnp.bfloat16), values, preferred_element_type=jnp.float32)
        attended = (mixed / totals).astype(jnp.bfloat16)
        for h in range(local_heads):
            attended_ref[
                k * local_length : (k + 1) * local_length, h * HEAD_WIDTH : (h + 1) * HEAD_WIDTH
            ] = attended[h * local_length : (h + 1) * local_length]
    project_into(role_count, attended_ref, proj_refs, partial_refs)


def project_into(role_count, attended_ref, proj_refs, partial_refs):
    rows = attended_ref.shape[0] // role_count
    odd_ref, *even_refs = partial_refs
    at = 0
    for proj_ref in proj_refs:
        width = proj_ref.shape[1]
        product = jnp.dot(
            attended_ref[...], proj_ref[...], preferred_element_type=jnp.float32
        ).astype(jnp.bfloat16)
        for k in range(role_count):
            part = product[k * rows : (k + 1) * rows]
            if k % 2:
                odd_ref[k // 2 * rows : (k // 2 + 1) * rows, at : at + width] = part
            else:
                even_refs[k // 2][:, at : at + width] = part
        at += width


def project_kernel(weight_count, role_count, attended_ref, *refs):
    project_into(role_count, attended_ref, refs[:weight_count], refs[weight_count:])


def partial_shapes(role_count, rows, width):
    return [jax.ShapeDtypeStruct((rows * (role_count // 2), width), jnp.bfloat16)] + [
        jax.ShapeDtypeStruct((rows, width), jnp.bfloat16)
    ] * (role_count // 2)


def norm_kernel(
    near_count, far_count, at_ref, residual_ref, gain_ref, expert_ref, share_ref, *refs
):
    near = refs[:near_count]
    far = refs[near_count : near_count + far_count]
    hidden_ref, normed_ref = refs[near_count + far_count :]
    seq_index = at_ref[0]
    rows, features = hidden_ref.shape
    width = near[0].shape[1] // 2
    at = 0
    for group in (near, far):
        total = group[0][:rows].astype(jnp.float32)
        for part in group[1:]:
            total = total + part[:rows].astype(jnp.float32)
        for j in range(total.shape[1] // width):
            columns = pl.ds(pl.multiple_of((seq_index ^ at) * width, width), width)
            hidden_ref[:, columns] = total[:, j * width : (j + 1) * width] + residual_ref[
                0, :, columns
            ].astype(jnp.float32)
            at += 1
    hidden = hidden_ref[...]
    variance = jnp.mean(hidden * hidden, axis=1, keepdims=True)
    normed = hidden * lax.rsqrt(variance + epsilon) * gain_ref[...]
    normed_ref[:, :features] = normed.astype(jnp.bfloat16)
    lane = lax.broadcasted_iota(jnp.int32, (rows, GATE_COLUMNS), 1)
    half = GATE_COLUMNS // 2
    shares = jnp.zeros((rows, GATE_COLUMNS), jnp.float32)
    for k in range(expert_ref.shape[2]):
        named = expert_ref[0, :, k : k + 1]
        shares = shares + jnp.where(lane % half == named, share_ref[0, :, k : k + 1], 0.0)
    first = shares.astype(jnp.bfloat16).astype(jnp.float32)
    normed_ref[:, features:] = jnp.where(lane < half, first, shares - first).astype(jnp.bfloat16)


def expert_kernel(token_count, at_ref, *refs):
    token_refs = refs[:token_count]
    gate_ref, up_ref, down_ref, keep_ref, send_ref, activated_ref = refs[token_count:]
    features, units = gate_ref.shape[1:]
    tokens = jnp.concatenate([ref[:, :features] for ref in token_refs], axis=0)
    gates = jnp.concatenate([ref[:, features:] for ref in token_refs], axis=0)
    lane = lax.broadcasted_iota(jnp.int32, gates.shape, 1)
    mine = lane % (GATE_COLUMNS // 2) == at_ref[2]
    share = jnp.sum(jnp.where(mine, gates.astype(jnp.float32), 0.0), axis=1, keepdims=True)
    block = 256 if units % 256 == 0 else units
    for f in range(0, units, block):
        gate_hidden = jnp.dot(
            tokens, gate_ref[0, :, f : f + block], preferred_element_type=jnp.float32
        )
        up_hidden = jnp.dot(tokens, up_ref[0, :, f : f + block], preferred_element_type=jnp.float32)
        activated_ref[:, f : f + block] = (
            gate_hidden / (1.0 + jnp.exp(-gate_hidden)) * up_hidden
        ).astype(jnp.bfloat16)
    kept = keep_ref.shape[0]
    block = 512 if features % 512 == 0 else features
    for c in range(0, features, block):
        product = jnp.dot(
            activated_ref[...], down_ref[0, :, c : c + block], preferred_element_type=jnp.float32
        )
        product = (product * share).astype(jnp.bfloat16)
        keep_ref[:, c : c + block] = product[:kept]
        send_ref[:, c : c + block] = product[kept:]


def run_expert(at, tokens, gate_weight, up_weight, down_weight):
    units = gate_weight.shape[2]
    width = gate_weight.shape[1]
    rows = sum(part.shape[0] for part in tokens)
    half = jax.ShapeDtypeStruct((rows // 2, width), jnp.bfloat16)
    return pl.pallas_call(
        partial(expert_kernel, len(tokens)),
        in_specs=[pl.BlockSpec(memory_space=pltpu.SMEM)] + in_vmem(len(tokens) + 3),
        out_specs=in_vmem(2),
        out_shape=[half, half],
        scratch_shapes=[pltpu.VMEM((rows, units), jnp.bfloat16)],
        compiler_params=pltpu.CompilerParams(vmem_limit_bytes=24 * MIB),
        cost_estimate=pl.CostEstimate(
            flops=6 * rows * width * units, bytes_accessed=4 * rows * width, transcendentals=0
        ),
    )(at, *tokens, gate_weight, up_weight, down_weight)


def after(array, *others):
    return lax.optimization_barrier((array, *others))[0]


def added(terms):
    total = terms[0].astype(jnp.float32)
    for term in terms[1:]:
        total = total + term.astype(jnp.float32)
    return total


def gathered_shards(
    query_rows,
    encoded_key_rows,
    value_matrix_rows,
    output_weight,
    residual,
    norm_gain,
    route_experts,
    route_gates,
    gate_weight,
    up_weight,
    down_weight,
):
    seq_count = lax.axis_size("seq")
    role_count = lax.axis_size("role")
    seq_index = lax.axis_index("seq")
    role_index = lax.axis_index("role")
    batch_count, local_length, query_width = query_rows.shape
    local_heads = query_width // HEAD_WIDTH
    group_width = QUERY_HEADS // KEY_VALUE_HEADS
    role_bits = [1 << n for n in range(role_count.bit_length() - 1)]
    at = jnp.stack([seq_index, role_index, seq_index * role_count + role_index]).astype(jnp.int32)

    def over_role(array, k):
        return lax.ppermute(array, "role", [(i, i ^ k) for i in range(role_count)])

    def over_seq(array, j):
        return lax.ppermute(array, "seq", [(i, i ^ j) for i in range(seq_count)])

    pieces = []
    for k in range(role_count):
        head = ((role_index ^ k) * local_heads // group_width) * HEAD_WIDTH
        piece = jnp.concatenate(
            [
                lax.dynamic_slice_in_dim(encoded_key_rows, head, HEAD_WIDTH, 2),
                lax.dynamic_slice_in_dim(value_matrix_rows, head, HEAD_WIDTH, 2),
            ],
            axis=2,
        )
        pieces.append(piece if k == 0 else over_role(piece, k))
    block = jnp.concatenate(pieces, axis=1)
    same_core = [block] + [over_seq(block, j) for j in range(2, seq_count, 2)]
    blocks = []
    for part in same_core:
        blocks += [part, over_seq(part, 1)]

    near_proj = [output_weight, over_seq(output_weight, 1)]
    across_proj = [over_seq(output_weight, j) for j in range(2, seq_count, 2)]

    rows = batch_count * local_length
    near_width = 2 * output_weight.shape[1]
    attended, *near = pl.pallas_call(
        partial(attend_kernel, seq_count, role_count),
        in_specs=[pl.BlockSpec(memory_space=pltpu.SMEM)] + in_vmem(3 + seq_count),
        out_specs=in_vmem(2 + role_count // 2),
        out_shape=[jax.ShapeDtypeStruct((rows, query_width), jnp.bfloat16)]
        + partial_shapes(role_count, local_length, near_width),
        compiler_params=pltpu.CompilerParams(vmem_limit_bytes=16 * MIB),
        cost_estimate=SHORT,
    )(at, query_rows, *blocks, *near_proj)
    far_proj = []
    for part in across_proj:
        part = after(part, attended)
        far_proj += [part, over_seq(part, 1)]
    far_width = len(far_proj) * output_weight.shape[1]
    far = pl.pallas_call(
        partial(project_kernel, len(far_proj), role_count),
        in_specs=in_vmem(1 + len(far_proj)),
        out_specs=in_vmem(1 + role_count // 2),
        out_shape=partial_shapes(role_count, local_length, far_width),
        compiler_params=pltpu.CompilerParams(vmem_limit_bytes=16 * MIB),
        cost_estimate=SHORT,
    )(attended, *far_proj)

    def summed_over_role(parts):
        odd, *even = parts
        slots = {2 * n: [part] for n, part in enumerate(even)}
        for bit in role_bits:
            if bit == 1:
                sent = list(range(1, role_count, 2))
                leaving = odd
            else:
                sent = [k for k in sorted(slots) if k & bit]
                leaving = [added(slots.pop(k)).astype(jnp.bfloat16) for k in sent]
                leaving = leaving[0] if len(leaving) == 1 else jnp.concatenate(leaving, axis=0)
            came = over_role(leaving, bit)
            for n, k in enumerate(sent):
                slots[k ^ bit].append(came[n * local_length : (n + 1) * local_length])
        return slots[0]

    near, far = summed_over_role(near), summed_over_role(far)
    width = residual.shape[2]
    hidden, normed = pl.pallas_call(
        partial(norm_kernel, len(near), len(far)),
        in_specs=[pl.BlockSpec(memory_space=pltpu.SMEM)] + in_vmem(4 + len(near) + len(far)),
        out_specs=in_vmem(2),
        out_shape=[
            jax.ShapeDtypeStruct((local_length, width), jnp.float32),
            jax.ShapeDtypeStruct((local_length, width + GATE_COLUMNS), jnp.bfloat16),
        ],
        compiler_params=pltpu.CompilerParams(vmem_limit_bytes=12 * MIB),
        cost_estimate=SHORT,
    )(at, residual, norm_gain.reshape(1, width), route_experts, route_gates, *near, *far)

    across_steps = range(2, seq_count, 2)

    def walk(k, bits):
        found = [k]
        for n, bit in enumerate(bits):
            found += walk(k | bit, bits[n + 1 :])
        return found

    order = walk(0, role_bits[::-1])

    def across(part):
        return [over_seq(part, j) for j in across_steps]

    def expert(parts, *before):
        tokens = parts + [over_seq(part, 1) for part in parts]
        if before:
            tokens = lax.optimization_barrier((*tokens, *before))[: len(tokens)]
        return run_expert(at, tokens, gate_weight, up_weight, down_weight)

    planes = {bit: over_role(normed, bit) for bit in role_bits}
    planes[0] = normed
    same_core = {0: [normed] + across(normed)}
    keep, send = {}, {}
    keep[0], send[0] = expert(same_core[0], *(planes[bit] for bit in role_bits))
    for n, k in enumerate(order[1:]):
        if n > 0:
            planes[k] = after(planes[k], planes[order[n]])
        for bit in reversed(role_bits):
            if bit < (k & -k):
                planes[k | bit] = over_role(planes[k], bit)
        same_core[k] = [planes[k]] + across(planes[k])

    if role_count > 2:
        send[0] = after(send[0], planes[order[2]], *same_core[order[1]][1:])
    slots, leaving = {}, {}

    def give_back(k, *before):
        came = over_seq(after(send[k], *before) if before else send[k], 1)
        slots[k], leaving[k] = [keep[k][:local_length], came[:local_length]], []
        for n, j in enumerate(across_steps):
            chunk = slice((n + 1) * local_length, (n + 2) * local_length)
            leaving[k].append(added([keep[k][chunk], came[chunk]]).astype(jnp.bfloat16))
            slots[k].append(over_seq(leaving[k][-1], j))

    for n, k in enumerate(order[1:], 1):
        following = order[n + 1] if n + 1 < role_count else None
        before = [] if following is None else [planes[following]]
        before += leaving[order[n - 1]] if n > 1 else [keep[0]]
        keep[k], send[k] = expert(same_core[k], *before)
        give_back(k, *(slots[order[1]][2:] if following is None else same_core[following][1:]))
    give_back(0, *leaving[order[-1]])
    for bit in role_bits:
        for k in [k for k in sorted(slots, reverse=True) if k & bit]:
            slots[k ^ bit].append(over_role(added(slots.pop(k)).astype(jnp.bfloat16), bit))
    return added([hidden] + slots[0]).astype(jnp.bfloat16).reshape(residual.shape)


def solution(mesh):
    placed = (
        P("groups", "seq", "role"),
        P("groups", ("seq", "role"), None),
        P("groups", ("seq", "role"), None),
        P("role", "seq"),
        P(("groups", "role"), "seq", None),
        P(),
        P(("groups", "role"), "seq", None),
        P(("groups", "role"), "seq", None),
        P(("seq", "role"), None, None),
        P(("seq", "role"), None, None),
        P(("seq", "role"), None, None),
    )
    experts = mesh.shape["seq"] * mesh.shape["role"]
    return jax.shard_map(
        gathered_shards if experts <= 2 * TOPK else routed_shards,
        mesh=mesh,
        in_specs=placed,
        out_specs=P(("groups", "role"), "seq", None),
        check_vma=False,
    )
```

```python
from functools import partial

import jax
import jax.numpy as jnp
from jax import lax
from jax.experimental import pallas as pl
from jax.experimental.pallas import tpu as pltpu
from jax.sharding import PartitionSpec as P

D = 2048
QUERY_HEADS = 32
KEY_VALUE_HEADS = 4
HEAD_WIDTH = 128
TOPK = 8


epsilon = 1e-06
masked_score = -1e30
EXPERT_VMEM = 16 * 2**20
SMALL_VMEM = 12 * 2**20
COPY_VMEM = 4 * 2**20
GATE_COLUMNS = 128
SHORT = pl.CostEstimate(flops=2 * 10**9, bytes_accessed=4 * 2**20, transcendentals=0)


def score_block(queries, every_key, query_position, block_start, block_width, score_scale):
    keys_part = lax.slice_in_dim(every_key, block_start, block_start + block_width, axis=0)
    raw_scores = (
        jnp.einsum("qhd,kd->hqk", queries, keys_part, preferred_element_type=jnp.float32)
        * score_scale
    )
    key_position = block_start + jnp.arange(block_width, dtype=jnp.int32)
    return jnp.where(
        key_position[None, None, :] <= query_position[None, :, None], raw_scores, masked_score
    )


def value_block(rounded, every_value, block_start, block_width):
    prob_block = lax.slice_in_dim(rounded, block_start, block_start + block_width, axis=2)
    values_part = lax.slice_in_dim(every_value, block_start, block_start + block_width, axis=0)
    return jnp.einsum("hqk,kd->qhd", prob_block, values_part, preferred_element_type=jnp.float32)


def routed_shards(
    query_rows,
    encoded_key_rows,
    value_matrix_rows,
    output_weight,
    residual,
    norm_gain,
    route_experts,
    route_gates,
    gate_weight,
    up_weight,
    down_weight,
):
    seq_count = lax.axis_size("seq")
    role_count = lax.axis_size("role")
    seq_index = lax.axis_index("seq")
    role_index = lax.axis_index("role")
    batch_count = query_rows.shape[0]
    local_length = query_rows.shape[1]
    local_heads = query_rows.shape[2] // HEAD_WIDTH
    full_length = local_length * seq_count
    query_group_width = QUERY_HEADS // KEY_VALUE_HEADS
    head_pick = role_index * local_heads // query_group_width
    role_keys, role_values = (
        lax.all_gather(encoded_key_rows, "role", axis=1, tiled=True),
        lax.all_gather(value_matrix_rows, "role", axis=1, tiled=True),
    )
    head_keys = lax.dynamic_slice_in_dim(role_keys, head_pick * HEAD_WIDTH, HEAD_WIDTH, 2)
    head_values = lax.dynamic_slice_in_dim(role_values, head_pick * HEAD_WIDTH, HEAD_WIDTH, 2)
    whole_keys, whole_values, whole_proj = (
        lax.all_gather(head_keys, "seq", axis=1, tiled=True),
        lax.all_gather(head_values, "seq", axis=1, tiled=True),
        lax.all_gather(output_weight, "seq", axis=1, tiled=True),
    )
    key_width = full_length // 8
    score_scale = HEAD_WIDTH ** (-0.5)
    query_position = seq_index * local_length + jnp.arange(local_length, dtype=jnp.int32)
    last_needed = (seq_index + 1) * local_length

    def one_sequence(operands):
        own_queries, every_key, every_value = operands
        queries = own_queries.reshape(local_length, local_heads, HEAD_WIDTH)
        pieces = []
        for number in range(8):
            block_start = number * key_width
            compute = partial(
                score_block, queries, every_key, query_position, block_start, key_width, score_scale
            )
            skipped = partial(
                jnp.full, (local_heads, local_length, key_width), masked_score, jnp.float32
            )
            pieces.append(lax.cond(block_start < last_needed, compute, skipped))
        scores = jnp.concatenate(pieces, axis=2)
        row_peak = jnp.max(scores, axis=2, keepdims=True)
        weights = jnp.exp(scores - row_peak)
        totals = jnp.sum(weights, axis=2, keepdims=True)
        rounded = weights.astype(jnp.bfloat16)
        mixed_rows = jnp.zeros((local_length, local_heads, HEAD_WIDTH), jnp.float32)
        for number in range(8):
            block_start = number * key_width
            product = partial(value_block, rounded, every_value, block_start, key_width)
            nothing = partial(jnp.zeros, (local_length, local_heads, HEAD_WIDTH), jnp.float32)
            mixed_rows = mixed_rows + lax.cond(block_start < last_needed, product, nothing)
        attended = (mixed_rows / totals.transpose(1, 0, 2)).astype(jnp.bfloat16)
        return attended.reshape(local_length, local_heads * HEAD_WIDTH)

    attended = lax.map(one_sequence, (query_rows, whole_keys, whole_values))
    flat_attended = attended.reshape(batch_count * local_length, local_heads * HEAD_WIDTH)
    projected = lax.psum_scatter(
        jnp.dot(flat_attended, whole_proj, preferred_element_type=jnp.float32).astype(jnp.bfloat16),
        "role",
        scatter_dimension=0,
        tiled=True,
    ).astype(jnp.float32)
    hidden = residual[0].astype(jnp.float32) + projected
    variance = jnp.mean(hidden * hidden, axis=-1, keepdims=True)
    normed = (hidden * lax.rsqrt(variance + epsilon) * norm_gain).astype(jnp.bfloat16)
    expert_ids = route_experts.reshape(-1)
    gate_values = route_gates.reshape(-1)
    experts_local = gate_weight.shape[0]
    device_count = seq_count * role_count
    expert_count = experts_local * device_count
    assign = expert_ids.shape[0]
    capacity = assign // expert_count + 1
    onehot = (expert_ids[:, None] == jnp.arange(expert_count, dtype=jnp.int32)[None, :]).astype(
        jnp.int32
    )
    earlier = jnp.cumsum(onehot, axis=0) - onehot
    slot_rank = jnp.sum(earlier * onehot, axis=1)
    slot_index = expert_ids * capacity + slot_rank
    source_token = jnp.arange(assign, dtype=jnp.int32) // TOPK
    slot_token = jnp.zeros((expert_count * capacity,), jnp.int32).at[slot_index].set(source_token)
    slot_used = jnp.zeros((expert_count * capacity,), jnp.bfloat16).at[slot_index].set(1.0)
    outgoing = (normed[slot_token] * slot_used[:, None]).reshape(
        device_count, experts_local, capacity, D
    )
    incoming = lax.all_to_all(outgoing, ("seq", "role"), split_axis=0, concat_axis=0, tiled=True)
    gate_hidden = jnp.einsum(
        "sjcd,jdf->sjcf", incoming, gate_weight, preferred_element_type=jnp.float32
    )
    up_hidden = jnp.einsum(
        "sjcd,jdf->sjcf", incoming, up_weight, preferred_element_type=jnp.float32
    )
    activated = (jax.nn.silu(gate_hidden) * up_hidden).astype(jnp.bfloat16)
    returned = lax.all_to_all(
        jnp.einsum(
            "sjcf,jfd->sjcd", activated, down_weight, preferred_element_type=jnp.float32
        ).astype(jnp.bfloat16),
        ("seq", "role"),
        split_axis=0,
        concat_axis=0,
        tiled=True,
    )
    gathered = returned.reshape(expert_count * capacity, D)[slot_index]
    weighted = gathered.astype(jnp.float32) * gate_values[:, None]
    expert_sum = jnp.sum(weighted.reshape(-1, TOPK, D), axis=1)
    return (hidden + expert_sum).astype(jnp.bfloat16).reshape(residual.shape)


def in_vmem(count):
    return [pl.BlockSpec(memory_space=pltpu.VMEM)] * count


def attend_kernel(seq_count, role_count, at_ref, query_ref, own_proj_ref, *refs):
    refs = refs[2:]
    blocks = refs[:seq_count]
    beside_proj_ref, attended_ref = refs[seq_count : seq_count + 2]
    partial_refs = refs[seq_count + 2 :]
    seq_index, role_index = at_ref[0], at_ref[1]
    local_length = query_ref.shape[1]
    local_heads = query_ref.shape[2] // HEAD_WIDTH
    per_role = local_length // role_count
    rows = local_heads * local_length
    keys_all = seq_count * local_length
    slot = lax.broadcasted_iota(jnp.int32, (rows, keys_all), 1)
    block_number, within = slot // local_length, slot % local_length
    key_position = (
        (seq_index ^ block_number) * local_length
        + (role_index ^ (within // per_role)) * per_role
        + within % per_role
    )
    query_position = (
        seq_index * local_length
        + lax.broadcasted_iota(jnp.int32, (rows, keys_all), 0) % local_length
    )
    seen = key_position <= query_position
    scale = HEAD_WIDTH ** (-0.5)
    for k in range(role_count):
        b = role_index ^ k
        own = query_ref[b]
        queries = jnp.concatenate(
            [own[:, h * HEAD_WIDTH : (h + 1) * HEAD_WIDTH] for h in range(local_heads)], axis=0
        )
        key_value = jnp.concatenate([block[b] for block in blocks], axis=0)
        keys, values = key_value[:, :HEAD_WIDTH], key_value[:, HEAD_WIDTH:]
        scores = lax.dot_general(
            queries, keys, (((1,), (1,)), ((), ())), preferred_element_type=jnp.float32
        )
        scores = jnp.where(seen, scores * scale, masked_score)
        weights = jnp.exp(scores - jnp.max(scores, axis=1, keepdims=True))
        totals = jnp.sum(weights, axis=1, keepdims=True)
        mixed = jnp.dot(weights.astype(jnp.bfloat16), values, preferred_element_type=jnp.float32)
        attended = (mixed / totals).astype(jnp.bfloat16)
        for h in range(local_heads):
            attended_ref[
                k * local_length : (k + 1) * local_length, h * HEAD_WIDTH : (h + 1) * HEAD_WIDTH
            ] = attended[h * local_length : (h + 1) * local_length]
    project_into(role_count, attended_ref, [[own_proj_ref], [beside_proj_ref]], partial_refs)


def join_kernel(count, *refs):
    out_ref, token_ref = refs[-2:]
    token_ref[...] = jnp.zeros_like(token_ref)
    at = 0
    for ref in refs[:count]:
        size = ref.shape[1]
        out_ref[:, at : at + size, :] = ref[...]
        at += size


def rows_kernel(first, from_ref, *refs):
    to_ref, sem = refs[-2:]
    copy = pltpu.make_async_copy(from_ref.at[pl.ds(first, to_ref.shape[0]), :], to_ref, sem)
    copy.start()
    copy.wait()


def role_groups(role_count):
    last = role_count // 2
    bits = [1 << n for n in range(last.bit_length() - 1)]
    return [[k for k in range(role_count) if k & -k == bit] for bit in bits] + [[0, last]]


def project_into(role_count, attended_ref, proj_blocks, partial_refs):
    rows = attended_ref.shape[0] // role_count
    at = 0
    for pieces in proj_blocks:
        width = pieces[0].shape[1]
        product, start = None, 0
        for piece in pieces:
            depth = piece.shape[0]
            term = jnp.dot(
                attended_ref[:, start : start + depth],
                piece[...],
                preferred_element_type=jnp.float32,
            )
            product = term if product is None else product + term
            start += depth
        product = product.astype(jnp.bfloat16)
        for group, partial_ref in zip(role_groups(role_count), partial_refs):
            for n, k in enumerate(group):
                partial_ref[n * rows : (n + 1) * rows, at : at + width] = product[
                    k * rows : (k + 1) * rows
                ]
        at += width


def project_kernel(piece_count, role_count, attended_ref, *refs):
    partial_refs = refs[-len(role_groups(role_count)) :]
    proj_refs = refs[1 : -len(partial_refs)]
    blocks = [proj_refs[n : n + piece_count] for n in range(0, len(proj_refs), piece_count)]
    project_into(role_count, attended_ref, blocks, partial_refs)


def partial_shapes(role_count, rows, width):
    return [
        jax.ShapeDtypeStruct((rows * len(group), width), jnp.bfloat16)
        for group in role_groups(role_count)
    ]


def norm_kernel(block_width, at_ref, residual_ref, gain_ref, route_ref, other_route_ref, *refs):
    *refs, hidden_ref, normed_ref, other_normed_ref, other_ref = refs
    seq_index = at_ref[0]
    rows, features = hidden_ref.shape
    at = 0
    for sent, came, *terms in (refs[: len(refs) // 2], refs[len(refs) // 2 :]):
        total = came[rows:].astype(jnp.float32)
        for term in terms:
            total = total + term[:rows].astype(jnp.float32)
        other = sent[rows:].astype(jnp.float32) + came[:rows].astype(jnp.float32)
        for j in range(total.shape[1] // block_width):
            block = slice(j * block_width, (j + 1) * block_width)
            start = pl.multiple_of((seq_index ^ at) * block_width, block_width)
            columns = pl.ds(start, block_width)
            hidden_ref[:, columns] = total[:, block] + residual_ref[:, columns].astype(jnp.float32)
            other_ref[:, columns] = other[:, block]
            at += 1
    lane = lax.broadcasted_iota(jnp.int32, (rows, GATE_COLUMNS), 1)
    half = GATE_COLUMNS // 2
    expert = (lane % half).astype(jnp.float32)
    for from_ref, routes, to_ref in (
        (hidden_ref, route_ref, normed_ref),
        (other_ref, other_route_ref, other_normed_ref),
    ):
        hidden = from_ref[...]
        variance = jnp.mean(hidden * hidden, axis=1, keepdims=True)
        normed = hidden * lax.rsqrt(variance + epsilon) * gain_ref[...]
        to_ref[:, :features] = normed.astype(jnp.bfloat16)
        shares = jnp.zeros((rows, GATE_COLUMNS), jnp.float32)
        count = routes.shape[1] // 2
        for k in range(count):
            named = routes[:, k : k + 1]
            shares = shares + jnp.where(expert == named, routes[:, count + k : count + k + 1], 0.0)
        first = shares.astype(jnp.bfloat16).astype(jnp.float32)
        to_ref[:, features:] = jnp.where(lane < half, first, shares - first).astype(jnp.bfloat16)


def expert_kernel(token_count, at_ref, *refs):
    token_refs = refs[:token_count]
    gate_ref, up_ref, down_ref, keep_ref, send_ref, activated_ref = refs[token_count:]
    features, units = gate_ref.shape[1:]
    tokens = jnp.concatenate([ref[:, :features] for ref in token_refs], axis=0)
    gates = jnp.concatenate([ref[:, features:] for ref in token_refs], axis=0)
    lane = lax.broadcasted_iota(jnp.int32, gates.shape, 1)
    mine = lane % (GATE_COLUMNS // 2) == at_ref[2]
    share = jnp.sum(jnp.where(mine, gates.astype(jnp.float32), 0.0), axis=1, keepdims=True)
    block = 256 if units % 256 == 0 else units
    for f in range(0, units, block):
        gate_hidden = jnp.dot(
            tokens, gate_ref[0, :, f : f + block], preferred_element_type=jnp.float32
        )
        up_hidden = jnp.dot(tokens, up_ref[0, :, f : f + block], preferred_element_type=jnp.float32)
        activated_ref[:, f : f + block] = (
            gate_hidden / (1.0 + jnp.exp(-gate_hidden)) * up_hidden
        ).astype(jnp.bfloat16)
    kept = keep_ref.shape[0]
    block = 512 if features % 512 == 0 else features
    for c in range(0, features, block):
        product = jnp.dot(
            activated_ref[...], down_ref[0, :, c : c + block], preferred_element_type=jnp.float32
        )
        product = (product * share).astype(jnp.bfloat16)
        keep_ref[:, c : c + block] = product[:kept]
        send_ref[:, c : c + block] = product[kept:]


def run_expert(at, tokens, gate_weight, up_weight, down_weight):
    units = gate_weight.shape[2]
    width = gate_weight.shape[1]
    rows = sum(part.shape[0] for part in tokens)
    half = jax.ShapeDtypeStruct((rows // 2, width), jnp.bfloat16)
    return pl.pallas_call(
        partial(expert_kernel, len(tokens)),
        in_specs=[pl.BlockSpec(memory_space=pltpu.SMEM)] + in_vmem(len(tokens) + 3),
        out_specs=in_vmem(2),
        out_shape=[half, half],
        scratch_shapes=[pltpu.VMEM((rows, units), jnp.bfloat16)],
        compiler_params=pltpu.CompilerParams(vmem_limit_bytes=EXPERT_VMEM),
        cost_estimate=pl.CostEstimate(
            flops=6 * rows * width * units, bytes_accessed=4 * rows * width, transcendentals=0
        ),
    )(at, *tokens, gate_weight, up_weight, down_weight)


def after(array, *others):
    return lax.optimization_barrier((array, *others))[0]


def added(terms):
    total = terms[0].astype(jnp.float32)
    for term in terms[1:]:
        total = total + term.astype(jnp.float32)
    return total


def gathered_shards(
    query_rows,
    encoded_key_rows,
    value_matrix_rows,
    output_weight,
    residual,
    norm_gain,
    route_experts,
    route_gates,
    gate_weight,
    up_weight,
    down_weight,
):
    seq_count = lax.axis_size("seq")
    role_count = lax.axis_size("role")
    seq_index = lax.axis_index("seq")
    role_index = lax.axis_index("role")
    batch_count, local_length, query_width = query_rows.shape
    local_heads = query_width // HEAD_WIDTH
    group_width = QUERY_HEADS // KEY_VALUE_HEADS
    role_bits = [1 << n for n in range(role_count.bit_length() - 1)]
    at = jnp.stack([seq_index, role_index, seq_index * role_count + role_index]).astype(jnp.int32)

    def over_role(array, k):
        return lax.ppermute(array, "role", [(i, i ^ k) for i in range(role_count)])

    def over_seq(array, j):
        return lax.ppermute(array, "seq", [(i, i ^ j) for i in range(seq_count)])

    beside_proj = over_seq(output_weight, 1)
    first_rows = output_weight.shape[0] // 4
    block_width = output_weight.shape[1]
    first_proj = output_weight[:first_rows]
    across_proj = [[over_seq(first_proj, j)] for j in range(2, seq_count, 2)]

    pieces = []
    for k in range(role_count):
        head = ((role_index ^ k) * local_heads // group_width) * HEAD_WIDTH
        piece = jnp.concatenate(
            [
                lax.dynamic_slice_in_dim(encoded_key_rows, head, HEAD_WIDTH, 2),
                lax.dynamic_slice_in_dim(value_matrix_rows, head, HEAD_WIDTH, 2),
            ],
            axis=2,
        )
        pieces.append(piece if k == 0 else over_role(piece, k))
    block, block_token = pl.pallas_call(
        partial(join_kernel, len(pieces)),
        in_specs=in_vmem(len(pieces)) + [pl.BlockSpec(memory_space=pl.ANY)] * len(across_proj),
        out_specs=in_vmem(2),
        out_shape=[
            jax.ShapeDtypeStruct((batch_count, local_length, 2 * HEAD_WIDTH), jnp.bfloat16),
            jax.ShapeDtypeStruct((8, 128), jnp.float32),
        ],
        compiler_params=pltpu.CompilerParams(vmem_limit_bytes=COPY_VMEM),
        cost_estimate=SHORT,
    )(*pieces, *(parts[0] for parts in across_proj))
    same_core = [block] + [over_seq(block, j) for j in range(2, seq_count, 2)]
    blocks = []
    for part in same_core:
        blocks += [part, over_seq(part, 1)]
    rest_proj = after(output_weight[first_rows:], block_token)
    for n, j in enumerate(range(2, seq_count, 2)):
        across_proj[n].append(over_seq(rest_proj, j))

    last = role_count // 2
    routes = jnp.concatenate([route_experts[0].astype(jnp.float32), route_gates[0]], axis=1)
    other_routes = over_role(routes, last)
    residual_blocks = [
        lax.dynamic_slice_in_dim(residual[0], (seq_index ^ j) * block_width, block_width, 1)
        for j in range(seq_count)
    ]
    near_residual = jnp.concatenate(residual_blocks[:2], axis=1)
    far_residual = jnp.concatenate(residual_blocks[2:], axis=1)

    rows = batch_count * local_length
    near_width = 2 * output_weight.shape[1]
    groups = role_groups(role_count)
    attended, *near = pl.pallas_call(
        partial(attend_kernel, seq_count, role_count),
        in_specs=[pl.BlockSpec(memory_space=pltpu.SMEM)]
        + in_vmem(2)
        + [pl.BlockSpec(memory_space=pl.ANY)] * 2
        + in_vmem(1 + seq_count),
        out_specs=in_vmem(1 + len(groups)),
        out_shape=[jax.ShapeDtypeStruct((rows, query_width), jnp.bfloat16)]
        + partial_shapes(role_count, local_length, near_width),
        compiler_params=pltpu.CompilerParams(vmem_limit_bytes=SMALL_VMEM),
        cost_estimate=SHORT,
    )(at, query_rows, output_weight, block_token, other_routes, *blocks, beside_proj)
    def summed_over_role(parts, extra):
        terms = [[part] for part in parts]
        for n, group in enumerate(groups[:-1]):
            bit = 1 << n
            leaving = terms[n][0] if len(terms[n]) == 1 else added(terms[n]).astype(jnp.bfloat16)
            came = over_role(leaving, bit)
            for m in range(n + 1, len(groups)):
                at_rows = [group.index(k ^ bit) for k in groups[m]]
                if at_rows == list(range(len(group))):
                    terms[m].append(came)
                else:
                    split = [came[i * local_length : (i + 1) * local_length] for i in at_rows]
                    terms[m].append(jnp.concatenate(split, axis=0))
        extra = jnp.pad(extra, ((0, local_length), (0, 0)))
        sent = added(terms[-1] + [extra]).astype(jnp.bfloat16)
        return terms[-1], sent, over_role(sent, last)

    near_terms, *near_last = summed_over_role(near, near_residual)
    far_proj = []
    for parts in across_proj:
        parts = [after(part, near_last[0]) for part in parts]
        far_proj += parts + [over_seq(part, 1) for part in parts]
    far_width = 2 * len(across_proj) * output_weight.shape[1]
    far = pl.pallas_call(
        partial(project_kernel, len(across_proj[0]), role_count),
        in_specs=in_vmem(1) + [pl.BlockSpec(memory_space=pl.ANY)] + in_vmem(len(far_proj)),
        out_specs=in_vmem(len(groups)),
        out_shape=partial_shapes(role_count, local_length, far_width),
        compiler_params=pltpu.CompilerParams(vmem_limit_bytes=SMALL_VMEM),
        cost_estimate=SHORT,
    )(attended, near_last[1], *far_proj)

    width = residual.shape[2]
    row_shape = jax.ShapeDtypeStruct((local_length, width + GATE_COLUMNS), jnp.bfloat16)
    far_terms, *far_last = summed_over_role(far, far_residual)
    norm_args = [residual[0], norm_gain.reshape(1, width), routes, other_routes]
    norm_args += near_last + near_terms + far_last + far_terms
    hidden, normed, other_normed = pl.pallas_call(
        partial(norm_kernel, block_width),
        in_specs=[pl.BlockSpec(memory_space=pltpu.SMEM)] + in_vmem(len(norm_args)),
        out_specs=in_vmem(3),
        out_shape=[
            jax.ShapeDtypeStruct((local_length, width), jnp.float32),
            row_shape,
            row_shape,
        ],
        scratch_shapes=[pltpu.VMEM((local_length, width), jnp.float32)],
        compiler_params=pltpu.CompilerParams(vmem_limit_bytes=SMALL_VMEM),
        cost_estimate=SHORT,
    )(at, *norm_args)

    across_steps = range(2, seq_count, 2)

    def walk(k, bits):
        found = [k]
        for n, bit in enumerate(bits):
            found += walk(k | bit, bits[n + 1 :])
        return found

    def across(part):
        return [over_seq(part, j) for j in across_steps]

    def expert(k, before, *others):
        late = [after(part, *before) for part in crossed[k]] if before else crossed[k]
        tokens = [planes[k]] + late
        tokens += [over_seq(part, 1) for part in tokens]
        if others:
            tokens = lax.optimization_barrier((*tokens, *others))[: len(tokens)]
        return run_expert(at, tokens, gate_weight, up_weight, down_weight)

    def combine(k, *before):
        came = over_seq(after(send[k], *before) if before else send[k], 1)
        sums = []
        for n in range(len(across_steps)):
            chunk = slice((n + 1) * local_length, (n + 2) * local_length)
            sums.append(added([keep[k][chunk], came[chunk]]).astype(jnp.bfloat16))
        return [keep[k][:local_length], came[:local_length]], sums

    order = walk(0, role_bits[::-1])
    planes = {0: normed, last: other_normed}
    crossed = {0: across(normed)}
    for k in order:
        if k not in planes:
            bit = k & -k
            planes[k] = over_role(planes[k ^ bit], bit)
    for n, k in enumerate(order[1:], 1):
        if n > 2:
            planes[k] = after(planes[k], planes[order[n - 1]])
        crossed[k] = across(planes[k])
    keep, send, slots, leaving = {}, {}, {}, {}
    for n, k in enumerate(order):
        others = []
        if n > 0 and n + 1 == role_count:
            slots[order[n - 1]], leaving[order[n - 1]] = combine(order[n - 1])
            others = leaving[order[n - 1]]
        before = [keep[order[n - 1]]] if n > 0 else []
        if n + 2 < role_count:
            before.append(planes[order[n + 2]])
        keep[k], send[k] = expert(k, before, *others)
        if n > 0 and n + 2 == role_count:
            send[k] = after(send[k], *crossed[order[n + 1]])
    passed = first_passed = []
    for k in sorted(send, reverse=True):
        if k not in slots:
            slots[k], leaving[k] = combine(k, *(first_passed if k == order[-1] else []))
        if passed:
            leaving[k] = [after(part, *passed) for part in leaving[k]]
        came = [over_seq(part, j) for part, j in zip(leaving[k], across_steps)]
        slots[k] += came
        passed = came if k > 1 else leaving[k]
        first_passed = first_passed or passed
    for bit in role_bits:
        for k in [k for k in sorted(slots, reverse=True) if k & bit]:
            slots[k ^ bit].append(over_role(added(slots.pop(k)).astype(jnp.bfloat16), bit))
    return added([hidden] + slots[0]).astype(jnp.bfloat16).reshape(residual.shape)


def solution(mesh):
    placed = (
        P("groups", "seq", "role"),
        P("groups", ("seq", "role"), None),
        P("groups", ("seq", "role"), None),
        P("role", "seq"),
        P(("groups", "role"), "seq", None),
        P(),
        P(("groups", "role"), "seq", None),
        P(("groups", "role"), "seq", None),
        P(("seq", "role"), None, None),
        P(("seq", "role"), None, None),
        P(("seq", "role"), None, None),
    )
    experts = mesh.shape["seq"] * mesh.shape["role"]
    return jax.shard_map(
        gathered_shards if experts <= 2 * TOPK else routed_shards,
        mesh=mesh,
        in_specs=placed,
        out_specs=P(("groups", "role"), "seq", None),
        check_vma=False,
    )
```

```python
from functools import partial

import jax
import jax.numpy as jnp
from jax import lax
from jax.experimental import pallas as pl
from jax.experimental.pallas import tpu as pltpu
from jax.sharding import PartitionSpec as P

D = 2048
QUERY_HEADS = 32
KEY_VALUE_HEADS = 4
HEAD_WIDTH = 128
TOPK = 8


epsilon = 1e-06
masked_score = -1e30
EXPERT_VMEM = 16 * 2**20
SMALL_VMEM = 12 * 2**20
COPY_VMEM = 4 * 2**20
GATE_COLUMNS = 128
SHORT = pl.CostEstimate(flops=2 * 10**9, bytes_accessed=4 * 2**20, transcendentals=0)


def score_block(queries, every_key, query_position, block_start, block_width, score_scale):
    keys_part = lax.slice_in_dim(every_key, block_start, block_start + block_width, axis=0)
    raw_scores = (
        jnp.einsum("qhd,kd->hqk", queries, keys_part, preferred_element_type=jnp.float32)
        * score_scale
    )
    key_position = block_start + jnp.arange(block_width, dtype=jnp.int32)
    return jnp.where(
        key_position[None, None, :] <= query_position[None, :, None], raw_scores, masked_score
    )


def value_block(rounded, every_value, block_start, block_width):
    prob_block = lax.slice_in_dim(rounded, block_start, block_start + block_width, axis=2)
    values_part = lax.slice_in_dim(every_value, block_start, block_start + block_width, axis=0)
    return jnp.einsum("hqk,kd->qhd", prob_block, values_part, preferred_element_type=jnp.float32)


def routed_shards(
    query_rows,
    encoded_key_rows,
    value_matrix_rows,
    output_weight,
    residual,
    norm_gain,
    route_experts,
    route_gates,
    gate_weight,
    up_weight,
    down_weight,
):
    seq_count = lax.axis_size("seq")
    role_count = lax.axis_size("role")
    seq_index = lax.axis_index("seq")
    role_index = lax.axis_index("role")
    batch_count = query_rows.shape[0]
    local_length = query_rows.shape[1]
    local_heads = query_rows.shape[2] // HEAD_WIDTH
    full_length = local_length * seq_count
    query_group_width = QUERY_HEADS // KEY_VALUE_HEADS
    head_pick = role_index * local_heads // query_group_width
    role_keys, role_values = (
        lax.all_gather(encoded_key_rows, "role", axis=1, tiled=True),
        lax.all_gather(value_matrix_rows, "role", axis=1, tiled=True),
    )
    head_keys = lax.dynamic_slice_in_dim(role_keys, head_pick * HEAD_WIDTH, HEAD_WIDTH, 2)
    head_values = lax.dynamic_slice_in_dim(role_values, head_pick * HEAD_WIDTH, HEAD_WIDTH, 2)
    whole_keys, whole_values, whole_proj = (
        lax.all_gather(head_keys, "seq", axis=1, tiled=True),
        lax.all_gather(head_values, "seq", axis=1, tiled=True),
        lax.all_gather(output_weight, "seq", axis=1, tiled=True),
    )
    key_width = full_length // 8
    score_scale = HEAD_WIDTH ** (-0.5)
    query_position = seq_index * local_length + jnp.arange(local_length, dtype=jnp.int32)
    last_needed = (seq_index + 1) * local_length

    def one_sequence(operands):
        own_queries, every_key, every_value = operands
        queries = own_queries.reshape(local_length, local_heads, HEAD_WIDTH)
        pieces = []
        for number in range(8):
            block_start = number * key_width
            compute = partial(
                score_block, queries, every_key, query_position, block_start, key_width, score_scale
            )
            skipped = partial(
                jnp.full, (local_heads, local_length, key_width), masked_score, jnp.float32
            )
            pieces.append(lax.cond(block_start < last_needed, compute, skipped))
        scores = jnp.concatenate(pieces, axis=2)
        row_peak = jnp.max(scores, axis=2, keepdims=True)
        weights = jnp.exp(scores - row_peak)
        totals = jnp.sum(weights, axis=2, keepdims=True)
        rounded = weights.astype(jnp.bfloat16)
        mixed_rows = jnp.zeros((local_length, local_heads, HEAD_WIDTH), jnp.float32)
        for number in range(8):
            block_start = number * key_width
            product = partial(value_block, rounded, every_value, block_start, key_width)
            nothing = partial(jnp.zeros, (local_length, local_heads, HEAD_WIDTH), jnp.float32)
            mixed_rows = mixed_rows + lax.cond(block_start < last_needed, product, nothing)
        attended = (mixed_rows / totals.transpose(1, 0, 2)).astype(jnp.bfloat16)
        return attended.reshape(local_length, local_heads * HEAD_WIDTH)

    attended = lax.map(one_sequence, (query_rows, whole_keys, whole_values))
    flat_attended = attended.reshape(batch_count * local_length, local_heads * HEAD_WIDTH)
    projected = lax.psum_scatter(
        jnp.dot(flat_attended, whole_proj, preferred_element_type=jnp.float32).astype(jnp.bfloat16),
        "role",
        scatter_dimension=0,
        tiled=True,
    ).astype(jnp.float32)
    hidden = residual[0].astype(jnp.float32) + projected
    variance = jnp.mean(hidden * hidden, axis=-1, keepdims=True)
    normed = (hidden * lax.rsqrt(variance + epsilon) * norm_gain).astype(jnp.bfloat16)
    expert_ids = route_experts.reshape(-1)
    gate_values = route_gates.reshape(-1)
    experts_local = gate_weight.shape[0]
    device_count = seq_count * role_count
    expert_count = experts_local * device_count
    assign = expert_ids.shape[0]
    capacity = assign // expert_count + 1
    onehot = (expert_ids[:, None] == jnp.arange(expert_count, dtype=jnp.int32)[None, :]).astype(
        jnp.int32
    )
    earlier = jnp.cumsum(onehot, axis=0) - onehot
    slot_rank = jnp.sum(earlier * onehot, axis=1)
    slot_index = expert_ids * capacity + slot_rank
    source_token = jnp.arange(assign, dtype=jnp.int32) // TOPK
    slot_token = jnp.zeros((expert_count * capacity,), jnp.int32).at[slot_index].set(source_token)
    slot_used = jnp.zeros((expert_count * capacity,), jnp.bfloat16).at[slot_index].set(1.0)
    outgoing = (normed[slot_token] * slot_used[:, None]).reshape(
        device_count, experts_local, capacity, D
    )
    incoming = lax.all_to_all(outgoing, ("seq", "role"), split_axis=0, concat_axis=0, tiled=True)
    gate_hidden = jnp.einsum(
        "sjcd,jdf->sjcf", incoming, gate_weight, preferred_element_type=jnp.float32
    )
    up_hidden = jnp.einsum(
        "sjcd,jdf->sjcf", incoming, up_weight, preferred_element_type=jnp.float32
    )
    activated = (jax.nn.silu(gate_hidden) * up_hidden).astype(jnp.bfloat16)
    returned = lax.all_to_all(
        jnp.einsum(
            "sjcf,jfd->sjcd", activated, down_weight, preferred_element_type=jnp.float32
        ).astype(jnp.bfloat16),
        ("seq", "role"),
        split_axis=0,
        concat_axis=0,
        tiled=True,
    )
    gathered = returned.reshape(expert_count * capacity, D)[slot_index]
    weighted = gathered.astype(jnp.float32) * gate_values[:, None]
    expert_sum = jnp.sum(weighted.reshape(-1, TOPK, D), axis=1)
    return (hidden + expert_sum).astype(jnp.bfloat16).reshape(residual.shape)


def in_hbm(*arrays):
    return [pltpu.with_memory_space_constraint(array, pltpu.HBM) for array in arrays]


def hbm_specs(count):
    return [pl.BlockSpec(memory_space=pltpu.HBM)] * count


def fetch_scratch(*arrays):
    return [pltpu.VMEM(array.shape, array.dtype) for array in arrays] + [
        pltpu.SemaphoreType.DMA((len(arrays),))
    ]


def start_fetch(from_refs, scratch):
    *buffers, sems = scratch
    copies = [
        pltpu.make_async_copy(from_ref, buffer, sems.at[n])
        for n, (from_ref, buffer) in enumerate(zip(from_refs, buffers))
    ]
    for copy in copies:
        copy.start()
    return copies, buffers


def in_vmem(count):
    return [pl.BlockSpec(memory_space=pltpu.VMEM)] * count


def attend_kernel(seq_count, role_count, at_ref, token_ref, *refs):
    count = seq_count + 3
    outputs = len(role_groups(role_count)) + 1
    attended_ref, *partial_refs = refs[count : count + outputs]
    copies, (query_ref, *buffers) = start_fetch(refs[:count], refs[count + outputs :])
    blocks, proj_refs = buffers[:seq_count], buffers[seq_count:]
    seq_index, role_index = at_ref[0], at_ref[1]
    local_length = query_ref.shape[1]
    local_heads = query_ref.shape[2] // HEAD_WIDTH
    per_role = local_length // role_count
    rows = local_heads * local_length
    keys_all = seq_count * local_length
    slot = lax.broadcasted_iota(jnp.int32, (rows, keys_all), 1)
    block_number, within = slot // local_length, slot % local_length
    key_position = (
        (seq_index ^ block_number) * local_length
        + (role_index ^ (within // per_role)) * per_role
        + within % per_role
    )
    query_position = (
        seq_index * local_length
        + lax.broadcasted_iota(jnp.int32, (rows, keys_all), 0) % local_length
    )
    seen = key_position <= query_position
    scale = HEAD_WIDTH ** (-0.5)
    for copy in copies[: 1 + seq_count]:
        copy.wait()
    for k in range(role_count):
        b = role_index ^ k
        own = query_ref[b]
        queries = jnp.concatenate(
            [own[:, h * HEAD_WIDTH : (h + 1) * HEAD_WIDTH] for h in range(local_heads)], axis=0
        )
        key_value = jnp.concatenate([block[b] for block in blocks], axis=0)
        keys, values = key_value[:, :HEAD_WIDTH], key_value[:, HEAD_WIDTH:]
        scores = lax.dot_general(
            queries, keys, (((1,), (1,)), ((), ())), preferred_element_type=jnp.float32
        )
        scores = jnp.where(seen, scores * scale, masked_score)
        weights = jnp.exp(scores - jnp.max(scores, axis=1, keepdims=True))
        totals = jnp.sum(weights, axis=1, keepdims=True)
        mixed = jnp.dot(weights.astype(jnp.bfloat16), values, preferred_element_type=jnp.float32)
        attended = (mixed / totals).astype(jnp.bfloat16)
        for h in range(local_heads):
            attended_ref[
                k * local_length : (k + 1) * local_length, h * HEAD_WIDTH : (h + 1) * HEAD_WIDTH
            ] = attended[h * local_length : (h + 1) * local_length]
    for copy in copies[1 + seq_count :]:
        copy.wait()
    project_into(role_count, attended_ref, [[ref] for ref in proj_refs], partial_refs)


def join_kernel(count, *refs):
    out_ref, token_ref = refs[-2:]
    token_ref[...] = jnp.zeros_like(token_ref)
    at = 0
    for ref in refs[:count]:
        size = ref.shape[1]
        out_ref[:, at : at + size, :] = ref[...]
        at += size


def rows_kernel(first, from_ref, *refs):
    to_ref, sem = refs[-2:]
    copy = pltpu.make_async_copy(from_ref.at[pl.ds(first, to_ref.shape[0]), :], to_ref, sem)
    copy.start()
    copy.wait()


def role_groups(role_count):
    last = role_count // 2
    bits = [1 << n for n in range(last.bit_length() - 1)]
    return [[k for k in range(role_count) if k & -k == bit] for bit in bits] + [[0, last]]


def project_into(role_count, attended_ref, proj_blocks, partial_refs):
    rows = attended_ref.shape[0] // role_count
    at = 0
    for pieces in proj_blocks:
        width = pieces[0].shape[1]
        product, start = None, 0
        for piece in pieces:
            depth = piece.shape[0]
            term = jnp.dot(
                attended_ref[:, start : start + depth],
                piece[...],
                preferred_element_type=jnp.float32,
            )
            product = term if product is None else product + term
            start += depth
        product = product.astype(jnp.bfloat16)
        for group, partial_ref in zip(role_groups(role_count), partial_refs):
            for n, k in enumerate(group):
                partial_ref[n * rows : (n + 1) * rows, at : at + width] = product[
                    k * rows : (k + 1) * rows
                ]
        at += width


def project_kernel(piece_count, role_count, *refs):
    outputs = len(role_groups(role_count))
    count = (len(refs) - outputs - 1) // 2
    copies, (attended_ref, *proj_refs) = start_fetch(refs[:count], refs[count + outputs :])
    for copy in copies:
        copy.wait()
    blocks = [proj_refs[n : n + piece_count] for n in range(0, len(proj_refs), piece_count)]
    project_into(role_count, attended_ref, blocks, refs[count : count + outputs])


def partial_shapes(role_count, rows, width):
    return [
        jax.ShapeDtypeStruct((rows * len(group), width), jnp.bfloat16)
        for group in role_groups(role_count)
    ]


def norm_kernel(block_width, at_ref, gain_ref, route_ref, other_route_ref, *refs):
    hidden_ref, normed_ref, other_normed_ref, other_ref = refs[4:8]
    copies, (near, near_came, far, far_came) = start_fetch(refs[:4], refs[8:])
    seq_index = at_ref[0]
    rows, features = hidden_ref.shape
    at = 0
    for sent, came in ((near, near_came), (far, far_came)):
        for copy in copies[:2]:
            copy.wait()
        copies = copies[2:]
        own = sent[:rows].astype(jnp.float32) + came[rows:].astype(jnp.float32)
        other = sent[rows:].astype(jnp.float32) + came[:rows].astype(jnp.float32)
        for j in range(own.shape[1] // block_width):
            block = slice(j * block_width, (j + 1) * block_width)
            start = pl.multiple_of((seq_index ^ at) * block_width, block_width)
            columns = pl.ds(start, block_width)
            hidden_ref[:, columns] = own[:, block]
            other_ref[:, columns] = other[:, block]
            at += 1
    lane = lax.broadcasted_iota(jnp.int32, (rows, GATE_COLUMNS), 1)
    half = GATE_COLUMNS // 2
    expert = (lane % half).astype(jnp.float32)
    for from_ref, routes, to_ref in (
        (hidden_ref, route_ref, normed_ref),
        (other_ref, other_route_ref, other_normed_ref),
    ):
        hidden = from_ref[...]
        variance = jnp.mean(hidden * hidden, axis=1, keepdims=True)
        normed = hidden * lax.rsqrt(variance + epsilon) * gain_ref[...]
        to_ref[:, :features] = normed.astype(jnp.bfloat16)
        shares = jnp.zeros((rows, GATE_COLUMNS), jnp.float32)
        count = routes.shape[1] // 2
        for k in range(count):
            named = routes[:, k : k + 1]
            shares = shares + jnp.where(expert == named, routes[:, count + k : count + k + 1], 0.0)
        first = shares.astype(jnp.bfloat16).astype(jnp.float32)
        to_ref[:, features:] = jnp.where(lane < half, first, shares - first).astype(jnp.bfloat16)


def expert_kernel(token_count, at_ref, *refs):
    token_refs = refs[:token_count]
    gate_ref, up_ref, down_ref, keep_ref, send_ref, activated_ref = refs[token_count:]
    features, units = gate_ref.shape[1:]
    tokens = jnp.concatenate([ref[:, :features] for ref in token_refs], axis=0)
    gates = jnp.concatenate([ref[:, features:] for ref in token_refs], axis=0)
    lane = lax.broadcasted_iota(jnp.int32, gates.shape, 1)
    mine = lane % (GATE_COLUMNS // 2) == at_ref[2]
    share = jnp.sum(jnp.where(mine, gates.astype(jnp.float32), 0.0), axis=1, keepdims=True)
    block = 256 if units % 256 == 0 else units
    for f in range(0, units, block):
        gate_hidden = jnp.dot(
            tokens, gate_ref[0, :, f : f + block], preferred_element_type=jnp.float32
        )
        up_hidden = jnp.dot(tokens, up_ref[0, :, f : f + block], preferred_element_type=jnp.float32)
        activated_ref[:, f : f + block] = (
            gate_hidden / (1.0 + jnp.exp(-gate_hidden)) * up_hidden
        ).astype(jnp.bfloat16)
    kept = keep_ref.shape[0]
    block = 512 if features % 512 == 0 else features
    for c in range(0, features, block):
        product = jnp.dot(
            activated_ref[...], down_ref[0, :, c : c + block], preferred_element_type=jnp.float32
        )
        product = (product * share).astype(jnp.bfloat16)
        keep_ref[:, c : c + block] = product[:kept]
        send_ref[:, c : c + block] = product[kept:]


def run_expert(at, tokens, gate_weight, up_weight, down_weight):
    units = gate_weight.shape[2]
    width = gate_weight.shape[1]
    rows = sum(part.shape[0] for part in tokens)
    half = jax.ShapeDtypeStruct((rows // 2, width), jnp.bfloat16)
    return pl.pallas_call(
        partial(expert_kernel, len(tokens)),
        in_specs=[pl.BlockSpec(memory_space=pltpu.SMEM)] + in_vmem(len(tokens) + 3),
        out_specs=in_vmem(2),
        out_shape=[half, half],
        scratch_shapes=[pltpu.VMEM((rows, units), jnp.bfloat16)],
        compiler_params=pltpu.CompilerParams(vmem_limit_bytes=EXPERT_VMEM),
        cost_estimate=pl.CostEstimate(
            flops=6 * rows * width * units, bytes_accessed=4 * rows * width, transcendentals=0
        ),
    )(at, *tokens, gate_weight, up_weight, down_weight)


def after(array, *others):
    return lax.optimization_barrier((array, *others))[0]


def added(terms):
    total = terms[0].astype(jnp.float32)
    for term in terms[1:]:
        total = total + term.astype(jnp.float32)
    return total


def gathered_shards(
    query_rows,
    encoded_key_rows,
    value_matrix_rows,
    output_weight,
    residual,
    norm_gain,
    route_experts,
    route_gates,
    gate_weight,
    up_weight,
    down_weight,
):
    seq_count = lax.axis_size("seq")
    role_count = lax.axis_size("role")
    seq_index = lax.axis_index("seq")
    role_index = lax.axis_index("role")
    batch_count, local_length, query_width = query_rows.shape
    local_heads = query_width // HEAD_WIDTH
    group_width = QUERY_HEADS // KEY_VALUE_HEADS
    role_bits = [1 << n for n in range(role_count.bit_length() - 1)]
    at = jnp.stack([seq_index, role_index, seq_index * role_count + role_index]).astype(jnp.int32)

    def over_role(array, k):
        return lax.ppermute(array, "role", [(i, i ^ k) for i in range(role_count)])

    def over_seq(array, j):
        return lax.ppermute(array, "seq", [(i, i ^ j) for i in range(seq_count)])

    beside_proj = over_seq(output_weight, 1)
    first_rows = output_weight.shape[0] // 2
    block_width = output_weight.shape[1]
    first_proj = output_weight[:first_rows]
    across_proj = [[over_seq(first_proj, j)] for j in range(2, seq_count, 2)]

    pieces = []
    for k in range(role_count):
        head = ((role_index ^ k) * local_heads // group_width) * HEAD_WIDTH
        piece = jnp.concatenate(
            [
                lax.dynamic_slice_in_dim(encoded_key_rows, head, HEAD_WIDTH, 2),
                lax.dynamic_slice_in_dim(value_matrix_rows, head, HEAD_WIDTH, 2),
            ],
            axis=2,
        )
        pieces.append(piece if k == 0 else over_role(piece, k))
    block, block_token = pl.pallas_call(
        partial(join_kernel, len(pieces)),
        in_specs=in_vmem(len(pieces)) + [pl.BlockSpec(memory_space=pl.ANY)] * len(across_proj),
        out_specs=in_vmem(2),
        out_shape=[
            jax.ShapeDtypeStruct((batch_count, local_length, 2 * HEAD_WIDTH), jnp.bfloat16),
            jax.ShapeDtypeStruct((8, 128), jnp.float32),
        ],
        compiler_params=pltpu.CompilerParams(vmem_limit_bytes=COPY_VMEM),
        cost_estimate=SHORT,
    )(*pieces, *(parts[0] for parts in across_proj))
    same_core = [block] + [over_seq(block, j) for j in range(2, seq_count, 2)]
    blocks = []
    for part in same_core:
        blocks += [part, over_seq(part, 1)]
    rest_proj = after(output_weight[first_rows:], block_token)
    for n, j in enumerate(range(2, seq_count, 2)):
        across_proj[n].append(over_seq(rest_proj, j))

    last = role_count // 2
    routes = jnp.concatenate([route_experts[0].astype(jnp.float32), route_gates[0]], axis=1)
    residual_blocks = [
        lax.dynamic_slice_in_dim(residual[0], (seq_index ^ j) * block_width, block_width, 1)
        for j in range(seq_count)
    ]
    near_residual = jnp.concatenate(residual_blocks[:2], axis=1)
    far_residual = jnp.concatenate(residual_blocks[2:], axis=1)

    rows = batch_count * local_length
    near_width = 2 * output_weight.shape[1]
    groups = role_groups(role_count)
    attend_args = in_hbm(query_rows, *blocks, output_weight, beside_proj)
    attended, *near = pl.pallas_call(
        partial(attend_kernel, seq_count, role_count),
        in_specs=[pl.BlockSpec(memory_space=pltpu.SMEM), pl.BlockSpec(memory_space=pl.ANY)]
        + hbm_specs(len(attend_args)),
        out_specs=in_vmem(1 + len(groups)),
        out_shape=[jax.ShapeDtypeStruct((rows, query_width), jnp.bfloat16)]
        + partial_shapes(role_count, local_length, near_width),
        scratch_shapes=fetch_scratch(*attend_args),
        compiler_params=pltpu.CompilerParams(vmem_limit_bytes=SMALL_VMEM),
        cost_estimate=SHORT,
    )(at, block_token, *attend_args)

    def summed_over_role(parts, extra, *before):
        terms = [[part] for part in parts]
        for n, group in enumerate(groups[:-1]):
            bit = 1 << n
            leaving = terms[n][0] if len(terms[n]) == 1 else added(terms[n]).astype(jnp.bfloat16)
            came = over_role(leaving, bit)
            for m in range(n + 1, len(groups)):
                at_rows = [group.index(k ^ bit) for k in groups[m]]
                if at_rows == list(range(len(group))):
                    terms[m].append(came)
                else:
                    split = [came[i * local_length : (i + 1) * local_length] for i in at_rows]
                    terms[m].append(jnp.concatenate(split, axis=0))
        extra = jnp.pad(after(extra, *before) if before else extra, ((0, local_length), (0, 0)))
        sent = added(terms[-1] + [extra]).astype(jnp.bfloat16)
        return sent, over_role(sent, last)

    near_last = summed_over_role(near, near_residual)
    other_routes = over_role(after(routes, near_last[1]), last)
    far_proj = []
    for parts in across_proj:
        parts = [after(part, near_last[0]) for part in parts]
        far_proj += parts + [over_seq(part, 1) for part in parts]
    far_width = 2 * len(across_proj) * output_weight.shape[1]
    project_args = in_hbm(attended, *far_proj)
    far = pl.pallas_call(
        partial(project_kernel, len(across_proj[0]), role_count),
        in_specs=hbm_specs(len(project_args)),
        out_specs=in_vmem(len(groups)),
        out_shape=partial_shapes(role_count, local_length, far_width),
        scratch_shapes=fetch_scratch(*project_args),
        compiler_params=pltpu.CompilerParams(vmem_limit_bytes=SMALL_VMEM),
        cost_estimate=SHORT,
    )(*project_args)

    width = residual.shape[2]
    row_shape = jax.ShapeDtypeStruct((local_length, width + GATE_COLUMNS), jnp.bfloat16)
    far_last = summed_over_role(far, far_residual, other_routes)
    sums = in_hbm(*near_last, *far_last)
    hidden, normed, other_normed = pl.pallas_call(
        partial(norm_kernel, block_width),
        in_specs=[pl.BlockSpec(memory_space=pltpu.SMEM)] + in_vmem(3) + hbm_specs(len(sums)),
        out_specs=in_vmem(3),
        out_shape=[
            jax.ShapeDtypeStruct((local_length, width), jnp.float32),
            row_shape,
            row_shape,
        ],
        scratch_shapes=[pltpu.VMEM((local_length, width), jnp.float32)] + fetch_scratch(*sums),
        compiler_params=pltpu.CompilerParams(vmem_limit_bytes=SMALL_VMEM),
        cost_estimate=SHORT,
    )(at, norm_gain.reshape(1, width), routes, other_routes, *sums)

    across_steps = range(2, seq_count, 2)

    def walk(k, bits):
        found = [k]
        for n, bit in enumerate(bits):
            found += walk(k | bit, bits[n + 1 :])
        return found

    lower_bits = role_bits[:-1][::-1]
    order = walk(last, lower_bits) + walk(0, lower_bits)
    planes = {0: normed, last: other_normed}
    crossed = {k: [over_seq(planes[k], j) for j in across_steps] for k in (last, 0)}
    for k in order:
        if k in (0, last):
            first = planes[k] if k == last else after(normed, *crossed[last])
            for bit in lower_bits:
                planes[k | bit] = over_role(first, bit)
                crossed[k | bit] = [over_role(part, bit) for part in crossed[k]]
        else:
            for bit in lower_bits:
                if bit < (k & -k):
                    planes[k | bit] = over_role(planes[k], bit)
                    crossed[k | bit] = [over_role(part, bit) for part in crossed[k]]

    keep, send, slots, leaving, passed = {}, {}, {}, {}, {}

    def expert(k, before, *others):
        late = [after(part, *before) for part in crossed[k]] if before else crossed[k]
        tokens = [planes[k]] + late
        tokens += [over_seq(part, 1) for part in tokens]
        if others:
            tokens = lax.optimization_barrier((*tokens, *others))[: len(tokens)]
        return run_expert(at, tokens, gate_weight, up_weight, down_weight)

    def combine(k, *before):
        came = over_seq(after(send[k], *before) if before else send[k], 1)
        sums = []
        for n in range(len(across_steps)):
            chunk = slice((n + 1) * local_length, (n + 2) * local_length)
            sums.append(added([keep[k][chunk], came[chunk]]).astype(jnp.bfloat16))
        return [keep[k][:local_length], came[:local_length]], sums

    def pass_on(k):
        passed[k] = [over_seq(part, j) for part, j in zip(leaving[k], across_steps)]
        slots[k] += passed[k]

    final = order[-1]
    for n, k in enumerate(order):
        previous = order[n - 1]
        before = [keep[previous]] if n else [planes[order[1]]]
        others = leaving[previous] if n and previous else []
        if n == 0:
            others = crossed[order[1]] + crossed[0]
        if n and k == final:
            far_plane = order[1]
            slots[far_plane] = [added(slots[far_plane]).astype(jnp.bfloat16)]
            others = others + slots[far_plane]
        keep[k], send[k] = expert(k, before, *others)
        waits = passed.get(previous, []) if n else []
        if 0 < n and k != final:
            waits = waits + ([planes[final]] if k else crossed[final])
        slots[k], leaving[k] = combine(k, *waits)
        if k:
            pass_on(k)
    leaving[0] = [after(part, *leaving[final]) for part in leaving[0]]
    pass_on(0)
    for bit in role_bits:
        for k in [k for k in sorted(slots, reverse=True) if k & bit]:
            slots[k ^ bit].append(over_role(added(slots.pop(k)).astype(jnp.bfloat16), bit))
    return added([hidden] + slots[0]).astype(jnp.bfloat16).reshape(residual.shape)


def solution(mesh):
    placed = (
        P("groups", "seq", "role"),
        P("groups", ("seq", "role"), None),
        P("groups", ("seq", "role"), None),
        P("role", "seq"),
        P(("groups", "role"), "seq", None),
        P(),
        P(("groups", "role"), "seq", None),
        P(("groups", "role"), "seq", None),
        P(("seq", "role"), None, None),
        P(("seq", "role"), None, None),
        P(("seq", "role"), None, None),
    )
    experts = mesh.shape["seq"] * mesh.shape["role"]
    return jax.shard_map(
        gathered_shards if experts <= 2 * TOPK else routed_shards,
        mesh=mesh,
        in_specs=placed,
        out_specs=P(("groups", "role"), "seq", None),
        check_vma=False,
    )
```

```python
from functools import partial

import jax
import jax.numpy as jnp
from jax import lax
from jax.experimental import pallas as pl
from jax.experimental.pallas import tpu as pltpu
from jax.sharding import PartitionSpec as P

D = 2048
QUERY_HEADS = 32
KEY_VALUE_HEADS = 4
HEAD_WIDTH = 128
TOPK = 8


epsilon = 1e-06
masked_score = -1e30
EXPERT_VMEM = 16 * 2**20
SMALL_VMEM = 12 * 2**20
COPY_VMEM = 4 * 2**20
GATE_COLUMNS = 128
NOTHING = pl.CostEstimate(flops=1, bytes_accessed=1, transcendentals=0)
SHORT = pl.CostEstimate(flops=2 * 10**9, bytes_accessed=4 * 2**20, transcendentals=0)
LONG = pl.CostEstimate(flops=10**10, bytes_accessed=1, transcendentals=0)


def score_block(queries, every_key, query_position, block_start, block_width, score_scale):
    keys_part = lax.slice_in_dim(every_key, block_start, block_start + block_width, axis=0)
    raw_scores = (
        jnp.einsum("qhd,kd->hqk", queries, keys_part, preferred_element_type=jnp.float32)
        * score_scale
    )
    key_position = block_start + jnp.arange(block_width, dtype=jnp.int32)
    return jnp.where(
        key_position[None, None, :] <= query_position[None, :, None], raw_scores, masked_score
    )


def value_block(rounded, every_value, block_start, block_width):
    prob_block = lax.slice_in_dim(rounded, block_start, block_start + block_width, axis=2)
    values_part = lax.slice_in_dim(every_value, block_start, block_start + block_width, axis=0)
    return jnp.einsum("hqk,kd->qhd", prob_block, values_part, preferred_element_type=jnp.float32)


def routed_shards(
    query_rows,
    encoded_key_rows,
    value_matrix_rows,
    output_weight,
    residual,
    norm_gain,
    route_experts,
    route_gates,
    gate_weight,
    up_weight,
    down_weight,
):
    seq_count = lax.axis_size("seq")
    role_count = lax.axis_size("role")
    seq_index = lax.axis_index("seq")
    role_index = lax.axis_index("role")
    batch_count = query_rows.shape[0]
    local_length = query_rows.shape[1]
    local_heads = query_rows.shape[2] // HEAD_WIDTH
    full_length = local_length * seq_count
    query_group_width = QUERY_HEADS // KEY_VALUE_HEADS
    head_pick = role_index * local_heads // query_group_width
    role_keys, role_values = (
        lax.all_gather(encoded_key_rows, "role", axis=1, tiled=True),
        lax.all_gather(value_matrix_rows, "role", axis=1, tiled=True),
    )
    head_keys = lax.dynamic_slice_in_dim(role_keys, head_pick * HEAD_WIDTH, HEAD_WIDTH, 2)
    head_values = lax.dynamic_slice_in_dim(role_values, head_pick * HEAD_WIDTH, HEAD_WIDTH, 2)
    whole_keys, whole_values, whole_proj = (
        lax.all_gather(head_keys, "seq", axis=1, tiled=True),
        lax.all_gather(head_values, "seq", axis=1, tiled=True),
        lax.all_gather(output_weight, "seq", axis=1, tiled=True),
    )
    key_width = full_length // 8
    score_scale = HEAD_WIDTH ** (-0.5)
    query_position = seq_index * local_length + jnp.arange(local_length, dtype=jnp.int32)
    last_needed = (seq_index + 1) * local_length

    def one_sequence(operands):
        own_queries, every_key, every_value = operands
        queries = own_queries.reshape(local_length, local_heads, HEAD_WIDTH)
        pieces = []
        for number in range(8):
            block_start = number * key_width
            compute = partial(
                score_block, queries, every_key, query_position, block_start, key_width, score_scale
            )
            skipped = partial(
                jnp.full, (local_heads, local_length, key_width), masked_score, jnp.float32
            )
            pieces.append(lax.cond(block_start < last_needed, compute, skipped))
        scores = jnp.concatenate(pieces, axis=2)
        row_peak = jnp.max(scores, axis=2, keepdims=True)
        weights = jnp.exp(scores - row_peak)
        totals = jnp.sum(weights, axis=2, keepdims=True)
        rounded = weights.astype(jnp.bfloat16)
        mixed_rows = jnp.zeros((local_length, local_heads, HEAD_WIDTH), jnp.float32)
        for number in range(8):
            block_start = number * key_width
            product = partial(value_block, rounded, every_value, block_start, key_width)
            nothing = partial(jnp.zeros, (local_length, local_heads, HEAD_WIDTH), jnp.float32)
            mixed_rows = mixed_rows + lax.cond(block_start < last_needed, product, nothing)
        attended = (mixed_rows / totals.transpose(1, 0, 2)).astype(jnp.bfloat16)
        return attended.reshape(local_length, local_heads * HEAD_WIDTH)

    attended = lax.map(one_sequence, (query_rows, whole_keys, whole_values))
    flat_attended = attended.reshape(batch_count * local_length, local_heads * HEAD_WIDTH)
    projected = lax.psum_scatter(
        jnp.dot(flat_attended, whole_proj, preferred_element_type=jnp.float32).astype(jnp.bfloat16),
        "role",
        scatter_dimension=0,
        tiled=True,
    ).astype(jnp.float32)
    hidden = residual[0].astype(jnp.float32) + projected
    variance = jnp.mean(hidden * hidden, axis=-1, keepdims=True)
    normed = (hidden * lax.rsqrt(variance + epsilon) * norm_gain).astype(jnp.bfloat16)
    expert_ids = route_experts.reshape(-1)
    gate_values = route_gates.reshape(-1)
    experts_local = gate_weight.shape[0]
    device_count = seq_count * role_count
    expert_count = experts_local * device_count
    assign = expert_ids.shape[0]
    capacity = assign // expert_count + 1
    onehot = (expert_ids[:, None] == jnp.arange(expert_count, dtype=jnp.int32)[None, :]).astype(
        jnp.int32
    )
    earlier = jnp.cumsum(onehot, axis=0) - onehot
    slot_rank = jnp.sum(earlier * onehot, axis=1)
    slot_index = expert_ids * capacity + slot_rank
    source_token = jnp.arange(assign, dtype=jnp.int32) // TOPK
    slot_token = jnp.zeros((expert_count * capacity,), jnp.int32).at[slot_index].set(source_token)
    slot_used = jnp.zeros((expert_count * capacity,), jnp.bfloat16).at[slot_index].set(1.0)
    outgoing = (normed[slot_token] * slot_used[:, None]).reshape(
        device_count, experts_local, capacity, D
    )
    incoming = lax.all_to_all(outgoing, ("seq", "role"), split_axis=0, concat_axis=0, tiled=True)
    gate_hidden = jnp.einsum(
        "sjcd,jdf->sjcf", incoming, gate_weight, preferred_element_type=jnp.float32
    )
    up_hidden = jnp.einsum(
        "sjcd,jdf->sjcf", incoming, up_weight, preferred_element_type=jnp.float32
    )
    activated = (jax.nn.silu(gate_hidden) * up_hidden).astype(jnp.bfloat16)
    returned = lax.all_to_all(
        jnp.einsum(
            "sjcf,jfd->sjcd", activated, down_weight, preferred_element_type=jnp.float32
        ).astype(jnp.bfloat16),
        ("seq", "role"),
        split_axis=0,
        concat_axis=0,
        tiled=True,
    )
    gathered = returned.reshape(expert_count * capacity, D)[slot_index]
    weighted = gathered.astype(jnp.float32) * gate_values[:, None]
    expert_sum = jnp.sum(weighted.reshape(-1, TOPK, D), axis=1)
    return (hidden + expert_sum).astype(jnp.bfloat16).reshape(residual.shape)


def in_hbm(*arrays):
    return [pltpu.with_memory_space_constraint(array, pltpu.HBM) for array in arrays]


def hbm_specs(count):
    return [pl.BlockSpec(memory_space=pltpu.HBM)] * count


def fetch_scratch(*arrays):
    return [pltpu.VMEM(array.shape, array.dtype) for array in arrays] + [
        pltpu.SemaphoreType.DMA((len(arrays),))
    ]


def start_fetch(from_refs, scratch):
    *buffers, sems = scratch
    copies = [
        pltpu.make_async_copy(from_ref, buffer, sems.at[n])
        for n, (from_ref, buffer) in enumerate(zip(from_refs, buffers))
    ]
    for copy in copies:
        copy.start()
    return copies, buffers


def in_vmem(count):
    return [pl.BlockSpec(memory_space=pltpu.VMEM)] * count


def attend_kernel(seq_count, role_count, at_ref, token_ref, *refs):
    count = seq_count + 3
    outputs = len(role_groups(role_count)) + 1
    attended_ref, *partial_refs = refs[count : count + outputs]
    copies, (query_ref, *buffers) = start_fetch(refs[:count], refs[count + outputs :])
    blocks, proj_refs = buffers[:seq_count], buffers[seq_count:]
    seq_index, role_index = at_ref[0], at_ref[1]
    local_length = query_ref.shape[1]
    local_heads = query_ref.shape[2] // HEAD_WIDTH
    per_role = local_length // role_count
    rows = local_heads * local_length
    keys_all = seq_count * local_length
    slot = lax.broadcasted_iota(jnp.int32, (rows, keys_all), 1)
    block_number, within = slot // local_length, slot % local_length
    key_position = (
        (seq_index ^ block_number) * local_length
        + (role_index ^ (within // per_role)) * per_role
        + within % per_role
    )
    query_position = (
        seq_index * local_length
        + lax.broadcasted_iota(jnp.int32, (rows, keys_all), 0) % local_length
    )
    seen = key_position <= query_position
    scale = HEAD_WIDTH ** (-0.5)
    for copy in copies[: 1 + seq_count]:
        copy.wait()
    for k in range(role_count):
        b = role_index ^ k
        own = query_ref[b]
        queries = jnp.concatenate(
            [own[:, h * HEAD_WIDTH : (h + 1) * HEAD_WIDTH] for h in range(local_heads)], axis=0
        )
        key_value = jnp.concatenate([block[b] for block in blocks], axis=0)
        keys, values = key_value[:, :HEAD_WIDTH], key_value[:, HEAD_WIDTH:]
        scores = lax.dot_general(
            queries, keys, (((1,), (1,)), ((), ())), preferred_element_type=jnp.float32
        )
        scores = jnp.where(seen, scores * scale, masked_score)
        weights = jnp.exp(scores - jnp.max(scores, axis=1, keepdims=True))
        totals = jnp.sum(weights, axis=1, keepdims=True)
        mixed = jnp.dot(weights.astype(jnp.bfloat16), values, preferred_element_type=jnp.float32)
        attended = (mixed / totals).astype(jnp.bfloat16)
        for h in range(local_heads):
            attended_ref[
                k * local_length : (k + 1) * local_length, h * HEAD_WIDTH : (h + 1) * HEAD_WIDTH
            ] = attended[h * local_length : (h + 1) * local_length]
    for copy in copies[1 + seq_count :]:
        copy.wait()
    project_into(role_count, attended_ref, [[ref] for ref in proj_refs], partial_refs)


def join_kernel(count, *refs):
    out_ref, token_ref = refs[-2:]
    token_ref[...] = jnp.zeros_like(token_ref)
    at = 0
    for ref in refs[:count]:
        size = ref.shape[1]
        out_ref[:, at : at + size, :] = ref[...]
        at += size


def rows_kernel(first, from_ref, *refs):
    to_ref, sem = refs[-2:]
    copy = pltpu.make_async_copy(from_ref.at[pl.ds(first, to_ref.shape[0]), :], to_ref, sem)
    copy.start()
    copy.wait()


def role_groups(role_count):
    last = role_count // 2
    bits = [1 << n for n in range(last.bit_length() - 1)]
    return [[k for k in range(role_count) if k & -k == bit] for bit in bits] + [[0, last]]


def project_into(role_count, attended_ref, proj_blocks, partial_refs):
    rows = attended_ref.shape[0] // role_count
    at = 0
    for pieces in proj_blocks:
        width = pieces[0].shape[1]
        product, start = None, 0
        for piece in pieces:
            depth = piece.shape[0]
            term = jnp.dot(
                attended_ref[:, start : start + depth],
                piece[...],
                preferred_element_type=jnp.float32,
            )
            product = term if product is None else product + term
            start += depth
        product = product.astype(jnp.bfloat16)
        for group, partial_ref in zip(role_groups(role_count), partial_refs):
            for n, k in enumerate(group):
                partial_ref[n * rows : (n + 1) * rows, at : at + width] = product[
                    k * rows : (k + 1) * rows
                ]
        at += width


def project_kernel(piece_count, role_count, *refs):
    outputs = len(role_groups(role_count))
    count = (len(refs) - outputs - 1) // 2
    copies, (attended_ref, *proj_refs) = start_fetch(refs[:count], refs[count + outputs :])
    for copy in copies:
        copy.wait()
    blocks = [proj_refs[n : n + piece_count] for n in range(0, len(proj_refs), piece_count)]
    project_into(role_count, attended_ref, blocks, refs[count : count + outputs])


def partial_shapes(role_count, rows, width):
    return [
        jax.ShapeDtypeStruct((rows * len(group), width), jnp.bfloat16)
        for group in role_groups(role_count)
    ]


def near_kernel(sent_ref, came_ref, own_ref, other_ref, *scratch):
    copies, (sent, came) = start_fetch((sent_ref, came_ref), scratch)
    for copy in copies:
        copy.wait()
    rows = own_ref.shape[0]
    own_ref[...] = sent[:rows].astype(jnp.float32) + came[rows:].astype(jnp.float32)
    other_ref[...] = sent[rows:].astype(jnp.float32) + came[:rows].astype(jnp.float32)


def norm_kernel(block_width, at_ref, gain_ref, route_ref, other_route_ref, *refs):
    hidden_ref, normed_ref, other_normed_ref, other_ref = refs[4:8]
    copies, (own_near, other_near, far, far_came) = start_fetch(refs[:4], refs[8:])
    seq_index = at_ref[0]
    rows, features = hidden_ref.shape
    for copy in copies:
        copy.wait()
    own_far = far[:rows].astype(jnp.float32) + far_came[rows:].astype(jnp.float32)
    other_far = far[rows:].astype(jnp.float32) + far_came[:rows].astype(jnp.float32)
    for to_ref, parts in ((hidden_ref, (own_near, own_far)), (other_ref, (other_near, other_far))):
        at = 0
        for part in parts:
            for j in range(part.shape[1] // block_width):
                start = pl.multiple_of((seq_index ^ at) * block_width, block_width)
                block = part[:, j * block_width : (j + 1) * block_width]
                to_ref[:, pl.ds(start, block_width)] = block
                at += 1
    lane = lax.broadcasted_iota(jnp.int32, (rows, GATE_COLUMNS), 1)
    half = GATE_COLUMNS // 2
    expert = (lane % half).astype(jnp.float32)
    for from_ref, routes, to_ref in (
        (hidden_ref, route_ref, normed_ref),
        (other_ref, other_route_ref, other_normed_ref),
    ):
        hidden = from_ref[...]
        variance = jnp.mean(hidden * hidden, axis=1, keepdims=True)
        normed = hidden * lax.rsqrt(variance + epsilon) * gain_ref[...]
        to_ref[:, :features] = normed.astype(jnp.bfloat16)
        shares = jnp.zeros((rows, GATE_COLUMNS), jnp.float32)
        count = routes.shape[1] // 2
        for k in range(count):
            named = routes[:, k : k + 1]
            shares = shares + jnp.where(expert == named, routes[:, count + k : count + k + 1], 0.0)
        first = shares.astype(jnp.bfloat16).astype(jnp.float32)
        to_ref[:, features:] = jnp.where(lane < half, first, shares - first).astype(jnp.bfloat16)


def expert_kernel(token_count, at_ref, *refs):
    token_refs = refs[:token_count]
    gate_ref, up_ref, down_ref, keep_ref, send_ref, activated_ref = refs[token_count:]
    features, units = gate_ref.shape[1:]
    tokens = jnp.concatenate([ref[:, :features] for ref in token_refs], axis=0)
    gates = jnp.concatenate([ref[:, features:] for ref in token_refs], axis=0)
    lane = lax.broadcasted_iota(jnp.int32, gates.shape, 1)
    mine = lane % (GATE_COLUMNS // 2) == at_ref[2]
    share = jnp.sum(jnp.where(mine, gates.astype(jnp.float32), 0.0), axis=1, keepdims=True)
    block = 256 if units % 256 == 0 else units
    for f in range(0, units, block):
        gate_hidden = jnp.dot(
            tokens, gate_ref[0, :, f : f + block], preferred_element_type=jnp.float32
        )
        up_hidden = jnp.dot(tokens, up_ref[0, :, f : f + block], preferred_element_type=jnp.float32)
        activated_ref[:, f : f + block] = (
            gate_hidden / (1.0 + jnp.exp(-gate_hidden)) * up_hidden
        ).astype(jnp.bfloat16)
    kept = keep_ref.shape[0]
    block = 512 if features % 512 == 0 else features
    for c in range(0, features, block):
        product = jnp.dot(
            activated_ref[...], down_ref[0, :, c : c + block], preferred_element_type=jnp.float32
        )
        product = (product * share).astype(jnp.bfloat16)
        keep_ref[:, c : c + block] = product[:kept]
        send_ref[:, c : c + block] = product[kept:]


def run_expert(at, tokens, gate_weight, up_weight, down_weight):
    units = gate_weight.shape[2]
    width = gate_weight.shape[1]
    rows = sum(part.shape[0] for part in tokens)
    half = jax.ShapeDtypeStruct((rows // 2, width), jnp.bfloat16)
    return pl.pallas_call(
        partial(expert_kernel, len(tokens)),
        in_specs=[pl.BlockSpec(memory_space=pltpu.SMEM)] + in_vmem(len(tokens) + 3),
        out_specs=in_vmem(2),
        out_shape=[half, half],
        scratch_shapes=[pltpu.VMEM((rows, units), jnp.bfloat16)],
        compiler_params=pltpu.CompilerParams(vmem_limit_bytes=EXPERT_VMEM),
        cost_estimate=NOTHING,
    )(at, *tokens, gate_weight, up_weight, down_weight)


def after(array, *others):
    return lax.optimization_barrier((array, *others))[0]


def added(terms):
    total = terms[0].astype(jnp.float32)
    for term in terms[1:]:
        total = total + term.astype(jnp.float32)
    return total


def gathered_shards(
    query_rows,
    encoded_key_rows,
    value_matrix_rows,
    output_weight,
    residual,
    norm_gain,
    route_experts,
    route_gates,
    gate_weight,
    up_weight,
    down_weight,
):
    seq_count = lax.axis_size("seq")
    role_count = lax.axis_size("role")
    seq_index = lax.axis_index("seq")
    role_index = lax.axis_index("role")
    batch_count, local_length, query_width = query_rows.shape
    local_heads = query_width // HEAD_WIDTH
    group_width = QUERY_HEADS // KEY_VALUE_HEADS
    role_bits = [1 << n for n in range(role_count.bit_length() - 1)]
    at = jnp.stack([seq_index, role_index, seq_index * role_count + role_index]).astype(jnp.int32)

    def over_role(array, k):
        return lax.ppermute(array, "role", [(i, i ^ k) for i in range(role_count)])

    def over_seq(array, j):
        return lax.ppermute(array, "seq", [(i, i ^ j) for i in range(seq_count)])

    beside_proj = over_seq(output_weight, 1)
    first_rows = output_weight.shape[0] // 8 * 3
    block_width = output_weight.shape[1]

    pieces = []
    for k in range(role_count):
        head = ((role_index ^ k) * local_heads // group_width) * HEAD_WIDTH
        piece = jnp.concatenate(
            [
                lax.dynamic_slice_in_dim(encoded_key_rows, head, HEAD_WIDTH, 2),
                lax.dynamic_slice_in_dim(value_matrix_rows, head, HEAD_WIDTH, 2),
            ],
            axis=2,
        )
        pieces.append(piece)
    first_proj = output_weight[:first_rows]
    pieces = [piece if k == 0 else over_role(piece, k) for k, piece in enumerate(pieces)]
    across_proj = [[over_seq(first_proj, j)] for j in range(2, seq_count, 2)]
    block, block_token = pl.pallas_call(
        partial(join_kernel, len(pieces)),
        in_specs=in_vmem(len(pieces)) + [pl.BlockSpec(memory_space=pl.ANY)] * len(across_proj),
        out_specs=in_vmem(2),
        out_shape=[
            jax.ShapeDtypeStruct((batch_count, local_length, 2 * HEAD_WIDTH), jnp.bfloat16),
            jax.ShapeDtypeStruct((8, 128), jnp.float32),
        ],
        compiler_params=pltpu.CompilerParams(vmem_limit_bytes=COPY_VMEM),
        cost_estimate=SHORT,
    )(*pieces, *(parts[0] for parts in across_proj))
    same_core = [block] + [over_seq(block, j) for j in range(2, seq_count, 2)]
    blocks = []
    for part in same_core:
        blocks += [part, over_seq(part, 1)]
    rest_proj = after(output_weight[first_rows:], block_token)
    for n, j in enumerate(range(2, seq_count, 2)):
        across_proj[n].append(over_seq(rest_proj, j))

    last = role_count // 2
    routes = jnp.concatenate([route_experts[0].astype(jnp.float32), route_gates[0]], axis=1)
    other_routes = over_role(routes, last)
    residual_blocks = [
        lax.dynamic_slice_in_dim(residual[0], (seq_index ^ j) * block_width, block_width, 1)
        for j in range(seq_count)
    ]
    near_residual = jnp.concatenate(residual_blocks[:2], axis=1)
    far_residual = jnp.concatenate(residual_blocks[2:], axis=1)

    rows = batch_count * local_length
    near_width = 2 * output_weight.shape[1]
    groups = role_groups(role_count)
    attend_args = in_hbm(query_rows, *blocks, output_weight, beside_proj)
    attended, *near = pl.pallas_call(
        partial(attend_kernel, seq_count, role_count),
        in_specs=[pl.BlockSpec(memory_space=pltpu.SMEM), pl.BlockSpec(memory_space=pl.ANY)]
        + hbm_specs(len(attend_args)),
        out_specs=in_vmem(1 + len(groups)),
        out_shape=[jax.ShapeDtypeStruct((rows, query_width), jnp.bfloat16)]
        + partial_shapes(role_count, local_length, near_width),
        scratch_shapes=fetch_scratch(*attend_args),
        compiler_params=pltpu.CompilerParams(vmem_limit_bytes=SMALL_VMEM),
        cost_estimate=SHORT,
    )(at, block_token, *attend_args)

    def summed_over_role(parts, extra, *before):
        terms = [[part] for part in parts]
        for n, group in enumerate(groups[:-1]):
            bit = 1 << n
            leaving = terms[n][0] if len(terms[n]) == 1 else added(terms[n]).astype(jnp.bfloat16)
            came = over_role(leaving, bit)
            for m in range(n + 1, len(groups)):
                at_rows = [group.index(k ^ bit) for k in groups[m]]
                if at_rows == list(range(len(group))):
                    terms[m].append(came)
                else:
                    split = [came[i * local_length : (i + 1) * local_length] for i in at_rows]
                    terms[m].append(jnp.concatenate(split, axis=0))
        extra = jnp.pad(after(extra, *before) if before else extra, ((0, local_length), (0, 0)))
        sent = added(terms[-1] + [extra]).astype(jnp.bfloat16)
        return sent, over_role(sent, last)

    near_last = summed_over_role(near, near_residual)
    near_args = in_hbm(*near_last)
    near_sums = pl.pallas_call(
        near_kernel,
        in_specs=hbm_specs(2),
        out_specs=in_vmem(2),
        out_shape=[jax.ShapeDtypeStruct((local_length, near_width), jnp.float32)] * 2,
        scratch_shapes=fetch_scratch(*near_args),
        compiler_params=pltpu.CompilerParams(vmem_limit_bytes=COPY_VMEM),
        cost_estimate=LONG,
    )(*near_args)
    far_proj = []
    for parts in across_proj:
        parts = [after(part, near_last[0]) for part in parts]
        far_proj += parts + [over_seq(part, 1) for part in parts]
    far_width = 2 * len(across_proj) * output_weight.shape[1]
    project_args = in_hbm(attended, *far_proj)
    far = pl.pallas_call(
        partial(project_kernel, len(across_proj[0]), role_count),
        in_specs=hbm_specs(len(project_args)),
        out_specs=in_vmem(len(groups)),
        out_shape=partial_shapes(role_count, local_length, far_width),
        scratch_shapes=fetch_scratch(*project_args),
        compiler_params=pltpu.CompilerParams(vmem_limit_bytes=SMALL_VMEM),
        cost_estimate=SHORT,
    )(*project_args)

    width = residual.shape[2]
    row_shape = jax.ShapeDtypeStruct((local_length, width + GATE_COLUMNS), jnp.bfloat16)
    far_last = summed_over_role(far, far_residual, near_sums[0])
    sums = in_hbm(*near_sums, *far_last)
    hidden, normed, other_normed = pl.pallas_call(
        partial(norm_kernel, block_width),
        in_specs=[pl.BlockSpec(memory_space=pltpu.SMEM)] + in_vmem(3) + hbm_specs(len(sums)),
        out_specs=in_vmem(3),
        out_shape=[
            jax.ShapeDtypeStruct((local_length, width), jnp.float32),
            row_shape,
            row_shape,
        ],
        scratch_shapes=[pltpu.VMEM((local_length, width), jnp.float32)] + fetch_scratch(*sums),
        compiler_params=pltpu.CompilerParams(vmem_limit_bytes=SMALL_VMEM),
        cost_estimate=SHORT,
    )(at, norm_gain.reshape(1, width), routes, other_routes, *sums)

    across_steps = range(2, seq_count, 2)

    def walk(k, bits):
        found = [k]
        for n, bit in enumerate(bits):
            found += walk(k | bit, bits[n + 1 :])
        return found

    lower_bits = role_bits[:-1][::-1]
    order = walk(last, lower_bits) + walk(0, lower_bits)
    planes = {0: normed, last: other_normed}
    crossed = {}

    def across(part):
        return [over_seq(part, j) for j in across_steps]

    for k in order:
        if k not in planes:
            bit = k & -k
            planes[k] = over_role(planes[k ^ bit], bit)
        if k == 0:
            crossed[k] = across(after(normed, planes[order[1]]))
        elif k < last:
            crossed[k] = [over_role(part, k & -k) for part in crossed[k ^ (k & -k)]]
        else:
            crossed[k] = across(planes[k])

    keep, send, slots, leaving, passed = {}, {}, {}, {}, {}

    def expert(k, before, *others):
        late = [after(part, *before) for part in crossed[k]] if before else crossed[k]
        tokens = [planes[k]] + late
        tokens += [over_seq(part, 1) for part in tokens]
        if others:
            tokens = lax.optimization_barrier((*tokens, *others))[: len(tokens)]
        return run_expert(at, tokens, gate_weight, up_weight, down_weight)

    def combine(k, *before):
        came = over_seq(after(send[k], *before) if before else send[k], 1)
        sums = []
        for n in range(len(across_steps)):
            chunk = slice((n + 1) * local_length, (n + 2) * local_length)
            sums.append(added([keep[k][chunk], came[chunk]]).astype(jnp.bfloat16))
        return [keep[k][:local_length], came[:local_length]], sums

    def pass_on(k):
        passed[k] = [over_seq(part, j) for part, j in zip(leaving[k], across_steps)]
        slots[k] += passed[k]

    final, far_plane = order[-1], order[1]
    for n, k in enumerate(order):
        before = [keep[order[n - 1]]] if n else [planes[far_plane]]
        others, waits = [], []
        if k == last:
            waits = crossed[far_plane] + [planes[final]]
        elif k == far_plane:
            others, waits = leaving[last], crossed[0]
        elif k == 0:
            others = leaving[far_plane]
            leaving[last] = [after(part, *passed[far_plane]) for part in leaving[last]]
            pass_on(last)
        elif k == final:
            slots[far_plane] = [added(slots[far_plane]).astype(jnp.bfloat16)]
            others = slots[far_plane] + leaving[last]
        keep[k], send[k] = expert(k, before, *others)
        if k != 0:
            slots[k], leaving[k] = combine(k, *waits)
        if k not in (0, last):
            pass_on(k)
    slots[0], leaving[0] = combine(0, *passed[last], *crossed[final])
    leaving[0] = [after(part, *leaving[final]) for part in leaving[0]]
    pass_on(0)
    for bit in role_bits:
        for k in [k for k in sorted(slots, reverse=True) if k & bit]:
            going = added(slots.pop(k)).astype(jnp.bfloat16)
            if k == last:
                going = after(going, *leaving[final])
            slots[k ^ bit].append(over_role(going, bit))
    return added([hidden] + slots[0]).astype(jnp.bfloat16).reshape(residual.shape)


def solution(mesh):
    placed = (
        P("groups", "seq", "role"),
        P("groups", ("seq", "role"), None),
        P("groups", ("seq", "role"), None),
        P("role", "seq"),
        P(("groups", "role"), "seq", None),
        P(),
        P(("groups", "role"), "seq", None),
        P(("groups", "role"), "seq", None),
        P(("seq", "role"), None, None),
        P(("seq", "role"), None, None),
        P(("seq", "role"), None, None),
    )
    experts = mesh.shape["seq"] * mesh.shape["role"]
    return jax.shard_map(
        gathered_shards if experts <= 2 * TOPK else routed_shards,
        mesh=mesh,
        in_specs=placed,
        out_specs=P(("groups", "role"), "seq", None),
        check_vma=False,
    )
```

```python
from functools import partial

import jax
import jax.numpy as jnp
from jax import lax
from jax.experimental import pallas as pl
from jax.experimental.pallas import tpu as pltpu
from jax.sharding import PartitionSpec as P

D = 2048
QUERY_HEADS = 32
KEY_VALUE_HEADS = 4
HEAD_WIDTH = 128
TOPK = 8


epsilon = 1e-06
masked_score = -1e30
EXPERT_VMEM = 16 * 2**20
SMALL_VMEM = 12 * 2**20
COPY_VMEM = 4 * 2**20
GATE_COLUMNS = 128
NOTHING = pl.CostEstimate(flops=1, bytes_accessed=1, transcendentals=0)
SHORT = pl.CostEstimate(flops=2 * 10**9, bytes_accessed=4 * 2**20, transcendentals=0)
LONG = pl.CostEstimate(flops=10**10, bytes_accessed=1, transcendentals=0)


def score_block(queries, every_key, query_position, block_start, block_width, score_scale):
    keys_part = lax.slice_in_dim(every_key, block_start, block_start + block_width, axis=0)
    raw_scores = (
        jnp.einsum("qhd,kd->hqk", queries, keys_part, preferred_element_type=jnp.float32)
        * score_scale
    )
    key_position = block_start + jnp.arange(block_width, dtype=jnp.int32)
    return jnp.where(
        key_position[None, None, :] <= query_position[None, :, None], raw_scores, masked_score
    )


def value_block(rounded, every_value, block_start, block_width):
    prob_block = lax.slice_in_dim(rounded, block_start, block_start + block_width, axis=2)
    values_part = lax.slice_in_dim(every_value, block_start, block_start + block_width, axis=0)
    return jnp.einsum("hqk,kd->qhd", prob_block, values_part, preferred_element_type=jnp.float32)


def routed_shards(
    query_rows,
    encoded_key_rows,
    value_matrix_rows,
    output_weight,
    residual,
    norm_gain,
    route_experts,
    route_gates,
    gate_weight,
    up_weight,
    down_weight,
):
    seq_count = lax.axis_size("seq")
    role_count = lax.axis_size("role")
    seq_index = lax.axis_index("seq")
    role_index = lax.axis_index("role")
    batch_count = query_rows.shape[0]
    local_length = query_rows.shape[1]
    local_heads = query_rows.shape[2] // HEAD_WIDTH
    full_length = local_length * seq_count
    query_group_width = QUERY_HEADS // KEY_VALUE_HEADS
    head_pick = role_index * local_heads // query_group_width
    role_keys, role_values = (
        lax.all_gather(encoded_key_rows, "role", axis=1, tiled=True),
        lax.all_gather(value_matrix_rows, "role", axis=1, tiled=True),
    )
    head_keys = lax.dynamic_slice_in_dim(role_keys, head_pick * HEAD_WIDTH, HEAD_WIDTH, 2)
    head_values = lax.dynamic_slice_in_dim(role_values, head_pick * HEAD_WIDTH, HEAD_WIDTH, 2)
    whole_keys, whole_values, whole_proj = (
        lax.all_gather(head_keys, "seq", axis=1, tiled=True),
        lax.all_gather(head_values, "seq", axis=1, tiled=True),
        lax.all_gather(output_weight, "seq", axis=1, tiled=True),
    )
    key_width = full_length // 8
    score_scale = HEAD_WIDTH ** (-0.5)
    query_position = seq_index * local_length + jnp.arange(local_length, dtype=jnp.int32)
    last_needed = (seq_index + 1) * local_length

    def one_sequence(operands):
        own_queries, every_key, every_value = operands
        queries = own_queries.reshape(local_length, local_heads, HEAD_WIDTH)
        pieces = []
        for number in range(8):
            block_start = number * key_width
            compute = partial(
                score_block, queries, every_key, query_position, block_start, key_width, score_scale
            )
            skipped = partial(
                jnp.full, (local_heads, local_length, key_width), masked_score, jnp.float32
            )
            pieces.append(lax.cond(block_start < last_needed, compute, skipped))
        scores = jnp.concatenate(pieces, axis=2)
        row_peak = jnp.max(scores, axis=2, keepdims=True)
        weights = jnp.exp(scores - row_peak)
        totals = jnp.sum(weights, axis=2, keepdims=True)
        rounded = weights.astype(jnp.bfloat16)
        mixed_rows = jnp.zeros((local_length, local_heads, HEAD_WIDTH), jnp.float32)
        for number in range(8):
            block_start = number * key_width
            product = partial(value_block, rounded, every_value, block_start, key_width)
            nothing = partial(jnp.zeros, (local_length, local_heads, HEAD_WIDTH), jnp.float32)
            mixed_rows = mixed_rows + lax.cond(block_start < last_needed, product, nothing)
        attended = (mixed_rows / totals.transpose(1, 0, 2)).astype(jnp.bfloat16)
        return attended.reshape(local_length, local_heads * HEAD_WIDTH)

    attended = lax.map(one_sequence, (query_rows, whole_keys, whole_values))
    flat_attended = attended.reshape(batch_count * local_length, local_heads * HEAD_WIDTH)
    projected = lax.psum_scatter(
        jnp.dot(flat_attended, whole_proj, preferred_element_type=jnp.float32).astype(jnp.bfloat16),
        "role",
        scatter_dimension=0,
        tiled=True,
    ).astype(jnp.float32)
    hidden = residual[0].astype(jnp.float32) + projected
    variance = jnp.mean(hidden * hidden, axis=-1, keepdims=True)
    normed = (hidden * lax.rsqrt(variance + epsilon) * norm_gain).astype(jnp.bfloat16)
    expert_ids = route_experts.reshape(-1)
    gate_values = route_gates.reshape(-1)
    experts_local = gate_weight.shape[0]
    device_count = seq_count * role_count
    expert_count = experts_local * device_count
    assign = expert_ids.shape[0]
    capacity = assign // expert_count + 1
    onehot = (expert_ids[:, None] == jnp.arange(expert_count, dtype=jnp.int32)[None, :]).astype(
        jnp.int32
    )
    earlier = jnp.cumsum(onehot, axis=0) - onehot
    slot_rank = jnp.sum(earlier * onehot, axis=1)
    slot_index = expert_ids * capacity + slot_rank
    source_token = jnp.arange(assign, dtype=jnp.int32) // TOPK
    slot_token = jnp.zeros((expert_count * capacity,), jnp.int32).at[slot_index].set(source_token)
    slot_used = jnp.zeros((expert_count * capacity,), jnp.bfloat16).at[slot_index].set(1.0)
    outgoing = (normed[slot_token] * slot_used[:, None]).reshape(
        device_count, experts_local, capacity, D
    )
    incoming = lax.all_to_all(outgoing, ("seq", "role"), split_axis=0, concat_axis=0, tiled=True)
    gate_hidden = jnp.einsum(
        "sjcd,jdf->sjcf", incoming, gate_weight, preferred_element_type=jnp.float32
    )
    up_hidden = jnp.einsum(
        "sjcd,jdf->sjcf", incoming, up_weight, preferred_element_type=jnp.float32
    )
    activated = (jax.nn.silu(gate_hidden) * up_hidden).astype(jnp.bfloat16)
    returned = lax.all_to_all(
        jnp.einsum(
            "sjcf,jfd->sjcd", activated, down_weight, preferred_element_type=jnp.float32
        ).astype(jnp.bfloat16),
        ("seq", "role"),
        split_axis=0,
        concat_axis=0,
        tiled=True,
    )
    gathered = returned.reshape(expert_count * capacity, D)[slot_index]
    weighted = gathered.astype(jnp.float32) * gate_values[:, None]
    expert_sum = jnp.sum(weighted.reshape(-1, TOPK, D), axis=1)
    return (hidden + expert_sum).astype(jnp.bfloat16).reshape(residual.shape)


def in_hbm(*arrays):
    return [pltpu.with_memory_space_constraint(array, pltpu.HBM) for array in arrays]


def hbm_specs(count):
    return [pl.BlockSpec(memory_space=pltpu.HBM)] * count


def fetch_scratch(*arrays):
    return [pltpu.VMEM(array.shape, array.dtype) for array in arrays] + [
        pltpu.SemaphoreType.DMA((len(arrays),))
    ]


def start_fetch(from_refs, scratch):
    *buffers, sems = scratch
    copies = [
        pltpu.make_async_copy(from_ref, buffer, sems.at[n])
        for n, (from_ref, buffer) in enumerate(zip(from_refs, buffers))
    ]
    for copy in copies:
        copy.start()
    return copies, buffers


def in_vmem(count):
    return [pl.BlockSpec(memory_space=pltpu.VMEM)] * count


def attend_kernel(seq_count, role_count, at_ref, *refs):
    count = seq_count + 3
    outputs = len(role_groups(role_count)) + 1
    attended_ref, *partial_refs = refs[count : count + outputs]
    copies, (query_ref, *buffers) = start_fetch(refs[:count], refs[count + outputs :])
    blocks, proj_refs = buffers[:seq_count], buffers[seq_count:]
    seq_index, role_index = at_ref[0], at_ref[1]
    local_length = query_ref.shape[1]
    local_heads = query_ref.shape[2] // HEAD_WIDTH
    per_role = local_length // role_count
    rows = local_heads * local_length
    keys_all = seq_count * local_length
    slot = lax.broadcasted_iota(jnp.int32, (rows, keys_all), 1)
    block_number, within = slot // local_length, slot % local_length
    key_position = (
        (seq_index ^ block_number) * local_length
        + (role_index ^ (within // per_role)) * per_role
        + within % per_role
    )
    query_position = (
        seq_index * local_length
        + lax.broadcasted_iota(jnp.int32, (rows, keys_all), 0) % local_length
    )
    seen = key_position <= query_position
    scale = HEAD_WIDTH ** (-0.5)
    for copy in copies[: 1 + seq_count]:
        copy.wait()
    for k in range(role_count):
        b = role_index ^ k
        own = query_ref[b]
        queries = jnp.concatenate(
            [own[:, h * HEAD_WIDTH : (h + 1) * HEAD_WIDTH] for h in range(local_heads)], axis=0
        )
        key_value = jnp.concatenate([block[b] for block in blocks], axis=0)
        keys, values = key_value[:, :HEAD_WIDTH], key_value[:, HEAD_WIDTH:]
        scores = lax.dot_general(
            queries, keys, (((1,), (1,)), ((), ())), preferred_element_type=jnp.float32
        )
        scores = jnp.where(seen, scores * scale, masked_score)
        weights = jnp.exp(scores - jnp.max(scores, axis=1, keepdims=True))
        totals = jnp.sum(weights, axis=1, keepdims=True)
        mixed = jnp.dot(weights.astype(jnp.bfloat16), values, preferred_element_type=jnp.float32)
        attended = (mixed / totals).astype(jnp.bfloat16)
        for h in range(local_heads):
            attended_ref[
                k * local_length : (k + 1) * local_length, h * HEAD_WIDTH : (h + 1) * HEAD_WIDTH
            ] = attended[h * local_length : (h + 1) * local_length]
    for copy in copies[1 + seq_count :]:
        copy.wait()
    project_into(role_count, attended_ref, proj_refs, partial_refs)


def join_kernel(*refs):
    *piece_refs, out_ref = refs
    at = 0
    for ref in piece_refs:
        size = ref.shape[1]
        out_ref[:, at : at + size, :] = ref[...]
        at += size


def role_groups(role_count):
    last = role_count // 2
    bits = [1 << n for n in range(last.bit_length() - 1)]
    return [[k for k in range(role_count) if k & -k == bit] for bit in bits] + [[0, last]]


def project_into(role_count, attended_ref, proj_refs, partial_refs):
    rows = attended_ref.shape[0] // role_count
    at = 0
    for proj_ref in proj_refs:
        width = proj_ref.shape[1]
        product = jnp.dot(
            attended_ref[...], proj_ref[...], preferred_element_type=jnp.float32
        ).astype(jnp.bfloat16)
        for group, partial_ref in zip(role_groups(role_count), partial_refs):
            for n, k in enumerate(group):
                partial_ref[n * rows : (n + 1) * rows, at : at + width] = product[
                    k * rows : (k + 1) * rows
                ]
        at += width


def project_kernel(role_count, *refs):
    outputs = len(role_groups(role_count))
    count = (len(refs) - outputs - 1) // 2
    copies, (attended_ref, *proj_refs) = start_fetch(refs[:count], refs[count + outputs :])
    for copy in copies:
        copy.wait()
    project_into(role_count, attended_ref, proj_refs, refs[count : count + outputs])


def partial_shapes(role_count, rows, width):
    return [
        jax.ShapeDtypeStruct((rows * len(group), width), jnp.bfloat16)
        for group in role_groups(role_count)
    ]


def near_kernel(sent_ref, came_ref, own_ref, other_ref, *scratch):
    copies, (sent, came) = start_fetch((sent_ref, came_ref), scratch)
    for copy in copies:
        copy.wait()
    rows = own_ref.shape[0]
    own_ref[...] = sent[:rows].astype(jnp.float32) + came[rows:].astype(jnp.float32)
    other_ref[...] = sent[rows:].astype(jnp.float32) + came[:rows].astype(jnp.float32)


def sum_kernel(far_count, route_ref, other_route_ref, *refs):
    count = 2 + 2 * far_count
    out_refs = refs[count : count + 2]
    copies, buffers = start_fetch(refs[:count], refs[count + 2 :])
    rows, width = buffers[0].shape
    for copy in copies[:2]:
        copy.wait()
    lane = lax.broadcasted_iota(jnp.int32, (rows, GATE_COLUMNS), 1)
    half = GATE_COLUMNS // 2
    expert = (lane % half).astype(jnp.float32)
    for own_ref, routes, out_ref in zip(buffers[:2], (route_ref, other_route_ref), out_refs):
        out_ref[:rows, :width] = own_ref[...].astype(jnp.bfloat16)
        shares = jnp.zeros((rows, GATE_COLUMNS), jnp.float32)
        routed = routes.shape[1] // 2
        for k in range(routed):
            named, weight = routes[:, k : k + 1], routes[:, routed + k : routed + k + 1]
            shares = shares + jnp.where(expert == named, weight, 0.0)
        first = shares.astype(jnp.bfloat16).astype(jnp.float32)
        out_ref[:rows, width:] = jnp.where(lane < half, first, shares - first).astype(jnp.bfloat16)
        out_ref[rows:, width:] = jnp.zeros((out_ref.shape[0] - rows, GATE_COLUMNS), jnp.bfloat16)
    for copy in copies[2:]:
        copy.wait()
    for n in range(far_count):
        sent, came = buffers[2 + 2 * n : 4 + 2 * n]
        to = slice((n + 1) * rows, (n + 2) * rows)
        for out_ref, mine, other in (
            (out_refs[0], sent[:rows], came[rows:]),
            (out_refs[1], sent[rows:], came[:rows]),
        ):
            total = mine.astype(jnp.float32) + other.astype(jnp.float32)
            out_ref[to, :width] = total.astype(jnp.bfloat16)


def norm_kernel(chips, at_ref, gain_ref, *refs):
    parts, (normed_ref, *hidden_refs, whole_ref) = refs[:chips], refs[chips:]
    seq_index = at_ref[0]
    features = whole_ref.shape[1]
    rows = whole_ref.shape[0] // chips
    width = features // chips // 2
    for n, part in enumerate(parts):
        for m in range(chips):
            to, source = slice(m * rows, (m + 1) * rows), slice((m ^ n) * rows, (m ^ n) * rows + rows)
            for j in range(2):
                start = pl.multiple_of((seq_index ^ (2 * n + j)) * width, width)
                whole_ref[to, pl.ds(start, width)] = part[
                    source, j * width : (j + 1) * width
                ].astype(jnp.float32)
        normed_ref[n * rows : (n + 1) * rows, features:] = part[:rows, 2 * width :]
    hidden = whole_ref[...]
    variance = jnp.mean(hidden * hidden, axis=1, keepdims=True)
    normed = hidden * lax.rsqrt(variance + epsilon) * gain_ref[...]
    normed_ref[:, :features] = normed.astype(jnp.bfloat16)
    for hidden_ref in hidden_refs:
        hidden_ref[...] = hidden[:rows]


def expert_kernel(token_count, at_ref, *refs):
    token_refs = refs[:token_count]
    gate_ref, up_ref, down_ref, keep_ref, send_ref, activated_ref = refs[token_count:]
    features, units = gate_ref.shape[1:]
    tokens = jnp.concatenate([ref[:, :features] for ref in token_refs], axis=0)
    gates = jnp.concatenate([ref[:, features:] for ref in token_refs], axis=0)
    lane = lax.broadcasted_iota(jnp.int32, gates.shape, 1)
    mine = lane % (GATE_COLUMNS // 2) == at_ref[2]
    share = jnp.sum(jnp.where(mine, gates.astype(jnp.float32), 0.0), axis=1, keepdims=True)
    block = 256 if units % 256 == 0 else units
    for f in range(0, units, block):
        gate_hidden = jnp.dot(
            tokens, gate_ref[0, :, f : f + block], preferred_element_type=jnp.float32
        )
        up_hidden = jnp.dot(tokens, up_ref[0, :, f : f + block], preferred_element_type=jnp.float32)
        activated_ref[:, f : f + block] = (
            gate_hidden / (1.0 + jnp.exp(-gate_hidden)) * up_hidden
        ).astype(jnp.bfloat16)
    kept = keep_ref.shape[0]
    block = 512 if features % 512 == 0 else features
    for c in range(0, features, block):
        product = jnp.dot(
            activated_ref[...], down_ref[0, :, c : c + block], preferred_element_type=jnp.float32
        )
        product = (product * share).astype(jnp.bfloat16)
        keep_ref[:, c : c + block] = product[:kept]
        send_ref[:, c : c + block] = product[kept:]


def run_expert(at, tokens, gate_weight, up_weight, down_weight):
    units = gate_weight.shape[2]
    width = gate_weight.shape[1]
    rows = sum(part.shape[0] for part in tokens)
    half = jax.ShapeDtypeStruct((rows // 2, width), jnp.bfloat16)
    return pl.pallas_call(
        partial(expert_kernel, len(tokens)),
        in_specs=[pl.BlockSpec(memory_space=pltpu.SMEM)] + in_vmem(len(tokens) + 3),
        out_specs=in_vmem(2),
        out_shape=[half, half],
        scratch_shapes=[pltpu.VMEM((rows, units), jnp.bfloat16)],
        compiler_params=pltpu.CompilerParams(vmem_limit_bytes=EXPERT_VMEM),
        cost_estimate=NOTHING,
    )(at, *tokens, gate_weight, up_weight, down_weight)


def after(array, *others):
    return lax.optimization_barrier((array, *others))[0]


def added(terms):
    total = terms[0].astype(jnp.float32)
    for term in terms[1:]:
        total = total + term.astype(jnp.float32)
    return total


def gathered_shards(
    query_rows,
    encoded_key_rows,
    value_matrix_rows,
    output_weight,
    residual,
    norm_gain,
    route_experts,
    route_gates,
    gate_weight,
    up_weight,
    down_weight,
):
    seq_count = lax.axis_size("seq")
    role_count = lax.axis_size("role")
    seq_index = lax.axis_index("seq")
    role_index = lax.axis_index("role")
    batch_count, local_length, query_width = query_rows.shape
    local_heads = query_width // HEAD_WIDTH
    group_width = QUERY_HEADS // KEY_VALUE_HEADS
    role_bits = [1 << n for n in range(role_count.bit_length() - 1)]
    at = jnp.stack([seq_index, role_index, seq_index * role_count + role_index]).astype(jnp.int32)

    def over_role(array, k):
        return lax.ppermute(array, "role", [(i, i ^ k) for i in range(role_count)])

    def over_seq(array, j):
        return lax.ppermute(array, "seq", [(i, i ^ j) for i in range(seq_count)])

    beside_proj = over_seq(output_weight, 1)
    block_width = output_weight.shape[1]
    across_steps = range(2, seq_count, 2)

    pieces = []
    for k in range(role_count):
        head = ((role_index ^ k) * local_heads // group_width) * HEAD_WIDTH
        piece = jnp.concatenate(
            [
                lax.dynamic_slice_in_dim(encoded_key_rows, head, HEAD_WIDTH, 2),
                lax.dynamic_slice_in_dim(value_matrix_rows, head, HEAD_WIDTH, 2),
            ],
            axis=2,
        )
        pieces.append(piece)
    pieces = [piece if k == 0 else over_role(piece, k) for k, piece in enumerate(pieces)]
    block = pl.pallas_call(
        join_kernel,
        in_specs=in_vmem(len(pieces)),
        out_specs=pl.BlockSpec(memory_space=pltpu.VMEM),
        out_shape=jax.ShapeDtypeStruct(
            (batch_count, local_length, 2 * HEAD_WIDTH), jnp.bfloat16
        ),
        compiler_params=pltpu.CompilerParams(vmem_limit_bytes=COPY_VMEM),
        cost_estimate=SHORT,
    )(*pieces)
    same_core = [block] + [over_seq(block, j) for j in across_steps]
    blocks = []
    for part in same_core:
        blocks += [part, over_seq(part, 1)]
    last = role_count // 2
    routes = jnp.concatenate([route_experts[0].astype(jnp.float32), route_gates[0]], axis=1)
    other_routes = over_role(routes, last)
    residual_blocks = [
        lax.dynamic_slice_in_dim(residual[0], (seq_index ^ j) * block_width, block_width, 1)
        for j in range(seq_count)
    ]
    residuals = [
        jnp.concatenate(residual_blocks[j : j + 2], axis=1) for j in range(0, seq_count, 2)
    ]
    residuals = [residuals[0]] + [over_seq(residuals[j // 2], j) for j in across_steps]

    rows = batch_count * local_length
    near_width = 2 * output_weight.shape[1]
    groups = role_groups(role_count)
    attend_args = in_hbm(query_rows, *blocks, output_weight, beside_proj)
    attended, *near = pl.pallas_call(
        partial(attend_kernel, seq_count, role_count),
        in_specs=[pl.BlockSpec(memory_space=pltpu.SMEM)] + hbm_specs(len(attend_args)),
        out_specs=in_vmem(1 + len(groups)),
        out_shape=[jax.ShapeDtypeStruct((rows, query_width), jnp.bfloat16)]
        + partial_shapes(role_count, local_length, near_width),
        scratch_shapes=fetch_scratch(*attend_args),
        compiler_params=pltpu.CompilerParams(vmem_limit_bytes=SMALL_VMEM),
        cost_estimate=SHORT,
    )(at, *attend_args)

    def summed_over_role(parts, extra, *before):
        terms = [[part] for part in parts]
        for n, group in enumerate(groups[:-1]):
            bit = 1 << n
            leaving = terms[n][0] if len(terms[n]) == 1 else added(terms[n]).astype(jnp.bfloat16)
            came = over_role(leaving, bit)
            for m in range(n + 1, len(groups)):
                at_rows = [group.index(k ^ bit) for k in groups[m]]
                if at_rows == list(range(len(group))):
                    terms[m].append(came)
                else:
                    split = [came[i * local_length : (i + 1) * local_length] for i in at_rows]
                    terms[m].append(jnp.concatenate(split, axis=0))
        extra = jnp.pad(after(extra, *before) if before else extra, ((0, local_length), (0, 0)))
        sent = added(terms[-1] + [extra]).astype(jnp.bfloat16)
        return sent

    near_sent = summed_over_role(near, residuals[0])
    near_args = in_hbm(near_sent, over_role(near_sent, last))
    near_sums = pl.pallas_call(
        near_kernel,
        in_specs=hbm_specs(2),
        out_specs=in_vmem(2),
        out_shape=[jax.ShapeDtypeStruct((local_length, near_width), jnp.float32)] * 2,
        scratch_shapes=fetch_scratch(*near_args),
        compiler_params=pltpu.CompilerParams(vmem_limit_bytes=COPY_VMEM),
        cost_estimate=LONG,
    )(*near_args)
    far_args = []
    for n, j in enumerate(across_steps, 1):
        project_args = in_hbm(over_seq(attended, j), output_weight, beside_proj)
        far = pl.pallas_call(
            partial(project_kernel, role_count),
            in_specs=hbm_specs(len(project_args)),
            out_specs=in_vmem(len(groups)),
            out_shape=partial_shapes(role_count, local_length, near_width),
            scratch_shapes=fetch_scratch(*project_args),
            compiler_params=pltpu.CompilerParams(vmem_limit_bytes=SMALL_VMEM),
            cost_estimate=SHORT,
        )(*project_args)
        far_sent = summed_over_role(far, residuals[n], near_sums[0])
        far_args += [far_sent, over_role(far_sent, last)]

    chips = 1 + len(across_steps)
    sum_args = in_hbm(*near_sums, *far_args)
    half_shape = jax.ShapeDtypeStruct(
        (chips * local_length, near_width + GATE_COLUMNS), jnp.bfloat16
    )
    own_half, other_half = pl.pallas_call(
        partial(sum_kernel, len(across_steps)),
        in_specs=in_vmem(2) + hbm_specs(len(sum_args)),
        out_specs=in_vmem(2),
        out_shape=[half_shape] * 2,
        scratch_shapes=fetch_scratch(*sum_args),
        compiler_params=pltpu.CompilerParams(vmem_limit_bytes=SMALL_VMEM),
        cost_estimate=SHORT,
    )(routes, other_routes, *sum_args)

    width = residual.shape[2]
    gain = norm_gain.reshape(1, width)

    def normed_rows(parts, *hidden_shape):
        rows = chips * local_length
        return pl.pallas_call(
            partial(norm_kernel, chips),
            in_specs=[pl.BlockSpec(memory_space=pltpu.SMEM)] + in_vmem(1 + chips),
            out_specs=in_vmem(1 + len(hidden_shape)),
            out_shape=[
                jax.ShapeDtypeStruct((rows, width + GATE_COLUMNS), jnp.bfloat16),
                *hidden_shape,
            ],
            scratch_shapes=[pltpu.VMEM((rows, width), jnp.float32)],
            compiler_params=pltpu.CompilerParams(vmem_limit_bytes=SMALL_VMEM),
            cost_estimate=NOTHING,
        )(at, gain, *parts)

    def walk(k, bits):
        found = [k]
        for n, bit in enumerate(bits):
            found += walk(k | bit, bits[n + 1 :])
        return found

    lower_bits = role_bits[:-1][::-1]
    order = walk(last, lower_bits) + walk(0, lower_bits)
    planes = {0: own_half, last: other_half}
    crossed = {}

    def across(part):
        return [over_seq(part, j) for j in across_steps]

    for k in order:
        if k not in planes:
            bit = k & -k
            planes[k] = over_role(planes[k ^ bit], bit)
        if k == 0:
            crossed[k] = across(after(own_half, planes[order[1]]))
        elif k < last:
            crossed[k] = [over_role(part, k & -k) for part in crossed[k ^ (k & -k)]]
        else:
            crossed[k] = across(planes[k])

    keep, send, slots, leaving, passed = {}, {}, {}, {}, {}

    hidden_shape = jax.ShapeDtypeStruct((local_length, width), jnp.float32)
    hidden = []

    def expert(k, before, *others):
        late = [after(part, *before) for part in crossed[k]] if before else crossed[k]
        normed, *own = normed_rows([planes[k]] + late, *([] if k else [hidden_shape]))
        hidden.extend(own)
        tokens = [normed, over_seq(normed, 1)]
        if others:
            tokens = lax.optimization_barrier((*tokens, *others))[: len(tokens)]
        return run_expert(at, tokens, gate_weight, up_weight, down_weight)

    def combine(k, *before):
        came = over_seq(after(send[k], *before) if before else send[k], 1)
        sums = []
        for n in range(len(across_steps)):
            chunk = slice((n + 1) * local_length, (n + 2) * local_length)
            sums.append(added([keep[k][chunk], came[chunk]]).astype(jnp.bfloat16))
        return [keep[k][:local_length], came[:local_length]], sums

    def pass_on(k):
        passed[k] = [over_seq(part, j) for part, j in zip(leaving[k], across_steps)]
        slots[k] += passed[k]

    final, far_plane = order[-1], order[1]
    for n, k in enumerate(order):
        before = [keep[order[n - 1]]] if n else [planes[far_plane]]
        others, waits = [], []
        if k == last:
            waits = crossed[far_plane] + [planes[final]]
        elif k == far_plane:
            others, waits = leaving[last], crossed[0]
        elif k == 0:
            others = leaving[far_plane]
            leaving[last] = [after(part, *passed[far_plane]) for part in leaving[last]]
            pass_on(last)
        elif k == final:
            slots[far_plane] = [added(slots[far_plane]).astype(jnp.bfloat16)]
            others = slots[far_plane] + leaving[last]
        keep[k], send[k] = expert(k, before, *others)
        if k != 0:
            slots[k], leaving[k] = combine(k, *waits)
        if k not in (0, last):
            pass_on(k)
    slots[0], leaving[0] = combine(0, *passed[last], *crossed[final])
    leaving[0] = [after(part, *leaving[final]) for part in leaving[0]]
    pass_on(0)
    for bit in role_bits:
        for k in [k for k in sorted(slots, reverse=True) if k & bit]:
            going = added(slots.pop(k)).astype(jnp.bfloat16)
            if k == last:
                going = after(going, *leaving[final])
            slots[k ^ bit].append(over_role(going, bit))
    return added(hidden + slots[0]).astype(jnp.bfloat16).reshape(residual.shape)


def solution(mesh):
    placed = (
        P("groups", "seq", "role"),
        P("groups", ("seq", "role"), None),
        P("groups", ("seq", "role"), None),
        P("role", "seq"),
        P(("groups", "role"), "seq", None),
        P(),
        P(("groups", "role"), "seq", None),
        P(("groups", "role"), "seq", None),
        P(("seq", "role"), None, None),
        P(("seq", "role"), None, None),
        P(("seq", "role"), None, None),
    )
    experts = mesh.shape["seq"] * mesh.shape["role"]
    return jax.shard_map(
        gathered_shards if experts <= 2 * TOPK else routed_shards,
        mesh=mesh,
        in_specs=placed,
        out_specs=P(("groups", "role"), "seq", None),
        check_vma=False,
    )
```

```python
from functools import partial

import jax
import jax.numpy as jnp
from jax import lax
from jax.experimental import pallas as pl
from jax.experimental.pallas import tpu as pltpu
from jax.sharding import PartitionSpec as P

D = 2048
QUERY_HEADS = 32
KEY_VALUE_HEADS = 4
HEAD_WIDTH = 128
TOPK = 8


epsilon = 1e-06
masked_score = -1e30
EXPERT_VMEM = 16 * 2**20
SMALL_VMEM = 12 * 2**20
COPY_VMEM = 4 * 2**20
GATE_COLUMNS = 128
NOTHING = pl.CostEstimate(flops=1, bytes_accessed=1, transcendentals=0)
SHORT = pl.CostEstimate(flops=2 * 10**9, bytes_accessed=4 * 2**20, transcendentals=0)
LONG = pl.CostEstimate(flops=10**10, bytes_accessed=1, transcendentals=0)


def score_block(queries, every_key, query_position, block_start, block_width, score_scale):
    keys_part = lax.slice_in_dim(every_key, block_start, block_start + block_width, axis=0)
    raw_scores = (
        jnp.einsum("qhd,kd->hqk", queries, keys_part, preferred_element_type=jnp.float32)
        * score_scale
    )
    key_position = block_start + jnp.arange(block_width, dtype=jnp.int32)
    return jnp.where(
        key_position[None, None, :] <= query_position[None, :, None], raw_scores, masked_score
    )


def value_block(rounded, every_value, block_start, block_width):
    prob_block = lax.slice_in_dim(rounded, block_start, block_start + block_width, axis=2)
    values_part = lax.slice_in_dim(every_value, block_start, block_start + block_width, axis=0)
    return jnp.einsum("hqk,kd->qhd", prob_block, values_part, preferred_element_type=jnp.float32)


def routed_shards(
    query_rows,
    encoded_key_rows,
    value_matrix_rows,
    output_weight,
    residual,
    norm_gain,
    route_experts,
    route_gates,
    gate_weight,
    up_weight,
    down_weight,
):
    seq_count = lax.axis_size("seq")
    role_count = lax.axis_size("role")
    seq_index = lax.axis_index("seq")
    role_index = lax.axis_index("role")
    batch_count = query_rows.shape[0]
    local_length = query_rows.shape[1]
    local_heads = query_rows.shape[2] // HEAD_WIDTH
    full_length = local_length * seq_count
    query_group_width = QUERY_HEADS // KEY_VALUE_HEADS
    head_pick = role_index * local_heads // query_group_width
    role_keys, role_values = (
        lax.all_gather(encoded_key_rows, "role", axis=1, tiled=True),
        lax.all_gather(value_matrix_rows, "role", axis=1, tiled=True),
    )
    head_keys = lax.dynamic_slice_in_dim(role_keys, head_pick * HEAD_WIDTH, HEAD_WIDTH, 2)
    head_values = lax.dynamic_slice_in_dim(role_values, head_pick * HEAD_WIDTH, HEAD_WIDTH, 2)
    whole_keys, whole_values, whole_proj = (
        lax.all_gather(head_keys, "seq", axis=1, tiled=True),
        lax.all_gather(head_values, "seq", axis=1, tiled=True),
        lax.all_gather(output_weight, "seq", axis=1, tiled=True),
    )
    key_width = full_length // 8
    score_scale = HEAD_WIDTH ** (-0.5)
    query_position = seq_index * local_length + jnp.arange(local_length, dtype=jnp.int32)
    last_needed = (seq_index + 1) * local_length

    def one_sequence(operands):
        own_queries, every_key, every_value = operands
        queries = own_queries.reshape(local_length, local_heads, HEAD_WIDTH)
        pieces = []
        for number in range(8):
            block_start = number * key_width
            compute = partial(
                score_block, queries, every_key, query_position, block_start, key_width, score_scale
            )
            skipped = partial(
                jnp.full, (local_heads, local_length, key_width), masked_score, jnp.float32
            )
            pieces.append(lax.cond(block_start < last_needed, compute, skipped))
        scores = jnp.concatenate(pieces, axis=2)
        row_peak = jnp.max(scores, axis=2, keepdims=True)
        weights = jnp.exp(scores - row_peak)
        totals = jnp.sum(weights, axis=2, keepdims=True)
        rounded = weights.astype(jnp.bfloat16)
        mixed_rows = jnp.zeros((local_length, local_heads, HEAD_WIDTH), jnp.float32)
        for number in range(8):
            block_start = number * key_width
            product = partial(value_block, rounded, every_value, block_start, key_width)
            nothing = partial(jnp.zeros, (local_length, local_heads, HEAD_WIDTH), jnp.float32)
            mixed_rows = mixed_rows + lax.cond(block_start < last_needed, product, nothing)
        attended = (mixed_rows / totals.transpose(1, 0, 2)).astype(jnp.bfloat16)
        return attended.reshape(local_length, local_heads * HEAD_WIDTH)

    attended = lax.map(one_sequence, (query_rows, whole_keys, whole_values))
    flat_attended = attended.reshape(batch_count * local_length, local_heads * HEAD_WIDTH)
    projected = lax.psum_scatter(
        jnp.dot(flat_attended, whole_proj, preferred_element_type=jnp.float32).astype(jnp.bfloat16),
        "role",
        scatter_dimension=0,
        tiled=True,
    ).astype(jnp.float32)
    hidden = residual[0].astype(jnp.float32) + projected
    variance = jnp.mean(hidden * hidden, axis=-1, keepdims=True)
    normed = (hidden * lax.rsqrt(variance + epsilon) * norm_gain).astype(jnp.bfloat16)
    expert_ids = route_experts.reshape(-1)
    gate_values = route_gates.reshape(-1)
    experts_local = gate_weight.shape[0]
    device_count = seq_count * role_count
    expert_count = experts_local * device_count
    assign = expert_ids.shape[0]
    capacity = assign // expert_count + 1
    onehot = (expert_ids[:, None] == jnp.arange(expert_count, dtype=jnp.int32)[None, :]).astype(
        jnp.int32
    )
    earlier = jnp.cumsum(onehot, axis=0) - onehot
    slot_rank = jnp.sum(earlier * onehot, axis=1)
    slot_index = expert_ids * capacity + slot_rank
    source_token = jnp.arange(assign, dtype=jnp.int32) // TOPK
    slot_token = jnp.zeros((expert_count * capacity,), jnp.int32).at[slot_index].set(source_token)
    slot_used = jnp.zeros((expert_count * capacity,), jnp.bfloat16).at[slot_index].set(1.0)
    outgoing = (normed[slot_token] * slot_used[:, None]).reshape(
        device_count, experts_local, capacity, D
    )
    incoming = lax.all_to_all(outgoing, ("seq", "role"), split_axis=0, concat_axis=0, tiled=True)
    gate_hidden = jnp.einsum(
        "sjcd,jdf->sjcf", incoming, gate_weight, preferred_element_type=jnp.float32
    )
    up_hidden = jnp.einsum(
        "sjcd,jdf->sjcf", incoming, up_weight, preferred_element_type=jnp.float32
    )
    activated = (jax.nn.silu(gate_hidden) * up_hidden).astype(jnp.bfloat16)
    returned = lax.all_to_all(
        jnp.einsum(
            "sjcf,jfd->sjcd", activated, down_weight, preferred_element_type=jnp.float32
        ).astype(jnp.bfloat16),
        ("seq", "role"),
        split_axis=0,
        concat_axis=0,
        tiled=True,
    )
    gathered = returned.reshape(expert_count * capacity, D)[slot_index]
    weighted = gathered.astype(jnp.float32) * gate_values[:, None]
    expert_sum = jnp.sum(weighted.reshape(-1, TOPK, D), axis=1)
    return (hidden + expert_sum).astype(jnp.bfloat16).reshape(residual.shape)


def in_hbm(*arrays):
    return [pltpu.with_memory_space_constraint(array, pltpu.HBM) for array in arrays]


def hbm_specs(count):
    return [pl.BlockSpec(memory_space=pltpu.HBM)] * count


def fetch_scratch(*arrays):
    return [pltpu.VMEM(array.shape, array.dtype) for array in arrays] + [
        pltpu.SemaphoreType.DMA((len(arrays),))
    ]


def start_fetch(from_refs, scratch):
    *buffers, sems = scratch
    copies = [
        pltpu.make_async_copy(from_ref, buffer, sems.at[n])
        for n, (from_ref, buffer) in enumerate(zip(from_refs, buffers))
    ]
    for copy in copies:
        copy.start()
    return copies, buffers


def in_vmem(count):
    return [pl.BlockSpec(memory_space=pltpu.VMEM)] * count


def attend_kernel(seq_count, role_count, at_ref, *refs):
    last_block, *refs = refs
    count = seq_count + 2
    outputs = len(role_groups(role_count)) + 2
    odd_ref, even_ref, *partial_refs = refs[count : count + outputs]
    *scratch, attended_ref = refs[count + outputs :]
    copies, (query_ref, *buffers) = start_fetch(refs[:count], scratch)
    blocks, proj_refs = buffers[: seq_count - 1] + [last_block], buffers[seq_count - 1 :]
    seq_index, role_index = at_ref[0], at_ref[1]
    local_length = query_ref.shape[1]
    local_heads = query_ref.shape[2] // HEAD_WIDTH
    per_role = local_length // role_count
    rows = local_heads * local_length
    keys_all = seq_count * local_length
    slot = lax.broadcasted_iota(jnp.int32, (rows, keys_all), 1)
    block_number, within = slot // local_length, slot % local_length
    key_position = (
        (seq_index ^ block_number) * local_length
        + (role_index ^ (within // per_role)) * per_role
        + within % per_role
    )
    query_position = (
        seq_index * local_length
        + lax.broadcasted_iota(jnp.int32, (rows, keys_all), 0) % local_length
    )
    seen = key_position <= query_position
    scale = HEAD_WIDTH ** (-0.5)
    for copy in copies[:seq_count]:
        copy.wait()
    for k in range(role_count):
        b = role_index ^ k
        own = query_ref[b]
        queries = jnp.concatenate(
            [own[:, h * HEAD_WIDTH : (h + 1) * HEAD_WIDTH] for h in range(local_heads)], axis=0
        )
        key_value = jnp.concatenate([block[b] for block in blocks], axis=0)
        keys, values = key_value[:, :HEAD_WIDTH], key_value[:, HEAD_WIDTH:]
        scores = lax.dot_general(
            queries, keys, (((1,), (1,)), ((), ())), preferred_element_type=jnp.float32
        )
        scores = jnp.where(seen, scores * scale, masked_score)
        weights = jnp.exp(scores - jnp.max(scores, axis=1, keepdims=True))
        totals = jnp.sum(weights, axis=1, keepdims=True)
        mixed = jnp.dot(weights.astype(jnp.bfloat16), values, preferred_element_type=jnp.float32)
        attended = (mixed / totals).astype(jnp.bfloat16)
        for h in range(local_heads):
            attended_ref[
                k * local_length : (k + 1) * local_length, h * HEAD_WIDTH : (h + 1) * HEAD_WIDTH
            ] = attended[h * local_length : (h + 1) * local_length]
    for slots_ref, first in ((odd_ref, 1), (even_ref, 0)):
        for n, k in enumerate(range(first, role_count, 2)):
            to = slice(n * local_length, (n + 1) * local_length)
            slots_ref[to] = attended_ref[k * local_length : (k + 1) * local_length]
    for copy in copies[seq_count:]:
        copy.wait()
    project_into(range(role_count), role_groups(role_count), attended_ref, proj_refs, partial_refs)


def join_kernel(*refs):
    *piece_refs, _, out_ref = refs
    at = 0
    for ref in piece_refs:
        size = ref.shape[1]
        out_ref[:, at : at + size, :] = ref[...]
        at += size


def role_groups(role_count):
    last = role_count // 2
    bits = [1 << n for n in range(last.bit_length() - 1)]
    return [[k for k in range(role_count) if k & -k == bit] for bit in bits] + [[0, last]]


def project_into(slots, groups, attended_ref, proj_refs, partial_refs):
    slots = list(slots)
    rows = attended_ref.shape[0] // len(slots)
    at = 0
    for proj_ref in proj_refs:
        width = proj_ref.shape[1]
        product = jnp.dot(
            attended_ref[...], proj_ref[...], preferred_element_type=jnp.float32
        ).astype(jnp.bfloat16)
        for group, partial_ref in zip(groups, partial_refs):
            for n, k in enumerate(group):
                start = slots.index(k) * rows
                partial_ref[n * rows : (n + 1) * rows, at : at + width] = product[
                    start : start + rows
                ]
        at += width


def project_kernel(slots, groups, attended_ref, *refs):
    count = (len(refs) - len(groups) - 1) // 2
    copies, proj_refs = start_fetch(refs[:count], refs[count + len(groups) :])
    for copy in copies:
        copy.wait()
    project_into(slots, groups, attended_ref, proj_refs, refs[count : count + len(groups)])


def partial_shapes(groups, rows, width):
    return [jax.ShapeDtypeStruct((rows * len(group), width), jnp.bfloat16) for group in groups]


def near_kernel(sent_ref, came_ref, own_ref, other_ref, *scratch):
    copies, (sent, came) = start_fetch((sent_ref, came_ref), scratch)
    for copy in copies:
        copy.wait()
    rows = own_ref.shape[0]
    own_ref[...] = sent[:rows].astype(jnp.float32) + came[rows:].astype(jnp.float32)
    other_ref[...] = sent[rows:].astype(jnp.float32) + came[:rows].astype(jnp.float32)


def sum_kernel(far_count, route_ref, other_route_ref, *refs):
    count = 2 + 2 * far_count
    out_refs, both_ref = refs[count : count + 2], refs[count + 2]
    copies, buffers = start_fetch(refs[:count], refs[count + 3 :])
    rows, width = buffers[0].shape
    for copy in copies[:2]:
        copy.wait()
    lane = lax.broadcasted_iota(jnp.int32, (rows, GATE_COLUMNS), 1)
    half = GATE_COLUMNS // 2
    expert = (lane % half).astype(jnp.float32)
    for own_ref, routes, out_ref in zip(buffers[:2], (route_ref, other_route_ref), out_refs):
        out_ref[:rows, :width] = own_ref[...].astype(jnp.bfloat16)
        shares = jnp.zeros((rows, GATE_COLUMNS), jnp.float32)
        routed = routes.shape[1] // 2
        for k in range(routed):
            named, weight = routes[:, k : k + 1], routes[:, routed + k : routed + k + 1]
            shares = shares + jnp.where(expert == named, weight, 0.0)
        first = shares.astype(jnp.bfloat16).astype(jnp.float32)
        out_ref[:rows, width:] = jnp.where(lane < half, first, shares - first).astype(jnp.bfloat16)
        out_ref[rows:, width:] = jnp.zeros((out_ref.shape[0] - rows, GATE_COLUMNS), jnp.bfloat16)
    for copy in copies[2:]:
        copy.wait()
    for n in range(far_count):
        sent, came = buffers[2 + 2 * n : 4 + 2 * n]
        to = slice((n + 1) * rows, (n + 2) * rows)
        for out_ref, mine, other in (
            (out_refs[0], sent[:rows], came[rows:]),
            (out_refs[1], sent[rows:], came[:rows]),
        ):
            total = mine.astype(jnp.float32) + other.astype(jnp.float32)
            out_ref[to, :width] = total.astype(jnp.bfloat16)
    size = both_ref.shape[0] // 2
    for n, out_ref in enumerate(out_refs):
        both_ref[n * size : (n + 1) * size] = out_ref[...]


def norm_kernel(chips, first_row, at_ref, gain_ref, *refs):
    parts, (normed_ref, *hidden_refs, whole_ref) = refs[:chips], refs[chips:]
    seq_index = at_ref[0]
    features = whole_ref.shape[1]
    rows = whole_ref.shape[0] // chips
    width = features // chips // 2
    for n, part in enumerate(parts):
        above = first_row if n else 0
        for m in range(chips):
            to = slice(m * rows, (m + 1) * rows)
            source = slice(above + (m ^ n) * rows, above + (m ^ n) * rows + rows)
            for j in range(2):
                start = pl.multiple_of((seq_index ^ (2 * n + j)) * width, width)
                whole_ref[to, pl.ds(start, width)] = part[
                    source, j * width : (j + 1) * width
                ].astype(jnp.float32)
        normed_ref[n * rows : (n + 1) * rows, features:] = part[above : above + rows, 2 * width :]
    hidden = whole_ref[...]
    variance = jnp.mean(hidden * hidden, axis=1, keepdims=True)
    normed = hidden * lax.rsqrt(variance + epsilon) * gain_ref[...]
    normed_ref[:, :features] = normed.astype(jnp.bfloat16)
    for hidden_ref in hidden_refs:
        hidden_ref[...] = hidden[:rows]


def expert_kernel(token_count, at_ref, *refs):
    token_refs = refs[:token_count]
    gate_ref, up_ref, down_ref, keep_ref, send_ref, activated_ref = refs[token_count:]
    features, units = gate_ref.shape[1:]
    tokens = jnp.concatenate([ref[:, :features] for ref in token_refs], axis=0)
    gates = jnp.concatenate([ref[:, features:] for ref in token_refs], axis=0)
    lane = lax.broadcasted_iota(jnp.int32, gates.shape, 1)
    mine = lane % (GATE_COLUMNS // 2) == at_ref[2]
    share = jnp.sum(jnp.where(mine, gates.astype(jnp.float32), 0.0), axis=1, keepdims=True)
    block = 256 if units % 256 == 0 else units
    for f in range(0, units, block):
        gate_hidden = jnp.dot(
            tokens, gate_ref[0, :, f : f + block], preferred_element_type=jnp.float32
        )
        up_hidden = jnp.dot(tokens, up_ref[0, :, f : f + block], preferred_element_type=jnp.float32)
        activated_ref[:, f : f + block] = (
            gate_hidden / (1.0 + jnp.exp(-gate_hidden)) * up_hidden
        ).astype(jnp.bfloat16)
    kept = keep_ref.shape[0]
    block = 512 if features % 512 == 0 else features
    for c in range(0, features, block):
        product = jnp.dot(
            activated_ref[...], down_ref[0, :, c : c + block], preferred_element_type=jnp.float32
        )
        product = (product * share).astype(jnp.bfloat16)
        keep_ref[:, c : c + block] = product[:kept]
        send_ref[:, c : c + block] = product[kept:]


def run_expert(at, tokens, gate_weight, up_weight, down_weight):
    units = gate_weight.shape[2]
    width = gate_weight.shape[1]
    rows = sum(part.shape[0] for part in tokens)
    half = jax.ShapeDtypeStruct((rows // 2, width), jnp.bfloat16)
    return pl.pallas_call(
        partial(expert_kernel, len(tokens)),
        in_specs=[pl.BlockSpec(memory_space=pltpu.SMEM)] + in_vmem(len(tokens) + 3),
        out_specs=in_vmem(2),
        out_shape=[half, half],
        scratch_shapes=[pltpu.VMEM((rows, units), jnp.bfloat16)],
        compiler_params=pltpu.CompilerParams(vmem_limit_bytes=EXPERT_VMEM),
        cost_estimate=NOTHING,
    )(at, *tokens, gate_weight, up_weight, down_weight)


def after(array, *others):
    return lax.optimization_barrier((array, *others))[0]


def added(terms):
    total = terms[0].astype(jnp.float32)
    for term in terms[1:]:
        total = total + term.astype(jnp.float32)
    return total


def gathered_shards(
    query_rows,
    encoded_key_rows,
    value_matrix_rows,
    output_weight,
    residual,
    norm_gain,
    route_experts,
    route_gates,
    gate_weight,
    up_weight,
    down_weight,
):
    seq_count = lax.axis_size("seq")
    role_count = lax.axis_size("role")
    seq_index = lax.axis_index("seq")
    role_index = lax.axis_index("role")
    batch_count, local_length, query_width = query_rows.shape
    local_heads = query_width // HEAD_WIDTH
    group_width = QUERY_HEADS // KEY_VALUE_HEADS
    role_bits = [1 << n for n in range(role_count.bit_length() - 1)]
    at = jnp.stack([seq_index, role_index, seq_index * role_count + role_index]).astype(jnp.int32)

    def over_role(array, k):
        return lax.ppermute(array, "role", [(i, i ^ k) for i in range(role_count)])

    def over_seq(array, j):
        return lax.ppermute(array, "seq", [(i, i ^ j) for i in range(seq_count)])

    beside_proj = over_seq(output_weight, 1)
    block_width = output_weight.shape[1]
    across_steps = range(2, seq_count, 2)

    pieces = []
    for k in range(role_count):
        head = ((role_index ^ k) * local_heads // group_width) * HEAD_WIDTH
        piece = jnp.concatenate(
            [
                lax.dynamic_slice_in_dim(encoded_key_rows, head, HEAD_WIDTH, 2),
                lax.dynamic_slice_in_dim(value_matrix_rows, head, HEAD_WIDTH, 2),
            ],
            axis=2,
        )
        pieces.append(piece)
    pieces = [piece if k == 0 else over_role(piece, k) for k, piece in enumerate(pieces)]
    block = pl.pallas_call(
        join_kernel,
        in_specs=in_vmem(len(pieces)) + [pl.BlockSpec(memory_space=pl.ANY)],
        out_specs=pl.BlockSpec(memory_space=pltpu.VMEM),
        out_shape=jax.ShapeDtypeStruct(
            (batch_count, local_length, 2 * HEAD_WIDTH), jnp.bfloat16
        ),
        compiler_params=pltpu.CompilerParams(vmem_limit_bytes=COPY_VMEM),
        cost_estimate=SHORT,
    )(*pieces, beside_proj)
    same_core = [block] + [over_seq(block, j) for j in across_steps]
    blocks = []
    for part in same_core:
        blocks += [part, over_seq(part, 1)]
    last = role_count // 2
    routes = jnp.concatenate([route_experts[0].astype(jnp.float32), route_gates[0]], axis=1)
    other_routes = over_role(routes, last)
    residual_blocks = [
        lax.dynamic_slice_in_dim(residual[0], (seq_index ^ j) * block_width, block_width, 1)
        for j in range(seq_count)
    ]
    residuals = [
        jnp.concatenate(residual_blocks[j : j + 2], axis=1) for j in range(0, seq_count, 2)
    ]
    residuals = [residuals[0]] + [over_seq(residuals[j // 2], j) for j in across_steps]

    rows = batch_count * local_length
    near_width = 2 * output_weight.shape[1]
    groups = role_groups(role_count)
    attend_args = in_hbm(query_rows, *blocks[:-1], output_weight, beside_proj)
    half_rows = jax.ShapeDtypeStruct((rows // 2, query_width), jnp.bfloat16)
    odd_rows, even_rows, *near = pl.pallas_call(
        partial(attend_kernel, seq_count, role_count),
        in_specs=[pl.BlockSpec(memory_space=pltpu.SMEM)] + in_vmem(1) + hbm_specs(len(attend_args)),
        out_specs=in_vmem(2 + len(groups)),
        out_shape=[half_rows] * 2 + partial_shapes(groups, local_length, near_width),
        scratch_shapes=fetch_scratch(*attend_args) + [pltpu.VMEM((rows, query_width), jnp.bfloat16)],
        compiler_params=pltpu.CompilerParams(vmem_limit_bytes=SMALL_VMEM),
        cost_estimate=SHORT,
    )(at, blocks[-1], *attend_args)

    def summed_over_role(parts, extra, *before):
        terms = [[part] for part in parts]
        for n, group in enumerate(groups[:-1]):
            bit = 1 << n
            leaving = terms[n][0] if len(terms[n]) == 1 else added(terms[n]).astype(jnp.bfloat16)
            came = over_role(leaving, bit)
            for m in range(n + 1, len(groups)):
                at_rows = [group.index(k ^ bit) for k in groups[m]]
                if at_rows == list(range(len(group))):
                    terms[m].append(came)
                else:
                    split = [came[i * local_length : (i + 1) * local_length] for i in at_rows]
                    terms[m].append(jnp.concatenate(split, axis=0))
        extra = jnp.pad(after(extra, *before) if before else extra, ((0, local_length), (0, 0)))
        sent = added(terms[-1] + [extra]).astype(jnp.bfloat16)
        return sent

    near_sent = summed_over_role(near, residuals[0])
    near_args = in_hbm(near_sent, over_role(near_sent, last))
    near_sums = pl.pallas_call(
        near_kernel,
        in_specs=hbm_specs(2),
        out_specs=in_vmem(2),
        out_shape=[jax.ShapeDtypeStruct((local_length, near_width), jnp.float32)] * 2,
        scratch_shapes=fetch_scratch(*near_args),
        compiler_params=pltpu.CompilerParams(vmem_limit_bytes=COPY_VMEM),
        cost_estimate=LONG,
    )(*near_args)
    far_args = []
    for n, j in enumerate(across_steps, 1):
        far = []
        for half, first in ((odd_rows, 1), (even_rows, 0)):
            parts = groups[:1] if first else groups[1:]
            far += pl.pallas_call(
                partial(project_kernel, range(first, role_count, 2), parts),
                in_specs=in_vmem(1) + hbm_specs(2),
                out_specs=in_vmem(len(parts)),
                out_shape=partial_shapes(parts, local_length, near_width),
                scratch_shapes=fetch_scratch(output_weight, beside_proj),
                compiler_params=pltpu.CompilerParams(vmem_limit_bytes=SMALL_VMEM),
                cost_estimate=SHORT,
            )(over_seq(half, j), *in_hbm(output_weight, beside_proj))
        far_sent = summed_over_role(far, residuals[n], near_sums[0])
        far_args += [far_sent, over_role(far_sent, last)]

    chips = 1 + len(across_steps)
    sum_args = in_hbm(*near_sums, *far_args)
    half_size = chips * local_length
    half_shape, both_shape = [
        jax.ShapeDtypeStruct((size, near_width + GATE_COLUMNS), jnp.bfloat16)
        for size in (half_size, 2 * half_size)
    ]
    own_half, other_half, both_halves = pl.pallas_call(
        partial(sum_kernel, len(across_steps)),
        in_specs=in_vmem(2) + hbm_specs(len(sum_args)),
        out_specs=in_vmem(3),
        out_shape=[half_shape, half_shape, both_shape],
        scratch_shapes=fetch_scratch(*sum_args),
        compiler_params=pltpu.CompilerParams(vmem_limit_bytes=SMALL_VMEM),
        cost_estimate=SHORT,
    )(routes, other_routes, *sum_args)

    width = residual.shape[2]
    gain = norm_gain.reshape(1, width)

    def normed_rows(parts, first_row, *hidden_shape):
        rows = chips * local_length
        return pl.pallas_call(
            partial(norm_kernel, chips, first_row),
            in_specs=[pl.BlockSpec(memory_space=pltpu.SMEM)] + in_vmem(1 + chips),
            out_specs=in_vmem(1 + len(hidden_shape)),
            out_shape=[
                jax.ShapeDtypeStruct((rows, width + GATE_COLUMNS), jnp.bfloat16),
                *hidden_shape,
            ],
            scratch_shapes=[pltpu.VMEM((rows, width), jnp.float32)],
            compiler_params=pltpu.CompilerParams(vmem_limit_bytes=SMALL_VMEM),
            cost_estimate=NOTHING,
        )(at, gain, *parts)

    def walk(k, bits):
        found = [k]
        for n, bit in enumerate(bits):
            found += walk(k | bit, bits[n + 1 :])
        return found

    lower_bits = role_bits[:-1][::-1]
    order = walk(last, lower_bits) + walk(0, lower_bits)
    planes = {0: own_half, last: other_half}
    crossed = {}

    def across(part):
        return [over_seq(part, j) for j in across_steps]

    both_across = across(both_halves)
    for k in order:
        if k not in planes:
            bit = k & -k
            planes[k] = over_role(planes[k ^ bit], bit)
        if k in (0, last):
            crossed[k] = both_across
        elif k < last:
            source = k ^ (k & -k)
            came = [part[:half_size] for part in crossed[source]] if source == 0 else crossed[source]
            crossed[k] = [over_role(part, k & -k) for part in came]
        else:
            crossed[k] = across(planes[k])

    keep, send, slots, leaving, passed = {}, {}, {}, {}, {}

    hidden_shape = jax.ShapeDtypeStruct((local_length, width), jnp.float32)
    hidden = []

    def expert(k, before, *others):
        late = [after(part, *before) for part in crossed[k]] if before else crossed[k]
        first_row = half_size if k == last else 0
        normed, *own = normed_rows([planes[k]] + late, first_row, *([] if k else [hidden_shape]))
        hidden.extend(own)
        tokens = [normed, over_seq(normed, 1)]
        if others:
            tokens = lax.optimization_barrier((*tokens, *others))[: len(tokens)]
        return run_expert(at, tokens, gate_weight, up_weight, down_weight)

    def combine(k, *before):
        came = over_seq(after(send[k], *before) if before else send[k], 1)
        sums = []
        for n in range(len(across_steps)):
            chunk = slice((n + 1) * local_length, (n + 2) * local_length)
            sums.append(added([keep[k][chunk], came[chunk]]).astype(jnp.bfloat16))
        return [keep[k][:local_length], came[:local_length]], sums

    def pass_on(k):
        passed[k] = [over_seq(part, j) for part, j in zip(leaving[k], across_steps)]
        slots[k] += passed[k]

    final, far_plane = order[-1], order[1]
    for n, k in enumerate(order):
        before = [keep[order[n - 1]]] if n else [planes[far_plane]]
        others, waits = [], []
        if k == last:
            waits = crossed[far_plane] + [planes[final]]
        elif k == far_plane:
            others = leaving[last]
        elif k == 0:
            others = leaving[far_plane]
            leaving[last] = [after(part, *passed[far_plane]) for part in leaving[last]]
            pass_on(last)
        elif k == final:
            slots[far_plane] = [added(slots[far_plane]).astype(jnp.bfloat16)]
            others = slots[far_plane] + leaving[last]
        keep[k], send[k] = expert(k, before, *others)
        if k != 0:
            slots[k], leaving[k] = combine(k, *waits)
        if k not in (0, last):
            pass_on(k)
    slots[0], leaving[0] = combine(0, *passed[last], *crossed[final])
    leaving[0] = [after(part, *leaving[final]) for part in leaving[0]]
    pass_on(0)
    for bit in role_bits:
        for k in [k for k in sorted(slots, reverse=True) if k & bit]:
            going = added(slots.pop(k)).astype(jnp.bfloat16)
            if k == last:
                going = after(going, *leaving[final])
            slots[k ^ bit].append(over_role(going, bit))
    return added(hidden + slots[0]).astype(jnp.bfloat16).reshape(residual.shape)


def solution(mesh):
    placed = (
        P("groups", "seq", "role"),
        P("groups", ("seq", "role"), None),
        P("groups", ("seq", "role"), None),
        P("role", "seq"),
        P(("groups", "role"), "seq", None),
        P(),
        P(("groups", "role"), "seq", None),
        P(("groups", "role"), "seq", None),
        P(("seq", "role"), None, None),
        P(("seq", "role"), None, None),
        P(("seq", "role"), None, None),
    )
    experts = mesh.shape["seq"] * mesh.shape["role"]
    return jax.shard_map(
        gathered_shards if experts <= 2 * TOPK else routed_shards,
        mesh=mesh,
        in_specs=placed,
        out_specs=P(("groups", "role"), "seq", None),
        check_vma=False,
    )
```

```python
from functools import partial

import jax
import jax.numpy as jnp
from jax import lax
from jax.experimental import pallas as pl
from jax.experimental.pallas import tpu as pltpu
from jax.sharding import PartitionSpec as P

D = 2048
QUERY_HEADS = 32
KEY_VALUE_HEADS = 4
HEAD_WIDTH = 128
TOPK = 8


epsilon = 1e-06
masked_score = -1e30
EXPERT_VMEM = 16 * 2**20
SMALL_VMEM = 12 * 2**20
COPY_VMEM = 4 * 2**20
GATE_COLUMNS = 128
NOTHING = pl.CostEstimate(flops=1, bytes_accessed=1, transcendentals=0)
SHORT = pl.CostEstimate(flops=2 * 10**9, bytes_accessed=4 * 2**20, transcendentals=0)
LONG = pl.CostEstimate(flops=10**10, bytes_accessed=1, transcendentals=0)


def score_block(queries, every_key, query_position, block_start, block_width, score_scale):
    keys_part = lax.slice_in_dim(every_key, block_start, block_start + block_width, axis=0)
    raw_scores = (
        jnp.einsum("qhd,kd->hqk", queries, keys_part, preferred_element_type=jnp.float32)
        * score_scale
    )
    key_position = block_start + jnp.arange(block_width, dtype=jnp.int32)
    return jnp.where(
        key_position[None, None, :] <= query_position[None, :, None], raw_scores, masked_score
    )


def value_block(rounded, every_value, block_start, block_width):
    prob_block = lax.slice_in_dim(rounded, block_start, block_start + block_width, axis=2)
    values_part = lax.slice_in_dim(every_value, block_start, block_start + block_width, axis=0)
    return jnp.einsum("hqk,kd->qhd", prob_block, values_part, preferred_element_type=jnp.float32)


def routed_shards(
    query_rows,
    encoded_key_rows,
    value_matrix_rows,
    output_weight,
    residual,
    norm_gain,
    route_experts,
    route_gates,
    gate_weight,
    up_weight,
    down_weight,
):
    seq_count = lax.axis_size("seq")
    role_count = lax.axis_size("role")
    seq_index = lax.axis_index("seq")
    role_index = lax.axis_index("role")
    batch_count = query_rows.shape[0]
    local_length = query_rows.shape[1]
    local_heads = query_rows.shape[2] // HEAD_WIDTH
    full_length = local_length * seq_count
    query_group_width = QUERY_HEADS // KEY_VALUE_HEADS
    head_pick = role_index * local_heads // query_group_width
    role_keys, role_values = (
        lax.all_gather(encoded_key_rows, "role", axis=1, tiled=True),
        lax.all_gather(value_matrix_rows, "role", axis=1, tiled=True),
    )
    head_keys = lax.dynamic_slice_in_dim(role_keys, head_pick * HEAD_WIDTH, HEAD_WIDTH, 2)
    head_values = lax.dynamic_slice_in_dim(role_values, head_pick * HEAD_WIDTH, HEAD_WIDTH, 2)
    whole_keys, whole_values, whole_proj = (
        lax.all_gather(head_keys, "seq", axis=1, tiled=True),
        lax.all_gather(head_values, "seq", axis=1, tiled=True),
        lax.all_gather(output_weight, "seq", axis=1, tiled=True),
    )
    key_width = full_length // 8
    score_scale = HEAD_WIDTH ** (-0.5)
    query_position = seq_index * local_length + jnp.arange(local_length, dtype=jnp.int32)
    last_needed = (seq_index + 1) * local_length

    def one_sequence(operands):
        own_queries, every_key, every_value = operands
        queries = own_queries.reshape(local_length, local_heads, HEAD_WIDTH)
        pieces = []
        for number in range(8):
            block_start = number * key_width
            compute = partial(
                score_block, queries, every_key, query_position, block_start, key_width, score_scale
            )
            skipped = partial(
                jnp.full, (local_heads, local_length, key_width), masked_score, jnp.float32
            )
            pieces.append(lax.cond(block_start < last_needed, compute, skipped))
        scores = jnp.concatenate(pieces, axis=2)
        row_peak = jnp.max(scores, axis=2, keepdims=True)
        weights = jnp.exp(scores - row_peak)
        totals = jnp.sum(weights, axis=2, keepdims=True)
        rounded = weights.astype(jnp.bfloat16)
        mixed_rows = jnp.zeros((local_length, local_heads, HEAD_WIDTH), jnp.float32)
        for number in range(8):
            block_start = number * key_width
            product = partial(value_block, rounded, every_value, block_start, key_width)
            nothing = partial(jnp.zeros, (local_length, local_heads, HEAD_WIDTH), jnp.float32)
            mixed_rows = mixed_rows + lax.cond(block_start < last_needed, product, nothing)
        attended = (mixed_rows / totals.transpose(1, 0, 2)).astype(jnp.bfloat16)
        return attended.reshape(local_length, local_heads * HEAD_WIDTH)

    attended = lax.map(one_sequence, (query_rows, whole_keys, whole_values))
    flat_attended = attended.reshape(batch_count * local_length, local_heads * HEAD_WIDTH)
    projected = lax.psum_scatter(
        jnp.dot(flat_attended, whole_proj, preferred_element_type=jnp.float32).astype(jnp.bfloat16),
        "role",
        scatter_dimension=0,
        tiled=True,
    ).astype(jnp.float32)
    hidden = residual[0].astype(jnp.float32) + projected
    variance = jnp.mean(hidden * hidden, axis=-1, keepdims=True)
    normed = (hidden * lax.rsqrt(variance + epsilon) * norm_gain).astype(jnp.bfloat16)
    expert_ids = route_experts.reshape(-1)
    gate_values = route_gates.reshape(-1)
    experts_local = gate_weight.shape[0]
    device_count = seq_count * role_count
    expert_count = experts_local * device_count
    assign = expert_ids.shape[0]
    capacity = assign // expert_count + 1
    onehot = (expert_ids[:, None] == jnp.arange(expert_count, dtype=jnp.int32)[None, :]).astype(
        jnp.int32
    )
    earlier = jnp.cumsum(onehot, axis=0) - onehot
    slot_rank = jnp.sum(earlier * onehot, axis=1)
    slot_index = expert_ids * capacity + slot_rank
    source_token = jnp.arange(assign, dtype=jnp.int32) // TOPK
    slot_token = jnp.zeros((expert_count * capacity,), jnp.int32).at[slot_index].set(source_token)
    slot_used = jnp.zeros((expert_count * capacity,), jnp.bfloat16).at[slot_index].set(1.0)
    outgoing = (normed[slot_token] * slot_used[:, None]).reshape(
        device_count, experts_local, capacity, D
    )
    incoming = lax.all_to_all(outgoing, ("seq", "role"), split_axis=0, concat_axis=0, tiled=True)
    gate_hidden = jnp.einsum(
        "sjcd,jdf->sjcf", incoming, gate_weight, preferred_element_type=jnp.float32
    )
    up_hidden = jnp.einsum(
        "sjcd,jdf->sjcf", incoming, up_weight, preferred_element_type=jnp.float32
    )
    activated = (jax.nn.silu(gate_hidden) * up_hidden).astype(jnp.bfloat16)
    returned = lax.all_to_all(
        jnp.einsum(
            "sjcf,jfd->sjcd", activated, down_weight, preferred_element_type=jnp.float32
        ).astype(jnp.bfloat16),
        ("seq", "role"),
        split_axis=0,
        concat_axis=0,
        tiled=True,
    )
    gathered = returned.reshape(expert_count * capacity, D)[slot_index]
    weighted = gathered.astype(jnp.float32) * gate_values[:, None]
    expert_sum = jnp.sum(weighted.reshape(-1, TOPK, D), axis=1)
    return (hidden + expert_sum).astype(jnp.bfloat16).reshape(residual.shape)


def in_hbm(*arrays):
    return [pltpu.with_memory_space_constraint(array, pltpu.HBM) for array in arrays]


def hbm_specs(count):
    return [pl.BlockSpec(memory_space=pltpu.HBM)] * count


def fetch_scratch(*arrays):
    return [pltpu.VMEM(array.shape, array.dtype) for array in arrays] + [
        pltpu.SemaphoreType.DMA((len(arrays),))
    ]


def start_fetch(from_refs, scratch):
    *buffers, sems = scratch
    copies = [
        pltpu.make_async_copy(from_ref, buffer, sems.at[n])
        for n, (from_ref, buffer) in enumerate(zip(from_refs, buffers))
    ]
    for copy in copies:
        copy.start()
    return copies, buffers


def in_vmem(count):
    return [pl.BlockSpec(memory_space=pltpu.VMEM)] * count


def attend_kernel(seq_count, role_count, at_ref, *refs):
    last_block, *refs = refs
    count = seq_count + 2
    outputs = len(role_groups(role_count)) + 2
    odd_ref, even_ref, *partial_refs = refs[count : count + outputs]
    *scratch, attended_ref = refs[count + outputs :]
    copies, (query_ref, *buffers) = start_fetch(refs[:count], scratch)
    blocks, proj_refs = buffers[: seq_count - 1] + [last_block], buffers[seq_count - 1 :]
    seq_index, role_index = at_ref[0], at_ref[1]
    local_length = query_ref.shape[1]
    local_heads = query_ref.shape[2] // HEAD_WIDTH
    per_role = local_length // role_count
    rows = local_heads * local_length
    keys_all = seq_count * local_length
    slot = lax.broadcasted_iota(jnp.int32, (rows, keys_all), 1)
    block_number, within = slot // local_length, slot % local_length
    key_position = (
        (seq_index ^ block_number) * local_length
        + (role_index ^ (within // per_role)) * per_role
        + within % per_role
    )
    query_position = (
        seq_index * local_length
        + lax.broadcasted_iota(jnp.int32, (rows, keys_all), 0) % local_length
    )
    seen = key_position <= query_position
    scale = HEAD_WIDTH ** (-0.5)
    for copy in copies[:seq_count]:
        copy.wait()
    for k in range(role_count):
        b = role_index ^ k
        own = query_ref[b]
        queries = jnp.concatenate(
            [own[:, h * HEAD_WIDTH : (h + 1) * HEAD_WIDTH] for h in range(local_heads)], axis=0
        )
        key_value = jnp.concatenate([block[b] for block in blocks], axis=0)
        keys, values = key_value[:, :HEAD_WIDTH], key_value[:, HEAD_WIDTH:]
        scores = lax.dot_general(
            queries, keys, (((1,), (1,)), ((), ())), preferred_element_type=jnp.float32
        )
        scores = jnp.where(seen, scores * scale, masked_score)
        weights = jnp.exp(scores - jnp.max(scores, axis=1, keepdims=True))
        totals = jnp.sum(weights, axis=1, keepdims=True)
        mixed = jnp.dot(weights.astype(jnp.bfloat16), values, preferred_element_type=jnp.float32)
        attended = (mixed / totals).astype(jnp.bfloat16)
        for h in range(local_heads):
            attended_ref[
                k * local_length : (k + 1) * local_length, h * HEAD_WIDTH : (h + 1) * HEAD_WIDTH
            ] = attended[h * local_length : (h + 1) * local_length]
    for slots_ref, first in ((odd_ref, 1), (even_ref, 0)):
        for n, k in enumerate(range(first, role_count, 2)):
            to = slice(n * local_length, (n + 1) * local_length)
            slots_ref[to] = attended_ref[k * local_length : (k + 1) * local_length]
    for copy in copies[seq_count:]:
        copy.wait()
    project_into(range(role_count), role_groups(role_count), attended_ref, proj_refs, partial_refs)


def join_kernel(*refs):
    *piece_refs, out_ref = refs
    at = 0
    for ref in piece_refs:
        size = ref.shape[1]
        out_ref[:, at : at + size, :] = ref[...]
        at += size


def role_groups(role_count):
    last = role_count // 2
    bits = [1 << n for n in range(last.bit_length() - 1)]
    return [[k for k in range(role_count) if k & -k == bit] for bit in bits] + [[0, last]]


def project_into(slots, groups, attended_ref, proj_refs, partial_refs):
    slots = list(slots)
    rows = attended_ref.shape[0] // len(slots)
    at = 0
    for proj_ref in proj_refs:
        width = proj_ref.shape[1]
        product = jnp.dot(
            attended_ref[...], proj_ref[...], preferred_element_type=jnp.float32
        ).astype(jnp.bfloat16)
        for group, partial_ref in zip(groups, partial_refs):
            for n, k in enumerate(group):
                start = slots.index(k) * rows
                partial_ref[n * rows : (n + 1) * rows, at : at + width] = product[
                    start : start + rows
                ]
        at += width


def project_kernel(slots, groups, attended_ref, *refs):
    count = (len(refs) - len(groups) - 1) // 2
    copies, proj_refs = start_fetch(refs[:count], refs[count + len(groups) :])
    for copy in copies:
        copy.wait()
    project_into(slots, groups, attended_ref, proj_refs, refs[count : count + len(groups)])


def partial_shapes(groups, rows, width):
    return [jax.ShapeDtypeStruct((rows * len(group), width), jnp.bfloat16) for group in groups]


def marker_kernel(came_ref, token_ref):
    token_ref[...] = jnp.zeros_like(token_ref)


def sum_kernel(chips, token_ref, route_ref, other_route_ref, *refs):
    count = 2 * chips
    out_refs, both_ref = refs[count : count + 2], refs[count + 2]
    copies, buffers = start_fetch(refs[:count], refs[count + 3 :])
    rows, width = buffers[0].shape
    rows //= 2
    lane = lax.broadcasted_iota(jnp.int32, (rows, GATE_COLUMNS), 1)
    half = GATE_COLUMNS // 2
    expert = (lane % half).astype(jnp.float32)
    size = both_ref.shape[0] // 2
    for p, routes in enumerate((route_ref, other_route_ref)):
        shares = jnp.zeros((rows, GATE_COLUMNS), jnp.float32)
        routed = routes.shape[1] // 2
        for k in range(routed):
            named, weight = routes[:, k : k + 1], routes[:, routed + k : routed + k + 1]
            shares = shares + jnp.where(expert == named, weight, 0.0)
        first = shares.astype(jnp.bfloat16).astype(jnp.float32)
        terms = jnp.where(lane < half, first, shares - first).astype(jnp.bfloat16)
        nothing = jnp.zeros((size - rows, GATE_COLUMNS), jnp.bfloat16)
        for to_ref, start in ((out_refs[p], 0), (both_ref, p * size)):
            to_ref[start : start + rows, width:] = terms
            to_ref[start + rows : start + size, width:] = nothing
    for n in range(chips):
        for copy in copies[2 * n : 2 * n + 2]:
            copy.wait()
        sent, came = buffers[2 * n : 2 * n + 2]
        for p in range(2):
            total = sent[p * rows : (p + 1) * rows].astype(jnp.float32)
            total = total + came[(1 - p) * rows : (2 - p) * rows].astype(jnp.float32)
            for to_ref, start in ((out_refs[p], n * rows), (both_ref, p * size + n * rows)):
                to_ref[start : start + rows, :width] = total.astype(jnp.bfloat16)


def norm_kernel(chips, first_row, at_ref, gain_ref, *refs):
    parts, (normed_ref, *hidden_refs, whole_ref) = refs[:chips], refs[chips:]
    seq_index = at_ref[0]
    features = whole_ref.shape[1]
    rows = whole_ref.shape[0] // chips
    width = features // chips // 2
    for n, part in enumerate(parts):
        above = first_row if n else 0
        for m in range(chips):
            to = slice(m * rows, (m + 1) * rows)
            source = slice(above + (m ^ n) * rows, above + (m ^ n) * rows + rows)
            for j in range(2):
                start = pl.multiple_of((seq_index ^ (2 * n + j)) * width, width)
                whole_ref[to, pl.ds(start, width)] = part[
                    source, j * width : (j + 1) * width
                ].astype(jnp.float32)
        normed_ref[n * rows : (n + 1) * rows, features:] = part[above : above + rows, 2 * width :]
    hidden = whole_ref[...]
    variance = jnp.mean(hidden * hidden, axis=1, keepdims=True)
    normed = hidden * lax.rsqrt(variance + epsilon) * gain_ref[...]
    normed_ref[:, :features] = normed.astype(jnp.bfloat16)
    for hidden_ref in hidden_refs:
        hidden_ref[...] = hidden[:rows]


def expert_kernel(token_count, at_ref, *refs):
    token_refs = refs[:token_count]
    gate_ref, up_ref, down_ref, keep_ref, send_ref, activated_ref = refs[token_count:]
    features, units = gate_ref.shape[1:]
    tokens = jnp.concatenate([ref[:, :features] for ref in token_refs], axis=0)
    gates = jnp.concatenate([ref[:, features:] for ref in token_refs], axis=0)
    lane = lax.broadcasted_iota(jnp.int32, gates.shape, 1)
    mine = lane % (GATE_COLUMNS // 2) == at_ref[2]
    share = jnp.sum(jnp.where(mine, gates.astype(jnp.float32), 0.0), axis=1, keepdims=True)
    block = 256 if units % 256 == 0 else units
    for f in range(0, units, block):
        gate_hidden = jnp.dot(
            tokens, gate_ref[0, :, f : f + block], preferred_element_type=jnp.float32
        )
        up_hidden = jnp.dot(tokens, up_ref[0, :, f : f + block], preferred_element_type=jnp.float32)
        activated_ref[:, f : f + block] = (
            gate_hidden / (1.0 + jnp.exp(-gate_hidden)) * up_hidden
        ).astype(jnp.bfloat16)
    kept = keep_ref.shape[0]
    block = 512 if features % 512 == 0 else features
    for c in range(0, features, block):
        product = jnp.dot(
            activated_ref[...], down_ref[0, :, c : c + block], preferred_element_type=jnp.float32
        )
        product = (product * share).astype(jnp.bfloat16)
        keep_ref[:, c : c + block] = product[:kept]
        send_ref[:, c : c + block] = product[kept:]


def run_expert(at, tokens, gate_weight, up_weight, down_weight):
    units = gate_weight.shape[2]
    width = gate_weight.shape[1]
    rows = sum(part.shape[0] for part in tokens)
    half = jax.ShapeDtypeStruct((rows // 2, width), jnp.bfloat16)
    return pl.pallas_call(
        partial(expert_kernel, len(tokens)),
        in_specs=[pl.BlockSpec(memory_space=pltpu.SMEM)] + in_vmem(len(tokens) + 3),
        out_specs=in_vmem(2),
        out_shape=[half, half],
        scratch_shapes=[pltpu.VMEM((rows, units), jnp.bfloat16)],
        compiler_params=pltpu.CompilerParams(vmem_limit_bytes=EXPERT_VMEM),
        cost_estimate=NOTHING,
    )(at, *tokens, gate_weight, up_weight, down_weight)


def after(array, *others):
    return lax.optimization_barrier((array, *others))[0]


def added(terms):
    total = terms[0].astype(jnp.float32)
    for term in terms[1:]:
        total = total + term.astype(jnp.float32)
    return total


def gathered_shards(
    query_rows,
    encoded_key_rows,
    value_matrix_rows,
    output_weight,
    residual,
    norm_gain,
    route_experts,
    route_gates,
    gate_weight,
    up_weight,
    down_weight,
):
    seq_count = lax.axis_size("seq")
    role_count = lax.axis_size("role")
    seq_index = lax.axis_index("seq")
    role_index = lax.axis_index("role")
    batch_count, local_length, query_width = query_rows.shape
    local_heads = query_width // HEAD_WIDTH
    group_width = QUERY_HEADS // KEY_VALUE_HEADS
    role_bits = [1 << n for n in range(role_count.bit_length() - 1)]
    at = jnp.stack([seq_index, role_index, seq_index * role_count + role_index]).astype(jnp.int32)

    def over_role(array, k):
        return lax.ppermute(array, "role", [(i, i ^ k) for i in range(role_count)])

    def over_seq(array, j):
        return lax.ppermute(array, "seq", [(i, i ^ j) for i in range(seq_count)])

    beside_proj = over_seq(output_weight, 1)
    block_width = output_weight.shape[1]
    across_steps = range(2, seq_count, 2)

    pieces = []
    for k in range(role_count):
        head = ((role_index ^ k) * local_heads // group_width) * HEAD_WIDTH
        piece = jnp.concatenate(
            [
                lax.dynamic_slice_in_dim(encoded_key_rows, head, HEAD_WIDTH, 2),
                lax.dynamic_slice_in_dim(value_matrix_rows, head, HEAD_WIDTH, 2),
            ],
            axis=2,
        )
        pieces.append(piece)
    pieces[-1] = after(pieces[-1], beside_proj)
    pieces = [piece if k == 0 else over_role(piece, k) for k, piece in enumerate(pieces)]
    block = pl.pallas_call(
        join_kernel,
        in_specs=in_vmem(len(pieces)),
        out_specs=pl.BlockSpec(memory_space=pltpu.VMEM),
        out_shape=jax.ShapeDtypeStruct(
            (batch_count, local_length, 2 * HEAD_WIDTH), jnp.bfloat16
        ),
        compiler_params=pltpu.CompilerParams(vmem_limit_bytes=COPY_VMEM),
        cost_estimate=SHORT,
    )(*pieces)
    same_core = [block] + [over_seq(block, j) for j in across_steps]
    blocks = []
    for part in same_core:
        blocks += [part, over_seq(part, 1)]
    last = role_count // 2
    routes = jnp.concatenate([route_experts[0].astype(jnp.float32), route_gates[0]], axis=1)
    other_routes = over_role(routes, last)
    residual_blocks = [
        lax.dynamic_slice_in_dim(residual[0], (seq_index ^ j) * block_width, block_width, 1)
        for j in range(seq_count)
    ]
    residuals = [
        jnp.concatenate(residual_blocks[j : j + 2], axis=1) for j in range(0, seq_count, 2)
    ]
    residuals = [residuals[0]] + [over_seq(residuals[j // 2], j) for j in across_steps]

    rows = batch_count * local_length
    near_width = 2 * output_weight.shape[1]
    groups = role_groups(role_count)
    attend_args = in_hbm(query_rows, *blocks[:-1], output_weight, beside_proj)
    half_rows = jax.ShapeDtypeStruct((rows // 2, query_width), jnp.bfloat16)
    odd_rows, even_rows, *near = pl.pallas_call(
        partial(attend_kernel, seq_count, role_count),
        in_specs=[pl.BlockSpec(memory_space=pltpu.SMEM)] + in_vmem(1) + hbm_specs(len(attend_args)),
        out_specs=in_vmem(2 + len(groups)),
        out_shape=[half_rows] * 2 + partial_shapes(groups, local_length, near_width),
        scratch_shapes=fetch_scratch(*attend_args) + [pltpu.VMEM((rows, query_width), jnp.bfloat16)],
        compiler_params=pltpu.CompilerParams(vmem_limit_bytes=SMALL_VMEM),
        cost_estimate=SHORT,
    )(at, blocks[-1], *attend_args)

    def summed_over_role(parts, extra, *before):
        terms = [[part] for part in parts]
        for n, group in enumerate(groups[:-1]):
            bit = 1 << n
            leaving = terms[n][0] if len(terms[n]) == 1 else added(terms[n]).astype(jnp.bfloat16)
            came = over_role(leaving, bit)
            for m in range(n + 1, len(groups)):
                at_rows = [group.index(k ^ bit) for k in groups[m]]
                if at_rows == list(range(len(group))):
                    terms[m].append(came)
                else:
                    split = [came[i * local_length : (i + 1) * local_length] for i in at_rows]
                    terms[m].append(jnp.concatenate(split, axis=0))
        extra = jnp.pad(after(extra, *before) if before else extra, ((0, local_length), (0, 0)))
        sent = added(terms[-1] + [extra]).astype(jnp.bfloat16)
        return sent

    near_sent = summed_over_role(near, residuals[0])
    near_came = over_role(near_sent, last)
    near_token = pl.pallas_call(
        marker_kernel,
        in_specs=[pl.BlockSpec(memory_space=pl.ANY)],
        out_specs=pl.BlockSpec(memory_space=pltpu.VMEM),
        out_shape=jax.ShapeDtypeStruct((8, 128), jnp.float32),
        compiler_params=pltpu.CompilerParams(vmem_limit_bytes=COPY_VMEM),
        cost_estimate=LONG,
    )(near_came)
    sums = [near_sent, near_came]
    for n, j in enumerate(across_steps, 1):
        far = []
        for half, first in ((odd_rows, 1), (even_rows, 0)):
            parts = groups[:1] if first else groups[1:]
            far += pl.pallas_call(
                partial(project_kernel, range(first, role_count, 2), parts),
                in_specs=in_vmem(1) + hbm_specs(2),
                out_specs=in_vmem(len(parts)),
                out_shape=partial_shapes(parts, local_length, near_width),
                scratch_shapes=fetch_scratch(output_weight, beside_proj),
                compiler_params=pltpu.CompilerParams(vmem_limit_bytes=SMALL_VMEM),
                cost_estimate=SHORT,
            )(over_seq(half, j), *in_hbm(output_weight, beside_proj))
        far_sent = summed_over_role(far, residuals[n], near_token)
        sums += [far_sent, over_role(far_sent, last)]

    chips = 1 + len(across_steps)
    sum_args = in_hbm(*sums)
    half_size = chips * local_length
    half_shape, both_shape = [
        jax.ShapeDtypeStruct((size, near_width + GATE_COLUMNS), jnp.bfloat16)
        for size in (half_size, 2 * half_size)
    ]
    own_half, other_half, both_halves = pl.pallas_call(
        partial(sum_kernel, chips),
        in_specs=[pl.BlockSpec(memory_space=pl.ANY)] + in_vmem(2) + hbm_specs(len(sum_args)),
        out_specs=in_vmem(3),
        out_shape=[half_shape, half_shape, both_shape],
        scratch_shapes=fetch_scratch(*sum_args),
        compiler_params=pltpu.CompilerParams(vmem_limit_bytes=SMALL_VMEM),
        cost_estimate=SHORT,
    )(near_token, routes, other_routes, *sum_args)

    width = residual.shape[2]
    gain = norm_gain.reshape(1, width)

    def normed_rows(parts, first_row, *hidden_shape):
        rows = chips * local_length
        return pl.pallas_call(
            partial(norm_kernel, chips, first_row),
            in_specs=[pl.BlockSpec(memory_space=pltpu.SMEM)] + in_vmem(1 + chips),
            out_specs=in_vmem(1 + len(hidden_shape)),
            out_shape=[
                jax.ShapeDtypeStruct((rows, width + GATE_COLUMNS), jnp.bfloat16),
                *hidden_shape,
            ],
            scratch_shapes=[pltpu.VMEM((rows, width), jnp.float32)],
            compiler_params=pltpu.CompilerParams(vmem_limit_bytes=SMALL_VMEM),
            cost_estimate=NOTHING,
        )(at, gain, *parts)

    def walk(k, bits):
        found = [k]
        for n, bit in enumerate(bits):
            found += walk(k | bit, bits[n + 1 :])
        return found

    lower_bits = role_bits[:-1][::-1]
    order = walk(last, lower_bits) + walk(0, lower_bits)
    planes = {0: own_half, last: other_half}
    crossed = {}

    def across(part):
        return [over_seq(part, j) for j in across_steps]

    both_across = across(both_halves)
    for k in order:
        if k not in planes:
            bit = k & -k
            held = planes[k ^ bit]
            planes[k] = over_role(after(held, planes[order[1]]) if k < last else held, bit)
        if k in (0, last):
            crossed[k] = both_across
        elif k < last:
            source = k ^ (k & -k)
            came = [part[:half_size] for part in crossed[source]] if source == 0 else crossed[source]
            crossed[k] = [over_role(part, k & -k) for part in came]
        else:
            crossed[k] = across(after(planes[k], *both_across))

    keep, send, slots, leaving, passed = {}, {}, {}, {}, {}

    hidden_shape = jax.ShapeDtypeStruct((local_length, width), jnp.float32)
    hidden = []

    hidden_shape = jax.ShapeDtypeStruct((local_length, width), jnp.float32)
    hidden = []

    def prepared(k, *first):
        late = [after(part, *first) for part in crossed[k]] if first else crossed[k]
        first_row = half_size if k == last else 0
        normed, *own = normed_rows([planes[k]] + late, first_row, *([] if k else [hidden_shape]))
        hidden.extend(own)
        return [normed, over_seq(normed, 1)]

    def expert(tokens, *others):
        if others:
            tokens = lax.optimization_barrier((*tokens, *others))[: len(tokens)]
        return run_expert(at, tokens, gate_weight, up_weight, down_weight)

    def combine(k, *before):
        came = over_seq(after(send[k], *before) if before else send[k], 1)
        sums = []
        for n in range(len(across_steps)):
            chunk = slice((n + 1) * local_length, (n + 2) * local_length)
            sums.append(added([keep[k][chunk], came[chunk]]).astype(jnp.bfloat16))
        return [keep[k][:local_length], came[:local_length]], sums

    def pass_on(k):
        passed[k] = [over_seq(part, j) for part, j in zip(leaving[k], across_steps)]
        slots[k] += passed[k]

    far_plane, final = order[1], order[-1]
    ready = {far_plane: prepared(far_plane, planes[final], *crossed[final])}
    ready[final] = prepared(final)
    keep[far_plane], send[far_plane] = expert(ready[far_plane], ready[final][0])
    ready |= {k: prepared(k, keep[far_plane]) for k in (last, 0)}
    slots[far_plane], leaving[far_plane] = combine(far_plane)
    leaving[far_plane] = [after(part, ready[last][0], ready[0][0]) for part in leaving[far_plane]]
    pass_on(far_plane)
    keep[last], send[last] = expert(ready[last], keep[far_plane], *leaving[far_plane])
    slots[last], leaving[last] = combine(last)
    leaving[last] = [after(part, *passed[far_plane]) for part in leaving[last]]
    pass_on(last)
    keep[final], send[final] = expert(ready[final], keep[last])
    slots[far_plane] = [added(slots[far_plane]).astype(jnp.bfloat16)]
    slots[final], leaving[final] = combine(final, *passed[far_plane])
    leaving[final] = [after(part, *leaving[last]) for part in leaving[final]]
    pass_on(final)
    keep[0], send[0] = expert(ready[0], keep[final], *leaving[last])
    slots[0], leaving[0] = combine(0, *passed[last])
    leaving[0] = [after(part, *leaving[final]) for part in leaving[0]]
    pass_on(0)
    for bit in role_bits:
        for k in [k for k in sorted(slots, reverse=True) if k & bit]:
            going = added(slots.pop(k)).astype(jnp.bfloat16)
            if k == last:
                going = after(going, *leaving[final])
            slots[k ^ bit].append(over_role(going, bit))
    return added(hidden + slots[0]).astype(jnp.bfloat16).reshape(residual.shape)


def solution(mesh):
    placed = (
        P("groups", "seq", "role"),
        P("groups", ("seq", "role"), None),
        P("groups", ("seq", "role"), None),
        P("role", "seq"),
        P(("groups", "role"), "seq", None),
        P(),
        P(("groups", "role"), "seq", None),
        P(("groups", "role"), "seq", None),
        P(("seq", "role"), None, None),
        P(("seq", "role"), None, None),
        P(("seq", "role"), None, None),
    )
    experts = mesh.shape["seq"] * mesh.shape["role"]
    return jax.shard_map(
        gathered_shards if experts <= 2 * TOPK else routed_shards,
        mesh=mesh,
        in_specs=placed,
        out_specs=P(("groups", "role"), "seq", None),
        check_vma=False,
    )
```

```python
from functools import partial

import jax
import jax.numpy as jnp
from jax import lax
from jax.experimental import pallas as pl
from jax.experimental.pallas import tpu as pltpu
from jax.sharding import PartitionSpec as P

D = 2048
QUERY_HEADS = 32
KEY_VALUE_HEADS = 4
HEAD_WIDTH = 128
TOPK = 8


epsilon = 1e-06
masked_score = -1e30
EXPERT_VMEM = 16 * 2**20
SMALL_VMEM = 12 * 2**20
COPY_VMEM = 4 * 2**20
GATE_COLUMNS = 128
NOTHING = pl.CostEstimate(flops=1, bytes_accessed=1, transcendentals=0)
SHORT = pl.CostEstimate(flops=2 * 10**9, bytes_accessed=4 * 2**20, transcendentals=0)
LONG = pl.CostEstimate(flops=10**10, bytes_accessed=1, transcendentals=0)


def score_block(queries, every_key, query_position, block_start, block_width, score_scale):
    keys_part = lax.slice_in_dim(every_key, block_start, block_start + block_width, axis=0)
    raw_scores = (
        jnp.einsum("qhd,kd->hqk", queries, keys_part, preferred_element_type=jnp.float32)
        * score_scale
    )
    key_position = block_start + jnp.arange(block_width, dtype=jnp.int32)
    return jnp.where(
        key_position[None, None, :] <= query_position[None, :, None], raw_scores, masked_score
    )


def value_block(rounded, every_value, block_start, block_width):
    prob_block = lax.slice_in_dim(rounded, block_start, block_start + block_width, axis=2)
    values_part = lax.slice_in_dim(every_value, block_start, block_start + block_width, axis=0)
    return jnp.einsum("hqk,kd->qhd", prob_block, values_part, preferred_element_type=jnp.float32)


def routed_shards(
    query_rows,
    encoded_key_rows,
    value_matrix_rows,
    output_weight,
    residual,
    norm_gain,
    route_experts,
    route_gates,
    gate_weight,
    up_weight,
    down_weight,
):
    seq_count = lax.axis_size("seq")
    role_count = lax.axis_size("role")
    seq_index = lax.axis_index("seq")
    role_index = lax.axis_index("role")
    batch_count = query_rows.shape[0]
    local_length = query_rows.shape[1]
    local_heads = query_rows.shape[2] // HEAD_WIDTH
    full_length = local_length * seq_count
    query_group_width = QUERY_HEADS // KEY_VALUE_HEADS
    head_pick = role_index * local_heads // query_group_width
    role_keys, role_values = (
        lax.all_gather(encoded_key_rows, "role", axis=1, tiled=True),
        lax.all_gather(value_matrix_rows, "role", axis=1, tiled=True),
    )
    head_keys = lax.dynamic_slice_in_dim(role_keys, head_pick * HEAD_WIDTH, HEAD_WIDTH, 2)
    head_values = lax.dynamic_slice_in_dim(role_values, head_pick * HEAD_WIDTH, HEAD_WIDTH, 2)
    whole_keys, whole_values, whole_proj = (
        lax.all_gather(head_keys, "seq", axis=1, tiled=True),
        lax.all_gather(head_values, "seq", axis=1, tiled=True),
        lax.all_gather(output_weight, "seq", axis=1, tiled=True),
    )
    key_width = full_length // 8
    score_scale = HEAD_WIDTH ** (-0.5)
    query_position = seq_index * local_length + jnp.arange(local_length, dtype=jnp.int32)
    last_needed = (seq_index + 1) * local_length

    def one_sequence(operands):
        own_queries, every_key, every_value = operands
        queries = own_queries.reshape(local_length, local_heads, HEAD_WIDTH)
        pieces = []
        for number in range(8):
            block_start = number * key_width
            compute = partial(
                score_block, queries, every_key, query_position, block_start, key_width, score_scale
            )
            skipped = partial(
                jnp.full, (local_heads, local_length, key_width), masked_score, jnp.float32
            )
            pieces.append(lax.cond(block_start < last_needed, compute, skipped))
        scores = jnp.concatenate(pieces, axis=2)
        row_peak = jnp.max(scores, axis=2, keepdims=True)
        weights = jnp.exp(scores - row_peak)
        totals = jnp.sum(weights, axis=2, keepdims=True)
        rounded = weights.astype(jnp.bfloat16)
        mixed_rows = jnp.zeros((local_length, local_heads, HEAD_WIDTH), jnp.float32)
        for number in range(8):
            block_start = number * key_width
            product = partial(value_block, rounded, every_value, block_start, key_width)
            nothing = partial(jnp.zeros, (local_length, local_heads, HEAD_WIDTH), jnp.float32)
            mixed_rows = mixed_rows + lax.cond(block_start < last_needed, product, nothing)
        attended = (mixed_rows / totals.transpose(1, 0, 2)).astype(jnp.bfloat16)
        return attended.reshape(local_length, local_heads * HEAD_WIDTH)

    attended = lax.map(one_sequence, (query_rows, whole_keys, whole_values))
    flat_attended = attended.reshape(batch_count * local_length, local_heads * HEAD_WIDTH)
    projected = lax.psum_scatter(
        jnp.dot(flat_attended, whole_proj, preferred_element_type=jnp.float32).astype(jnp.bfloat16),
        "role",
        scatter_dimension=0,
        tiled=True,
    ).astype(jnp.float32)
    hidden = residual[0].astype(jnp.float32) + projected
    variance = jnp.mean(hidden * hidden, axis=-1, keepdims=True)
    normed = (hidden * lax.rsqrt(variance + epsilon) * norm_gain).astype(jnp.bfloat16)
    expert_ids = route_experts.reshape(-1)
    gate_values = route_gates.reshape(-1)
    experts_local = gate_weight.shape[0]
    device_count = seq_count * role_count
    expert_count = experts_local * device_count
    assign = expert_ids.shape[0]
    capacity = assign // expert_count + 1
    onehot = (expert_ids[:, None] == jnp.arange(expert_count, dtype=jnp.int32)[None, :]).astype(
        jnp.int32
    )
    earlier = jnp.cumsum(onehot, axis=0) - onehot
    slot_rank = jnp.sum(earlier * onehot, axis=1)
    slot_index = expert_ids * capacity + slot_rank
    source_token = jnp.arange(assign, dtype=jnp.int32) // TOPK
    slot_token = jnp.zeros((expert_count * capacity,), jnp.int32).at[slot_index].set(source_token)
    slot_used = jnp.zeros((expert_count * capacity,), jnp.bfloat16).at[slot_index].set(1.0)
    outgoing = (normed[slot_token] * slot_used[:, None]).reshape(
        device_count, experts_local, capacity, D
    )
    incoming = lax.all_to_all(outgoing, ("seq", "role"), split_axis=0, concat_axis=0, tiled=True)
    gate_hidden = jnp.einsum(
        "sjcd,jdf->sjcf", incoming, gate_weight, preferred_element_type=jnp.float32
    )
    up_hidden = jnp.einsum(
        "sjcd,jdf->sjcf", incoming, up_weight, preferred_element_type=jnp.float32
    )
    activated = (jax.nn.silu(gate_hidden) * up_hidden).astype(jnp.bfloat16)
    returned = lax.all_to_all(
        jnp.einsum(
            "sjcf,jfd->sjcd", activated, down_weight, preferred_element_type=jnp.float32
        ).astype(jnp.bfloat16),
        ("seq", "role"),
        split_axis=0,
        concat_axis=0,
        tiled=True,
    )
    gathered = returned.reshape(expert_count * capacity, D)[slot_index]
    weighted = gathered.astype(jnp.float32) * gate_values[:, None]
    expert_sum = jnp.sum(weighted.reshape(-1, TOPK, D), axis=1)
    return (hidden + expert_sum).astype(jnp.bfloat16).reshape(residual.shape)


def in_hbm(*arrays):
    return [pltpu.with_memory_space_constraint(array, pltpu.HBM) for array in arrays]


def hbm_specs(count):
    return [pl.BlockSpec(memory_space=pltpu.HBM)] * count


def fetch_scratch(*arrays):
    return [pltpu.VMEM(array.shape, array.dtype) for array in arrays] + [
        pltpu.SemaphoreType.DMA((len(arrays),))
    ]


def start_fetch(from_refs, scratch):
    *buffers, sems = scratch
    copies = [
        pltpu.make_async_copy(from_ref, buffer, sems.at[n])
        for n, (from_ref, buffer) in enumerate(zip(from_refs, buffers))
    ]
    for copy in copies:
        copy.start()
    return copies, buffers


def in_vmem(count):
    return [pl.BlockSpec(memory_space=pltpu.VMEM)] * count


def attend_kernel(seq_count, role_count, at_ref, *refs):
    last_block, *refs = refs
    count = seq_count + 2
    outputs = len(role_groups(role_count)) + 2
    odd_ref, even_ref, *partial_refs = refs[count : count + outputs]
    *scratch, attended_ref = refs[count + outputs :]
    copies, (query_ref, *buffers) = start_fetch(refs[:count], scratch)
    blocks, proj_refs = buffers[: seq_count - 1] + [last_block], buffers[seq_count - 1 :]
    seq_index, role_index = at_ref[0], at_ref[1]
    local_length = query_ref.shape[1]
    local_heads = query_ref.shape[2] // HEAD_WIDTH
    per_role = local_length // role_count
    rows = local_heads * local_length
    keys_all = seq_count * local_length
    slot = lax.broadcasted_iota(jnp.int32, (rows, keys_all), 1)
    block_number, within = slot // local_length, slot % local_length
    key_position = (
        (seq_index ^ block_number) * local_length
        + (role_index ^ (within // per_role)) * per_role
        + within % per_role
    )
    query_position = (
        seq_index * local_length
        + lax.broadcasted_iota(jnp.int32, (rows, keys_all), 0) % local_length
    )
    seen = key_position <= query_position
    scale = HEAD_WIDTH ** (-0.5)
    for copy in copies[:seq_count]:
        copy.wait()
    for k in range(role_count):
        b = role_index ^ k
        own = query_ref[b]
        queries = jnp.concatenate(
            [own[:, h * HEAD_WIDTH : (h + 1) * HEAD_WIDTH] for h in range(local_heads)], axis=0
        )
        key_value = jnp.concatenate([block[b] for block in blocks], axis=0)
        keys, values = key_value[:, :HEAD_WIDTH], key_value[:, HEAD_WIDTH:]
        scores = lax.dot_general(
            queries, keys, (((1,), (1,)), ((), ())), preferred_element_type=jnp.float32
        )
        scores = jnp.where(seen, scores * scale, masked_score)
        weights = jnp.exp(scores - jnp.max(scores, axis=1, keepdims=True))
        totals = jnp.sum(weights, axis=1, keepdims=True)
        mixed = jnp.dot(weights.astype(jnp.bfloat16), values, preferred_element_type=jnp.float32)
        attended = (mixed / totals).astype(jnp.bfloat16)
        for h in range(local_heads):
            attended_ref[
                k * local_length : (k + 1) * local_length, h * HEAD_WIDTH : (h + 1) * HEAD_WIDTH
            ] = attended[h * local_length : (h + 1) * local_length]
    for slots_ref, first in ((odd_ref, 1), (even_ref, 0)):
        for n, k in enumerate(range(first, role_count, 2)):
            to = slice(n * local_length, (n + 1) * local_length)
            slots_ref[to] = attended_ref[k * local_length : (k + 1) * local_length]
    for copy in copies[seq_count:]:
        copy.wait()
    project_into(range(role_count), role_groups(role_count), attended_ref, proj_refs, partial_refs)


def join_kernel(*refs):
    *piece_refs, out_ref = refs
    at = 0
    for ref in piece_refs:
        size = ref.shape[1]
        out_ref[:, at : at + size, :] = ref[...]
        at += size


def role_groups(role_count):
    last = role_count // 2
    bits = [1 << n for n in range(last.bit_length() - 1)]
    return [[k for k in range(role_count) if k & -k == bit] for bit in bits] + [[0, last]]


def project_into(slots, groups, attended_ref, proj_refs, partial_refs):
    slots = list(slots)
    rows = attended_ref.shape[0] // len(slots)
    at = 0
    for proj_ref in proj_refs:
        width = proj_ref.shape[1]
        product = jnp.dot(
            attended_ref[...], proj_ref[...], preferred_element_type=jnp.float32
        ).astype(jnp.bfloat16)
        for group, partial_ref in zip(groups, partial_refs):
            for n, k in enumerate(group):
                start = slots.index(k) * rows
                partial_ref[n * rows : (n + 1) * rows, at : at + width] = product[
                    start : start + rows
                ]
        at += width


def project_kernel(slots, groups, attended_ref, *refs):
    count = (len(refs) - len(groups) - 1) // 2
    copies, proj_refs = start_fetch(refs[:count], refs[count + len(groups) :])
    for copy in copies:
        copy.wait()
    project_into(slots, groups, attended_ref, proj_refs, refs[count : count + len(groups)])


def partial_shapes(groups, rows, width):
    return [jax.ShapeDtypeStruct((rows * len(group), width), jnp.bfloat16) for group in groups]


def marker_kernel(came_ref, token_ref):
    token_ref[...] = jnp.zeros_like(token_ref)


def sum_kernel(chips, token_ref, route_ref, other_route_ref, last_ref, *refs):
    count = 2 * chips - 1
    out_refs, both_ref = refs[count : count + 2], refs[count + 2]
    copies, buffers = start_fetch(refs[:count], refs[count + 3 :])
    buffers = list(buffers) + [last_ref]
    rows, width = buffers[0].shape
    rows //= 2
    lane = lax.broadcasted_iota(jnp.int32, (rows, GATE_COLUMNS), 1)
    half = GATE_COLUMNS // 2
    expert = (lane % half).astype(jnp.float32)
    size = both_ref.shape[0] // 2
    for p, routes in enumerate((route_ref, other_route_ref)):
        shares = jnp.zeros((rows, GATE_COLUMNS), jnp.float32)
        routed = routes.shape[1] // 2
        for k in range(routed):
            named, weight = routes[:, k : k + 1], routes[:, routed + k : routed + k + 1]
            shares = shares + jnp.where(expert == named, weight, 0.0)
        first = shares.astype(jnp.bfloat16).astype(jnp.float32)
        terms = jnp.where(lane < half, first, shares - first).astype(jnp.bfloat16)
        nothing = jnp.zeros((size - rows, GATE_COLUMNS), jnp.bfloat16)
        for to_ref, start in ((out_refs[p], 0), (both_ref, p * size)):
            to_ref[start : start + rows, width:] = terms
            to_ref[start + rows : start + size, width:] = nothing
    for n in range(chips):
        for copy in copies[2 * n : 2 * n + 2]:
            copy.wait()
        sent, came = buffers[2 * n : 2 * n + 2]
        for p in range(2):
            total = sent[p * rows : (p + 1) * rows].astype(jnp.float32)
            total = total + came[(1 - p) * rows : (2 - p) * rows].astype(jnp.float32)
            for to_ref, start in ((out_refs[p], n * rows), (both_ref, p * size + n * rows)):
                to_ref[start : start + rows, :width] = total.astype(jnp.bfloat16)


def norm_kernel(chips, first_row, at_ref, gain_ref, *refs):
    parts, (normed_ref, *hidden_refs, whole_ref) = refs[:chips], refs[chips:]
    seq_index = at_ref[0]
    features = whole_ref.shape[1]
    rows = whole_ref.shape[0] // chips
    width = features // chips // 2
    for n, part in enumerate(parts):
        above = first_row if n else 0
        for m in range(chips):
            to = slice(m * rows, (m + 1) * rows)
            source = slice(above + (m ^ n) * rows, above + (m ^ n) * rows + rows)
            for j in range(2):
                start = pl.multiple_of((seq_index ^ (2 * n + j)) * width, width)
                whole_ref[to, pl.ds(start, width)] = part[
                    source, j * width : (j + 1) * width
                ].astype(jnp.float32)
        normed_ref[n * rows : (n + 1) * rows, features:] = part[above : above + rows, 2 * width :]
    hidden = whole_ref[...]
    variance = jnp.mean(hidden * hidden, axis=1, keepdims=True)
    normed = hidden * lax.rsqrt(variance + epsilon) * gain_ref[...]
    normed_ref[:, :features] = normed.astype(jnp.bfloat16)
    for hidden_ref in hidden_refs:
        hidden_ref[...] = hidden[:rows]


def expert_kernel(token_count, at_ref, *refs):
    token_refs = refs[:token_count]
    gate_ref, up_ref, down_ref, keep_ref, send_ref, activated_ref = refs[token_count:]
    features, units = gate_ref.shape[1:]
    tokens = jnp.concatenate([ref[:, :features] for ref in token_refs], axis=0)
    gates = jnp.concatenate([ref[:, features:] for ref in token_refs], axis=0)
    lane = lax.broadcasted_iota(jnp.int32, gates.shape, 1)
    mine = lane % (GATE_COLUMNS // 2) == at_ref[2]
    share = jnp.sum(jnp.where(mine, gates.astype(jnp.float32), 0.0), axis=1, keepdims=True)
    block = 256 if units % 256 == 0 else units
    for f in range(0, units, block):
        gate_hidden = jnp.dot(
            tokens, gate_ref[0, :, f : f + block], preferred_element_type=jnp.float32
        )
        up_hidden = jnp.dot(tokens, up_ref[0, :, f : f + block], preferred_element_type=jnp.float32)
        activated_ref[:, f : f + block] = (
            gate_hidden / (1.0 + jnp.exp(-gate_hidden)) * up_hidden
        ).astype(jnp.bfloat16)
    kept = keep_ref.shape[0]
    block = 512 if features % 512 == 0 else features
    for c in range(0, features, block):
        product = jnp.dot(
            activated_ref[...], down_ref[0, :, c : c + block], preferred_element_type=jnp.float32
        )
        product = (product * share).astype(jnp.bfloat16)
        keep_ref[:, c : c + block] = product[:kept]
        send_ref[:, c : c + block] = product[kept:]


def run_expert(at, tokens, gate_weight, up_weight, down_weight):
    units = gate_weight.shape[2]
    width = gate_weight.shape[1]
    rows = sum(part.shape[0] for part in tokens)
    half = jax.ShapeDtypeStruct((rows // 2, width), jnp.bfloat16)
    return pl.pallas_call(
        partial(expert_kernel, len(tokens)),
        in_specs=[pl.BlockSpec(memory_space=pltpu.SMEM)] + in_vmem(len(tokens) + 3),
        out_specs=in_vmem(2),
        out_shape=[half, half],
        scratch_shapes=[pltpu.VMEM((rows, units), jnp.bfloat16)],
        compiler_params=pltpu.CompilerParams(vmem_limit_bytes=EXPERT_VMEM),
        cost_estimate=NOTHING,
    )(at, *tokens, gate_weight, up_weight, down_weight)


def after(array, *others):
    return lax.optimization_barrier((array, *others))[0]


def added(terms):
    total = terms[0].astype(jnp.float32)
    for term in terms[1:]:
        total = total + term.astype(jnp.float32)
    return total


def gathered_shards(
    query_rows,
    encoded_key_rows,
    value_matrix_rows,
    output_weight,
    residual,
    norm_gain,
    route_experts,
    route_gates,
    gate_weight,
    up_weight,
    down_weight,
):
    seq_count = lax.axis_size("seq")
    role_count = lax.axis_size("role")
    seq_index = lax.axis_index("seq")
    role_index = lax.axis_index("role")
    batch_count, local_length, query_width = query_rows.shape
    local_heads = query_width // HEAD_WIDTH
    group_width = QUERY_HEADS // KEY_VALUE_HEADS
    role_bits = [1 << n for n in range(role_count.bit_length() - 1)]
    at = jnp.stack([seq_index, role_index, seq_index * role_count + role_index]).astype(jnp.int32)

    def over_role(array, k):
        return lax.ppermute(array, "role", [(i, i ^ k) for i in range(role_count)])

    def over_seq(array, j):
        return lax.ppermute(array, "seq", [(i, i ^ j) for i in range(seq_count)])

    beside_proj = over_seq(output_weight, 1)
    block_width = output_weight.shape[1]
    across_steps = range(2, seq_count, 2)

    pieces = []
    for k in range(role_count):
        head = ((role_index ^ k) * local_heads // group_width) * HEAD_WIDTH
        piece = jnp.concatenate(
            [
                lax.dynamic_slice_in_dim(encoded_key_rows, head, HEAD_WIDTH, 2),
                lax.dynamic_slice_in_dim(value_matrix_rows, head, HEAD_WIDTH, 2),
            ],
            axis=2,
        )
        pieces.append(piece)
    pieces[1] = after(pieces[1], beside_proj)
    pieces = [piece if k == 0 else over_role(piece, k) for k, piece in enumerate(pieces)]
    block = pl.pallas_call(
        join_kernel,
        in_specs=in_vmem(len(pieces)),
        out_specs=pl.BlockSpec(memory_space=pltpu.VMEM),
        out_shape=jax.ShapeDtypeStruct(
            (batch_count, local_length, 2 * HEAD_WIDTH), jnp.bfloat16
        ),
        compiler_params=pltpu.CompilerParams(vmem_limit_bytes=COPY_VMEM),
        cost_estimate=SHORT,
    )(*pieces)
    same_core = [block] + [over_seq(block, j) for j in across_steps]
    blocks = []
    for part in same_core:
        blocks += [part, over_seq(part, 1)]
    last = role_count // 2
    routes = jnp.concatenate([route_experts[0].astype(jnp.float32), route_gates[0]], axis=1)
    other_routes = over_role(routes, last)
    residual_blocks = [
        lax.dynamic_slice_in_dim(residual[0], (seq_index ^ j) * block_width, block_width, 1)
        for j in range(seq_count)
    ]
    residuals = [
        jnp.concatenate(residual_blocks[j : j + 2], axis=1) for j in range(0, seq_count, 2)
    ]
    residuals = [residuals[0]] + [over_seq(residuals[j // 2], j) for j in across_steps]

    rows = batch_count * local_length
    near_width = 2 * output_weight.shape[1]
    groups = role_groups(role_count)
    attend_args = in_hbm(query_rows, *blocks[:-1], output_weight, beside_proj)
    half_rows = jax.ShapeDtypeStruct((rows // 2, query_width), jnp.bfloat16)
    odd_rows, even_rows, *near = pl.pallas_call(
        partial(attend_kernel, seq_count, role_count),
        in_specs=[pl.BlockSpec(memory_space=pltpu.SMEM)] + in_vmem(1) + hbm_specs(len(attend_args)),
        out_specs=in_vmem(2 + len(groups)),
        out_shape=[half_rows] * 2 + partial_shapes(groups, local_length, near_width),
        scratch_shapes=fetch_scratch(*attend_args) + [pltpu.VMEM((rows, query_width), jnp.bfloat16)],
        compiler_params=pltpu.CompilerParams(vmem_limit_bytes=SMALL_VMEM),
        cost_estimate=SHORT,
    )(at, blocks[-1], *attend_args)

    def summed_over_role(parts, extra, *before):
        terms = [[part] for part in parts]
        for n, group in enumerate(groups[:-1]):
            bit = 1 << n
            leaving = terms[n][0] if len(terms[n]) == 1 else added(terms[n]).astype(jnp.bfloat16)
            came = over_role(leaving, bit)
            for m in range(n + 1, len(groups)):
                at_rows = [group.index(k ^ bit) for k in groups[m]]
                if at_rows == list(range(len(group))):
                    terms[m].append(came)
                else:
                    split = [came[i * local_length : (i + 1) * local_length] for i in at_rows]
                    terms[m].append(jnp.concatenate(split, axis=0))
        extra = jnp.pad(after(extra, *before) if before else extra, ((0, local_length), (0, 0)))
        sent = added(terms[-1] + [extra]).astype(jnp.bfloat16)
        return sent

    near_sent = summed_over_role(near, residuals[0])
    near_came = over_role(near_sent, last)
    near_token = pl.pallas_call(
        marker_kernel,
        in_specs=[pl.BlockSpec(memory_space=pl.ANY)],
        out_specs=pl.BlockSpec(memory_space=pltpu.VMEM),
        out_shape=jax.ShapeDtypeStruct((8, 128), jnp.float32),
        compiler_params=pltpu.CompilerParams(vmem_limit_bytes=COPY_VMEM),
        cost_estimate=LONG,
    )(near_came)
    sums = [near_sent, near_came]
    for n, j in enumerate(across_steps, 1):
        far = []
        for half, first in ((odd_rows, 1), (even_rows, 0)):
            parts = groups[:1] if first else groups[1:]
            far += pl.pallas_call(
                partial(project_kernel, range(first, role_count, 2), parts),
                in_specs=in_vmem(1) + hbm_specs(2),
                out_specs=in_vmem(len(parts)),
                out_shape=partial_shapes(parts, local_length, near_width),
                scratch_shapes=fetch_scratch(output_weight, beside_proj),
                compiler_params=pltpu.CompilerParams(vmem_limit_bytes=SMALL_VMEM),
                cost_estimate=SHORT,
            )(over_seq(half, j), *in_hbm(output_weight, beside_proj))
        far_sent = summed_over_role(far, residuals[n], near_token)
        sums += [far_sent, over_role(far_sent, last)]

    chips = 1 + len(across_steps)
    *sums, last_came = sums
    sum_args = in_hbm(*sums)
    half_size = chips * local_length
    half_shape, both_shape = [
        jax.ShapeDtypeStruct((size, near_width + GATE_COLUMNS), jnp.bfloat16)
        for size in (half_size, 2 * half_size)
    ]
    own_half, other_half, both_halves = pl.pallas_call(
        partial(sum_kernel, chips),
        in_specs=[pl.BlockSpec(memory_space=pl.ANY)] + in_vmem(3) + hbm_specs(len(sum_args)),
        out_specs=in_vmem(3),
        out_shape=[half_shape, half_shape, both_shape],
        scratch_shapes=fetch_scratch(*sum_args),
        compiler_params=pltpu.CompilerParams(vmem_limit_bytes=SMALL_VMEM),
        cost_estimate=SHORT,
    )(near_token, routes, other_routes, last_came, *sum_args)

    width = residual.shape[2]
    gain = norm_gain.reshape(1, width)

    def normed_rows(parts, first_row, *hidden_shape):
        rows = chips * local_length
        return pl.pallas_call(
            partial(norm_kernel, chips, first_row),
            in_specs=[pl.BlockSpec(memory_space=pltpu.SMEM)] + in_vmem(1 + chips),
            out_specs=in_vmem(1 + len(hidden_shape)),
            out_shape=[
                jax.ShapeDtypeStruct((rows, width + GATE_COLUMNS), jnp.bfloat16),
                *hidden_shape,
            ],
            scratch_shapes=[pltpu.VMEM((rows, width), jnp.float32)],
            compiler_params=pltpu.CompilerParams(vmem_limit_bytes=SMALL_VMEM),
            cost_estimate=NOTHING,
        )(at, gain, *parts)

    def walk(k, bits):
        found = [k]
        for n, bit in enumerate(bits):
            found += walk(k | bit, bits[n + 1 :])
        return found

    lower_bits = role_bits[:-1][::-1]
    order = walk(last, lower_bits) + walk(0, lower_bits)
    planes = {0: own_half, last: other_half}
    crossed = {}

    def across(part):
        return [over_seq(part, j) for j in across_steps]

    both_across = across(both_halves)
    for k in order:
        if k not in planes:
            bit = k & -k
            held = planes[k ^ bit]
            planes[k] = over_role(after(held, planes[order[1]]) if k < last else held, bit)
        if k in (0, last):
            crossed[k] = both_across
        elif k < last:
            source = k ^ (k & -k)
            came = [part[:half_size] for part in crossed[source]] if source == 0 else crossed[source]
            crossed[k] = [over_role(part, k & -k) for part in came]
        else:
            crossed[k] = across(after(planes[k], *both_across))

    keep, send, slots, leaving, passed = {}, {}, {}, {}, {}

    hidden_shape = jax.ShapeDtypeStruct((local_length, width), jnp.float32)
    hidden = []

    hidden_shape = jax.ShapeDtypeStruct((local_length, width), jnp.float32)
    hidden = []

    def prepared(k, *first):
        late = [after(part, *first) for part in crossed[k]] if first else crossed[k]
        first_row = half_size if k == last else 0
        normed, *own = normed_rows([planes[k]] + late, first_row, *([] if k else [hidden_shape]))
        hidden.extend(own)
        return [normed, over_seq(normed, 1)]

    def expert(tokens, *others):
        if others:
            tokens = lax.optimization_barrier((*tokens, *others))[: len(tokens)]
        return run_expert(at, tokens, gate_weight, up_weight, down_weight)

    def combine(k, *before):
        came = over_seq(after(send[k], *before) if before else send[k], 1)
        sums = []
        for n in range(len(across_steps)):
            chunk = slice((n + 1) * local_length, (n + 2) * local_length)
            sums.append(added([keep[k][chunk], came[chunk]]).astype(jnp.bfloat16))
        return [keep[k][:local_length], came[:local_length]], sums

    def pass_on(k):
        passed[k] = [over_seq(part, j) for part, j in zip(leaving[k], across_steps)]
        slots[k] += passed[k]

    far_plane, final = order[1], order[-1]
    ready = {far_plane: prepared(far_plane, planes[final], *crossed[final])}
    ready[final] = prepared(final)
    keep[far_plane], send[far_plane] = expert(ready[far_plane], ready[final][0])
    ready |= {k: prepared(k, keep[far_plane]) for k in (last, 0)}
    slots[far_plane], leaving[far_plane] = combine(far_plane)
    leaving[far_plane] = [after(part, ready[last][0], ready[0][0]) for part in leaving[far_plane]]
    pass_on(far_plane)
    keep[last], send[last] = expert(ready[last], keep[far_plane], *leaving[far_plane])
    slots[last], leaving[last] = combine(last)
    leaving[last] = [after(part, *passed[far_plane]) for part in leaving[last]]
    pass_on(last)
    keep[final], send[final] = expert(ready[final], keep[last])
    slots[far_plane] = [added(slots[far_plane]).astype(jnp.bfloat16)]
    slots[final], leaving[final] = combine(final, *passed[far_plane])
    leaving[final] = [after(part, *leaving[last]) for part in leaving[final]]
    pass_on(final)
    keep[0], send[0] = expert(ready[0], keep[final], *leaving[last])
    slots[0], leaving[0] = combine(0, *passed[last])
    leaving[0] = [after(part, *leaving[final]) for part in leaving[0]]
    pass_on(0)
    for bit in role_bits:
        for k in [k for k in sorted(slots, reverse=True) if k & bit]:
            going = added(slots.pop(k)).astype(jnp.bfloat16)
            if k == last:
                going = after(going, *leaving[final])
            slots[k ^ bit].append(over_role(going, bit))
    return added(hidden + slots[0]).astype(jnp.bfloat16).reshape(residual.shape)


def solution(mesh):
    placed = (
        P("groups", "seq", "role"),
        P("groups", ("seq", "role"), None),
        P("groups", ("seq", "role"), None),
        P("role", "seq"),
        P(("groups", "role"), "seq", None),
        P(),
        P(("groups", "role"), "seq", None),
        P(("groups", "role"), "seq", None),
        P(("seq", "role"), None, None),
        P(("seq", "role"), None, None),
        P(("seq", "role"), None, None),
    )
    experts = mesh.shape["seq"] * mesh.shape["role"]
    return jax.shard_map(
        gathered_shards if experts <= 2 * TOPK else routed_shards,
        mesh=mesh,
        in_specs=placed,
        out_specs=P(("groups", "role"), "seq", None),
        check_vma=False,
    )
```

```python
from functools import partial

import jax
import jax.numpy as jnp
from jax import lax
from jax.experimental import pallas as pl
from jax.experimental.pallas import tpu as pltpu
from jax.sharding import PartitionSpec as P

D = 2048
QUERY_HEADS = 32
KEY_VALUE_HEADS = 4
HEAD_WIDTH = 128
TOPK = 8


epsilon = 1e-06
masked_score = -1e30
EXPERT_VMEM = 16 * 2**20
SMALL_VMEM = 12 * 2**20
COPY_VMEM = 4 * 2**20
GATE_COLUMNS = 128
NOTHING = pl.CostEstimate(flops=1, bytes_accessed=1, transcendentals=0)
SHORT = pl.CostEstimate(flops=2 * 10**9, bytes_accessed=4 * 2**20, transcendentals=0)
LONG = pl.CostEstimate(flops=10**10, bytes_accessed=1, transcendentals=0)


def score_block(queries, every_key, query_position, block_start, block_width, score_scale):
    keys_part = lax.slice_in_dim(every_key, block_start, block_start + block_width, axis=0)
    raw_scores = (
        jnp.einsum("qhd,kd->hqk", queries, keys_part, preferred_element_type=jnp.float32)
        * score_scale
    )
    key_position = block_start + jnp.arange(block_width, dtype=jnp.int32)
    return jnp.where(
        key_position[None, None, :] <= query_position[None, :, None], raw_scores, masked_score
    )


def value_block(rounded, every_value, block_start, block_width):
    prob_block = lax.slice_in_dim(rounded, block_start, block_start + block_width, axis=2)
    values_part = lax.slice_in_dim(every_value, block_start, block_start + block_width, axis=0)
    return jnp.einsum("hqk,kd->qhd", prob_block, values_part, preferred_element_type=jnp.float32)


def routed_shards(
    query_rows,
    encoded_key_rows,
    value_matrix_rows,
    output_weight,
    residual,
    norm_gain,
    route_experts,
    route_gates,
    gate_weight,
    up_weight,
    down_weight,
):
    seq_count = lax.axis_size("seq")
    role_count = lax.axis_size("role")
    seq_index = lax.axis_index("seq")
    role_index = lax.axis_index("role")
    batch_count = query_rows.shape[0]
    local_length = query_rows.shape[1]
    local_heads = query_rows.shape[2] // HEAD_WIDTH
    full_length = local_length * seq_count
    query_group_width = QUERY_HEADS // KEY_VALUE_HEADS
    head_pick = role_index * local_heads // query_group_width
    role_keys, role_values = (
        lax.all_gather(encoded_key_rows, "role", axis=1, tiled=True),
        lax.all_gather(value_matrix_rows, "role", axis=1, tiled=True),
    )
    head_keys = lax.dynamic_slice_in_dim(role_keys, head_pick * HEAD_WIDTH, HEAD_WIDTH, 2)
    head_values = lax.dynamic_slice_in_dim(role_values, head_pick * HEAD_WIDTH, HEAD_WIDTH, 2)
    whole_keys, whole_values, whole_proj = (
        lax.all_gather(head_keys, "seq", axis=1, tiled=True),
        lax.all_gather(head_values, "seq", axis=1, tiled=True),
        lax.all_gather(output_weight, "seq", axis=1, tiled=True),
    )
    key_width = full_length // 8
    score_scale = HEAD_WIDTH ** (-0.5)
    query_position = seq_index * local_length + jnp.arange(local_length, dtype=jnp.int32)
    last_needed = (seq_index + 1) * local_length

    def one_sequence(operands):
        own_queries, every_key, every_value = operands
        queries = own_queries.reshape(local_length, local_heads, HEAD_WIDTH)
        pieces = []
        for number in range(8):
            block_start = number * key_width
            compute = partial(
                score_block, queries, every_key, query_position, block_start, key_width, score_scale
            )
            skipped = partial(
                jnp.full, (local_heads, local_length, key_width), masked_score, jnp.float32
            )
            pieces.append(lax.cond(block_start < last_needed, compute, skipped))
        scores = jnp.concatenate(pieces, axis=2)
        row_peak = jnp.max(scores, axis=2, keepdims=True)
        weights = jnp.exp(scores - row_peak)
        totals = jnp.sum(weights, axis=2, keepdims=True)
        rounded = weights.astype(jnp.bfloat16)
        mixed_rows = jnp.zeros((local_length, local_heads, HEAD_WIDTH), jnp.float32)
        for number in range(8):
            block_start = number * key_width
            product = partial(value_block, rounded, every_value, block_start, key_width)
            nothing = partial(jnp.zeros, (local_length, local_heads, HEAD_WIDTH), jnp.float32)
            mixed_rows = mixed_rows + lax.cond(block_start < last_needed, product, nothing)
        attended = (mixed_rows / totals.transpose(1, 0, 2)).astype(jnp.bfloat16)
        return attended.reshape(local_length, local_heads * HEAD_WIDTH)

    attended = lax.map(one_sequence, (query_rows, whole_keys, whole_values))
    flat_attended = attended.reshape(batch_count * local_length, local_heads * HEAD_WIDTH)
    projected = lax.psum_scatter(
        jnp.dot(flat_attended, whole_proj, preferred_element_type=jnp.float32).astype(jnp.bfloat16),
        "role",
        scatter_dimension=0,
        tiled=True,
    ).astype(jnp.float32)
    hidden = residual[0].astype(jnp.float32) + projected
    variance = jnp.mean(hidden * hidden, axis=-1, keepdims=True)
    normed = (hidden * lax.rsqrt(variance + epsilon) * norm_gain).astype(jnp.bfloat16)
    expert_ids = route_experts.reshape(-1)
    gate_values = route_gates.reshape(-1)
    experts_local = gate_weight.shape[0]
    device_count = seq_count * role_count
    expert_count = experts_local * device_count
    assign = expert_ids.shape[0]
    capacity = assign // expert_count + 1
    onehot = (expert_ids[:, None] == jnp.arange(expert_count, dtype=jnp.int32)[None, :]).astype(
        jnp.int32
    )
    earlier = jnp.cumsum(onehot, axis=0) - onehot
    slot_rank = jnp.sum(earlier * onehot, axis=1)
    slot_index = expert_ids * capacity + slot_rank
    source_token = jnp.arange(assign, dtype=jnp.int32) // TOPK
    slot_token = jnp.zeros((expert_count * capacity,), jnp.int32).at[slot_index].set(source_token)
    slot_used = jnp.zeros((expert_count * capacity,), jnp.bfloat16).at[slot_index].set(1.0)
    outgoing = (normed[slot_token] * slot_used[:, None]).reshape(
        device_count, experts_local, capacity, D
    )
    incoming = lax.all_to_all(outgoing, ("seq", "role"), split_axis=0, concat_axis=0, tiled=True)
    gate_hidden = jnp.einsum(
        "sjcd,jdf->sjcf", incoming, gate_weight, preferred_element_type=jnp.float32
    )
    up_hidden = jnp.einsum(
        "sjcd,jdf->sjcf", incoming, up_weight, preferred_element_type=jnp.float32
    )
    activated = (jax.nn.silu(gate_hidden) * up_hidden).astype(jnp.bfloat16)
    returned = lax.all_to_all(
        jnp.einsum(
            "sjcf,jfd->sjcd", activated, down_weight, preferred_element_type=jnp.float32
        ).astype(jnp.bfloat16),
        ("seq", "role"),
        split_axis=0,
        concat_axis=0,
        tiled=True,
    )
    gathered = returned.reshape(expert_count * capacity, D)[slot_index]
    weighted = gathered.astype(jnp.float32) * gate_values[:, None]
    expert_sum = jnp.sum(weighted.reshape(-1, TOPK, D), axis=1)
    return (hidden + expert_sum).astype(jnp.bfloat16).reshape(residual.shape)


def in_hbm(*arrays):
    return [pltpu.with_memory_space_constraint(array, pltpu.HBM) for array in arrays]


def hbm_specs(count):
    return [pl.BlockSpec(memory_space=pltpu.HBM)] * count


def fetch_scratch(*arrays):
    return [pltpu.VMEM(array.shape, array.dtype) for array in arrays] + [
        pltpu.SemaphoreType.DMA((len(arrays),))
    ]


def start_fetch(from_refs, scratch):
    *buffers, sems = scratch
    copies = [
        pltpu.make_async_copy(from_ref, buffer, sems.at[n])
        for n, (from_ref, buffer) in enumerate(zip(from_refs, buffers))
    ]
    for copy in copies:
        copy.start()
    return copies, buffers


def in_vmem(count):
    return [pl.BlockSpec(memory_space=pltpu.VMEM)] * count


def attend_kernel(seq_count, role_count, slots, groups, at_ref, *refs):
    last_block, *refs = refs
    count = seq_count + 2
    attended_ref, *partial_refs = refs[count : count + 1 + len(groups)]
    copies, (query_ref, *buffers) = start_fetch(refs[:count], refs[count + 1 + len(groups) :])
    blocks, proj_refs = buffers[: seq_count - 1] + [last_block], buffers[seq_count - 1 :]
    seq_index, role_index = at_ref[0], at_ref[1]
    local_length = query_ref.shape[1]
    local_heads = query_ref.shape[2] // HEAD_WIDTH
    per_role = local_length // role_count
    rows = local_heads * local_length
    keys_all = seq_count * local_length
    slot = lax.broadcasted_iota(jnp.int32, (rows, keys_all), 1)
    block_number, within = slot // local_length, slot % local_length
    key_position = (
        (seq_index ^ block_number) * local_length
        + (role_index ^ (within // per_role)) * per_role
        + within % per_role
    )
    query_position = (
        seq_index * local_length
        + lax.broadcasted_iota(jnp.int32, (rows, keys_all), 0) % local_length
    )
    seen = key_position <= query_position
    scale = HEAD_WIDTH ** (-0.5)
    for copy in copies[:seq_count]:
        copy.wait()
    for n, k in enumerate(slots):
        b = role_index ^ k
        own = query_ref[b]
        queries = jnp.concatenate(
            [own[:, h * HEAD_WIDTH : (h + 1) * HEAD_WIDTH] for h in range(local_heads)], axis=0
        )
        key_value = jnp.concatenate([block[b] for block in blocks], axis=0)
        keys, values = key_value[:, :HEAD_WIDTH], key_value[:, HEAD_WIDTH:]
        scores = lax.dot_general(
            queries, keys, (((1,), (1,)), ((), ())), preferred_element_type=jnp.float32
        )
        scores = jnp.where(seen, scores * scale, masked_score)
        weights = jnp.exp(scores - jnp.max(scores, axis=1, keepdims=True))
        totals = jnp.sum(weights, axis=1, keepdims=True)
        mixed = jnp.dot(weights.astype(jnp.bfloat16), values, preferred_element_type=jnp.float32)
        attended = (mixed / totals).astype(jnp.bfloat16)
        for h in range(local_heads):
            attended_ref[
                n * local_length : (n + 1) * local_length, h * HEAD_WIDTH : (h + 1) * HEAD_WIDTH
            ] = attended[h * local_length : (h + 1) * local_length]
    for copy in copies[seq_count:]:
        copy.wait()
    project_into(slots, groups, attended_ref, proj_refs, partial_refs)


def join_kernel(*refs):
    *piece_refs, out_ref = refs
    at = 0
    for ref in piece_refs:
        size = ref.shape[1]
        out_ref[:, at : at + size, :] = ref[...]
        at += size


def role_groups(role_count):
    last = role_count // 2
    bits = [1 << n for n in range(last.bit_length() - 1)]
    return [[k for k in range(role_count) if k & -k == bit] for bit in bits] + [[0, last]]


def project_into(slots, groups, attended_ref, proj_refs, partial_refs):
    slots = list(slots)
    rows = attended_ref.shape[0] // len(slots)
    at = 0
    for proj_ref in proj_refs:
        width = proj_ref.shape[1]
        product = jnp.dot(
            attended_ref[...], proj_ref[...], preferred_element_type=jnp.float32
        ).astype(jnp.bfloat16)
        for group, partial_ref in zip(groups, partial_refs):
            for n, k in enumerate(group):
                start = slots.index(k) * rows
                partial_ref[n * rows : (n + 1) * rows, at : at + width] = product[
                    start : start + rows
                ]
        at += width


def project_kernel(slots, groups, attended_ref, order_ref, *refs):
    count = (len(refs) - len(groups) - 1) // 2
    copies, proj_refs = start_fetch(refs[:count], refs[count + len(groups) :])
    for copy in copies:
        copy.wait()
    project_into(slots, groups, attended_ref, proj_refs, refs[count : count + len(groups)])


def partial_shapes(groups, rows, width):
    return [jax.ShapeDtypeStruct((rows * len(group), width), jnp.bfloat16) for group in groups]


def near_sum_kernel(route_ref, other_route_ref, came_ref, sent_any, *refs):
    out_refs, both_ref = refs[:2], refs[2]
    copies, (sent,) = start_fetch([sent_any], refs[3:])
    rows, width = sent.shape[0] // 2, sent.shape[1]
    lane = lax.broadcasted_iota(jnp.int32, (rows, GATE_COLUMNS), 1)
    half = GATE_COLUMNS // 2
    expert = (lane % half).astype(jnp.float32)
    for p, routes in enumerate((route_ref, other_route_ref)):
        shares = jnp.zeros((rows, GATE_COLUMNS), jnp.float32)
        routed = routes.shape[1] // 2
        for k in range(routed):
            named, weight = routes[:, k : k + 1], routes[:, routed + k : routed + k + 1]
            shares = shares + jnp.where(expert == named, weight, 0.0)
        first = shares.astype(jnp.bfloat16).astype(jnp.float32)
        terms = jnp.where(lane < half, first, shares - first).astype(jnp.bfloat16)
        out_refs[p][:, width:] = terms
        both_ref[p * rows : (p + 1) * rows, width:] = terms
    copies[0].wait()
    for p in range(2):
        total = sent[p * rows : (p + 1) * rows].astype(jnp.float32)
        total = total + came_ref[(1 - p) * rows : (2 - p) * rows].astype(jnp.float32)
        out_refs[p][:, :width] = total.astype(jnp.bfloat16)
        both_ref[p * rows : (p + 1) * rows, :width] = total.astype(jnp.bfloat16)


def far_sum_kernel(rows, order_count, *refs):
    refs = refs[order_count:]
    chips = (len(refs) - 4) // 3
    came_refs, sent_any = refs[:chips], refs[chips : 2 * chips]
    own_ref, other_ref, both_ref = refs[2 * chips : 2 * chips + 3]
    copies, sent_refs = start_fetch(sent_any, refs[2 * chips + 3 :])
    for copy in copies:
        copy.wait()
    size = chips * rows
    for n, (sent, came) in enumerate(zip(sent_refs, came_refs)):
        to = slice(n * rows, (n + 1) * rows)
        for p, out_ref in enumerate((own_ref, other_ref)):
            total = sent[p * rows : (p + 1) * rows].astype(jnp.float32)
            total = total + came[(1 - p) * rows : (2 - p) * rows].astype(jnp.float32)
            out_ref[to] = total.astype(jnp.bfloat16)
            both_ref[p * size + n * rows : p * size + (n + 1) * rows] = total.astype(jnp.bfloat16)


def norm_kernel(chips, near_row, far_row, at_ref, gain_ref, *refs):
    parts, (normed_ref, *hidden_refs, whole_ref) = refs[: 2 * chips], refs[2 * chips :]
    seq_index = at_ref[0]
    features = whole_ref.shape[1]
    rows = whole_ref.shape[0] // chips
    width = features // chips // 2
    for n in range(chips):
        near, far = parts[2 * n : 2 * n + 2]
        for m in range(chips):
            part = far if m else near
            first = ((far_row if m else near_row) if n else 0) + (m - 1 if m else 0) * rows
            to = slice((n ^ m) * rows, ((n ^ m) + 1) * rows)
            for j in range(2):
                start = pl.multiple_of((seq_index ^ (2 * n + j)) * width, width)
                whole_ref[to, pl.ds(start, width)] = part[
                    first : first + rows, j * width : (j + 1) * width
                ].astype(jnp.float32)
        first = near_row if n else 0
        normed_ref[n * rows : (n + 1) * rows, features:] = near[first : first + rows, 2 * width :]
    hidden = whole_ref[...]
    variance = jnp.mean(hidden * hidden, axis=1, keepdims=True)
    normed = hidden * lax.rsqrt(variance + epsilon) * gain_ref[...]
    normed_ref[:, :features] = normed.astype(jnp.bfloat16)
    for hidden_ref in hidden_refs:
        hidden_ref[...] = hidden[:rows]


def expert_kernel(token_count, at_ref, *refs):
    token_refs = refs[:token_count]
    gate_ref, up_ref, down_ref, keep_ref, send_ref, activated_ref = refs[token_count:]
    features, units = gate_ref.shape[1:]
    tokens = jnp.concatenate([ref[:, :features] for ref in token_refs], axis=0)
    gates = jnp.concatenate([ref[:, features:] for ref in token_refs], axis=0)
    lane = lax.broadcasted_iota(jnp.int32, gates.shape, 1)
    mine = lane % (GATE_COLUMNS // 2) == at_ref[2]
    share = jnp.sum(jnp.where(mine, gates.astype(jnp.float32), 0.0), axis=1, keepdims=True)
    block = 256 if units % 256 == 0 else units
    for f in range(0, units, block):
        gate_hidden = jnp.dot(
            tokens, gate_ref[0, :, f : f + block], preferred_element_type=jnp.float32
        )
        up_hidden = jnp.dot(tokens, up_ref[0, :, f : f + block], preferred_element_type=jnp.float32)
        activated_ref[:, f : f + block] = (
            gate_hidden / (1.0 + jnp.exp(-gate_hidden)) * up_hidden
        ).astype(jnp.bfloat16)
    kept = keep_ref.shape[0]
    block = 512 if features % 512 == 0 else features
    for c in range(0, features, block):
        product = jnp.dot(
            activated_ref[...], down_ref[0, :, c : c + block], preferred_element_type=jnp.float32
        )
        product = (product * share).astype(jnp.bfloat16)
        keep_ref[:, c : c + block] = product[:kept]
        send_ref[:, c : c + block] = product[kept:]


def run_expert(at, tokens, gate_weight, up_weight, down_weight):
    units = gate_weight.shape[2]
    width = gate_weight.shape[1]
    rows = sum(part.shape[0] for part in tokens)
    half = jax.ShapeDtypeStruct((rows // 2, width), jnp.bfloat16)
    return pl.pallas_call(
        partial(expert_kernel, len(tokens)),
        in_specs=[pl.BlockSpec(memory_space=pltpu.SMEM)] + in_vmem(len(tokens) + 3),
        out_specs=in_vmem(2),
        out_shape=[half, half],
        scratch_shapes=[pltpu.VMEM((rows, units), jnp.bfloat16)],
        compiler_params=pltpu.CompilerParams(vmem_limit_bytes=EXPERT_VMEM),
        cost_estimate=NOTHING,
    )(at, *tokens, gate_weight, up_weight, down_weight)


def after(array, *others):
    return lax.optimization_barrier((array, *others))[0]


def added(terms):
    total = terms[0].astype(jnp.float32)
    for term in terms[1:]:
        total = total + term.astype(jnp.float32)
    return total


def gathered_shards(
    query_rows,
    encoded_key_rows,
    value_matrix_rows,
    output_weight,
    residual,
    norm_gain,
    route_experts,
    route_gates,
    gate_weight,
    up_weight,
    down_weight,
):
    seq_count = lax.axis_size("seq")
    role_count = lax.axis_size("role")
    seq_index = lax.axis_index("seq")
    role_index = lax.axis_index("role")
    batch_count, local_length, query_width = query_rows.shape
    local_heads = query_width // HEAD_WIDTH
    group_width = QUERY_HEADS // KEY_VALUE_HEADS
    role_bits = [1 << n for n in range(role_count.bit_length() - 1)]
    at = jnp.stack([seq_index, role_index, seq_index * role_count + role_index]).astype(jnp.int32)

    def over_role(array, k):
        return lax.ppermute(array, "role", [(i, i ^ k) for i in range(role_count)])

    def over_seq(array, j):
        return lax.ppermute(array, "seq", [(i, i ^ j) for i in range(seq_count)])

    beside_proj = over_seq(output_weight, 1)
    block_width = output_weight.shape[1]
    across_steps = range(2, seq_count, 2)

    pieces = []
    for k in range(role_count):
        head = ((role_index ^ k) * local_heads // group_width) * HEAD_WIDTH
        piece = jnp.concatenate(
            [
                lax.dynamic_slice_in_dim(encoded_key_rows, head, HEAD_WIDTH, 2),
                lax.dynamic_slice_in_dim(value_matrix_rows, head, HEAD_WIDTH, 2),
            ],
            axis=2,
        )
        pieces.append(piece)
    pieces[1] = after(pieces[1], beside_proj)
    pieces = [piece if k == 0 else over_role(piece, k) for k, piece in enumerate(pieces)]
    block = pl.pallas_call(
        join_kernel,
        in_specs=in_vmem(len(pieces)),
        out_specs=pl.BlockSpec(memory_space=pltpu.VMEM),
        out_shape=jax.ShapeDtypeStruct(
            (batch_count, local_length, 2 * HEAD_WIDTH), jnp.bfloat16
        ),
        compiler_params=pltpu.CompilerParams(vmem_limit_bytes=COPY_VMEM),
        cost_estimate=SHORT,
    )(*pieces)
    same_core = [block] + [over_seq(block, j) for j in across_steps]
    blocks = []
    for part in same_core:
        blocks += [part, over_seq(part, 1)]
    last = role_count // 2
    routes = jnp.concatenate([route_experts[0].astype(jnp.float32), route_gates[0]], axis=1)
    residual_blocks = [
        lax.dynamic_slice_in_dim(residual[0], (seq_index ^ j) * block_width, block_width, 1)
        for j in range(seq_count)
    ]
    residuals = [
        jnp.concatenate(residual_blocks[j : j + 2], axis=1) for j in range(0, seq_count, 2)
    ]
    residuals = [residuals[0]] + [over_seq(residuals[j // 2], j) for j in across_steps]

    rows = batch_count * local_length
    near_width = 2 * output_weight.shape[1]
    groups = role_groups(role_count)
    attend_args = in_hbm(query_rows, *blocks[:-1], output_weight, beside_proj)
    slot_sets = [(range(1, role_count, 2), groups[:1]), (range(0, role_count, 2), groups[1:])]
    attended, near = [], []
    for slots, parts in slot_sets:
        half_rows = jax.ShapeDtypeStruct((rows // 2, query_width), jnp.bfloat16)
        half, *partials = pl.pallas_call(
            partial(attend_kernel, seq_count, role_count, slots, parts),
            in_specs=[pl.BlockSpec(memory_space=pltpu.SMEM)]
            + in_vmem(1)
            + hbm_specs(len(attend_args)),
            out_specs=in_vmem(1 + len(parts)),
            out_shape=[half_rows] + partial_shapes(parts, local_length, near_width),
            scratch_shapes=fetch_scratch(*attend_args),
            compiler_params=pltpu.CompilerParams(vmem_limit_bytes=SMALL_VMEM),
            cost_estimate=SHORT,
        )(at, blocks[-1], *attend_args)
        attended.append(half)
        near += partials

    other_routes = over_role(routes, last)

    def summed_over_role(parts, extra, *before):
        terms = [[part] for part in parts]
        for n, group in enumerate(groups[:-1]):
            bit = 1 << n
            leaving = terms[n][0] if len(terms[n]) == 1 else added(terms[n]).astype(jnp.bfloat16)
            came = over_role(leaving, bit)
            for m in range(n + 1, len(groups)):
                at_rows = [group.index(k ^ bit) for k in groups[m]]
                if at_rows == list(range(len(group))):
                    terms[m].append(came)
                else:
                    split = [came[i * local_length : (i + 1) * local_length] for i in at_rows]
                    terms[m].append(jnp.concatenate(split, axis=0))
        extra = jnp.pad(after(extra, *before) if before else extra, ((0, local_length), (0, 0)))
        sent = added(terms[-1] + [extra]).astype(jnp.bfloat16)
        return sent

    near_sent = summed_over_role(near, residuals[0])
    near_came = over_role(near_sent, last)
    near_args = in_hbm(near_sent)
    own_shape, both_shape = [
        jax.ShapeDtypeStruct((size, near_width + GATE_COLUMNS), jnp.bfloat16)
        for size in (local_length, 2 * local_length)
    ]
    near_halves = pl.pallas_call(
        near_sum_kernel,
        in_specs=in_vmem(3) + hbm_specs(1),
        out_specs=in_vmem(3),
        out_shape=[own_shape, own_shape, both_shape],
        scratch_shapes=fetch_scratch(*near_args),
        compiler_params=pltpu.CompilerParams(vmem_limit_bytes=SMALL_VMEM),
        cost_estimate=LONG,
    )(routes, other_routes, near_came, *near_args)

    def walk(k, bits):
        found = [k]
        for n, bit in enumerate(bits):
            found += walk(k | bit, bits[n + 1 :])
        return found

    lower_bits = role_bits[:-1][::-1]
    order = walk(last, lower_bits) + walk(0, lower_bits)
    far_plane, final = order[1], order[-1]

    def across(part):
        return [over_seq(part, j) for j in across_steps]

    def spread(own, other, both):
        planes, crossed = {0: own, last: other}, {}
        both_across = across(both)
        size = own.shape[0]
        for k in order:
            if k not in planes:
                bit = k & -k
                held = planes[k ^ bit]
                planes[k] = over_role(after(held, planes[far_plane]) if k < last else held, bit)
            if k in (0, last):
                crossed[k] = both_across
            elif k < last:
                source = k ^ (k & -k)
                came = [part[:size] for part in crossed[source]] if source == 0 else crossed[source]
                crossed[k] = [over_role(part, k & -k) for part in came]
            else:
                crossed[k] = across(after(planes[k], *both_across))
        return planes, crossed

    near_planes, near_crossed = spread(*near_halves)

    sent, came = [], []
    for n, j in enumerate(across_steps, 1):
        far = []
        for half, (slots, parts) in zip(attended, slot_sets):
            far += pl.pallas_call(
                partial(project_kernel, slots, parts),
                in_specs=in_vmem(1) + [pl.BlockSpec(memory_space=pl.ANY)] + hbm_specs(2),
                out_specs=in_vmem(len(parts)),
                out_shape=partial_shapes(parts, local_length, near_width),
                scratch_shapes=fetch_scratch(output_weight, beside_proj),
                compiler_params=pltpu.CompilerParams(vmem_limit_bytes=SMALL_VMEM),
                cost_estimate=SHORT,
            )(over_seq(half, j), other_routes, *in_hbm(output_weight, beside_proj))
        sent.append(summed_over_role(far, residuals[n], near_halves[0]))
        came.append(over_role(sent[-1], last))

    chips = 1 + len(across_steps)
    far_args = in_hbm(*sent)
    far_rows = (chips - 1) * local_length
    far_shape, far_both_shape = [
        jax.ShapeDtypeStruct((size, near_width), jnp.bfloat16) for size in (far_rows, 2 * far_rows)
    ]
    first_come = [*near_crossed[0], near_planes[far_plane], *near_crossed[far_plane]]
    first_come.append(near_planes[final])
    far_halves = pl.pallas_call(
        partial(far_sum_kernel, local_length, len(first_come)),
        in_specs=[pl.BlockSpec(memory_space=pl.ANY)] * len(first_come)
        + in_vmem(len(came))
        + hbm_specs(len(far_args)),
        out_specs=in_vmem(3),
        out_shape=[far_shape, far_shape, far_both_shape],
        scratch_shapes=fetch_scratch(*far_args),
        compiler_params=pltpu.CompilerParams(vmem_limit_bytes=SMALL_VMEM),
        cost_estimate=SHORT,
    )(*first_come, *came, *far_args)
    far_planes, far_crossed = spread(*far_halves)

    width = residual.shape[2]
    gain = norm_gain.reshape(1, width)

    def normed_rows(parts, second, *hidden_shape):
        rows = chips * local_length
        firsts = (local_length, far_rows) if second else (0, 0)
        return pl.pallas_call(
            partial(norm_kernel, chips, *firsts),
            in_specs=[pl.BlockSpec(memory_space=pltpu.SMEM)] + in_vmem(1 + 2 * chips),
            out_specs=in_vmem(1 + len(hidden_shape)),
            out_shape=[
                jax.ShapeDtypeStruct((rows, width + GATE_COLUMNS), jnp.bfloat16),
                *hidden_shape,
            ],
            scratch_shapes=[pltpu.VMEM((rows, width), jnp.float32)],
            compiler_params=pltpu.CompilerParams(vmem_limit_bytes=SMALL_VMEM),
            cost_estimate=NOTHING,
        )(at, gain, *parts)

    keep, send, slots, leaving, passed = {}, {}, {}, {}, {}

    hidden_shape = jax.ShapeDtypeStruct((local_length, width), jnp.float32)
    hidden = []

    hidden_shape = jax.ShapeDtypeStruct((local_length, width), jnp.float32)
    hidden = []

    def prepared(k, *first):
        late = far_crossed[k]
        if first:
            late = [after(part, *first) for part in late]
        parts = [near_planes[k], far_planes[k]]
        for pair in zip(near_crossed[k], late):
            parts += pair
        normed, *own = normed_rows(parts, k == last, *([] if k else [hidden_shape]))
        hidden.extend(own)
        return [normed, over_seq(normed, 1)]

    def expert(tokens, *others):
        if others:
            tokens = lax.optimization_barrier((*tokens, *others))[: len(tokens)]
        return run_expert(at, tokens, gate_weight, up_weight, down_weight)

    def combine(k, *before):
        came = over_seq(after(send[k], *before) if before else send[k], 1)
        sums = []
        for n in range(len(across_steps)):
            chunk = slice((n + 1) * local_length, (n + 2) * local_length)
            sums.append(added([keep[k][chunk], came[chunk]]).astype(jnp.bfloat16))
        return [keep[k][:local_length], came[:local_length]], sums

    def pass_on(k):
        passed[k] = [over_seq(part, j) for part, j in zip(leaving[k], across_steps)]
        slots[k] += passed[k]

    ready = {far_plane: prepared(far_plane, far_planes[final], *far_crossed[final])}
    ready[final] = prepared(final)
    keep[far_plane], send[far_plane] = expert(ready[far_plane], ready[final][0])
    ready |= {k: prepared(k, keep[far_plane]) for k in (last, 0)}
    slots[far_plane], leaving[far_plane] = combine(far_plane)
    leaving[far_plane] = [after(part, ready[last][0], ready[0][0]) for part in leaving[far_plane]]
    pass_on(far_plane)
    keep[last], send[last] = expert(ready[last], keep[far_plane], *leaving[far_plane])
    slots[last], leaving[last] = combine(last)
    leaving[last] = [after(part, *passed[far_plane]) for part in leaving[last]]
    pass_on(last)
    keep[final], send[final] = expert(ready[final], keep[last])
    slots[far_plane] = [added(slots[far_plane]).astype(jnp.bfloat16)]
    slots[final], leaving[final] = combine(final, *passed[far_plane])
    leaving[final] = [after(part, *leaving[last]) for part in leaving[final]]
    pass_on(final)
    keep[0], send[0] = expert(ready[0], keep[final], *leaving[last])
    slots[0], leaving[0] = combine(0, *passed[last])
    leaving[0] = [after(part, *leaving[final]) for part in leaving[0]]
    pass_on(0)
    for bit in role_bits:
        for k in [k for k in sorted(slots, reverse=True) if k & bit]:
            going = added(slots.pop(k)).astype(jnp.bfloat16)
            if k == last:
                going = after(going, *leaving[final])
            slots[k ^ bit].append(over_role(going, bit))
    return added(hidden + slots[0]).astype(jnp.bfloat16).reshape(residual.shape)


def solution(mesh):
    placed = (
        P("groups", "seq", "role"),
        P("groups", ("seq", "role"), None),
        P("groups", ("seq", "role"), None),
        P("role", "seq"),
        P(("groups", "role"), "seq", None),
        P(),
        P(("groups", "role"), "seq", None),
        P(("groups", "role"), "seq", None),
        P(("seq", "role"), None, None),
        P(("seq", "role"), None, None),
        P(("seq", "role"), None, None),
    )
    experts = mesh.shape["seq"] * mesh.shape["role"]
    return jax.shard_map(
        gathered_shards if experts <= 2 * TOPK else routed_shards,
        mesh=mesh,
        in_specs=placed,
        out_specs=P(("groups", "role"), "seq", None),
        check_vma=False,
    )
```

```python
from functools import partial

import jax
import jax.numpy as jnp
from jax import lax
from jax.experimental import pallas as pl
from jax.experimental.pallas import tpu as pltpu
from jax.sharding import PartitionSpec as P

D = 2048
QUERY_HEADS = 32
KEY_VALUE_HEADS = 4
HEAD_WIDTH = 128
TOPK = 8


epsilon = 1e-06
masked_score = -1e30
EXPERT_VMEM = 16 * 2**20
SMALL_VMEM = 12 * 2**20
COPY_VMEM = 4 * 2**20
GATE_COLUMNS = 128
NOTHING = pl.CostEstimate(flops=1, bytes_accessed=1, transcendentals=0)
SHORT = pl.CostEstimate(flops=2 * 10**9, bytes_accessed=4 * 2**20, transcendentals=0)
LONG = pl.CostEstimate(flops=10**10, bytes_accessed=1, transcendentals=0)


def score_block(queries, every_key, query_position, block_start, block_width, score_scale):
    keys_part = lax.slice_in_dim(every_key, block_start, block_start + block_width, axis=0)
    raw_scores = (
        jnp.einsum("qhd,kd->hqk", queries, keys_part, preferred_element_type=jnp.float32)
        * score_scale
    )
    key_position = block_start + jnp.arange(block_width, dtype=jnp.int32)
    return jnp.where(
        key_position[None, None, :] <= query_position[None, :, None], raw_scores, masked_score
    )


def value_block(rounded, every_value, block_start, block_width):
    prob_block = lax.slice_in_dim(rounded, block_start, block_start + block_width, axis=2)
    values_part = lax.slice_in_dim(every_value, block_start, block_start + block_width, axis=0)
    return jnp.einsum("hqk,kd->qhd", prob_block, values_part, preferred_element_type=jnp.float32)


def routed_shards(
    query_rows,
    encoded_key_rows,
    value_matrix_rows,
    output_weight,
    residual,
    norm_gain,
    route_experts,
    route_gates,
    gate_weight,
    up_weight,
    down_weight,
):
    seq_count = lax.axis_size("seq")
    role_count = lax.axis_size("role")
    seq_index = lax.axis_index("seq")
    role_index = lax.axis_index("role")
    batch_count = query_rows.shape[0]
    local_length = query_rows.shape[1]
    local_heads = query_rows.shape[2] // HEAD_WIDTH
    full_length = local_length * seq_count
    query_group_width = QUERY_HEADS // KEY_VALUE_HEADS
    head_pick = role_index * local_heads // query_group_width
    role_keys, role_values = (
        lax.all_gather(encoded_key_rows, "role", axis=1, tiled=True),
        lax.all_gather(value_matrix_rows, "role", axis=1, tiled=True),
    )
    head_keys = lax.dynamic_slice_in_dim(role_keys, head_pick * HEAD_WIDTH, HEAD_WIDTH, 2)
    head_values = lax.dynamic_slice_in_dim(role_values, head_pick * HEAD_WIDTH, HEAD_WIDTH, 2)
    whole_keys, whole_values, whole_proj = (
        lax.all_gather(head_keys, "seq", axis=1, tiled=True),
        lax.all_gather(head_values, "seq", axis=1, tiled=True),
        lax.all_gather(output_weight, "seq", axis=1, tiled=True),
    )
    key_width = full_length // 8
    score_scale = HEAD_WIDTH ** (-0.5)
    query_position = seq_index * local_length + jnp.arange(local_length, dtype=jnp.int32)
    last_needed = (seq_index + 1) * local_length

    def one_sequence(operands):
        own_queries, every_key, every_value = operands
        queries = own_queries.reshape(local_length, local_heads, HEAD_WIDTH)
        pieces = []
        for number in range(8):
            block_start = number * key_width
            compute = partial(
                score_block, queries, every_key, query_position, block_start, key_width, score_scale
            )
            skipped = partial(
                jnp.full, (local_heads, local_length, key_width), masked_score, jnp.float32
            )
            pieces.append(lax.cond(block_start < last_needed, compute, skipped))
        scores = jnp.concatenate(pieces, axis=2)
        row_peak = jnp.max(scores, axis=2, keepdims=True)
        weights = jnp.exp(scores - row_peak)
        totals = jnp.sum(weights, axis=2, keepdims=True)
        rounded = weights.astype(jnp.bfloat16)
        mixed_rows = jnp.zeros((local_length, local_heads, HEAD_WIDTH), jnp.float32)
        for number in range(8):
            block_start = number * key_width
            product = partial(value_block, rounded, every_value, block_start, key_width)
            nothing = partial(jnp.zeros, (local_length, local_heads, HEAD_WIDTH), jnp.float32)
            mixed_rows = mixed_rows + lax.cond(block_start < last_needed, product, nothing)
        attended = (mixed_rows / totals.transpose(1, 0, 2)).astype(jnp.bfloat16)
        return attended.reshape(local_length, local_heads * HEAD_WIDTH)

    attended = lax.map(one_sequence, (query_rows, whole_keys, whole_values))
    flat_attended = attended.reshape(batch_count * local_length, local_heads * HEAD_WIDTH)
    projected = lax.psum_scatter(
        jnp.dot(flat_attended, whole_proj, preferred_element_type=jnp.float32).astype(jnp.bfloat16),
        "role",
        scatter_dimension=0,
        tiled=True,
    ).astype(jnp.float32)
    hidden = residual[0].astype(jnp.float32) + projected
    variance = jnp.mean(hidden * hidden, axis=-1, keepdims=True)
    normed = (hidden * lax.rsqrt(variance + epsilon) * norm_gain).astype(jnp.bfloat16)
    expert_ids = route_experts.reshape(-1)
    gate_values = route_gates.reshape(-1)
    experts_local = gate_weight.shape[0]
    device_count = seq_count * role_count
    expert_count = experts_local * device_count
    assign = expert_ids.shape[0]
    capacity = assign // expert_count + 1
    onehot = (expert_ids[:, None] == jnp.arange(expert_count, dtype=jnp.int32)[None, :]).astype(
        jnp.int32
    )
    earlier = jnp.cumsum(onehot, axis=0) - onehot
    slot_rank = jnp.sum(earlier * onehot, axis=1)
    slot_index = expert_ids * capacity + slot_rank
    source_token = jnp.arange(assign, dtype=jnp.int32) // TOPK
    slot_token = jnp.zeros((expert_count * capacity,), jnp.int32).at[slot_index].set(source_token)
    slot_used = jnp.zeros((expert_count * capacity,), jnp.bfloat16).at[slot_index].set(1.0)
    outgoing = (normed[slot_token] * slot_used[:, None]).reshape(
        device_count, experts_local, capacity, D
    )
    incoming = lax.all_to_all(outgoing, ("seq", "role"), split_axis=0, concat_axis=0, tiled=True)
    gate_hidden = jnp.einsum(
        "sjcd,jdf->sjcf", incoming, gate_weight, preferred_element_type=jnp.float32
    )
    up_hidden = jnp.einsum(
        "sjcd,jdf->sjcf", incoming, up_weight, preferred_element_type=jnp.float32
    )
    activated = (jax.nn.silu(gate_hidden) * up_hidden).astype(jnp.bfloat16)
    returned = lax.all_to_all(
        jnp.einsum(
            "sjcf,jfd->sjcd", activated, down_weight, preferred_element_type=jnp.float32
        ).astype(jnp.bfloat16),
        ("seq", "role"),
        split_axis=0,
        concat_axis=0,
        tiled=True,
    )
    gathered = returned.reshape(expert_count * capacity, D)[slot_index]
    weighted = gathered.astype(jnp.float32) * gate_values[:, None]
    expert_sum = jnp.sum(weighted.reshape(-1, TOPK, D), axis=1)
    return (hidden + expert_sum).astype(jnp.bfloat16).reshape(residual.shape)


def in_hbm(*arrays):
    return [pltpu.with_memory_space_constraint(array, pltpu.HBM) for array in arrays]


def hbm_specs(count):
    return [pl.BlockSpec(memory_space=pltpu.HBM)] * count


def fetch_scratch(*arrays):
    return [pltpu.VMEM(array.shape, array.dtype) for array in arrays] + [
        pltpu.SemaphoreType.DMA((len(arrays),))
    ]


def start_fetch(from_refs, scratch):
    *buffers, sems = scratch
    copies = [
        pltpu.make_async_copy(from_ref, buffer, sems.at[n])
        for n, (from_ref, buffer) in enumerate(zip(from_refs, buffers))
    ]
    for copy in copies:
        copy.start()
    return copies, buffers


def in_vmem(count):
    return [pl.BlockSpec(memory_space=pltpu.VMEM)] * count


def attend_kernel(seq_count, role_count, slots, groups, at_ref, *refs):
    last_block, *refs = refs
    count = seq_count + 2
    attended_ref, *partial_refs = refs[count : count + 1 + len(groups)]
    copies, (query_ref, *buffers) = start_fetch(refs[:count], refs[count + 1 + len(groups) :])
    blocks, proj_refs = buffers[: seq_count - 1] + [last_block], buffers[seq_count - 1 :]
    seq_index, role_index = at_ref[0], at_ref[1]
    local_length = query_ref.shape[1]
    local_heads = query_ref.shape[2] // HEAD_WIDTH
    per_role = local_length // role_count
    rows = local_heads * local_length
    keys_all = seq_count * local_length
    slot = lax.broadcasted_iota(jnp.int32, (rows, keys_all), 1)
    block_number, within = slot // local_length, slot % local_length
    key_position = (
        (seq_index ^ block_number) * local_length
        + (role_index ^ (within // per_role)) * per_role
        + within % per_role
    )
    query_position = (
        seq_index * local_length
        + lax.broadcasted_iota(jnp.int32, (rows, keys_all), 0) % local_length
    )
    seen = key_position <= query_position
    scale = HEAD_WIDTH ** (-0.5)
    for copy in copies[:seq_count]:
        copy.wait()
    for n, k in enumerate(slots):
        b = role_index ^ k
        own = query_ref[b]
        queries = jnp.concatenate(
            [own[:, h * HEAD_WIDTH : (h + 1) * HEAD_WIDTH] for h in range(local_heads)], axis=0
        )
        key_value = jnp.concatenate([block[b] for block in blocks], axis=0)
        keys, values = key_value[:, :HEAD_WIDTH], key_value[:, HEAD_WIDTH:]
        scores = lax.dot_general(
            queries, keys, (((1,), (1,)), ((), ())), preferred_element_type=jnp.float32
        )
        scores = jnp.where(seen, scores * scale, masked_score)
        weights = jnp.exp(scores - jnp.max(scores, axis=1, keepdims=True))
        totals = jnp.sum(weights, axis=1, keepdims=True)
        mixed = jnp.dot(weights.astype(jnp.bfloat16), values, preferred_element_type=jnp.float32)
        attended = (mixed / totals).astype(jnp.bfloat16)
        for h in range(local_heads):
            attended_ref[
                n * local_length : (n + 1) * local_length, h * HEAD_WIDTH : (h + 1) * HEAD_WIDTH
            ] = attended[h * local_length : (h + 1) * local_length]
    for copy in copies[seq_count:]:
        copy.wait()
    project_into(slots, groups, attended_ref, proj_refs, partial_refs)


def join_kernel(*refs):
    *piece_refs, out_ref = refs
    at = 0
    for ref in piece_refs:
        size = ref.shape[1]
        out_ref[:, at : at + size, :] = ref[...]
        at += size


def role_groups(role_count):
    last = role_count // 2
    bits = [1 << n for n in range(last.bit_length() - 1)]
    return [[k for k in range(role_count) if k & -k == bit] for bit in bits] + [[0, last]]


def project_into(slots, groups, attended_ref, proj_refs, partial_refs):
    slots = list(slots)
    rows = attended_ref.shape[0] // len(slots)
    at = 0
    for proj_ref in proj_refs:
        width = proj_ref.shape[1]
        product = jnp.dot(
            attended_ref[...], proj_ref[...], preferred_element_type=jnp.float32
        ).astype(jnp.bfloat16)
        for group, partial_ref in zip(groups, partial_refs):
            for n, k in enumerate(group):
                start = slots.index(k) * rows
                partial_ref[n * rows : (n + 1) * rows, at : at + width] = product[
                    start : start + rows
                ]
        at += width


def project_kernel(slots, groups, attended_ref, order_ref, *refs):
    count = (len(refs) - len(groups) - 1) // 2
    copies, proj_refs = start_fetch(refs[:count], refs[count + len(groups) :])
    for copy in copies:
        copy.wait()
    project_into(slots, groups, attended_ref, proj_refs, refs[count : count + len(groups)])


def partial_shapes(groups, rows, width):
    return [jax.ShapeDtypeStruct((rows * len(group), width), jnp.bfloat16) for group in groups]


def near_sum_kernel(route_ref, other_route_ref, came_ref, sent_any, *refs):
    out_refs, both_ref = refs[:2], refs[2]
    copies, (sent,) = start_fetch([sent_any], refs[3:])
    rows, width = sent.shape[0] // 2, sent.shape[1]
    lane = lax.broadcasted_iota(jnp.int32, (rows, GATE_COLUMNS), 1)
    half = GATE_COLUMNS // 2
    expert = (lane % half).astype(jnp.float32)
    for p, routes in enumerate((route_ref, other_route_ref)):
        shares = jnp.zeros((rows, GATE_COLUMNS), jnp.float32)
        routed = routes.shape[1] // 2
        for k in range(routed):
            named, weight = routes[:, k : k + 1], routes[:, routed + k : routed + k + 1]
            shares = shares + jnp.where(expert == named, weight, 0.0)
        first = shares.astype(jnp.bfloat16).astype(jnp.float32)
        terms = jnp.where(lane < half, first, shares - first).astype(jnp.bfloat16)
        out_refs[p][:, width:] = terms
        both_ref[p * rows : (p + 1) * rows, width:] = terms
    copies[0].wait()
    for p in range(2):
        total = sent[p * rows : (p + 1) * rows].astype(jnp.float32)
        total = total + came_ref[(1 - p) * rows : (2 - p) * rows].astype(jnp.float32)
        out_refs[p][:, :width] = total.astype(jnp.bfloat16)
        both_ref[p * rows : (p + 1) * rows, :width] = total.astype(jnp.bfloat16)


def far_sum_kernel(rows, order_count, *refs):
    refs = refs[order_count:]
    chips = (len(refs) - 4) // 3
    came_refs, sent_any = refs[:chips], refs[chips : 2 * chips]
    own_ref, other_ref, both_ref = refs[2 * chips : 2 * chips + 3]
    copies, sent_refs = start_fetch(sent_any, refs[2 * chips + 3 :])
    for copy in copies:
        copy.wait()
    size = chips * rows
    for n, (sent, came) in enumerate(zip(sent_refs, came_refs)):
        to = slice(n * rows, (n + 1) * rows)
        for p, out_ref in enumerate((own_ref, other_ref)):
            total = sent[p * rows : (p + 1) * rows].astype(jnp.float32)
            total = total + came[(1 - p) * rows : (2 - p) * rows].astype(jnp.float32)
            out_ref[to] = total.astype(jnp.bfloat16)
            both_ref[p * size + n * rows : p * size + (n + 1) * rows] = total.astype(jnp.bfloat16)


def norm_kernel(chips, near_row, far_row, at_ref, gain_ref, *refs):
    parts, (normed_ref, *hidden_refs, whole_ref) = refs[: 2 * chips], refs[2 * chips :]
    seq_index = at_ref[0]
    features = whole_ref.shape[1]
    rows = whole_ref.shape[0] // chips
    width = features // chips // 2
    for n in range(chips):
        near, far = parts[2 * n : 2 * n + 2]
        for m in range(chips):
            part = far if m else near
            first = ((far_row if m else near_row) if n else 0) + (m - 1 if m else 0) * rows
            to = slice((n ^ m) * rows, ((n ^ m) + 1) * rows)
            for j in range(2):
                start = pl.multiple_of((seq_index ^ (2 * n + j)) * width, width)
                whole_ref[to, pl.ds(start, width)] = part[
                    first : first + rows, j * width : (j + 1) * width
                ].astype(jnp.float32)
        first = near_row if n else 0
        normed_ref[n * rows : (n + 1) * rows, features:] = near[first : first + rows, 2 * width :]
    hidden = whole_ref[...]
    variance = jnp.mean(hidden * hidden, axis=1, keepdims=True)
    normed = hidden * lax.rsqrt(variance + epsilon) * gain_ref[...]
    normed_ref[:, :features] = normed.astype(jnp.bfloat16)
    for hidden_ref in hidden_refs:
        hidden_ref[...] = hidden[:rows]


def expert_kernel(token_count, at_ref, *refs):
    token_refs = refs[:token_count]
    gate_ref, up_ref, down_ref, keep_ref, send_ref, activated_ref = refs[token_count:]
    features, units = gate_ref.shape[1:]
    tokens = jnp.concatenate([ref[:, :features] for ref in token_refs], axis=0)
    gates = jnp.concatenate([ref[:, features:] for ref in token_refs], axis=0)
    lane = lax.broadcasted_iota(jnp.int32, gates.shape, 1)
    mine = lane % (GATE_COLUMNS // 2) == at_ref[2]
    share = jnp.sum(jnp.where(mine, gates.astype(jnp.float32), 0.0), axis=1, keepdims=True)
    block = 256 if units % 256 == 0 else units
    for f in range(0, units, block):
        gate_hidden = jnp.dot(
            tokens, gate_ref[0, :, f : f + block], preferred_element_type=jnp.float32
        )
        up_hidden = jnp.dot(tokens, up_ref[0, :, f : f + block], preferred_element_type=jnp.float32)
        activated_ref[:, f : f + block] = (
            gate_hidden / (1.0 + jnp.exp(-gate_hidden)) * up_hidden
        ).astype(jnp.bfloat16)
    kept = keep_ref.shape[0]
    block = 512 if features % 512 == 0 else features
    for c in range(0, features, block):
        product = jnp.dot(
            activated_ref[...], down_ref[0, :, c : c + block], preferred_element_type=jnp.float32
        )
        product = (product * share).astype(jnp.bfloat16)
        keep_ref[:, c : c + block] = product[:kept]
        send_ref[:, c : c + block] = product[kept:]


def run_expert(at, tokens, gate_weight, up_weight, down_weight):
    units = gate_weight.shape[2]
    width = gate_weight.shape[1]
    rows = sum(part.shape[0] for part in tokens)
    half = jax.ShapeDtypeStruct((rows // 2, width), jnp.bfloat16)
    return pl.pallas_call(
        partial(expert_kernel, len(tokens)),
        in_specs=[pl.BlockSpec(memory_space=pltpu.SMEM)] + in_vmem(len(tokens) + 3),
        out_specs=in_vmem(2),
        out_shape=[half, half],
        scratch_shapes=[pltpu.VMEM((rows, units), jnp.bfloat16)],
        compiler_params=pltpu.CompilerParams(vmem_limit_bytes=EXPERT_VMEM),
        cost_estimate=NOTHING,
    )(at, *tokens, gate_weight, up_weight, down_weight)


def after(array, *others):
    return lax.optimization_barrier((array, *others))[0]


def added(terms):
    total = terms[0].astype(jnp.float32)
    for term in terms[1:]:
        total = total + term.astype(jnp.float32)
    return total


def gathered_shards(
    query_rows,
    encoded_key_rows,
    value_matrix_rows,
    output_weight,
    residual,
    norm_gain,
    route_experts,
    route_gates,
    gate_weight,
    up_weight,
    down_weight,
):
    seq_count = lax.axis_size("seq")
    role_count = lax.axis_size("role")
    seq_index = lax.axis_index("seq")
    role_index = lax.axis_index("role")
    batch_count, local_length, query_width = query_rows.shape
    local_heads = query_width // HEAD_WIDTH
    group_width = QUERY_HEADS // KEY_VALUE_HEADS
    role_bits = [1 << n for n in range(role_count.bit_length() - 1)]
    at = jnp.stack([seq_index, role_index, seq_index * role_count + role_index]).astype(jnp.int32)

    def over_role(array, k):
        return lax.ppermute(array, "role", [(i, i ^ k) for i in range(role_count)])

    def over_seq(array, j):
        return lax.ppermute(array, "seq", [(i, i ^ j) for i in range(seq_count)])

    beside_proj = over_seq(output_weight, 1)
    block_width = output_weight.shape[1]
    across_steps = range(2, seq_count, 2)

    pieces = []
    for k in range(role_count):
        head = ((role_index ^ k) * local_heads // group_width) * HEAD_WIDTH
        piece = jnp.concatenate(
            [
                lax.dynamic_slice_in_dim(encoded_key_rows, head, HEAD_WIDTH, 2),
                lax.dynamic_slice_in_dim(value_matrix_rows, head, HEAD_WIDTH, 2),
            ],
            axis=2,
        )
        pieces.append(piece)
    pieces[1] = after(pieces[1], beside_proj)
    pieces = [piece if k == 0 else over_role(piece, k) for k, piece in enumerate(pieces)]
    block = pl.pallas_call(
        join_kernel,
        in_specs=in_vmem(len(pieces)),
        out_specs=pl.BlockSpec(memory_space=pltpu.VMEM),
        out_shape=jax.ShapeDtypeStruct(
            (batch_count, local_length, 2 * HEAD_WIDTH), jnp.bfloat16
        ),
        compiler_params=pltpu.CompilerParams(vmem_limit_bytes=COPY_VMEM),
        cost_estimate=SHORT,
    )(*pieces)
    same_core = [block] + [over_seq(block, j) for j in across_steps]
    blocks = []
    for part in same_core:
        blocks += [part, over_seq(part, 1)]
    last = role_count // 2
    routes = jnp.concatenate([route_experts[0].astype(jnp.float32), route_gates[0]], axis=1)
    residual_blocks = [
        lax.dynamic_slice_in_dim(residual[0], (seq_index ^ j) * block_width, block_width, 1)
        for j in range(seq_count)
    ]
    residuals = [
        jnp.concatenate(residual_blocks[j : j + 2], axis=1) for j in range(0, seq_count, 2)
    ]
    residuals = [residuals[0]] + [over_seq(residuals[j // 2], j) for j in across_steps]

    rows = batch_count * local_length
    near_width = 2 * output_weight.shape[1]
    groups = role_groups(role_count)
    attend_args = in_hbm(query_rows, *blocks[:-1], output_weight, beside_proj)
    slot_sets = [(range(1, role_count, 2), groups[:1]), (range(0, role_count, 2), groups[1:])]
    attended, near = [], []
    for slots, parts in slot_sets:
        half_rows = jax.ShapeDtypeStruct((rows // 2, query_width), jnp.bfloat16)
        half, *partials = pl.pallas_call(
            partial(attend_kernel, seq_count, role_count, slots, parts),
            in_specs=[pl.BlockSpec(memory_space=pltpu.SMEM)]
            + in_vmem(1)
            + hbm_specs(len(attend_args)),
            out_specs=in_vmem(1 + len(parts)),
            out_shape=[half_rows] + partial_shapes(parts, local_length, near_width),
            scratch_shapes=fetch_scratch(*attend_args),
            compiler_params=pltpu.CompilerParams(vmem_limit_bytes=SMALL_VMEM),
            cost_estimate=SHORT,
        )(at, blocks[-1], *attend_args)
        attended.append(half)
        near += partials

    other_routes = over_role(routes, last)

    def summed_over_role(parts, extra, *before):
        terms = [[part] for part in parts]
        for n, group in enumerate(groups[:-1]):
            bit = 1 << n
            leaving = terms[n][0] if len(terms[n]) == 1 else added(terms[n]).astype(jnp.bfloat16)
            came = over_role(leaving, bit)
            for m in range(n + 1, len(groups)):
                at_rows = [group.index(k ^ bit) for k in groups[m]]
                if at_rows == list(range(len(group))):
                    terms[m].append(came)
                else:
                    split = [came[i * local_length : (i + 1) * local_length] for i in at_rows]
                    terms[m].append(jnp.concatenate(split, axis=0))
        extra = jnp.pad(after(extra, *before) if before else extra, ((0, local_length), (0, 0)))
        sent = added(terms[-1] + [extra]).astype(jnp.bfloat16)
        return sent

    near_sent = summed_over_role(near, residuals[0])
    near_came = over_role(near_sent, last)
    near_args = in_hbm(near_sent)
    own_shape, both_shape = [
        jax.ShapeDtypeStruct((size, near_width + GATE_COLUMNS), jnp.bfloat16)
        for size in (local_length, 2 * local_length)
    ]
    near_halves = pl.pallas_call(
        near_sum_kernel,
        in_specs=in_vmem(3) + hbm_specs(1),
        out_specs=in_vmem(3),
        out_shape=[own_shape, own_shape, both_shape],
        scratch_shapes=fetch_scratch(*near_args),
        compiler_params=pltpu.CompilerParams(vmem_limit_bytes=SMALL_VMEM),
        cost_estimate=LONG,
    )(routes, other_routes, near_came, *near_args)

    def walk(k, bits):
        found = [k]
        for n, bit in enumerate(bits):
            found += walk(k | bit, bits[n + 1 :])
        return found

    lower_bits = role_bits[:-1][::-1]
    order = walk(last, lower_bits) + walk(0, lower_bits)
    far_plane, final = order[1], order[-1]

    def across(part):
        return [over_seq(part, j) for j in across_steps]

    def spread(own, other, both):
        planes, crossed = {0: own, last: other}, {}
        both_across = across(both)
        size = own.shape[0]
        for k in order:
            if k not in planes:
                bit = k & -k
                held = planes[k ^ bit]
                planes[k] = over_role(after(held, planes[far_plane]) if k < last else held, bit)
            if k in (0, last):
                crossed[k] = both_across
            elif k < last:
                source = k ^ (k & -k)
                came = [part[:size] for part in crossed[source]] if source == 0 else crossed[source]
                crossed[k] = [over_role(part, k & -k) for part in came]
            else:
                crossed[k] = across(after(planes[k], *both_across))
        return planes, crossed

    near_planes, near_crossed = spread(*near_halves)

    sent, came = [], []
    for n, j in enumerate(across_steps, 1):
        far = []
        for half, (slots, parts) in zip(attended, slot_sets):
            far += pl.pallas_call(
                partial(project_kernel, slots, parts),
                in_specs=in_vmem(1) + [pl.BlockSpec(memory_space=pl.ANY)] + hbm_specs(2),
                out_specs=in_vmem(len(parts)),
                out_shape=partial_shapes(parts, local_length, near_width),
                scratch_shapes=fetch_scratch(output_weight, beside_proj),
                compiler_params=pltpu.CompilerParams(vmem_limit_bytes=SMALL_VMEM),
                cost_estimate=SHORT,
            )(over_seq(half, j), other_routes, *in_hbm(output_weight, beside_proj))
        sent.append(summed_over_role(far, residuals[n], near_halves[0]))
        came.append(over_role(sent[-1], last))

    chips = 1 + len(across_steps)
    far_args = in_hbm(*sent)
    far_rows = (chips - 1) * local_length
    far_shape, far_both_shape = [
        jax.ShapeDtypeStruct((size, near_width), jnp.bfloat16) for size in (far_rows, 2 * far_rows)
    ]
    first_come = [*near_crossed[0], near_planes[far_plane], *near_crossed[far_plane]]
    first_come += [near_planes[final], *near_crossed[final]]
    far_halves = pl.pallas_call(
        partial(far_sum_kernel, local_length, len(first_come)),
        in_specs=[pl.BlockSpec(memory_space=pl.ANY)] * len(first_come)
        + in_vmem(len(came))
        + hbm_specs(len(far_args)),
        out_specs=in_vmem(3),
        out_shape=[far_shape, far_shape, far_both_shape],
        scratch_shapes=fetch_scratch(*far_args),
        compiler_params=pltpu.CompilerParams(vmem_limit_bytes=SMALL_VMEM),
        cost_estimate=SHORT,
    )(*first_come, *came, *far_args)
    far_planes, far_crossed = spread(*far_halves)

    width = residual.shape[2]
    gain = norm_gain.reshape(1, width)

    def normed_rows(parts, second, *hidden_shape):
        rows = chips * local_length
        firsts = (local_length, far_rows) if second else (0, 0)
        return pl.pallas_call(
            partial(norm_kernel, chips, *firsts),
            in_specs=[pl.BlockSpec(memory_space=pltpu.SMEM)] + in_vmem(1 + 2 * chips),
            out_specs=in_vmem(1 + len(hidden_shape)),
            out_shape=[
                jax.ShapeDtypeStruct((rows, width + GATE_COLUMNS), jnp.bfloat16),
                *hidden_shape,
            ],
            scratch_shapes=[pltpu.VMEM((rows, width), jnp.float32)],
            compiler_params=pltpu.CompilerParams(vmem_limit_bytes=SMALL_VMEM),
            cost_estimate=NOTHING,
        )(at, gain, *parts)

    keep, send, slots, leaving, passed = {}, {}, {}, {}, {}

    hidden_shape = jax.ShapeDtypeStruct((local_length, width), jnp.float32)
    hidden = []

    hidden_shape = jax.ShapeDtypeStruct((local_length, width), jnp.float32)
    hidden = []

    def prepared(k, *first):
        late = far_crossed[k]
        if first:
            late = [after(part, *first) for part in late]
        parts = [near_planes[k], far_planes[k]]
        for pair in zip(near_crossed[k], late):
            parts += pair
        normed, *own = normed_rows(parts, k == last, *([] if k else [hidden_shape]))
        hidden.extend(own)
        return [normed, over_seq(normed, 1)]

    def expert(tokens, *others):
        if others:
            tokens = lax.optimization_barrier((*tokens, *others))[: len(tokens)]
        return run_expert(at, tokens, gate_weight, up_weight, down_weight)

    def combine(k, *before):
        came = over_seq(after(send[k], *before) if before else send[k], 1)
        sums = []
        for n in range(len(across_steps)):
            chunk = slice((n + 1) * local_length, (n + 2) * local_length)
            sums.append(added([keep[k][chunk], came[chunk]]).astype(jnp.bfloat16))
        return [keep[k][:local_length], came[:local_length]], sums

    def pass_on(k):
        passed[k] = [over_seq(part, j) for part, j in zip(leaving[k], across_steps)]
        slots[k] += passed[k]

    ready = {far_plane: prepared(far_plane, far_planes[final], *far_crossed[final])}
    ready[final] = prepared(final)
    keep[far_plane], send[far_plane] = expert(ready[far_plane], ready[final][0])
    ready |= {k: prepared(k, keep[far_plane]) for k in (last, 0)}
    slots[far_plane], leaving[far_plane] = combine(far_plane)
    leaving[far_plane] = [after(part, ready[last][0], ready[0][0]) for part in leaving[far_plane]]
    pass_on(far_plane)
    keep[last], send[last] = expert(ready[last], keep[far_plane], *leaving[far_plane])
    slots[last], leaving[last] = combine(last)
    leaving[last] = [after(part, *passed[far_plane]) for part in leaving[last]]
    pass_on(last)
    keep[final], send[final] = expert(ready[final], keep[last])
    slots[far_plane] = [added(slots[far_plane]).astype(jnp.bfloat16)]
    slots[final], leaving[final] = combine(final, *passed[far_plane])
    leaving[final] = [after(part, *leaving[last]) for part in leaving[final]]
    pass_on(final)
    keep[0], send[0] = expert(ready[0], keep[final], *leaving[last])
    slots[0], leaving[0] = combine(0, *passed[last])
    leaving[0] = [after(part, *leaving[final]) for part in leaving[0]]
    pass_on(0)
    for bit in role_bits:
        for k in [k for k in sorted(slots, reverse=True) if k & bit]:
            going = added(slots.pop(k)).astype(jnp.bfloat16)
            if k == last:
                going = after(going, *leaving[final])
            slots[k ^ bit].append(over_role(going, bit))
    return added(hidden + slots[0]).astype(jnp.bfloat16).reshape(residual.shape)


def solution(mesh):
    placed = (
        P("groups", "seq", "role"),
        P("groups", ("seq", "role"), None),
        P("groups", ("seq", "role"), None),
        P("role", "seq"),
        P(("groups", "role"), "seq", None),
        P(),
        P(("groups", "role"), "seq", None),
        P(("groups", "role"), "seq", None),
        P(("seq", "role"), None, None),
        P(("seq", "role"), None, None),
        P(("seq", "role"), None, None),
    )
    experts = mesh.shape["seq"] * mesh.shape["role"]
    return jax.shard_map(
        gathered_shards if experts <= 2 * TOPK else routed_shards,
        mesh=mesh,
        in_specs=placed,
        out_specs=P(("groups", "role"), "seq", None),
        check_vma=False,
    )
```

```python
from functools import partial

import jax
import jax.numpy as jnp
from jax import lax
from jax.experimental import pallas as pl
from jax.experimental.pallas import tpu as pltpu
from jax.sharding import PartitionSpec as P

D = 2048
QUERY_HEADS = 32
KEY_VALUE_HEADS = 4
HEAD_WIDTH = 128
TOPK = 8


epsilon = 1e-06
masked_score = -1e30
EXPERT_VMEM = 16 * 2**20
SMALL_VMEM = 12 * 2**20
COPY_VMEM = 4 * 2**20
GATE_COLUMNS = 128
NOTHING = pl.CostEstimate(flops=1, bytes_accessed=1, transcendentals=0)
SHORT = pl.CostEstimate(flops=2 * 10**9, bytes_accessed=4 * 2**20, transcendentals=0)
LONG = pl.CostEstimate(flops=10**10, bytes_accessed=1, transcendentals=0)


def score_block(queries, every_key, query_position, block_start, block_width, score_scale):
    keys_part = lax.slice_in_dim(every_key, block_start, block_start + block_width, axis=0)
    raw_scores = (
        jnp.einsum("qhd,kd->hqk", queries, keys_part, preferred_element_type=jnp.float32)
        * score_scale
    )
    key_position = block_start + jnp.arange(block_width, dtype=jnp.int32)
    return jnp.where(
        key_position[None, None, :] <= query_position[None, :, None], raw_scores, masked_score
    )


def value_block(rounded, every_value, block_start, block_width):
    prob_block = lax.slice_in_dim(rounded, block_start, block_start + block_width, axis=2)
    values_part = lax.slice_in_dim(every_value, block_start, block_start + block_width, axis=0)
    return jnp.einsum("hqk,kd->qhd", prob_block, values_part, preferred_element_type=jnp.float32)


def routed_shards(
    query_rows,
    encoded_key_rows,
    value_matrix_rows,
    output_weight,
    residual,
    norm_gain,
    route_experts,
    route_gates,
    gate_weight,
    up_weight,
    down_weight,
):
    seq_count = lax.axis_size("seq")
    role_count = lax.axis_size("role")
    seq_index = lax.axis_index("seq")
    role_index = lax.axis_index("role")
    batch_count = query_rows.shape[0]
    local_length = query_rows.shape[1]
    local_heads = query_rows.shape[2] // HEAD_WIDTH
    full_length = local_length * seq_count
    query_group_width = QUERY_HEADS // KEY_VALUE_HEADS
    head_pick = role_index * local_heads // query_group_width
    role_keys, role_values = (
        lax.all_gather(encoded_key_rows, "role", axis=1, tiled=True),
        lax.all_gather(value_matrix_rows, "role", axis=1, tiled=True),
    )
    head_keys = lax.dynamic_slice_in_dim(role_keys, head_pick * HEAD_WIDTH, HEAD_WIDTH, 2)
    head_values = lax.dynamic_slice_in_dim(role_values, head_pick * HEAD_WIDTH, HEAD_WIDTH, 2)
    whole_keys, whole_values, whole_proj = (
        lax.all_gather(head_keys, "seq", axis=1, tiled=True),
        lax.all_gather(head_values, "seq", axis=1, tiled=True),
        lax.all_gather(output_weight, "seq", axis=1, tiled=True),
    )
    key_width = full_length // 8
    score_scale = HEAD_WIDTH ** (-0.5)
    query_position = seq_index * local_length + jnp.arange(local_length, dtype=jnp.int32)
    last_needed = (seq_index + 1) * local_length

    def one_sequence(operands):
        own_queries, every_key, every_value = operands
        queries = own_queries.reshape(local_length, local_heads, HEAD_WIDTH)
        pieces = []
        for number in range(8):
            block_start = number * key_width
            compute = partial(
                score_block, queries, every_key, query_position, block_start, key_width, score_scale
            )
            skipped = partial(
                jnp.full, (local_heads, local_length, key_width), masked_score, jnp.float32
            )
            pieces.append(lax.cond(block_start < last_needed, compute, skipped))
        scores = jnp.concatenate(pieces, axis=2)
        row_peak = jnp.max(scores, axis=2, keepdims=True)
        weights = jnp.exp(scores - row_peak)
        totals = jnp.sum(weights, axis=2, keepdims=True)
        rounded = weights.astype(jnp.bfloat16)
        mixed_rows = jnp.zeros((local_length, local_heads, HEAD_WIDTH), jnp.float32)
        for number in range(8):
            block_start = number * key_width
            product = partial(value_block, rounded, every_value, block_start, key_width)
            nothing = partial(jnp.zeros, (local_length, local_heads, HEAD_WIDTH), jnp.float32)
            mixed_rows = mixed_rows + lax.cond(block_start < last_needed, product, nothing)
        attended = (mixed_rows / totals.transpose(1, 0, 2)).astype(jnp.bfloat16)
        return attended.reshape(local_length, local_heads * HEAD_WIDTH)

    attended = lax.map(one_sequence, (query_rows, whole_keys, whole_values))
    flat_attended = attended.reshape(batch_count * local_length, local_heads * HEAD_WIDTH)
    projected = lax.psum_scatter(
        jnp.dot(flat_attended, whole_proj, preferred_element_type=jnp.float32).astype(jnp.bfloat16),
        "role",
        scatter_dimension=0,
        tiled=True,
    ).astype(jnp.float32)
    hidden = residual[0].astype(jnp.float32) + projected
    variance = jnp.mean(hidden * hidden, axis=-1, keepdims=True)
    normed = (hidden * lax.rsqrt(variance + epsilon) * norm_gain).astype(jnp.bfloat16)
    expert_ids = route_experts.reshape(-1)
    gate_values = route_gates.reshape(-1)
    experts_local = gate_weight.shape[0]
    device_count = seq_count * role_count
    expert_count = experts_local * device_count
    assign = expert_ids.shape[0]
    capacity = assign // expert_count + 1
    onehot = (expert_ids[:, None] == jnp.arange(expert_count, dtype=jnp.int32)[None, :]).astype(
        jnp.int32
    )
    earlier = jnp.cumsum(onehot, axis=0) - onehot
    slot_rank = jnp.sum(earlier * onehot, axis=1)
    slot_index = expert_ids * capacity + slot_rank
    source_token = jnp.arange(assign, dtype=jnp.int32) // TOPK
    slot_token = jnp.zeros((expert_count * capacity,), jnp.int32).at[slot_index].set(source_token)
    slot_used = jnp.zeros((expert_count * capacity,), jnp.bfloat16).at[slot_index].set(1.0)
    outgoing = (normed[slot_token] * slot_used[:, None]).reshape(
        device_count, experts_local, capacity, D
    )
    incoming = lax.all_to_all(outgoing, ("seq", "role"), split_axis=0, concat_axis=0, tiled=True)
    gate_hidden = jnp.einsum(
        "sjcd,jdf->sjcf", incoming, gate_weight, preferred_element_type=jnp.float32
    )
    up_hidden = jnp.einsum(
        "sjcd,jdf->sjcf", incoming, up_weight, preferred_element_type=jnp.float32
    )
    activated = (jax.nn.silu(gate_hidden) * up_hidden).astype(jnp.bfloat16)
    returned = lax.all_to_all(
        jnp.einsum(
            "sjcf,jfd->sjcd", activated, down_weight, preferred_element_type=jnp.float32
        ).astype(jnp.bfloat16),
        ("seq", "role"),
        split_axis=0,
        concat_axis=0,
        tiled=True,
    )
    gathered = returned.reshape(expert_count * capacity, D)[slot_index]
    weighted = gathered.astype(jnp.float32) * gate_values[:, None]
    expert_sum = jnp.sum(weighted.reshape(-1, TOPK, D), axis=1)
    return (hidden + expert_sum).astype(jnp.bfloat16).reshape(residual.shape)


def in_hbm(*arrays):
    return [pltpu.with_memory_space_constraint(array, pltpu.HBM) for array in arrays]


def hbm_specs(count):
    return [pl.BlockSpec(memory_space=pltpu.HBM)] * count


def fetch_scratch(*arrays):
    return [pltpu.VMEM(array.shape, array.dtype) for array in arrays] + [
        pltpu.SemaphoreType.DMA((len(arrays),))
    ]


def start_fetch(from_refs, scratch):
    *buffers, sems = scratch
    copies = [
        pltpu.make_async_copy(from_ref, buffer, sems.at[n])
        for n, (from_ref, buffer) in enumerate(zip(from_refs, buffers))
    ]
    for copy in copies:
        copy.start()
    return copies, buffers


def in_vmem(count):
    return [pl.BlockSpec(memory_space=pltpu.VMEM)] * count


def attend_kernel(seq_count, role_count, slots, groups, at_ref, *refs):
    last_block, *refs = refs
    count = seq_count + 2
    attended_ref, *partial_refs = refs[count : count + 1 + len(groups)]
    copies, (query_ref, *buffers) = start_fetch(refs[:count], refs[count + 1 + len(groups) :])
    blocks, proj_refs = buffers[: seq_count - 1] + [last_block], buffers[seq_count - 1 :]
    seq_index, role_index = at_ref[0], at_ref[1]
    local_length = query_ref.shape[1]
    local_heads = query_ref.shape[2] // HEAD_WIDTH
    per_role = local_length // role_count
    rows = local_heads * local_length
    keys_all = seq_count * local_length
    slot = lax.broadcasted_iota(jnp.int32, (rows, keys_all), 1)
    block_number, within = slot // local_length, slot % local_length
    key_position = (
        (seq_index ^ block_number) * local_length
        + (role_index ^ (within // per_role)) * per_role
        + within % per_role
    )
    query_position = (
        seq_index * local_length
        + lax.broadcasted_iota(jnp.int32, (rows, keys_all), 0) % local_length
    )
    seen = key_position <= query_position
    scale = HEAD_WIDTH ** (-0.5)
    for copy in copies[:seq_count]:
        copy.wait()
    for n, k in enumerate(slots):
        b = role_index ^ k
        own = query_ref[b]
        queries = jnp.concatenate(
            [own[:, h * HEAD_WIDTH : (h + 1) * HEAD_WIDTH] for h in range(local_heads)], axis=0
        )
        key_value = jnp.concatenate([block[b] for block in blocks], axis=0)
        keys, values = key_value[:, :HEAD_WIDTH], key_value[:, HEAD_WIDTH:]
        scores = lax.dot_general(
            queries, keys, (((1,), (1,)), ((), ())), preferred_element_type=jnp.float32
        )
        scores = jnp.where(seen, scores * scale, masked_score)
        weights = jnp.exp(scores - jnp.max(scores, axis=1, keepdims=True))
        totals = jnp.sum(weights, axis=1, keepdims=True)
        mixed = jnp.dot(weights.astype(jnp.bfloat16), values, preferred_element_type=jnp.float32)
        attended = (mixed / totals).astype(jnp.bfloat16)
        for h in range(local_heads):
            attended_ref[
                n * local_length : (n + 1) * local_length, h * HEAD_WIDTH : (h + 1) * HEAD_WIDTH
            ] = attended[h * local_length : (h + 1) * local_length]
    for copy in copies[seq_count:]:
        copy.wait()
    project_into(slots, groups, attended_ref, proj_refs, partial_refs)


def join_kernel(*refs):
    *piece_refs, out_ref = refs
    at = 0
    for ref in piece_refs:
        size = ref.shape[1]
        out_ref[:, at : at + size, :] = ref[...]
        at += size


def role_groups(role_count):
    last = role_count // 2
    bits = [1 << n for n in range(last.bit_length() - 1)]
    return [[k for k in range(role_count) if k & -k == bit] for bit in bits] + [[0, last]]


def project_into(slots, groups, attended_ref, proj_refs, partial_refs):
    slots = list(slots)
    rows = attended_ref.shape[0] // len(slots)
    at = 0
    for proj_ref in proj_refs:
        width = proj_ref.shape[1]
        product = jnp.dot(
            attended_ref[...], proj_ref[...], preferred_element_type=jnp.float32
        ).astype(jnp.bfloat16)
        for group, partial_ref in zip(groups, partial_refs):
            for n, k in enumerate(group):
                start = slots.index(k) * rows
                partial_ref[n * rows : (n + 1) * rows, at : at + width] = product[
                    start : start + rows
                ]
        at += width


def project_kernel(slots, groups, attended_ref, order_ref, *refs):
    count = (len(refs) - len(groups) - 1) // 2
    copies, proj_refs = start_fetch(refs[:count], refs[count + len(groups) :])
    for copy in copies:
        copy.wait()
    project_into(slots, groups, attended_ref, proj_refs, refs[count : count + len(groups)])


def partial_shapes(groups, rows, width):
    return [jax.ShapeDtypeStruct((rows * len(group), width), jnp.bfloat16) for group in groups]


def near_sum_kernel(route_ref, other_route_ref, came_ref, sent_any, *refs):
    out_refs, both_ref = refs[:2], refs[2]
    copies, (sent,) = start_fetch([sent_any], refs[3:])
    rows, width = sent.shape[0] // 2, sent.shape[1]
    lane = lax.broadcasted_iota(jnp.int32, (rows, GATE_COLUMNS), 1)
    half = GATE_COLUMNS // 2
    expert = (lane % half).astype(jnp.float32)
    for p, routes in enumerate((route_ref, other_route_ref)):
        shares = jnp.zeros((rows, GATE_COLUMNS), jnp.float32)
        routed = routes.shape[1] // 2
        for k in range(routed):
            named, weight = routes[:, k : k + 1], routes[:, routed + k : routed + k + 1]
            shares = shares + jnp.where(expert == named, weight, 0.0)
        first = shares.astype(jnp.bfloat16).astype(jnp.float32)
        terms = jnp.where(lane < half, first, shares - first).astype(jnp.bfloat16)
        out_refs[p][:, width:] = terms
        both_ref[p * rows : (p + 1) * rows, width:] = terms
    copies[0].wait()
    for p in range(2):
        total = sent[p * rows : (p + 1) * rows].astype(jnp.float32)
        total = total + came_ref[(1 - p) * rows : (2 - p) * rows].astype(jnp.float32)
        out_refs[p][:, :width] = total.astype(jnp.bfloat16)
        both_ref[p * rows : (p + 1) * rows, :width] = total.astype(jnp.bfloat16)


def far_sum_kernel(rows, order_count, *refs):
    refs = refs[order_count:]
    chips = (len(refs) - 4) // 3
    came_refs, sent_any = refs[:chips], refs[chips : 2 * chips]
    own_ref, other_ref, both_ref = refs[2 * chips : 2 * chips + 3]
    copies, sent_refs = start_fetch(sent_any, refs[2 * chips + 3 :])
    for copy in copies:
        copy.wait()
    size = chips * rows
    for n, (sent, came) in enumerate(zip(sent_refs, came_refs)):
        to = slice(n * rows, (n + 1) * rows)
        for p, out_ref in enumerate((own_ref, other_ref)):
            total = sent[p * rows : (p + 1) * rows].astype(jnp.float32)
            total = total + came[(1 - p) * rows : (2 - p) * rows].astype(jnp.float32)
            out_ref[to] = total.astype(jnp.bfloat16)
            both_ref[p * size + n * rows : p * size + (n + 1) * rows] = total.astype(jnp.bfloat16)


def norm_kernel(chips, near_row, far_row, at_ref, gain_ref, *refs):
    parts, (normed_ref, *hidden_refs, whole_ref) = refs[: 2 * chips], refs[2 * chips :]
    seq_index = at_ref[0]
    features = whole_ref.shape[1]
    rows = whole_ref.shape[0] // chips
    width = features // chips // 2
    for n in range(chips):
        near, far = parts[2 * n : 2 * n + 2]
        for m in range(chips):
            part = far if m else near
            first = ((far_row if m else near_row) if n else 0) + (m - 1 if m else 0) * rows
            to = slice((n ^ m) * rows, ((n ^ m) + 1) * rows)
            for j in range(2):
                start = pl.multiple_of((seq_index ^ (2 * n + j)) * width, width)
                whole_ref[to, pl.ds(start, width)] = part[
                    first : first + rows, j * width : (j + 1) * width
                ].astype(jnp.float32)
        first = near_row if n else 0
        normed_ref[n * rows : (n + 1) * rows, features:] = near[first : first + rows, 2 * width :]
    hidden = whole_ref[...]
    variance = jnp.mean(hidden * hidden, axis=1, keepdims=True)
    normed = hidden * lax.rsqrt(variance + epsilon) * gain_ref[...]
    normed_ref[:, :features] = normed.astype(jnp.bfloat16)
    for hidden_ref in hidden_refs:
        hidden_ref[...] = hidden[:rows]


def expert_kernel(token_count, at_ref, *refs):
    token_refs = refs[:token_count]
    gate_ref, up_ref, down_ref, keep_ref, send_ref, activated_ref = refs[token_count:]
    features, units = gate_ref.shape[1:]
    tokens = jnp.concatenate([ref[:, :features] for ref in token_refs], axis=0)
    gates = jnp.concatenate([ref[:, features:] for ref in token_refs], axis=0)
    lane = lax.broadcasted_iota(jnp.int32, gates.shape, 1)
    mine = lane % (GATE_COLUMNS // 2) == at_ref[2]
    share = jnp.sum(jnp.where(mine, gates.astype(jnp.float32), 0.0), axis=1, keepdims=True)
    block = 256 if units % 256 == 0 else units
    for f in range(0, units, block):
        gate_hidden = jnp.dot(
            tokens, gate_ref[0, :, f : f + block], preferred_element_type=jnp.float32
        )
        up_hidden = jnp.dot(tokens, up_ref[0, :, f : f + block], preferred_element_type=jnp.float32)
        activated_ref[:, f : f + block] = (
            gate_hidden / (1.0 + jnp.exp(-gate_hidden)) * up_hidden
        ).astype(jnp.bfloat16)
    kept = keep_ref.shape[0]
    block = 512 if features % 512 == 0 else features
    for c in range(0, features, block):
        product = jnp.dot(
            activated_ref[...], down_ref[0, :, c : c + block], preferred_element_type=jnp.float32
        )
        product = (product * share).astype(jnp.bfloat16)
        keep_ref[:, c : c + block] = product[:kept]
        send_ref[:, c : c + block] = product[kept:]


def run_expert(at, tokens, gate_weight, up_weight, down_weight):
    units = gate_weight.shape[2]
    width = gate_weight.shape[1]
    rows = sum(part.shape[0] for part in tokens)
    half = jax.ShapeDtypeStruct((rows // 2, width), jnp.bfloat16)
    return pl.pallas_call(
        partial(expert_kernel, len(tokens)),
        in_specs=[pl.BlockSpec(memory_space=pltpu.SMEM)] + in_vmem(len(tokens) + 3),
        out_specs=in_vmem(2),
        out_shape=[half, half],
        scratch_shapes=[pltpu.VMEM((rows, units), jnp.bfloat16)],
        compiler_params=pltpu.CompilerParams(vmem_limit_bytes=EXPERT_VMEM),
        cost_estimate=NOTHING,
    )(at, *tokens, gate_weight, up_weight, down_weight)


def after(array, *others):
    return lax.optimization_barrier((array, *others))[0]


def added(terms):
    total = terms[0].astype(jnp.float32)
    for term in terms[1:]:
        total = total + term.astype(jnp.float32)
    return total


def gathered_shards(
    query_rows,
    encoded_key_rows,
    value_matrix_rows,
    output_weight,
    residual,
    norm_gain,
    route_experts,
    route_gates,
    gate_weight,
    up_weight,
    down_weight,
):
    seq_count = lax.axis_size("seq")
    role_count = lax.axis_size("role")
    seq_index = lax.axis_index("seq")
    role_index = lax.axis_index("role")
    batch_count, local_length, query_width = query_rows.shape
    local_heads = query_width // HEAD_WIDTH
    group_width = QUERY_HEADS // KEY_VALUE_HEADS
    role_bits = [1 << n for n in range(role_count.bit_length() - 1)]
    at = jnp.stack([seq_index, role_index, seq_index * role_count + role_index]).astype(jnp.int32)

    def over_role(array, k):
        return lax.ppermute(array, "role", [(i, i ^ k) for i in range(role_count)])

    def over_seq(array, j):
        return lax.ppermute(array, "seq", [(i, i ^ j) for i in range(seq_count)])

    beside_proj = over_seq(output_weight, 1)
    block_width = output_weight.shape[1]
    across_steps = range(2, seq_count, 2)

    pieces = []
    for k in range(role_count):
        head = ((role_index ^ k) * local_heads // group_width) * HEAD_WIDTH
        piece = jnp.concatenate(
            [
                lax.dynamic_slice_in_dim(encoded_key_rows, head, HEAD_WIDTH, 2),
                lax.dynamic_slice_in_dim(value_matrix_rows, head, HEAD_WIDTH, 2),
            ],
            axis=2,
        )
        pieces.append(piece)
    pieces[1] = after(pieces[1], beside_proj)
    pieces = [piece if k == 0 else over_role(piece, k) for k, piece in enumerate(pieces)]
    block = pl.pallas_call(
        join_kernel,
        in_specs=in_vmem(len(pieces)),
        out_specs=pl.BlockSpec(memory_space=pltpu.VMEM),
        out_shape=jax.ShapeDtypeStruct(
            (batch_count, local_length, 2 * HEAD_WIDTH), jnp.bfloat16
        ),
        compiler_params=pltpu.CompilerParams(vmem_limit_bytes=COPY_VMEM),
        cost_estimate=SHORT,
    )(*pieces)
    same_core = [block] + [over_seq(block, j) for j in across_steps]
    blocks = []
    for part in same_core:
        blocks += [part, over_seq(part, 1)]
    last = role_count // 2
    routes = jnp.concatenate([route_experts[0].astype(jnp.float32), route_gates[0]], axis=1)
    residual_blocks = [
        lax.dynamic_slice_in_dim(residual[0], (seq_index ^ j) * block_width, block_width, 1)
        for j in range(seq_count)
    ]
    residuals = [
        jnp.concatenate(residual_blocks[j : j + 2], axis=1) for j in range(0, seq_count, 2)
    ]

    rows = batch_count * local_length
    near_width = 2 * output_weight.shape[1]
    groups = role_groups(role_count)
    attend_args = in_hbm(query_rows, *blocks[:-1], output_weight, beside_proj)
    slot_sets = [(range(1, role_count, 2), groups[:1]), (range(0, role_count, 2), groups[1:])]
    attended, near = [], []
    for slots, parts in slot_sets:
        half_rows = jax.ShapeDtypeStruct((rows // 2, query_width), jnp.bfloat16)
        half, *partials = pl.pallas_call(
            partial(attend_kernel, seq_count, role_count, slots, parts),
            in_specs=[pl.BlockSpec(memory_space=pltpu.SMEM)]
            + in_vmem(1)
            + hbm_specs(len(attend_args)),
            out_specs=in_vmem(1 + len(parts)),
            out_shape=[half_rows] + partial_shapes(parts, local_length, near_width),
            scratch_shapes=fetch_scratch(*attend_args),
            compiler_params=pltpu.CompilerParams(vmem_limit_bytes=SMALL_VMEM),
            cost_estimate=SHORT,
        )(at, blocks[-1], *attend_args)
        attended.append(half)
        near += partials

    for j in across_steps:
        residuals[j // 2] = over_seq(after(residuals[j // 2], attended[1]), j)
    other_routes = over_role(routes, last)

    def summed_over_role(parts, extra, *before):
        terms = [[part] for part in parts]
        for n, group in enumerate(groups[:-1]):
            bit = 1 << n
            leaving = terms[n][0] if len(terms[n]) == 1 else added(terms[n]).astype(jnp.bfloat16)
            came = over_role(leaving, bit)
            for m in range(n + 1, len(groups)):
                at_rows = [group.index(k ^ bit) for k in groups[m]]
                if at_rows == list(range(len(group))):
                    terms[m].append(came)
                else:
                    split = [came[i * local_length : (i + 1) * local_length] for i in at_rows]
                    terms[m].append(jnp.concatenate(split, axis=0))
        extra = jnp.pad(after(extra, *before) if before else extra, ((0, local_length), (0, 0)))
        sent = added(terms[-1] + [extra]).astype(jnp.bfloat16)
        return sent

    near_sent = summed_over_role(near, residuals[0])
    near_came = over_role(near_sent, last)
    near_args = in_hbm(near_sent)
    own_shape, both_shape = [
        jax.ShapeDtypeStruct((size, near_width + GATE_COLUMNS), jnp.bfloat16)
        for size in (local_length, 2 * local_length)
    ]
    near_halves = pl.pallas_call(
        near_sum_kernel,
        in_specs=in_vmem(3) + hbm_specs(1),
        out_specs=in_vmem(3),
        out_shape=[own_shape, own_shape, both_shape],
        scratch_shapes=fetch_scratch(*near_args),
        compiler_params=pltpu.CompilerParams(vmem_limit_bytes=SMALL_VMEM),
        cost_estimate=LONG,
    )(routes, other_routes, near_came, *near_args)

    def walk(k, bits):
        found = [k]
        for n, bit in enumerate(bits):
            found += walk(k | bit, bits[n + 1 :])
        return found

    lower_bits = role_bits[:-1][::-1]
    order = walk(last, lower_bits) + walk(0, lower_bits)
    far_plane, final = order[1], order[-1]

    def across(part):
        return [over_seq(part, j) for j in across_steps]

    def spread(own, other, both, ordered):
        planes, crossed = {0: own, last: other}, {}
        both_across = across(both)
        size = own.shape[0]
        for k in order:
            if k not in planes:
                bit = k & -k
                held = planes[k ^ bit]
                wait = ordered and k < last
                planes[k] = over_role(after(held, planes[far_plane]) if wait else held, bit)
            if k in (0, last):
                crossed[k] = both_across
            elif k < last:
                source = k ^ (k & -k)
                came = [part[:size] for part in crossed[source]] if source == 0 else crossed[source]
                crossed[k] = [over_role(part, k & -k) for part in came]
            else:
                crossed[k] = across(after(planes[k], *both_across))
        return planes, crossed

    near_planes, near_crossed = spread(*near_halves, False)

    sent, came = [], []
    for n, j in enumerate(across_steps, 1):
        far = []
        for half, (slots, parts) in zip(attended, slot_sets):
            far += pl.pallas_call(
                partial(project_kernel, slots, parts),
                in_specs=in_vmem(1) + [pl.BlockSpec(memory_space=pl.ANY)] + hbm_specs(2),
                out_specs=in_vmem(len(parts)),
                out_shape=partial_shapes(parts, local_length, near_width),
                scratch_shapes=fetch_scratch(output_weight, beside_proj),
                compiler_params=pltpu.CompilerParams(vmem_limit_bytes=SMALL_VMEM),
                cost_estimate=SHORT,
            )(over_seq(half, j), other_routes, *in_hbm(output_weight, beside_proj))
        sent.append(summed_over_role(far, residuals[n], near_halves[0]))
        came.append(over_role(sent[-1], last))

    chips = 1 + len(across_steps)
    far_args = in_hbm(*sent)
    far_rows = (chips - 1) * local_length
    far_shape, far_both_shape = [
        jax.ShapeDtypeStruct((size, near_width), jnp.bfloat16) for size in (far_rows, 2 * far_rows)
    ]
    first_come = [*near_crossed[0], near_planes[far_plane], *near_crossed[far_plane]]
    first_come += [near_planes[final], *near_crossed[final]]
    far_halves = pl.pallas_call(
        partial(far_sum_kernel, local_length, len(first_come)),
        in_specs=[pl.BlockSpec(memory_space=pl.ANY)] * len(first_come)
        + in_vmem(len(came))
        + hbm_specs(len(far_args)),
        out_specs=in_vmem(3),
        out_shape=[far_shape, far_shape, far_both_shape],
        scratch_shapes=fetch_scratch(*far_args),
        compiler_params=pltpu.CompilerParams(vmem_limit_bytes=SMALL_VMEM),
        cost_estimate=SHORT,
    )(*first_come, *came, *far_args)
    far_planes, far_crossed = spread(*far_halves, True)

    width = residual.shape[2]
    gain = norm_gain.reshape(1, width)

    def normed_rows(parts, second, *hidden_shape):
        rows = chips * local_length
        firsts = (local_length, far_rows) if second else (0, 0)
        return pl.pallas_call(
            partial(norm_kernel, chips, *firsts),
            in_specs=[pl.BlockSpec(memory_space=pltpu.SMEM)] + in_vmem(1 + 2 * chips),
            out_specs=in_vmem(1 + len(hidden_shape)),
            out_shape=[
                jax.ShapeDtypeStruct((rows, width + GATE_COLUMNS), jnp.bfloat16),
                *hidden_shape,
            ],
            scratch_shapes=[pltpu.VMEM((rows, width), jnp.float32)],
            compiler_params=pltpu.CompilerParams(vmem_limit_bytes=SMALL_VMEM),
            cost_estimate=NOTHING,
        )(at, gain, *parts)

    keep, send, slots, leaving, passed = {}, {}, {}, {}, {}

    hidden_shape = jax.ShapeDtypeStruct((local_length, width), jnp.float32)
    hidden = []

    hidden_shape = jax.ShapeDtypeStruct((local_length, width), jnp.float32)
    hidden = []

    def prepared(k, *first):
        late = far_crossed[k]
        if first:
            late = [after(part, *first) for part in late]
        parts = [near_planes[k], far_planes[k]]
        for pair in zip(near_crossed[k], late):
            parts += pair
        normed, *own = normed_rows(parts, k == last, *([] if k else [hidden_shape]))
        hidden.extend(own)
        return [normed, over_seq(normed, 1)]

    def expert(tokens, *others):
        if others:
            tokens = lax.optimization_barrier((*tokens, *others))[: len(tokens)]
        return run_expert(at, tokens, gate_weight, up_weight, down_weight)

    def combine(k, *before):
        came = over_seq(after(send[k], *before) if before else send[k], 1)
        sums = []
        for n in range(len(across_steps)):
            chunk = slice((n + 1) * local_length, (n + 2) * local_length)
            sums.append(added([keep[k][chunk], came[chunk]]).astype(jnp.bfloat16))
        return [keep[k][:local_length], came[:local_length]], sums

    def pass_on(k):
        passed[k] = [over_seq(part, j) for part, j in zip(leaving[k], across_steps)]
        slots[k] += passed[k]

    ready = {far_plane: prepared(far_plane, far_planes[final], *far_crossed[final])}
    ready[final] = prepared(final)
    keep[far_plane], send[far_plane] = expert(ready[far_plane], ready[final][0])
    ready |= {k: prepared(k, keep[far_plane]) for k in (last, 0)}
    slots[far_plane], leaving[far_plane] = combine(far_plane)
    leaving[far_plane] = [after(part, ready[last][0], ready[0][0]) for part in leaving[far_plane]]
    pass_on(far_plane)
    keep[last], send[last] = expert(ready[last], keep[far_plane], *leaving[far_plane])
    slots[last], leaving[last] = combine(last)
    leaving[last] = [after(part, *passed[far_plane]) for part in leaving[last]]
    pass_on(last)
    keep[final], send[final] = expert(ready[final], keep[last])
    slots[far_plane] = [added(slots[far_plane]).astype(jnp.bfloat16)]
    slots[final], leaving[final] = combine(final, *passed[far_plane])
    leaving[final] = [after(part, *leaving[last]) for part in leaving[final]]
    pass_on(final)
    keep[0], send[0] = expert(ready[0], keep[final], *leaving[last])
    slots[0], leaving[0] = combine(0, *passed[last])
    leaving[0] = [after(part, *leaving[final]) for part in leaving[0]]
    pass_on(0)
    for bit in role_bits:
        for k in [k for k in sorted(slots, reverse=True) if k & bit]:
            going = added(slots.pop(k)).astype(jnp.bfloat16)
            if k == last:
                going = after(going, *leaving[final])
            slots[k ^ bit].append(over_role(going, bit))
    return added(hidden + slots[0]).astype(jnp.bfloat16).reshape(residual.shape)


def solution(mesh):
    placed = (
        P("groups", "seq", "role"),
        P("groups", ("seq", "role"), None),
        P("groups", ("seq", "role"), None),
        P("role", "seq"),
        P(("groups", "role"), "seq", None),
        P(),
        P(("groups", "role"), "seq", None),
        P(("groups", "role"), "seq", None),
        P(("seq", "role"), None, None),
        P(("seq", "role"), None, None),
        P(("seq", "role"), None, None),
    )
    experts = mesh.shape["seq"] * mesh.shape["role"]
    return jax.shard_map(
        gathered_shards if experts <= 2 * TOPK else routed_shards,
        mesh=mesh,
        in_specs=placed,
        out_specs=P(("groups", "role"), "seq", None),
        check_vma=False,
    )
```

```python
from functools import partial

import jax
import jax.numpy as jnp
from jax import lax
from jax.experimental import pallas as pl
from jax.experimental.pallas import tpu as pltpu
from jax.sharding import PartitionSpec as P

D = 2048
QUERY_HEADS = 32
KEY_VALUE_HEADS = 4
HEAD_WIDTH = 128
TOPK = 8


epsilon = 1e-06
masked_score = -1e30
EXPERT_VMEM = 16 * 2**20
SMALL_VMEM = 12 * 2**20
COPY_VMEM = 4 * 2**20
GATE_COLUMNS = 128
NOTHING = pl.CostEstimate(flops=1, bytes_accessed=1, transcendentals=0)
SHORT = pl.CostEstimate(flops=2 * 10**9, bytes_accessed=4 * 2**20, transcendentals=0)
LONG = pl.CostEstimate(flops=10**10, bytes_accessed=1, transcendentals=0)


def score_block(queries, every_key, query_position, block_start, block_width, score_scale):
    keys_part = lax.slice_in_dim(every_key, block_start, block_start + block_width, axis=0)
    raw_scores = (
        jnp.einsum("qhd,kd->hqk", queries, keys_part, preferred_element_type=jnp.float32)
        * score_scale
    )
    key_position = block_start + jnp.arange(block_width, dtype=jnp.int32)
    return jnp.where(
        key_position[None, None, :] <= query_position[None, :, None], raw_scores, masked_score
    )


def value_block(rounded, every_value, block_start, block_width):
    prob_block = lax.slice_in_dim(rounded, block_start, block_start + block_width, axis=2)
    values_part = lax.slice_in_dim(every_value, block_start, block_start + block_width, axis=0)
    return jnp.einsum("hqk,kd->qhd", prob_block, values_part, preferred_element_type=jnp.float32)


def routed_shards(
    query_rows,
    encoded_key_rows,
    value_matrix_rows,
    output_weight,
    residual,
    norm_gain,
    route_experts,
    route_gates,
    gate_weight,
    up_weight,
    down_weight,
):
    seq_count = lax.axis_size("seq")
    role_count = lax.axis_size("role")
    seq_index = lax.axis_index("seq")
    role_index = lax.axis_index("role")
    batch_count = query_rows.shape[0]
    local_length = query_rows.shape[1]
    local_heads = query_rows.shape[2] // HEAD_WIDTH
    full_length = local_length * seq_count
    query_group_width = QUERY_HEADS // KEY_VALUE_HEADS
    head_pick = role_index * local_heads // query_group_width
    role_keys, role_values = (
        lax.all_gather(encoded_key_rows, "role", axis=1, tiled=True),
        lax.all_gather(value_matrix_rows, "role", axis=1, tiled=True),
    )
    head_keys = lax.dynamic_slice_in_dim(role_keys, head_pick * HEAD_WIDTH, HEAD_WIDTH, 2)
    head_values = lax.dynamic_slice_in_dim(role_values, head_pick * HEAD_WIDTH, HEAD_WIDTH, 2)
    whole_keys, whole_values, whole_proj = (
        lax.all_gather(head_keys, "seq", axis=1, tiled=True),
        lax.all_gather(head_values, "seq", axis=1, tiled=True),
        lax.all_gather(output_weight, "seq", axis=1, tiled=True),
    )
    key_width = full_length // 8
    score_scale = HEAD_WIDTH ** (-0.5)
    query_position = seq_index * local_length + jnp.arange(local_length, dtype=jnp.int32)
    last_needed = (seq_index + 1) * local_length

    def one_sequence(operands):
        own_queries, every_key, every_value = operands
        queries = own_queries.reshape(local_length, local_heads, HEAD_WIDTH)
        pieces = []
        for number in range(8):
            block_start = number * key_width
            compute = partial(
                score_block, queries, every_key, query_position, block_start, key_width, score_scale
            )
            skipped = partial(
                jnp.full, (local_heads, local_length, key_width), masked_score, jnp.float32
            )
            pieces.append(lax.cond(block_start < last_needed, compute, skipped))
        scores = jnp.concatenate(pieces, axis=2)
        row_peak = jnp.max(scores, axis=2, keepdims=True)
        weights = jnp.exp(scores - row_peak)
        totals = jnp.sum(weights, axis=2, keepdims=True)
        rounded = weights.astype(jnp.bfloat16)
        mixed_rows = jnp.zeros((local_length, local_heads, HEAD_WIDTH), jnp.float32)
        for number in range(8):
            block_start = number * key_width
            product = partial(value_block, rounded, every_value, block_start, key_width)
            nothing = partial(jnp.zeros, (local_length, local_heads, HEAD_WIDTH), jnp.float32)
            mixed_rows = mixed_rows + lax.cond(block_start < last_needed, product, nothing)
        attended = (mixed_rows / totals.transpose(1, 0, 2)).astype(jnp.bfloat16)
        return attended.reshape(local_length, local_heads * HEAD_WIDTH)

    attended = lax.map(one_sequence, (query_rows, whole_keys, whole_values))
    flat_attended = attended.reshape(batch_count * local_length, local_heads * HEAD_WIDTH)
    projected = lax.psum_scatter(
        jnp.dot(flat_attended, whole_proj, preferred_element_type=jnp.float32).astype(jnp.bfloat16),
        "role",
        scatter_dimension=0,
        tiled=True,
    ).astype(jnp.float32)
    hidden = residual[0].astype(jnp.float32) + projected
    variance = jnp.mean(hidden * hidden, axis=-1, keepdims=True)
    normed = (hidden * lax.rsqrt(variance + epsilon) * norm_gain).astype(jnp.bfloat16)
    expert_ids = route_experts.reshape(-1)
    gate_values = route_gates.reshape(-1)
    experts_local = gate_weight.shape[0]
    device_count = seq_count * role_count
    expert_count = experts_local * device_count
    assign = expert_ids.shape[0]
    capacity = assign // expert_count + 1
    onehot = (expert_ids[:, None] == jnp.arange(expert_count, dtype=jnp.int32)[None, :]).astype(
        jnp.int32
    )
    earlier = jnp.cumsum(onehot, axis=0) - onehot
    slot_rank = jnp.sum(earlier * onehot, axis=1)
    slot_index = expert_ids * capacity + slot_rank
    source_token = jnp.arange(assign, dtype=jnp.int32) // TOPK
    slot_token = jnp.zeros((expert_count * capacity,), jnp.int32).at[slot_index].set(source_token)
    slot_used = jnp.zeros((expert_count * capacity,), jnp.bfloat16).at[slot_index].set(1.0)
    outgoing = (normed[slot_token] * slot_used[:, None]).reshape(
        device_count, experts_local, capacity, D
    )
    incoming = lax.all_to_all(outgoing, ("seq", "role"), split_axis=0, concat_axis=0, tiled=True)
    gate_hidden = jnp.einsum(
        "sjcd,jdf->sjcf", incoming, gate_weight, preferred_element_type=jnp.float32
    )
    up_hidden = jnp.einsum(
        "sjcd,jdf->sjcf", incoming, up_weight, preferred_element_type=jnp.float32
    )
    activated = (jax.nn.silu(gate_hidden) * up_hidden).astype(jnp.bfloat16)
    returned = lax.all_to_all(
        jnp.einsum(
            "sjcf,jfd->sjcd", activated, down_weight, preferred_element_type=jnp.float32
        ).astype(jnp.bfloat16),
        ("seq", "role"),
        split_axis=0,
        concat_axis=0,
        tiled=True,
    )
    gathered = returned.reshape(expert_count * capacity, D)[slot_index]
    weighted = gathered.astype(jnp.float32) * gate_values[:, None]
    expert_sum = jnp.sum(weighted.reshape(-1, TOPK, D), axis=1)
    return (hidden + expert_sum).astype(jnp.bfloat16).reshape(residual.shape)


def in_hbm(*arrays):
    return [pltpu.with_memory_space_constraint(array, pltpu.HBM) for array in arrays]


def hbm_specs(count):
    return [pl.BlockSpec(memory_space=pltpu.HBM)] * count


def fetch_scratch(*arrays):
    return [pltpu.VMEM(array.shape, array.dtype) for array in arrays] + [
        pltpu.SemaphoreType.DMA((len(arrays),))
    ]


def start_fetch(from_refs, scratch):
    *buffers, sems = scratch
    copies = [
        pltpu.make_async_copy(from_ref, buffer, sems.at[n])
        for n, (from_ref, buffer) in enumerate(zip(from_refs, buffers))
    ]
    for copy in copies:
        copy.start()
    return copies, buffers


def in_vmem(count):
    return [pl.BlockSpec(memory_space=pltpu.VMEM)] * count


def attend_kernel(seq_count, role_count, slots, groups, at_ref, *refs):
    last_block, *refs = refs
    count = seq_count + 2
    attended_ref, *partial_refs = refs[count : count + 1 + len(groups)]
    copies, (query_ref, *buffers) = start_fetch(refs[:count], refs[count + 1 + len(groups) :])
    blocks, proj_refs = buffers[: seq_count - 1] + [last_block], buffers[seq_count - 1 :]
    seq_index, role_index = at_ref[0], at_ref[1]
    local_length = query_ref.shape[1]
    local_heads = query_ref.shape[2] // HEAD_WIDTH
    per_role = local_length // role_count
    rows = local_heads * local_length
    keys_all = seq_count * local_length
    slot = lax.broadcasted_iota(jnp.int32, (rows, keys_all), 1)
    block_number, within = slot // local_length, slot % local_length
    key_position = (
        (seq_index ^ block_number) * local_length
        + (role_index ^ (within // per_role)) * per_role
        + within % per_role
    )
    query_position = (
        seq_index * local_length
        + lax.broadcasted_iota(jnp.int32, (rows, keys_all), 0) % local_length
    )
    seen = key_position <= query_position
    scale = HEAD_WIDTH ** (-0.5)
    for copy in copies[:seq_count]:
        copy.wait()
    for n, k in enumerate(slots):
        b = role_index ^ k
        own = query_ref[b]
        queries = jnp.concatenate(
            [own[:, h * HEAD_WIDTH : (h + 1) * HEAD_WIDTH] for h in range(local_heads)], axis=0
        )
        key_value = jnp.concatenate([block[b] for block in blocks], axis=0)
        keys, values = key_value[:, :HEAD_WIDTH], key_value[:, HEAD_WIDTH:]
        scores = lax.dot_general(
            queries, keys, (((1,), (1,)), ((), ())), preferred_element_type=jnp.float32
        )
        scores = jnp.where(seen, scores * scale, masked_score)
        weights = jnp.exp(scores - jnp.max(scores, axis=1, keepdims=True))
        totals = jnp.sum(weights, axis=1, keepdims=True)
        mixed = jnp.dot(weights.astype(jnp.bfloat16), values, preferred_element_type=jnp.float32)
        attended = (mixed / totals).astype(jnp.bfloat16)
        for h in range(local_heads):
            attended_ref[
                n * local_length : (n + 1) * local_length, h * HEAD_WIDTH : (h + 1) * HEAD_WIDTH
            ] = attended[h * local_length : (h + 1) * local_length]
    for copy in copies[seq_count:]:
        copy.wait()
    project_into(slots, groups, attended_ref, proj_refs, partial_refs)


def join_kernel(*refs):
    *piece_refs, out_ref = refs
    at = 0
    for ref in piece_refs:
        size = ref.shape[1]
        out_ref[:, at : at + size, :] = ref[...]
        at += size


def role_groups(role_count):
    last = role_count // 2
    bits = [1 << n for n in range(last.bit_length() - 1)]
    return [[k for k in range(role_count) if k & -k == bit] for bit in bits] + [[0, last]]


def project_into(slots, groups, attended_ref, proj_refs, partial_refs):
    slots = list(slots)
    rows = attended_ref.shape[0] // len(slots)
    at = 0
    for proj_ref in proj_refs:
        width = proj_ref.shape[1]
        product = jnp.dot(
            attended_ref[...], proj_ref[...], preferred_element_type=jnp.float32
        ).astype(jnp.bfloat16)
        for group, partial_ref in zip(groups, partial_refs):
            for n, k in enumerate(group):
                start = slots.index(k) * rows
                partial_ref[n * rows : (n + 1) * rows, at : at + width] = product[
                    start : start + rows
                ]
        at += width


def project_kernel(slots, groups, attended_ref, order_ref, *refs):
    count = (len(refs) - len(groups) - 1) // 2
    copies, proj_refs = start_fetch(refs[:count], refs[count + len(groups) :])
    for copy in copies:
        copy.wait()
    project_into(slots, groups, attended_ref, proj_refs, refs[count : count + len(groups)])


def partial_shapes(groups, rows, width):
    return [jax.ShapeDtypeStruct((rows * len(group), width), jnp.bfloat16) for group in groups]


def near_sum_kernel(route_ref, other_route_ref, came_ref, sent_any, *refs):
    out_refs, both_ref = refs[:2], refs[2]
    copies, (sent,) = start_fetch([sent_any], refs[3:])
    rows, width = sent.shape[0] // 2, sent.shape[1]
    lane = lax.broadcasted_iota(jnp.int32, (rows, GATE_COLUMNS), 1)
    half = GATE_COLUMNS // 2
    expert = (lane % half).astype(jnp.float32)
    for p, routes in enumerate((route_ref, other_route_ref)):
        shares = jnp.zeros((rows, GATE_COLUMNS), jnp.float32)
        routed = routes.shape[1] // 2
        for k in range(routed):
            named, weight = routes[:, k : k + 1], routes[:, routed + k : routed + k + 1]
            shares = shares + jnp.where(expert == named, weight, 0.0)
        first = shares.astype(jnp.bfloat16).astype(jnp.float32)
        terms = jnp.where(lane < half, first, shares - first).astype(jnp.bfloat16)
        out_refs[p][:, width:] = terms
        both_ref[p * rows : (p + 1) * rows, width:] = terms
    copies[0].wait()
    for p in range(2):
        total = sent[p * rows : (p + 1) * rows].astype(jnp.float32)
        total = total + came_ref[(1 - p) * rows : (2 - p) * rows].astype(jnp.float32)
        out_refs[p][:, :width] = total.astype(jnp.bfloat16)
        both_ref[p * rows : (p + 1) * rows, :width] = total.astype(jnp.bfloat16)


def far_sum_kernel(rows, order_count, *refs):
    refs = refs[order_count:]
    chips = (len(refs) - 4) // 3
    came_refs, sent_any = refs[:chips], refs[chips : 2 * chips]
    own_ref, other_ref, both_ref = refs[2 * chips : 2 * chips + 3]
    copies, sent_refs = start_fetch(sent_any, refs[2 * chips + 3 :])
    for copy in copies:
        copy.wait()
    size = chips * rows
    for n, (sent, came) in enumerate(zip(sent_refs, came_refs)):
        to = slice(n * rows, (n + 1) * rows)
        for p, out_ref in enumerate((own_ref, other_ref)):
            total = sent[p * rows : (p + 1) * rows].astype(jnp.float32)
            total = total + came[(1 - p) * rows : (2 - p) * rows].astype(jnp.float32)
            out_ref[to] = total.astype(jnp.bfloat16)
            both_ref[p * size + n * rows : p * size + (n + 1) * rows] = total.astype(jnp.bfloat16)


def norm_kernel(chips, near_row, far_row, at_ref, gain_ref, *refs):
    parts, (normed_ref, *hidden_refs, whole_ref) = refs[: 2 * chips], refs[2 * chips :]
    seq_index = at_ref[0]
    features = whole_ref.shape[1]
    rows = whole_ref.shape[0] // chips
    width = features // chips // 2
    for n in range(chips):
        near, far = parts[2 * n : 2 * n + 2]
        for m in range(chips):
            part = far if m else near
            first = ((far_row if m else near_row) if n else 0) + (m - 1 if m else 0) * rows
            to = slice((n ^ m) * rows, ((n ^ m) + 1) * rows)
            for j in range(2):
                start = pl.multiple_of((seq_index ^ (2 * n + j)) * width, width)
                whole_ref[to, pl.ds(start, width)] = part[
                    first : first + rows, j * width : (j + 1) * width
                ].astype(jnp.float32)
        first = near_row if n else 0
        normed_ref[n * rows : (n + 1) * rows, features:] = near[first : first + rows, 2 * width :]
    hidden = whole_ref[...]
    variance = jnp.mean(hidden * hidden, axis=1, keepdims=True)
    normed = hidden * lax.rsqrt(variance + epsilon) * gain_ref[...]
    normed_ref[:, :features] = normed.astype(jnp.bfloat16)
    for hidden_ref in hidden_refs:
        hidden_ref[...] = hidden[:rows]


def expert_kernel(token_count, at_ref, *refs):
    token_refs = refs[:token_count]
    gate_ref, up_ref, down_ref, keep_ref, send_ref, activated_ref = refs[token_count:]
    features, units = gate_ref.shape[1:]
    tokens = jnp.concatenate([ref[:, :features] for ref in token_refs], axis=0)
    gates = jnp.concatenate([ref[:, features:] for ref in token_refs], axis=0)
    lane = lax.broadcasted_iota(jnp.int32, gates.shape, 1)
    mine = lane % (GATE_COLUMNS // 2) == at_ref[2]
    share = jnp.sum(jnp.where(mine, gates.astype(jnp.float32), 0.0), axis=1, keepdims=True)
    block = 256 if units % 256 == 0 else units
    for f in range(0, units, block):
        gate_hidden = jnp.dot(
            tokens, gate_ref[0, :, f : f + block], preferred_element_type=jnp.float32
        )
        up_hidden = jnp.dot(tokens, up_ref[0, :, f : f + block], preferred_element_type=jnp.float32)
        activated_ref[:, f : f + block] = (
            gate_hidden / (1.0 + jnp.exp(-gate_hidden)) * up_hidden
        ).astype(jnp.bfloat16)
    kept = keep_ref.shape[0]
    block = 512 if features % 512 == 0 else features
    for c in range(0, features, block):
        product = jnp.dot(
            activated_ref[...], down_ref[0, :, c : c + block], preferred_element_type=jnp.float32
        )
        product = (product * share).astype(jnp.bfloat16)
        keep_ref[:, c : c + block] = product[:kept]
        send_ref[:, c : c + block] = product[kept:]


def run_expert(at, tokens, gate_weight, up_weight, down_weight):
    units = gate_weight.shape[2]
    width = gate_weight.shape[1]
    rows = sum(part.shape[0] for part in tokens)
    half = jax.ShapeDtypeStruct((rows // 2, width), jnp.bfloat16)
    return pl.pallas_call(
        partial(expert_kernel, len(tokens)),
        in_specs=[pl.BlockSpec(memory_space=pltpu.SMEM)] + in_vmem(len(tokens) + 3),
        out_specs=in_vmem(2),
        out_shape=[half, half],
        scratch_shapes=[pltpu.VMEM((rows, units), jnp.bfloat16)],
        compiler_params=pltpu.CompilerParams(vmem_limit_bytes=EXPERT_VMEM),
        cost_estimate=NOTHING,
    )(at, *tokens, gate_weight, up_weight, down_weight)


def after(array, *others):
    return lax.optimization_barrier((array, *others))[0]


def added(terms):
    total = terms[0].astype(jnp.float32)
    for term in terms[1:]:
        total = total + term.astype(jnp.float32)
    return total


def gathered_shards(
    query_rows,
    encoded_key_rows,
    value_matrix_rows,
    output_weight,
    residual,
    norm_gain,
    route_experts,
    route_gates,
    gate_weight,
    up_weight,
    down_weight,
):
    seq_count = lax.axis_size("seq")
    role_count = lax.axis_size("role")
    seq_index = lax.axis_index("seq")
    role_index = lax.axis_index("role")
    batch_count, local_length, query_width = query_rows.shape
    local_heads = query_width // HEAD_WIDTH
    group_width = QUERY_HEADS // KEY_VALUE_HEADS
    role_bits = [1 << n for n in range(role_count.bit_length() - 1)]
    at = jnp.stack([seq_index, role_index, seq_index * role_count + role_index]).astype(jnp.int32)

    def over_role(array, k):
        return lax.ppermute(array, "role", [(i, i ^ k) for i in range(role_count)])

    def over_seq(array, j):
        return lax.ppermute(array, "seq", [(i, i ^ j) for i in range(seq_count)])

    beside_proj = over_seq(output_weight, 1)
    block_width = output_weight.shape[1]
    across_steps = range(2, seq_count, 2)

    pieces = []
    for k in range(role_count):
        head = ((role_index ^ k) * local_heads // group_width) * HEAD_WIDTH
        piece = jnp.concatenate(
            [
                lax.dynamic_slice_in_dim(encoded_key_rows, head, HEAD_WIDTH, 2),
                lax.dynamic_slice_in_dim(value_matrix_rows, head, HEAD_WIDTH, 2),
            ],
            axis=2,
        )
        pieces.append(piece)
    pieces[1] = after(pieces[1], beside_proj)
    pieces = [piece if k == 0 else over_role(piece, k) for k, piece in enumerate(pieces)]
    block = pl.pallas_call(
        join_kernel,
        in_specs=in_vmem(len(pieces)),
        out_specs=pl.BlockSpec(memory_space=pltpu.VMEM),
        out_shape=jax.ShapeDtypeStruct(
            (batch_count, local_length, 2 * HEAD_WIDTH), jnp.bfloat16
        ),
        compiler_params=pltpu.CompilerParams(vmem_limit_bytes=COPY_VMEM),
        cost_estimate=SHORT,
    )(*pieces)
    same_core = [block] + [over_seq(block, j) for j in across_steps]
    blocks = []
    for part in same_core:
        blocks += [part, over_seq(part, 1)]
    last = role_count // 2
    routes = jnp.concatenate([route_experts[0].astype(jnp.float32), route_gates[0]], axis=1)
    residual_blocks = [
        lax.dynamic_slice_in_dim(residual[0], (seq_index ^ j) * block_width, block_width, 1)
        for j in range(seq_count)
    ]
    residuals = [
        jnp.concatenate(residual_blocks[j : j + 2], axis=1) for j in range(0, seq_count, 2)
    ]

    rows = batch_count * local_length
    near_width = 2 * output_weight.shape[1]
    groups = role_groups(role_count)
    attend_args = in_hbm(query_rows, *blocks[:-1], output_weight, beside_proj)
    slot_sets = [(range(1, role_count, 2), groups[:1]), (range(0, role_count, 2), groups[1:])]
    attended, near = [], []
    for slots, parts in slot_sets:
        half_rows = jax.ShapeDtypeStruct((rows // 2, query_width), jnp.bfloat16)
        half, *partials = pl.pallas_call(
            partial(attend_kernel, seq_count, role_count, slots, parts),
            in_specs=[pl.BlockSpec(memory_space=pltpu.SMEM)]
            + in_vmem(1)
            + hbm_specs(len(attend_args)),
            out_specs=in_vmem(1 + len(parts)),
            out_shape=[half_rows] + partial_shapes(parts, local_length, near_width),
            scratch_shapes=fetch_scratch(*attend_args),
            compiler_params=pltpu.CompilerParams(vmem_limit_bytes=SMALL_VMEM),
            cost_estimate=SHORT,
        )(at, blocks[-1], *attend_args)
        attended.append(half)
        near += partials

    for j in across_steps:
        residuals[j // 2] = over_seq(after(residuals[j // 2], attended[1]), j)
    other_routes = over_role(routes, last)

    def summed_over_role(parts, extra, *before):
        terms = [[part] for part in parts]
        for n, group in enumerate(groups[:-1]):
            bit = 1 << n
            leaving = terms[n][0] if len(terms[n]) == 1 else added(terms[n]).astype(jnp.bfloat16)
            came = over_role(leaving, bit)
            for m in range(n + 1, len(groups)):
                at_rows = [group.index(k ^ bit) for k in groups[m]]
                if at_rows == list(range(len(group))):
                    terms[m].append(came)
                else:
                    split = [came[i * local_length : (i + 1) * local_length] for i in at_rows]
                    terms[m].append(jnp.concatenate(split, axis=0))
        extra = jnp.pad(after(extra, *before) if before else extra, ((0, local_length), (0, 0)))
        sent = added(terms[-1] + [extra]).astype(jnp.bfloat16)
        return sent

    near_sent = summed_over_role(near, residuals[0])
    near_came = over_role(near_sent, last)
    near_args = in_hbm(near_sent)
    own_shape, both_shape = [
        jax.ShapeDtypeStruct((size, near_width + GATE_COLUMNS), jnp.bfloat16)
        for size in (local_length, 2 * local_length)
    ]
    near_halves = pl.pallas_call(
        near_sum_kernel,
        in_specs=in_vmem(3) + hbm_specs(1),
        out_specs=in_vmem(3),
        out_shape=[own_shape, own_shape, both_shape],
        scratch_shapes=fetch_scratch(*near_args),
        compiler_params=pltpu.CompilerParams(vmem_limit_bytes=SMALL_VMEM),
        cost_estimate=LONG,
    )(routes, other_routes, near_came, *near_args)

    def walk(k, bits):
        found = [k]
        for n, bit in enumerate(bits):
            found += walk(k | bit, bits[n + 1 :])
        return found

    lower_bits = role_bits[:-1][::-1]
    order = walk(last, lower_bits) + walk(0, lower_bits)
    far_plane, final = order[1], order[-1]

    def across(part):
        return [over_seq(part, j) for j in across_steps]

    def spread(own, other, both, ordered):
        planes, crossed = {0: own, last: other}, {}
        both_across = across(both)
        size = own.shape[0]
        for k in order:
            if k not in planes:
                bit = k & -k
                held = planes[k ^ bit]
                wait = ordered and k < last
                planes[k] = over_role(after(held, planes[far_plane]) if wait else held, bit)
            if k in (0, last):
                crossed[k] = both_across
            elif k < last:
                source = k ^ (k & -k)
                came = [part[:size] for part in crossed[source]] if source == 0 else crossed[source]
                crossed[k] = [over_role(part, k & -k) for part in came]
            else:
                crossed[k] = across(after(planes[k], *both_across))
        return planes, crossed

    near_planes, near_crossed = spread(*near_halves, False)

    sent, came = [], []
    for n, j in enumerate(across_steps, 1):
        far = []
        for half, (slots, parts) in zip(attended, slot_sets):
            far += pl.pallas_call(
                partial(project_kernel, slots, parts),
                in_specs=in_vmem(1) + [pl.BlockSpec(memory_space=pl.ANY)] + hbm_specs(2),
                out_specs=in_vmem(len(parts)),
                out_shape=partial_shapes(parts, local_length, near_width),
                scratch_shapes=fetch_scratch(output_weight, beside_proj),
                compiler_params=pltpu.CompilerParams(vmem_limit_bytes=SMALL_VMEM),
                cost_estimate=SHORT,
            )(over_seq(half, j), other_routes, *in_hbm(output_weight, beside_proj))
        sent.append(summed_over_role(far, residuals[n], near_halves[0]))
        came.append(over_role(sent[-1], last))

    chips = 1 + len(across_steps)
    far_args = in_hbm(*sent)
    far_rows = (chips - 1) * local_length
    far_shape, far_both_shape = [
        jax.ShapeDtypeStruct((size, near_width), jnp.bfloat16) for size in (far_rows, 2 * far_rows)
    ]
    first_come = [*near_crossed[0], near_planes[far_plane], *near_crossed[far_plane]]
    first_come.append(near_planes[final])
    far_halves = pl.pallas_call(
        partial(far_sum_kernel, local_length, len(first_come)),
        in_specs=[pl.BlockSpec(memory_space=pl.ANY)] * len(first_come)
        + in_vmem(len(came))
        + hbm_specs(len(far_args)),
        out_specs=in_vmem(3),
        out_shape=[far_shape, far_shape, far_both_shape],
        scratch_shapes=fetch_scratch(*far_args),
        compiler_params=pltpu.CompilerParams(vmem_limit_bytes=SMALL_VMEM),
        cost_estimate=SHORT,
    )(*first_come, *came, *far_args)
    far_own, far_other, far_both = far_halves
    far_other = after(far_other, *near_crossed[final])
    far_planes, far_crossed = spread(far_own, far_other, far_both, True)

    width = residual.shape[2]
    gain = norm_gain.reshape(1, width)

    def normed_rows(parts, second, *hidden_shape):
        rows = chips * local_length
        firsts = (local_length, far_rows) if second else (0, 0)
        return pl.pallas_call(
            partial(norm_kernel, chips, *firsts),
            in_specs=[pl.BlockSpec(memory_space=pltpu.SMEM)] + in_vmem(1 + 2 * chips),
            out_specs=in_vmem(1 + len(hidden_shape)),
            out_shape=[
                jax.ShapeDtypeStruct((rows, width + GATE_COLUMNS), jnp.bfloat16),
                *hidden_shape,
            ],
            scratch_shapes=[pltpu.VMEM((rows, width), jnp.float32)],
            compiler_params=pltpu.CompilerParams(vmem_limit_bytes=SMALL_VMEM),
            cost_estimate=NOTHING,
        )(at, gain, *parts)

    keep, send, slots, leaving, passed = {}, {}, {}, {}, {}

    hidden_shape = jax.ShapeDtypeStruct((local_length, width), jnp.float32)
    hidden = []

    hidden_shape = jax.ShapeDtypeStruct((local_length, width), jnp.float32)
    hidden = []

    def prepared(k, *first):
        late = far_crossed[k]
        if first:
            late = [after(part, *first) for part in late]
        parts = [near_planes[k], far_planes[k]]
        for pair in zip(near_crossed[k], late):
            parts += pair
        normed, *own = normed_rows(parts, k == last, *([] if k else [hidden_shape]))
        hidden.extend(own)
        return [normed, over_seq(normed, 1)]

    def expert(tokens, *others):
        if others:
            tokens = lax.optimization_barrier((*tokens, *others))[: len(tokens)]
        return run_expert(at, tokens, gate_weight, up_weight, down_weight)

    def combine(k, *before):
        came = over_seq(after(send[k], *before) if before else send[k], 1)
        sums = []
        for n in range(len(across_steps)):
            chunk = slice((n + 1) * local_length, (n + 2) * local_length)
            sums.append(added([keep[k][chunk], came[chunk]]).astype(jnp.bfloat16))
        return [keep[k][:local_length], came[:local_length]], sums

    def pass_on(k):
        passed[k] = [over_seq(part, j) for part, j in zip(leaving[k], across_steps)]
        slots[k] += passed[k]

    ready = {far_plane: prepared(far_plane, far_planes[final], *far_crossed[final])}
    ready[final] = prepared(final)
    keep[far_plane], send[far_plane] = expert(ready[far_plane], ready[final][0])
    ready |= {k: prepared(k, keep[far_plane]) for k in (last, 0)}
    slots[far_plane], leaving[far_plane] = combine(far_plane)
    leaving[far_plane] = [after(part, ready[last][0], ready[0][0]) for part in leaving[far_plane]]
    pass_on(far_plane)
    keep[last], send[last] = expert(ready[last], keep[far_plane], *leaving[far_plane])
    slots[last], leaving[last] = combine(last)
    leaving[last] = [after(part, *passed[far_plane]) for part in leaving[last]]
    pass_on(last)
    keep[final], send[final] = expert(ready[final], keep[last])
    slots[far_plane] = [added(slots[far_plane]).astype(jnp.bfloat16)]
    slots[final], leaving[final] = combine(final, *passed[far_plane])
    leaving[final] = [after(part, *leaving[last]) for part in leaving[final]]
    pass_on(final)
    keep[0], send[0] = expert(ready[0], keep[final], *leaving[last])
    slots[0], leaving[0] = combine(0, *passed[last])
    leaving[0] = [after(part, *leaving[final]) for part in leaving[0]]
    pass_on(0)
    for bit in role_bits:
        for k in [k for k in sorted(slots, reverse=True) if k & bit]:
            going = added(slots.pop(k)).astype(jnp.bfloat16)
            if k == last:
                going = after(going, *leaving[final])
            slots[k ^ bit].append(over_role(going, bit))
    return added(hidden + slots[0]).astype(jnp.bfloat16).reshape(residual.shape)


def solution(mesh):
    placed = (
        P("groups", "seq", "role"),
        P("groups", ("seq", "role"), None),
        P("groups", ("seq", "role"), None),
        P("role", "seq"),
        P(("groups", "role"), "seq", None),
        P(),
        P(("groups", "role"), "seq", None),
        P(("groups", "role"), "seq", None),
        P(("seq", "role"), None, None),
        P(("seq", "role"), None, None),
        P(("seq", "role"), None, None),
    )
    experts = mesh.shape["seq"] * mesh.shape["role"]
    return jax.shard_map(
        gathered_shards if experts <= 2 * TOPK else routed_shards,
        mesh=mesh,
        in_specs=placed,
        out_specs=P(("groups", "role"), "seq", None),
        check_vma=False,
    )
```

```python
from functools import partial

import jax
import jax.numpy as jnp
from jax import lax
from jax.experimental import pallas as pl
from jax.experimental.pallas import tpu as pltpu
from jax.sharding import PartitionSpec as P

D = 2048
QUERY_HEADS = 32
KEY_VALUE_HEADS = 4
HEAD_WIDTH = 128
TOPK = 8


epsilon = 1e-06
masked_score = -1e30
EXPERT_VMEM = 16 * 2**20
SMALL_VMEM = 12 * 2**20
COPY_VMEM = 4 * 2**20
GATE_COLUMNS = 128
NOTHING = pl.CostEstimate(flops=1, bytes_accessed=1, transcendentals=0)
SHORT = pl.CostEstimate(flops=2 * 10**9, bytes_accessed=4 * 2**20, transcendentals=0)
LONG = pl.CostEstimate(flops=10**10, bytes_accessed=1, transcendentals=0)


def score_block(queries, every_key, query_position, block_start, block_width, score_scale):
    keys_part = lax.slice_in_dim(every_key, block_start, block_start + block_width, axis=0)
    raw_scores = (
        jnp.einsum("qhd,kd->hqk", queries, keys_part, preferred_element_type=jnp.float32)
        * score_scale
    )
    key_position = block_start + jnp.arange(block_width, dtype=jnp.int32)
    return jnp.where(
        key_position[None, None, :] <= query_position[None, :, None], raw_scores, masked_score
    )


def value_block(rounded, every_value, block_start, block_width):
    prob_block = lax.slice_in_dim(rounded, block_start, block_start + block_width, axis=2)
    values_part = lax.slice_in_dim(every_value, block_start, block_start + block_width, axis=0)
    return jnp.einsum("hqk,kd->qhd", prob_block, values_part, preferred_element_type=jnp.float32)


def routed_shards(
    query_rows,
    encoded_key_rows,
    value_matrix_rows,
    output_weight,
    residual,
    norm_gain,
    route_experts,
    route_gates,
    gate_weight,
    up_weight,
    down_weight,
):
    seq_count = lax.axis_size("seq")
    role_count = lax.axis_size("role")
    seq_index = lax.axis_index("seq")
    role_index = lax.axis_index("role")
    batch_count = query_rows.shape[0]
    local_length = query_rows.shape[1]
    local_heads = query_rows.shape[2] // HEAD_WIDTH
    full_length = local_length * seq_count
    query_group_width = QUERY_HEADS // KEY_VALUE_HEADS
    head_pick = role_index * local_heads // query_group_width
    role_keys, role_values = (
        lax.all_gather(encoded_key_rows, "role", axis=1, tiled=True),
        lax.all_gather(value_matrix_rows, "role", axis=1, tiled=True),
    )
    head_keys = lax.dynamic_slice_in_dim(role_keys, head_pick * HEAD_WIDTH, HEAD_WIDTH, 2)
    head_values = lax.dynamic_slice_in_dim(role_values, head_pick * HEAD_WIDTH, HEAD_WIDTH, 2)
    whole_keys, whole_values, whole_proj = (
        lax.all_gather(head_keys, "seq", axis=1, tiled=True),
        lax.all_gather(head_values, "seq", axis=1, tiled=True),
        lax.all_gather(output_weight, "seq", axis=1, tiled=True),
    )
    key_width = full_length // 8
    score_scale = HEAD_WIDTH ** (-0.5)
    query_position = seq_index * local_length + jnp.arange(local_length, dtype=jnp.int32)
    last_needed = (seq_index + 1) * local_length

    def one_sequence(operands):
        own_queries, every_key, every_value = operands
        queries = own_queries.reshape(local_length, local_heads, HEAD_WIDTH)
        pieces = []
        for number in range(8):
            block_start = number * key_width
            compute = partial(
                score_block, queries, every_key, query_position, block_start, key_width, score_scale
            )
            skipped = partial(
                jnp.full, (local_heads, local_length, key_width), masked_score, jnp.float32
            )
            pieces.append(lax.cond(block_start < last_needed, compute, skipped))
        scores = jnp.concatenate(pieces, axis=2)
        row_peak = jnp.max(scores, axis=2, keepdims=True)
        weights = jnp.exp(scores - row_peak)
        totals = jnp.sum(weights, axis=2, keepdims=True)
        rounded = weights.astype(jnp.bfloat16)
        mixed_rows = jnp.zeros((local_length, local_heads, HEAD_WIDTH), jnp.float32)
        for number in range(8):
            block_start = number * key_width
            product = partial(value_block, rounded, every_value, block_start, key_width)
            nothing = partial(jnp.zeros, (local_length, local_heads, HEAD_WIDTH), jnp.float32)
            mixed_rows = mixed_rows + lax.cond(block_start < last_needed, product, nothing)
        attended = (mixed_rows / totals.transpose(1, 0, 2)).astype(jnp.bfloat16)
        return attended.reshape(local_length, local_heads * HEAD_WIDTH)

    attended = lax.map(one_sequence, (query_rows, whole_keys, whole_values))
    flat_attended = attended.reshape(batch_count * local_length, local_heads * HEAD_WIDTH)
    projected = lax.psum_scatter(
        jnp.dot(flat_attended, whole_proj, preferred_element_type=jnp.float32).astype(jnp.bfloat16),
        "role",
        scatter_dimension=0,
        tiled=True,
    ).astype(jnp.float32)
    hidden = residual[0].astype(jnp.float32) + projected
    variance = jnp.mean(hidden * hidden, axis=-1, keepdims=True)
    normed = (hidden * lax.rsqrt(variance + epsilon) * norm_gain).astype(jnp.bfloat16)
    expert_ids = route_experts.reshape(-1)
    gate_values = route_gates.reshape(-1)
    experts_local = gate_weight.shape[0]
    device_count = seq_count * role_count
    expert_count = experts_local * device_count
    assign = expert_ids.shape[0]
    capacity = assign // expert_count + 1
    onehot = (expert_ids[:, None] == jnp.arange(expert_count, dtype=jnp.int32)[None, :]).astype(
        jnp.int32
    )
    earlier = jnp.cumsum(onehot, axis=0) - onehot
    slot_rank = jnp.sum(earlier * onehot, axis=1)
    slot_index = expert_ids * capacity + slot_rank
    source_token = jnp.arange(assign, dtype=jnp.int32) // TOPK
    slot_token = jnp.zeros((expert_count * capacity,), jnp.int32).at[slot_index].set(source_token)
    slot_used = jnp.zeros((expert_count * capacity,), jnp.bfloat16).at[slot_index].set(1.0)
    outgoing = (normed[slot_token] * slot_used[:, None]).reshape(
        device_count, experts_local, capacity, D
    )
    incoming = lax.all_to_all(outgoing, ("seq", "role"), split_axis=0, concat_axis=0, tiled=True)
    gate_hidden = jnp.einsum(
        "sjcd,jdf->sjcf", incoming, gate_weight, preferred_element_type=jnp.float32
    )
    up_hidden = jnp.einsum(
        "sjcd,jdf->sjcf", incoming, up_weight, preferred_element_type=jnp.float32
    )
    activated = (jax.nn.silu(gate_hidden) * up_hidden).astype(jnp.bfloat16)
    returned = lax.all_to_all(
        jnp.einsum(
            "sjcf,jfd->sjcd", activated, down_weight, preferred_element_type=jnp.float32
        ).astype(jnp.bfloat16),
        ("seq", "role"),
        split_axis=0,
        concat_axis=0,
        tiled=True,
    )
    gathered = returned.reshape(expert_count * capacity, D)[slot_index]
    weighted = gathered.astype(jnp.float32) * gate_values[:, None]
    expert_sum = jnp.sum(weighted.reshape(-1, TOPK, D), axis=1)
    return (hidden + expert_sum).astype(jnp.bfloat16).reshape(residual.shape)


def in_hbm(*arrays):
    return [pltpu.with_memory_space_constraint(array, pltpu.HBM) for array in arrays]


def hbm_specs(count):
    return [pl.BlockSpec(memory_space=pltpu.HBM)] * count


def fetch_scratch(*arrays):
    return [pltpu.VMEM(array.shape, array.dtype) for array in arrays] + [
        pltpu.SemaphoreType.DMA((len(arrays),))
    ]


def start_fetch(from_refs, scratch, started=None):
    *buffers, sems = scratch
    copies = [
        pltpu.make_async_copy(from_ref, buffer, sems.at[n])
        for n, (from_ref, buffer) in enumerate(zip(from_refs, buffers))
    ]
    for copy in copies[:started]:
        copy.start()
    return copies, buffers


def in_vmem(count):
    return [pl.BlockSpec(memory_space=pltpu.VMEM)] * count


def attend_kernel(seq_count, role_count, slots, groups, at_ref, *refs):
    last_block, *refs = refs
    count = seq_count + 2
    attended_ref, *partial_refs = refs[count : count + 1 + len(groups)]
    copies, (query_ref, *buffers) = start_fetch(
        refs[:count], refs[count + 1 + len(groups) :], seq_count
    )
    blocks, proj_refs = buffers[: seq_count - 1] + [last_block], buffers[seq_count - 1 :]
    seq_index, role_index = at_ref[0], at_ref[1]
    local_length = query_ref.shape[1]
    local_heads = query_ref.shape[2] // HEAD_WIDTH
    per_role = local_length // role_count
    rows = local_heads * local_length
    keys_all = seq_count * local_length
    slot = lax.broadcasted_iota(jnp.int32, (rows, keys_all), 1)
    block_number, within = slot // local_length, slot % local_length
    key_position = (
        (seq_index ^ block_number) * local_length
        + (role_index ^ (within // per_role)) * per_role
        + within % per_role
    )
    query_position = (
        seq_index * local_length
        + lax.broadcasted_iota(jnp.int32, (rows, keys_all), 0) % local_length
    )
    seen = key_position <= query_position
    scale = HEAD_WIDTH ** (-0.5)
    for copy in copies[:seq_count]:
        copy.wait()
    for copy in copies[seq_count:]:
        copy.start()
    for n, k in enumerate(slots):
        b = role_index ^ k
        own = query_ref[b]
        queries = jnp.concatenate(
            [own[:, h * HEAD_WIDTH : (h + 1) * HEAD_WIDTH] for h in range(local_heads)], axis=0
        )
        key_value = jnp.concatenate([block[b] for block in blocks], axis=0)
        keys, values = key_value[:, :HEAD_WIDTH], key_value[:, HEAD_WIDTH:]
        scores = lax.dot_general(
            queries, keys, (((1,), (1,)), ((), ())), preferred_element_type=jnp.float32
        )
        scores = jnp.where(seen, scores * scale, masked_score)
        weights = jnp.exp(scores - jnp.max(scores, axis=1, keepdims=True))
        totals = jnp.sum(weights, axis=1, keepdims=True)
        mixed = jnp.dot(weights.astype(jnp.bfloat16), values, preferred_element_type=jnp.float32)
        attended = (mixed / totals).astype(jnp.bfloat16)
        for h in range(local_heads):
            attended_ref[
                n * local_length : (n + 1) * local_length, h * HEAD_WIDTH : (h + 1) * HEAD_WIDTH
            ] = attended[h * local_length : (h + 1) * local_length]
    for copy in copies[seq_count:]:
        copy.wait()
    project_into(slots, groups, attended_ref, proj_refs, partial_refs)


def join_kernel(*refs):
    *piece_refs, out_ref = refs
    at = 0
    for ref in piece_refs:
        size = ref.shape[1]
        out_ref[:, at : at + size, :] = ref[...]
        at += size


def role_groups(role_count):
    last = role_count // 2
    bits = [1 << n for n in range(last.bit_length() - 1)]
    return [[k for k in range(role_count) if k & -k == bit] for bit in bits] + [[0, last]]


def project_into(slots, groups, attended_ref, proj_refs, partial_refs):
    slots = list(slots)
    rows = attended_ref.shape[0] // len(slots)
    at = 0
    for proj_ref in proj_refs:
        width = proj_ref.shape[1]
        product = jnp.dot(
            attended_ref[...], proj_ref[...], preferred_element_type=jnp.float32
        ).astype(jnp.bfloat16)
        for group, partial_ref in zip(groups, partial_refs):
            for n, k in enumerate(group):
                start = slots.index(k) * rows
                partial_ref[n * rows : (n + 1) * rows, at : at + width] = product[
                    start : start + rows
                ]
        at += width


def project_kernel(slots, groups, attended_ref, order_ref, *refs):
    count = (len(refs) - len(groups) - 1) // 2
    copies, proj_refs = start_fetch(refs[:count], refs[count + len(groups) :])
    for copy in copies:
        copy.wait()
    project_into(slots, groups, attended_ref, proj_refs, refs[count : count + len(groups)])


def partial_shapes(groups, rows, width):
    return [jax.ShapeDtypeStruct((rows * len(group), width), jnp.bfloat16) for group in groups]


def near_sum_kernel(route_ref, other_route_ref, came_ref, sent_any, *refs):
    out_refs, both_ref = refs[:2], refs[2]
    copies, (sent,) = start_fetch([sent_any], refs[3:])
    rows, width = sent.shape[0] // 2, sent.shape[1]
    lane = lax.broadcasted_iota(jnp.int32, (rows, GATE_COLUMNS), 1)
    half = GATE_COLUMNS // 2
    expert = (lane % half).astype(jnp.float32)
    for p, routes in enumerate((route_ref, other_route_ref)):
        shares = jnp.zeros((rows, GATE_COLUMNS), jnp.float32)
        routed = routes.shape[1] // 2
        for k in range(routed):
            named, weight = routes[:, k : k + 1], routes[:, routed + k : routed + k + 1]
            shares = shares + jnp.where(expert == named, weight, 0.0)
        first = shares.astype(jnp.bfloat16).astype(jnp.float32)
        terms = jnp.where(lane < half, first, shares - first).astype(jnp.bfloat16)
        out_refs[p][:, width:] = terms
        both_ref[p * rows : (p + 1) * rows, width:] = terms
    copies[0].wait()
    for p in range(2):
        total = sent[p * rows : (p + 1) * rows].astype(jnp.float32)
        total = total + came_ref[(1 - p) * rows : (2 - p) * rows].astype(jnp.float32)
        out_refs[p][:, :width] = total.astype(jnp.bfloat16)
        both_ref[p * rows : (p + 1) * rows, :width] = total.astype(jnp.bfloat16)


def far_sum_kernel(rows, order_count, *refs):
    refs = refs[order_count:]
    chips = (len(refs) - 4) // 3
    came_refs, sent_any = refs[:chips], refs[chips : 2 * chips]
    own_ref, other_ref, both_ref = refs[2 * chips : 2 * chips + 3]
    copies, sent_refs = start_fetch(sent_any, refs[2 * chips + 3 :])
    for copy in copies:
        copy.wait()
    size = chips * rows
    for n, (sent, came) in enumerate(zip(sent_refs, came_refs)):
        to = slice(n * rows, (n + 1) * rows)
        for p, out_ref in enumerate((own_ref, other_ref)):
            total = sent[p * rows : (p + 1) * rows].astype(jnp.float32)
            total = total + came[(1 - p) * rows : (2 - p) * rows].astype(jnp.float32)
            out_ref[to] = total.astype(jnp.bfloat16)
            both_ref[p * size + n * rows : p * size + (n + 1) * rows] = total.astype(jnp.bfloat16)


def norm_kernel(chips, near_row, far_row, at_ref, gain_ref, *refs):
    parts, (normed_ref, *hidden_refs, whole_ref) = refs[: 2 * chips], refs[2 * chips :]
    seq_index = at_ref[0]
    features = whole_ref.shape[1]
    rows = whole_ref.shape[0] // chips
    width = features // chips // 2
    for n in range(chips):
        near, far = parts[2 * n : 2 * n + 2]
        for m in range(chips):
            part = far if m else near
            first = ((far_row if m else near_row) if n else 0) + (m - 1 if m else 0) * rows
            to = slice((n ^ m) * rows, ((n ^ m) + 1) * rows)
            for j in range(2):
                start = pl.multiple_of((seq_index ^ (2 * n + j)) * width, width)
                whole_ref[to, pl.ds(start, width)] = part[
                    first : first + rows, j * width : (j + 1) * width
                ].astype(jnp.float32)
        first = near_row if n else 0
        normed_ref[n * rows : (n + 1) * rows, features:] = near[first : first + rows, 2 * width :]
    hidden = whole_ref[...]
    variance = jnp.mean(hidden * hidden, axis=1, keepdims=True)
    normed = hidden * lax.rsqrt(variance + epsilon) * gain_ref[...]
    normed_ref[:, :features] = normed.astype(jnp.bfloat16)
    for hidden_ref in hidden_refs:
        hidden_ref[...] = hidden[:rows]


def expert_kernel(token_count, at_ref, *refs):
    token_refs = refs[:token_count]
    gate_ref, up_ref, down_ref, keep_ref, send_ref, activated_ref = refs[token_count:]
    features, units = gate_ref.shape[1:]
    tokens = jnp.concatenate([ref[:, :features] for ref in token_refs], axis=0)
    gates = jnp.concatenate([ref[:, features:] for ref in token_refs], axis=0)
    lane = lax.broadcasted_iota(jnp.int32, gates.shape, 1)
    mine = lane % (GATE_COLUMNS // 2) == at_ref[2]
    share = jnp.sum(jnp.where(mine, gates.astype(jnp.float32), 0.0), axis=1, keepdims=True)
    block = 256 if units % 256 == 0 else units
    for f in range(0, units, block):
        gate_hidden = jnp.dot(
            tokens, gate_ref[0, :, f : f + block], preferred_element_type=jnp.float32
        )
        up_hidden = jnp.dot(tokens, up_ref[0, :, f : f + block], preferred_element_type=jnp.float32)
        activated_ref[:, f : f + block] = (
            gate_hidden / (1.0 + jnp.exp(-gate_hidden)) * up_hidden
        ).astype(jnp.bfloat16)
    kept = keep_ref.shape[0]
    block = 512 if features % 512 == 0 else features
    for c in range(0, features, block):
        product = jnp.dot(
            activated_ref[...], down_ref[0, :, c : c + block], preferred_element_type=jnp.float32
        )
        product = (product * share).astype(jnp.bfloat16)
        keep_ref[:, c : c + block] = product[:kept]
        send_ref[:, c : c + block] = product[kept:]


def run_expert(at, tokens, gate_weight, up_weight, down_weight):
    units = gate_weight.shape[2]
    width = gate_weight.shape[1]
    rows = sum(part.shape[0] for part in tokens)
    half = jax.ShapeDtypeStruct((rows // 2, width), jnp.bfloat16)
    return pl.pallas_call(
        partial(expert_kernel, len(tokens)),
        in_specs=[pl.BlockSpec(memory_space=pltpu.SMEM)] + in_vmem(len(tokens) + 3),
        out_specs=in_vmem(2),
        out_shape=[half, half],
        scratch_shapes=[pltpu.VMEM((rows, units), jnp.bfloat16)],
        compiler_params=pltpu.CompilerParams(vmem_limit_bytes=EXPERT_VMEM),
        cost_estimate=NOTHING,
    )(at, *tokens, gate_weight, up_weight, down_weight)


def after(array, *others):
    return lax.optimization_barrier((array, *others))[0]


def added(terms):
    total = terms[0].astype(jnp.float32)
    for term in terms[1:]:
        total = total + term.astype(jnp.float32)
    return total


def gathered_shards(
    query_rows,
    encoded_key_rows,
    value_matrix_rows,
    output_weight,
    residual,
    norm_gain,
    route_experts,
    route_gates,
    gate_weight,
    up_weight,
    down_weight,
):
    seq_count = lax.axis_size("seq")
    role_count = lax.axis_size("role")
    seq_index = lax.axis_index("seq")
    role_index = lax.axis_index("role")
    batch_count, local_length, query_width = query_rows.shape
    local_heads = query_width // HEAD_WIDTH
    group_width = QUERY_HEADS // KEY_VALUE_HEADS
    role_bits = [1 << n for n in range(role_count.bit_length() - 1)]
    at = jnp.stack([seq_index, role_index, seq_index * role_count + role_index]).astype(jnp.int32)

    def over_role(array, k):
        return lax.ppermute(array, "role", [(i, i ^ k) for i in range(role_count)])

    def over_seq(array, j):
        return lax.ppermute(array, "seq", [(i, i ^ j) for i in range(seq_count)])

    beside_proj = over_seq(output_weight, 1)
    block_width = output_weight.shape[1]
    across_steps = range(2, seq_count, 2)

    pieces = []
    for k in range(role_count):
        head = ((role_index ^ k) * local_heads // group_width) * HEAD_WIDTH
        piece = jnp.concatenate(
            [
                lax.dynamic_slice_in_dim(encoded_key_rows, head, HEAD_WIDTH, 2),
                lax.dynamic_slice_in_dim(value_matrix_rows, head, HEAD_WIDTH, 2),
            ],
            axis=2,
        )
        pieces.append(piece)
    pieces[1] = after(pieces[1], beside_proj)
    pieces = [piece if k == 0 else over_role(piece, k) for k, piece in enumerate(pieces)]
    block = pl.pallas_call(
        join_kernel,
        in_specs=in_vmem(len(pieces)),
        out_specs=pl.BlockSpec(memory_space=pltpu.VMEM),
        out_shape=jax.ShapeDtypeStruct(
            (batch_count, local_length, 2 * HEAD_WIDTH), jnp.bfloat16
        ),
        compiler_params=pltpu.CompilerParams(vmem_limit_bytes=COPY_VMEM),
        cost_estimate=SHORT,
    )(*pieces)
    same_core = [block] + [over_seq(block, j) for j in across_steps]
    blocks = []
    for part in same_core:
        blocks += [part, over_seq(part, 1)]
    last = role_count // 2
    routes = jnp.concatenate([route_experts[0].astype(jnp.float32), route_gates[0]], axis=1)
    residual_blocks = [
        lax.dynamic_slice_in_dim(residual[0], (seq_index ^ j) * block_width, block_width, 1)
        for j in range(seq_count)
    ]
    residuals = [
        jnp.concatenate(residual_blocks[j : j + 2], axis=1) for j in range(0, seq_count, 2)
    ]

    rows = batch_count * local_length
    near_width = 2 * output_weight.shape[1]
    groups = role_groups(role_count)
    attend_args = in_hbm(query_rows, *blocks[:-1], output_weight, beside_proj)
    slot_sets = [(range(1, role_count, 2), groups[:1]), (range(0, role_count, 2), groups[1:])]
    attended, near = [], []
    for slots, parts in slot_sets:
        half_rows = jax.ShapeDtypeStruct((rows // 2, query_width), jnp.bfloat16)
        half, *partials = pl.pallas_call(
            partial(attend_kernel, seq_count, role_count, slots, parts),
            in_specs=[pl.BlockSpec(memory_space=pltpu.SMEM)]
            + in_vmem(1)
            + hbm_specs(len(attend_args)),
            out_specs=in_vmem(1 + len(parts)),
            out_shape=[half_rows] + partial_shapes(parts, local_length, near_width),
            scratch_shapes=fetch_scratch(*attend_args),
            compiler_params=pltpu.CompilerParams(vmem_limit_bytes=SMALL_VMEM),
            cost_estimate=SHORT,
        )(at, blocks[-1], *attend_args)
        attended.append(half)
        near += partials

    for j in across_steps:
        residuals[j // 2] = over_seq(after(residuals[j // 2], attended[1]), j)
    other_routes = over_role(routes, last)

    def summed_over_role(parts, extra, *before):
        terms = [[part] for part in parts]
        for n, group in enumerate(groups[:-1]):
            bit = 1 << n
            leaving = terms[n][0] if len(terms[n]) == 1 else added(terms[n]).astype(jnp.bfloat16)
            came = over_role(leaving, bit)
            for m in range(n + 1, len(groups)):
                at_rows = [group.index(k ^ bit) for k in groups[m]]
                if at_rows == list(range(len(group))):
                    terms[m].append(came)
                else:
                    split = [came[i * local_length : (i + 1) * local_length] for i in at_rows]
                    terms[m].append(jnp.concatenate(split, axis=0))
        extra = jnp.pad(after(extra, *before) if before else extra, ((0, local_length), (0, 0)))
        sent = added(terms[-1] + [extra]).astype(jnp.bfloat16)
        return sent

    near_sent = summed_over_role(near, residuals[0])
    near_came = over_role(near_sent, last)
    near_args = in_hbm(near_sent)
    own_shape, both_shape = [
        jax.ShapeDtypeStruct((size, near_width + GATE_COLUMNS), jnp.bfloat16)
        for size in (local_length, 2 * local_length)
    ]
    near_halves = pl.pallas_call(
        near_sum_kernel,
        in_specs=in_vmem(3) + hbm_specs(1),
        out_specs=in_vmem(3),
        out_shape=[own_shape, own_shape, both_shape],
        scratch_shapes=fetch_scratch(*near_args),
        compiler_params=pltpu.CompilerParams(vmem_limit_bytes=SMALL_VMEM),
        cost_estimate=LONG,
    )(routes, other_routes, near_came, *near_args)

    def walk(k, bits):
        found = [k]
        for n, bit in enumerate(bits):
            found += walk(k | bit, bits[n + 1 :])
        return found

    lower_bits = role_bits[:-1][::-1]
    order = walk(last, lower_bits) + walk(0, lower_bits)
    far_plane, final = order[1], order[-1]

    def across(part):
        return [over_seq(part, j) for j in across_steps]

    def spread(own, other, both, ordered):
        planes, crossed = {0: own, last: other}, {}
        both_across = across(both)
        size = own.shape[0]
        for k in order:
            if k not in planes:
                bit = k & -k
                held = planes[k ^ bit]
                wait = ordered and k < last
                planes[k] = over_role(after(held, planes[far_plane]) if wait else held, bit)
            if k in (0, last):
                crossed[k] = both_across
            elif k < last:
                source = k ^ (k & -k)
                came = [part[:size] for part in crossed[source]] if source == 0 else crossed[source]
                crossed[k] = [over_role(part, k & -k) for part in came]
            else:
                crossed[k] = across(after(planes[k], *both_across))
        return planes, crossed

    near_planes, near_crossed = spread(*near_halves, False)

    sent, came = [], []
    for n, j in enumerate(across_steps, 1):
        far = []
        for half, (slots, parts) in zip(attended, slot_sets):
            far += pl.pallas_call(
                partial(project_kernel, slots, parts),
                in_specs=in_vmem(1) + [pl.BlockSpec(memory_space=pl.ANY)] + hbm_specs(2),
                out_specs=in_vmem(len(parts)),
                out_shape=partial_shapes(parts, local_length, near_width),
                scratch_shapes=fetch_scratch(output_weight, beside_proj),
                compiler_params=pltpu.CompilerParams(vmem_limit_bytes=SMALL_VMEM),
                cost_estimate=SHORT,
            )(over_seq(half, j), other_routes, *in_hbm(output_weight, beside_proj))
        sent.append(summed_over_role(far, residuals[n], near_halves[0]))
        came.append(over_role(sent[-1], last))

    chips = 1 + len(across_steps)
    far_args = in_hbm(*sent)
    far_rows = (chips - 1) * local_length
    far_shape, far_both_shape = [
        jax.ShapeDtypeStruct((size, near_width), jnp.bfloat16) for size in (far_rows, 2 * far_rows)
    ]
    first_come = [*near_crossed[0], near_planes[far_plane], *near_crossed[far_plane]]
    first_come.append(near_planes[final])
    far_halves = pl.pallas_call(
        partial(far_sum_kernel, local_length, len(first_come)),
        in_specs=[pl.BlockSpec(memory_space=pl.ANY)] * len(first_come)
        + in_vmem(len(came))
        + hbm_specs(len(far_args)),
        out_specs=in_vmem(3),
        out_shape=[far_shape, far_shape, far_both_shape],
        scratch_shapes=fetch_scratch(*far_args),
        compiler_params=pltpu.CompilerParams(vmem_limit_bytes=SMALL_VMEM),
        cost_estimate=SHORT,
    )(*first_come, *came, *far_args)
    far_own, far_other, far_both = far_halves
    far_other = after(far_other, *near_crossed[final])
    far_planes, far_crossed = spread(far_own, far_other, far_both, True)

    width = residual.shape[2]
    gain = norm_gain.reshape(1, width)

    def normed_rows(parts, second, *hidden_shape):
        rows = chips * local_length
        firsts = (local_length, far_rows) if second else (0, 0)
        return pl.pallas_call(
            partial(norm_kernel, chips, *firsts),
            in_specs=[pl.BlockSpec(memory_space=pltpu.SMEM)] + in_vmem(1 + 2 * chips),
            out_specs=in_vmem(1 + len(hidden_shape)),
            out_shape=[
                jax.ShapeDtypeStruct((rows, width + GATE_COLUMNS), jnp.bfloat16),
                *hidden_shape,
            ],
            scratch_shapes=[pltpu.VMEM((rows, width), jnp.float32)],
            compiler_params=pltpu.CompilerParams(vmem_limit_bytes=SMALL_VMEM),
            cost_estimate=NOTHING,
        )(at, gain, *parts)

    keep, send, slots, leaving, passed = {}, {}, {}, {}, {}

    hidden_shape = jax.ShapeDtypeStruct((local_length, width), jnp.float32)
    hidden = []

    hidden_shape = jax.ShapeDtypeStruct((local_length, width), jnp.float32)
    hidden = []

    def prepared(k, *first):
        late = far_crossed[k]
        if first:
            late = [after(part, *first) for part in late]
        parts = [near_planes[k], far_planes[k]]
        for pair in zip(near_crossed[k], late):
            parts += pair
        normed, *own = normed_rows(parts, k == last, *([] if k else [hidden_shape]))
        hidden.extend(own)
        return [normed, over_seq(normed, 1)]

    def expert(tokens, *others):
        if others:
            tokens = lax.optimization_barrier((*tokens, *others))[: len(tokens)]
        return run_expert(at, tokens, gate_weight, up_weight, down_weight)

    def combine(k, *before):
        came = over_seq(after(send[k], *before) if before else send[k], 1)
        sums = []
        for n in range(len(across_steps)):
            chunk = slice((n + 1) * local_length, (n + 2) * local_length)
            sums.append(added([keep[k][chunk], came[chunk]]).astype(jnp.bfloat16))
        return [keep[k][:local_length], came[:local_length]], sums

    def pass_on(k):
        passed[k] = [over_seq(part, j) for part, j in zip(leaving[k], across_steps)]
        slots[k] += passed[k]

    ready = {far_plane: prepared(far_plane, far_planes[final], *far_crossed[final])}
    ready[final] = prepared(final)
    keep[far_plane], send[far_plane] = expert(ready[far_plane], ready[final][0])
    ready |= {k: prepared(k, keep[far_plane]) for k in (last, 0)}
    slots[far_plane], leaving[far_plane] = combine(far_plane)
    leaving[far_plane] = [after(part, ready[last][0], ready[0][0]) for part in leaving[far_plane]]
    pass_on(far_plane)
    keep[last], send[last] = expert(ready[last], keep[far_plane], *leaving[far_plane])
    slots[last], leaving[last] = combine(last)
    leaving[last] = [after(part, *passed[far_plane]) for part in leaving[last]]
    pass_on(last)
    keep[final], send[final] = expert(ready[final], keep[last])
    slots[far_plane] = [added(slots[far_plane]).astype(jnp.bfloat16)]
    slots[final], leaving[final] = combine(final, *passed[far_plane])
    leaving[final] = [after(part, *leaving[last]) for part in leaving[final]]
    pass_on(final)
    keep[0], send[0] = expert(ready[0], keep[final], *leaving[last])
    slots[0], leaving[0] = combine(0, *passed[last])
    leaving[0] = [after(part, *leaving[final]) for part in leaving[0]]
    pass_on(0)
    for bit in role_bits:
        for k in [k for k in sorted(slots, reverse=True) if k & bit]:
            going = added(slots.pop(k)).astype(jnp.bfloat16)
            if k == last:
                going = after(going, *leaving[final])
            slots[k ^ bit].append(over_role(going, bit))
    early, late = slots[0][: -len(role_bits)], slots[0][-len(role_bits) :]
    early = lax.optimization_barrier(added(hidden + early))
    return added([early] + late).astype(jnp.bfloat16).reshape(residual.shape)


def solution(mesh):
    placed = (
        P("groups", "seq", "role"),
        P("groups", ("seq", "role"), None),
        P("groups", ("seq", "role"), None),
        P("role", "seq"),
        P(("groups", "role"), "seq", None),
        P(),
        P(("groups", "role"), "seq", None),
        P(("groups", "role"), "seq", None),
        P(("seq", "role"), None, None),
        P(("seq", "role"), None, None),
        P(("seq", "role"), None, None),
    )
    experts = mesh.shape["seq"] * mesh.shape["role"]
    return jax.shard_map(
        gathered_shards if experts <= 2 * TOPK else routed_shards,
        mesh=mesh,
        in_specs=placed,
        out_specs=P(("groups", "role"), "seq", None),
        check_vma=False,
    )
```

```python
from functools import partial

import jax
import jax.numpy as jnp
from jax import lax
from jax.experimental import pallas as pl
from jax.experimental.pallas import tpu as pltpu
from jax.sharding import PartitionSpec as P

D = 2048
QUERY_HEADS = 32
KEY_VALUE_HEADS = 4
HEAD_WIDTH = 128
TOPK = 8


epsilon = 1e-06
masked_score = -1e30
EXPERT_VMEM = 16 * 2**20
SMALL_VMEM = 12 * 2**20
COPY_VMEM = 4 * 2**20
GATE_COLUMNS = 128
NOTHING = pl.CostEstimate(flops=1, bytes_accessed=1, transcendentals=0)
SHORT = pl.CostEstimate(flops=2 * 10**9, bytes_accessed=4 * 2**20, transcendentals=0)
LONG = pl.CostEstimate(flops=10**10, bytes_accessed=1, transcendentals=0)


def score_block(queries, every_key, query_position, block_start, block_width, score_scale):
    keys_part = lax.slice_in_dim(every_key, block_start, block_start + block_width, axis=0)
    raw_scores = (
        jnp.einsum("qhd,kd->hqk", queries, keys_part, preferred_element_type=jnp.float32)
        * score_scale
    )
    key_position = block_start + jnp.arange(block_width, dtype=jnp.int32)
    return jnp.where(
        key_position[None, None, :] <= query_position[None, :, None], raw_scores, masked_score
    )


def value_block(rounded, every_value, block_start, block_width):
    prob_block = lax.slice_in_dim(rounded, block_start, block_start + block_width, axis=2)
    values_part = lax.slice_in_dim(every_value, block_start, block_start + block_width, axis=0)
    return jnp.einsum("hqk,kd->qhd", prob_block, values_part, preferred_element_type=jnp.float32)


def routed_shards(
    query_rows,
    encoded_key_rows,
    value_matrix_rows,
    output_weight,
    residual,
    norm_gain,
    route_experts,
    route_gates,
    gate_weight,
    up_weight,
    down_weight,
):
    seq_count = lax.axis_size("seq")
    role_count = lax.axis_size("role")
    seq_index = lax.axis_index("seq")
    role_index = lax.axis_index("role")
    batch_count = query_rows.shape[0]
    local_length = query_rows.shape[1]
    local_heads = query_rows.shape[2] // HEAD_WIDTH
    full_length = local_length * seq_count
    query_group_width = QUERY_HEADS // KEY_VALUE_HEADS
    head_pick = role_index * local_heads // query_group_width
    role_keys, role_values = (
        lax.all_gather(encoded_key_rows, "role", axis=1, tiled=True),
        lax.all_gather(value_matrix_rows, "role", axis=1, tiled=True),
    )
    head_keys = lax.dynamic_slice_in_dim(role_keys, head_pick * HEAD_WIDTH, HEAD_WIDTH, 2)
    head_values = lax.dynamic_slice_in_dim(role_values, head_pick * HEAD_WIDTH, HEAD_WIDTH, 2)
    whole_keys, whole_values, whole_proj = (
        lax.all_gather(head_keys, "seq", axis=1, tiled=True),
        lax.all_gather(head_values, "seq", axis=1, tiled=True),
        lax.all_gather(output_weight, "seq", axis=1, tiled=True),
    )
    key_width = full_length // 8
    score_scale = HEAD_WIDTH ** (-0.5)
    query_position = seq_index * local_length + jnp.arange(local_length, dtype=jnp.int32)
    last_needed = (seq_index + 1) * local_length

    def one_sequence(operands):
        own_queries, every_key, every_value = operands
        queries = own_queries.reshape(local_length, local_heads, HEAD_WIDTH)
        pieces = []
        for number in range(8):
            block_start = number * key_width
            compute = partial(
                score_block, queries, every_key, query_position, block_start, key_width, score_scale
            )
            skipped = partial(
                jnp.full, (local_heads, local_length, key_width), masked_score, jnp.float32
            )
            pieces.append(lax.cond(block_start < last_needed, compute, skipped))
        scores = jnp.concatenate(pieces, axis=2)
        row_peak = jnp.max(scores, axis=2, keepdims=True)
        weights = jnp.exp(scores - row_peak)
        totals = jnp.sum(weights, axis=2, keepdims=True)
        rounded = weights.astype(jnp.bfloat16)
        mixed_rows = jnp.zeros((local_length, local_heads, HEAD_WIDTH), jnp.float32)
        for number in range(8):
            block_start = number * key_width
            product = partial(value_block, rounded, every_value, block_start, key_width)
            nothing = partial(jnp.zeros, (local_length, local_heads, HEAD_WIDTH), jnp.float32)
            mixed_rows = mixed_rows + lax.cond(block_start < last_needed, product, nothing)
        attended = (mixed_rows / totals.transpose(1, 0, 2)).astype(jnp.bfloat16)
        return attended.reshape(local_length, local_heads * HEAD_WIDTH)

    attended = lax.map(one_sequence, (query_rows, whole_keys, whole_values))
    flat_attended = attended.reshape(batch_count * local_length, local_heads * HEAD_WIDTH)
    projected = lax.psum_scatter(
        jnp.dot(flat_attended, whole_proj, preferred_element_type=jnp.float32).astype(jnp.bfloat16),
        "role",
        scatter_dimension=0,
        tiled=True,
    ).astype(jnp.float32)
    hidden = residual[0].astype(jnp.float32) + projected
    variance = jnp.mean(hidden * hidden, axis=-1, keepdims=True)
    normed = (hidden * lax.rsqrt(variance + epsilon) * norm_gain).astype(jnp.bfloat16)
    expert_ids = route_experts.reshape(-1)
    gate_values = route_gates.reshape(-1)
    experts_local = gate_weight.shape[0]
    device_count = seq_count * role_count
    expert_count = experts_local * device_count
    assign = expert_ids.shape[0]
    capacity = assign // expert_count + 1
    onehot = (expert_ids[:, None] == jnp.arange(expert_count, dtype=jnp.int32)[None, :]).astype(
        jnp.int32
    )
    earlier = jnp.cumsum(onehot, axis=0) - onehot
    slot_rank = jnp.sum(earlier * onehot, axis=1)
    slot_index = expert_ids * capacity + slot_rank
    source_token = jnp.arange(assign, dtype=jnp.int32) // TOPK
    slot_token = jnp.zeros((expert_count * capacity,), jnp.int32).at[slot_index].set(source_token)
    slot_used = jnp.zeros((expert_count * capacity,), jnp.bfloat16).at[slot_index].set(1.0)
    outgoing = (normed[slot_token] * slot_used[:, None]).reshape(
        device_count, experts_local, capacity, D
    )
    incoming = lax.all_to_all(outgoing, ("seq", "role"), split_axis=0, concat_axis=0, tiled=True)
    gate_hidden = jnp.einsum(
        "sjcd,jdf->sjcf", incoming, gate_weight, preferred_element_type=jnp.float32
    )
    up_hidden = jnp.einsum(
        "sjcd,jdf->sjcf", incoming, up_weight, preferred_element_type=jnp.float32
    )
    activated = (jax.nn.silu(gate_hidden) * up_hidden).astype(jnp.bfloat16)
    returned = lax.all_to_all(
        jnp.einsum(
            "sjcf,jfd->sjcd", activated, down_weight, preferred_element_type=jnp.float32
        ).astype(jnp.bfloat16),
        ("seq", "role"),
        split_axis=0,
        concat_axis=0,
        tiled=True,
    )
    gathered = returned.reshape(expert_count * capacity, D)[slot_index]
    weighted = gathered.astype(jnp.float32) * gate_values[:, None]
    expert_sum = jnp.sum(weighted.reshape(-1, TOPK, D), axis=1)
    return (hidden + expert_sum).astype(jnp.bfloat16).reshape(residual.shape)


def in_hbm(*arrays):
    return [pltpu.with_memory_space_constraint(array, pltpu.HBM) for array in arrays]


def hbm_specs(count):
    return [pl.BlockSpec(memory_space=pltpu.HBM)] * count


def fetch_scratch(*arrays):
    return [pltpu.VMEM(array.shape, array.dtype) for array in arrays] + [
        pltpu.SemaphoreType.DMA((len(arrays),))
    ]


def start_fetch(from_refs, scratch):
    *buffers, sems = scratch
    copies = [
        pltpu.make_async_copy(from_ref, buffer, sems.at[n])
        for n, (from_ref, buffer) in enumerate(zip(from_refs, buffers))
    ]
    for copy in copies:
        copy.start()
    return copies, buffers


def in_vmem(count):
    return [pl.BlockSpec(memory_space=pltpu.VMEM)] * count


def attend_kernel(seq_count, role_count, slots, groups, at_ref, *refs):
    last_block, proj_ref, *refs = refs
    count = seq_count
    attended_ref, *partial_refs = refs[count : count + 1 + len(groups)]
    copies, (query_ref, *buffers) = start_fetch(refs[:count], refs[count + 1 + len(groups) :])
    blocks = buffers + [last_block]
    seq_index, role_index = at_ref[0], at_ref[1]
    local_length = query_ref.shape[1]
    local_heads = query_ref.shape[2] // HEAD_WIDTH
    per_role = local_length // role_count
    rows = local_heads * local_length
    keys_all = seq_count * local_length
    slot = lax.broadcasted_iota(jnp.int32, (rows, keys_all), 1)
    block_number, within = slot // local_length, slot % local_length
    key_position = (
        (seq_index ^ block_number) * local_length
        + (role_index ^ (within // per_role)) * per_role
        + within % per_role
    )
    query_position = (
        seq_index * local_length
        + lax.broadcasted_iota(jnp.int32, (rows, keys_all), 0) % local_length
    )
    seen = key_position <= query_position
    scale = HEAD_WIDTH ** (-0.5)
    for copy in copies:
        copy.wait()
    for n, k in enumerate(slots):
        b = role_index ^ k
        own = query_ref[b]
        queries = jnp.concatenate(
            [own[:, h * HEAD_WIDTH : (h + 1) * HEAD_WIDTH] for h in range(local_heads)], axis=0
        )
        key_value = jnp.concatenate([block[b] for block in blocks], axis=0)
        keys, values = key_value[:, :HEAD_WIDTH], key_value[:, HEAD_WIDTH:]
        scores = lax.dot_general(
            queries, keys, (((1,), (1,)), ((), ())), preferred_element_type=jnp.float32
        )
        scores = jnp.where(seen, scores * scale, masked_score)
        weights = jnp.exp(scores - jnp.max(scores, axis=1, keepdims=True))
        totals = jnp.sum(weights, axis=1, keepdims=True)
        mixed = jnp.dot(weights.astype(jnp.bfloat16), values, preferred_element_type=jnp.float32)
        attended = (mixed / totals).astype(jnp.bfloat16)
        for h in range(local_heads):
            attended_ref[
                n * local_length : (n + 1) * local_length, h * HEAD_WIDTH : (h + 1) * HEAD_WIDTH
            ] = attended[h * local_length : (h + 1) * local_length]
    project_into(slots, groups, attended_ref, proj_ref, partial_refs)


def columns_kernel(*refs):
    *from_refs, to_ref, sems = refs
    copies, at = [], 0
    for n, ref in enumerate(from_refs):
        width = ref.shape[1]
        copies.append(pltpu.make_async_copy(ref, to_ref.at[:, at : at + width], sems.at[n]))
        copies[-1].start()
        at += width
    for copy in copies:
        copy.wait()


def join_kernel(*refs):
    *piece_refs, out_ref = refs
    at = 0
    for ref in piece_refs:
        size = ref.shape[1]
        out_ref[:, at : at + size, :] = ref[...]
        at += size


def role_groups(role_count):
    last = role_count // 2
    bits = [1 << n for n in range(last.bit_length() - 1)]
    return [[k for k in range(role_count) if k & -k == bit] for bit in bits] + [[0, last]]


def project_into(slots, groups, attended_ref, proj_ref, partial_refs):
    slots = list(slots)
    rows = attended_ref.shape[0] // len(slots)
    width = 512 if proj_ref.shape[1] % 512 == 0 else proj_ref.shape[1]
    for at in range(0, proj_ref.shape[1], width):
        product = jnp.dot(
            attended_ref[...], proj_ref[:, at : at + width], preferred_element_type=jnp.float32
        ).astype(jnp.bfloat16)
        for group, partial_ref in zip(groups, partial_refs):
            for n, k in enumerate(group):
                start = slots.index(k) * rows
                partial_ref[n * rows : (n + 1) * rows, at : at + width] = product[
                    start : start + rows
                ]


def project_kernel(slots, groups, attended_ref, proj_ref, order_ref, *partial_refs):
    project_into(slots, groups, attended_ref, proj_ref, partial_refs)


def partial_shapes(groups, rows, width):
    return [jax.ShapeDtypeStruct((rows * len(group), width), jnp.bfloat16) for group in groups]


def near_sum_kernel(route_ref, other_route_ref, came_ref, sent_any, *refs):
    out_refs, both_ref = refs[:2], refs[2]
    copies, (sent,) = start_fetch([sent_any], refs[3:])
    rows, width = sent.shape[0] // 2, sent.shape[1]
    lane = lax.broadcasted_iota(jnp.int32, (rows, GATE_COLUMNS), 1)
    half = GATE_COLUMNS // 2
    expert = (lane % half).astype(jnp.float32)
    for p, routes in enumerate((route_ref, other_route_ref)):
        shares = jnp.zeros((rows, GATE_COLUMNS), jnp.float32)
        routed = routes.shape[1] // 2
        for k in range(routed):
            named, weight = routes[:, k : k + 1], routes[:, routed + k : routed + k + 1]
            shares = shares + jnp.where(expert == named, weight, 0.0)
        first = shares.astype(jnp.bfloat16).astype(jnp.float32)
        terms = jnp.where(lane < half, first, shares - first).astype(jnp.bfloat16)
        out_refs[p][:, width:] = terms
        both_ref[p * rows : (p + 1) * rows, width:] = terms
    copies[0].wait()
    for p in range(2):
        total = sent[p * rows : (p + 1) * rows].astype(jnp.float32)
        total = total + came_ref[(1 - p) * rows : (2 - p) * rows].astype(jnp.float32)
        out_refs[p][:, :width] = total.astype(jnp.bfloat16)
        both_ref[p * rows : (p + 1) * rows, :width] = total.astype(jnp.bfloat16)


def far_sum_kernel(rows, order_count, *refs):
    refs = refs[order_count:]
    chips = (len(refs) - 4) // 3
    came_refs, sent_any = refs[:chips], refs[chips : 2 * chips]
    own_ref, other_ref, both_ref = refs[2 * chips : 2 * chips + 3]
    copies, sent_refs = start_fetch(sent_any, refs[2 * chips + 3 :])
    for copy in copies:
        copy.wait()
    size = chips * rows
    for n, (sent, came) in enumerate(zip(sent_refs, came_refs)):
        to = slice(n * rows, (n + 1) * rows)
        for p, out_ref in enumerate((own_ref, other_ref)):
            total = sent[p * rows : (p + 1) * rows].astype(jnp.float32)
            total = total + came[(1 - p) * rows : (2 - p) * rows].astype(jnp.float32)
            out_ref[to] = total.astype(jnp.bfloat16)
            both_ref[p * size + n * rows : p * size + (n + 1) * rows] = total.astype(jnp.bfloat16)


def norm_kernel(chips, near_row, far_row, at_ref, gain_ref, *refs):
    parts, (normed_ref, *hidden_refs, whole_ref) = refs[: 2 * chips], refs[2 * chips :]
    seq_index = at_ref[0]
    features = whole_ref.shape[1]
    rows = whole_ref.shape[0] // chips
    width = features // chips // 2
    for n in range(chips):
        near, far = parts[2 * n : 2 * n + 2]
        for m in range(chips):
            part = far if m else near
            first = ((far_row if m else near_row) if n else 0) + (m - 1 if m else 0) * rows
            to = slice((n ^ m) * rows, ((n ^ m) + 1) * rows)
            for j in range(2):
                start = pl.multiple_of((seq_index ^ (2 * n + j)) * width, width)
                whole_ref[to, pl.ds(start, width)] = part[
                    first : first + rows, j * width : (j + 1) * width
                ].astype(jnp.float32)
        first = near_row if n else 0
        normed_ref[n * rows : (n + 1) * rows, features:] = near[first : first + rows, 2 * width :]
    hidden = whole_ref[...]
    variance = jnp.mean(hidden * hidden, axis=1, keepdims=True)
    normed = hidden * lax.rsqrt(variance + epsilon) * gain_ref[...]
    normed_ref[:, :features] = normed.astype(jnp.bfloat16)
    for hidden_ref in hidden_refs:
        hidden_ref[...] = hidden[:rows]


def expert_kernel(token_count, at_ref, *refs):
    token_refs = refs[:token_count]
    gate_ref, up_ref, down_ref, keep_ref, send_ref, activated_ref = refs[token_count:]
    features, units = gate_ref.shape[1:]
    tokens = jnp.concatenate([ref[:, :features] for ref in token_refs], axis=0)
    gates = jnp.concatenate([ref[:, features:] for ref in token_refs], axis=0)
    lane = lax.broadcasted_iota(jnp.int32, gates.shape, 1)
    mine = lane % (GATE_COLUMNS // 2) == at_ref[2]
    share = jnp.sum(jnp.where(mine, gates.astype(jnp.float32), 0.0), axis=1, keepdims=True)
    block = 256 if units % 256 == 0 else units
    for f in range(0, units, block):
        gate_hidden = jnp.dot(
            tokens, gate_ref[0, :, f : f + block], preferred_element_type=jnp.float32
        )
        up_hidden = jnp.dot(tokens, up_ref[0, :, f : f + block], preferred_element_type=jnp.float32)
        activated_ref[:, f : f + block] = (
            gate_hidden / (1.0 + jnp.exp(-gate_hidden)) * up_hidden
        ).astype(jnp.bfloat16)
    kept = keep_ref.shape[0]
    block = 512 if features % 512 == 0 else features
    for c in range(0, features, block):
        product = jnp.dot(
            activated_ref[...], down_ref[0, :, c : c + block], preferred_element_type=jnp.float32
        )
        product = (product * share).astype(jnp.bfloat16)
        keep_ref[:, c : c + block] = product[:kept]
        send_ref[:, c : c + block] = product[kept:]


def run_expert(at, tokens, gate_weight, up_weight, down_weight):
    units = gate_weight.shape[2]
    width = gate_weight.shape[1]
    rows = sum(part.shape[0] for part in tokens)
    half = jax.ShapeDtypeStruct((rows // 2, width), jnp.bfloat16)
    return pl.pallas_call(
        partial(expert_kernel, len(tokens)),
        in_specs=[pl.BlockSpec(memory_space=pltpu.SMEM)] + in_vmem(len(tokens) + 3),
        out_specs=in_vmem(2),
        out_shape=[half, half],
        scratch_shapes=[pltpu.VMEM((rows, units), jnp.bfloat16)],
        compiler_params=pltpu.CompilerParams(vmem_limit_bytes=EXPERT_VMEM),
        cost_estimate=NOTHING,
    )(at, *tokens, gate_weight, up_weight, down_weight)


def after(array, *others):
    return lax.optimization_barrier((array, *others))[0]


def added(terms):
    total = terms[0].astype(jnp.float32)
    for term in terms[1:]:
        total = total + term.astype(jnp.float32)
    return total


def gathered_shards(
    query_rows,
    encoded_key_rows,
    value_matrix_rows,
    output_weight,
    residual,
    norm_gain,
    route_experts,
    route_gates,
    gate_weight,
    up_weight,
    down_weight,
):
    seq_count = lax.axis_size("seq")
    role_count = lax.axis_size("role")
    seq_index = lax.axis_index("seq")
    role_index = lax.axis_index("role")
    batch_count, local_length, query_width = query_rows.shape
    local_heads = query_width // HEAD_WIDTH
    group_width = QUERY_HEADS // KEY_VALUE_HEADS
    role_bits = [1 << n for n in range(role_count.bit_length() - 1)]
    at = jnp.stack([seq_index, role_index, seq_index * role_count + role_index]).astype(jnp.int32)

    def over_role(array, k):
        return lax.ppermute(array, "role", [(i, i ^ k) for i in range(role_count)])

    def over_seq(array, j):
        return lax.ppermute(array, "seq", [(i, i ^ j) for i in range(seq_count)])

    beside_proj = over_seq(output_weight, 1)
    block_width = output_weight.shape[1]
    across_steps = range(2, seq_count, 2)

    pieces = []
    for k in range(role_count):
        head = ((role_index ^ k) * local_heads // group_width) * HEAD_WIDTH
        piece = jnp.concatenate(
            [
                lax.dynamic_slice_in_dim(encoded_key_rows, head, HEAD_WIDTH, 2),
                lax.dynamic_slice_in_dim(value_matrix_rows, head, HEAD_WIDTH, 2),
            ],
            axis=2,
        )
        pieces.append(piece)
    near_proj = pl.pallas_call(
        columns_kernel,
        in_specs=hbm_specs(1) + in_vmem(1),
        out_specs=pl.BlockSpec(memory_space=pltpu.VMEM),
        out_shape=jax.ShapeDtypeStruct((query_width, 2 * block_width), jnp.bfloat16),
        scratch_shapes=[pltpu.SemaphoreType.DMA((2,))],
        compiler_params=pltpu.CompilerParams(vmem_limit_bytes=COPY_VMEM),
        cost_estimate=NOTHING,
    )(*in_hbm(output_weight), beside_proj)
    pieces[1] = after(pieces[1], near_proj)
    pieces = [piece if k == 0 else over_role(piece, k) for k, piece in enumerate(pieces)]
    block = pl.pallas_call(
        join_kernel,
        in_specs=in_vmem(len(pieces)),
        out_specs=pl.BlockSpec(memory_space=pltpu.VMEM),
        out_shape=jax.ShapeDtypeStruct(
            (batch_count, local_length, 2 * HEAD_WIDTH), jnp.bfloat16
        ),
        compiler_params=pltpu.CompilerParams(vmem_limit_bytes=COPY_VMEM),
        cost_estimate=SHORT,
    )(*pieces)
    same_core = [block] + [over_seq(block, j) for j in across_steps]
    blocks = []
    for part in same_core:
        blocks += [part, over_seq(part, 1)]
    last = role_count // 2
    routes = jnp.concatenate([route_experts[0].astype(jnp.float32), route_gates[0]], axis=1)
    residual_blocks = [
        lax.dynamic_slice_in_dim(residual[0], (seq_index ^ j) * block_width, block_width, 1)
        for j in range(seq_count)
    ]
    residuals = [
        jnp.concatenate(residual_blocks[j : j + 2], axis=1) for j in range(0, seq_count, 2)
    ]

    rows = batch_count * local_length
    near_width = 2 * output_weight.shape[1]
    groups = role_groups(role_count)
    attend_args = in_hbm(query_rows, *blocks[:-1])
    slot_sets = [(range(1, role_count, 2), groups[:1]), (range(0, role_count, 2), groups[1:])]
    attended, near = [], []
    for slots, parts in slot_sets:
        half_rows = jax.ShapeDtypeStruct((rows // 2, query_width), jnp.bfloat16)
        half, *partials = pl.pallas_call(
            partial(attend_kernel, seq_count, role_count, slots, parts),
            in_specs=[pl.BlockSpec(memory_space=pltpu.SMEM)]
            + in_vmem(2)
            + hbm_specs(len(attend_args)),
            out_specs=in_vmem(1 + len(parts)),
            out_shape=[half_rows] + partial_shapes(parts, local_length, near_width),
            scratch_shapes=fetch_scratch(*attend_args),
            compiler_params=pltpu.CompilerParams(vmem_limit_bytes=SMALL_VMEM),
            cost_estimate=SHORT,
        )(at, blocks[-1], near_proj, *attend_args)
        attended.append(half)
        near += partials

    for j in across_steps:
        residuals[j // 2] = over_seq(after(residuals[j // 2], attended[1]), j)
    other_routes = over_role(routes, last)

    def summed_over_role(parts, extra, *before):
        terms = [[part] for part in parts]
        for n, group in enumerate(groups[:-1]):
            bit = 1 << n
            leaving = terms[n][0] if len(terms[n]) == 1 else added(terms[n]).astype(jnp.bfloat16)
            came = over_role(leaving, bit)
            for m in range(n + 1, len(groups)):
                at_rows = [group.index(k ^ bit) for k in groups[m]]
                if at_rows == list(range(len(group))):
                    terms[m].append(came)
                else:
                    split = [came[i * local_length : (i + 1) * local_length] for i in at_rows]
                    terms[m].append(jnp.concatenate(split, axis=0))
        extra = jnp.pad(after(extra, *before) if before else extra, ((0, local_length), (0, 0)))
        sent = added(terms[-1] + [extra]).astype(jnp.bfloat16)
        return sent

    near_sent = summed_over_role(near, residuals[0])
    near_came = over_role(near_sent, last)
    near_args = in_hbm(near_sent)
    own_shape, both_shape = [
        jax.ShapeDtypeStruct((size, near_width + GATE_COLUMNS), jnp.bfloat16)
        for size in (local_length, 2 * local_length)
    ]
    near_halves = pl.pallas_call(
        near_sum_kernel,
        in_specs=in_vmem(3) + hbm_specs(1),
        out_specs=in_vmem(3),
        out_shape=[own_shape, own_shape, both_shape],
        scratch_shapes=fetch_scratch(*near_args),
        compiler_params=pltpu.CompilerParams(vmem_limit_bytes=SMALL_VMEM),
        cost_estimate=LONG,
    )(routes, other_routes, near_came, *near_args)

    def walk(k, bits):
        found = [k]
        for n, bit in enumerate(bits):
            found += walk(k | bit, bits[n + 1 :])
        return found

    lower_bits = role_bits[:-1][::-1]
    order = walk(last, lower_bits) + walk(0, lower_bits)
    far_plane, final = order[1], order[-1]

    def across(part):
        return [over_seq(part, j) for j in across_steps]

    def spread(own, other, both, ordered):
        planes, crossed = {0: own, last: other}, {}
        both_across = across(both)
        size = own.shape[0]
        for k in order:
            if k not in planes:
                bit = k & -k
                held = planes[k ^ bit]
                wait = ordered and k < last
                planes[k] = over_role(after(held, planes[far_plane]) if wait else held, bit)
            if k in (0, last):
                crossed[k] = both_across
            elif k < last:
                source = k ^ (k & -k)
                came = [part[:size] for part in crossed[source]] if source == 0 else crossed[source]
                crossed[k] = [over_role(part, k & -k) for part in came]
            else:
                crossed[k] = across(after(planes[k], *both_across))
        return planes, crossed

    near_planes, near_crossed = spread(*near_halves, False)

    sent, came = [], []
    for n, j in enumerate(across_steps, 1):
        far = []
        for half, (slots, parts) in zip(attended, slot_sets):
            far += pl.pallas_call(
                partial(project_kernel, slots, parts),
                in_specs=in_vmem(2) + [pl.BlockSpec(memory_space=pl.ANY)],
                out_specs=in_vmem(len(parts)),
                out_shape=partial_shapes(parts, local_length, near_width),
                compiler_params=pltpu.CompilerParams(vmem_limit_bytes=SMALL_VMEM),
                cost_estimate=SHORT,
            )(over_seq(half, j), near_proj, other_routes)
        sent.append(summed_over_role(far, residuals[n], near_halves[0]))
        came.append(over_role(sent[-1], last))

    chips = 1 + len(across_steps)
    far_args = in_hbm(*sent)
    far_rows = (chips - 1) * local_length
    far_shape, far_both_shape = [
        jax.ShapeDtypeStruct((size, near_width), jnp.bfloat16) for size in (far_rows, 2 * far_rows)
    ]
    first_come = [*near_crossed[0], near_planes[far_plane], *near_crossed[far_plane]]
    first_come.append(near_planes[final])
    far_halves = pl.pallas_call(
        partial(far_sum_kernel, local_length, len(first_come)),
        in_specs=[pl.BlockSpec(memory_space=pl.ANY)] * len(first_come)
        + in_vmem(len(came))
        + hbm_specs(len(far_args)),
        out_specs=in_vmem(3),
        out_shape=[far_shape, far_shape, far_both_shape],
        scratch_shapes=fetch_scratch(*far_args),
        compiler_params=pltpu.CompilerParams(vmem_limit_bytes=SMALL_VMEM),
        cost_estimate=SHORT,
    )(*first_come, *came, *far_args)
    far_own, far_other, far_both = far_halves
    far_other = after(far_other, *near_crossed[final])
    far_planes, far_crossed = spread(far_own, far_other, far_both, True)

    width = residual.shape[2]
    gain = norm_gain.reshape(1, width)

    def normed_rows(parts, second, *hidden_shape):
        rows = chips * local_length
        firsts = (local_length, far_rows) if second else (0, 0)
        return pl.pallas_call(
            partial(norm_kernel, chips, *firsts),
            in_specs=[pl.BlockSpec(memory_space=pltpu.SMEM)] + in_vmem(1 + 2 * chips),
            out_specs=in_vmem(1 + len(hidden_shape)),
            out_shape=[
                jax.ShapeDtypeStruct((rows, width + GATE_COLUMNS), jnp.bfloat16),
                *hidden_shape,
            ],
            scratch_shapes=[pltpu.VMEM((rows, width), jnp.float32)],
            compiler_params=pltpu.CompilerParams(vmem_limit_bytes=SMALL_VMEM),
            cost_estimate=NOTHING,
        )(at, gain, *parts)

    keep, send, slots, leaving, passed = {}, {}, {}, {}, {}

    hidden_shape = jax.ShapeDtypeStruct((local_length, width), jnp.float32)
    hidden = []

    hidden_shape = jax.ShapeDtypeStruct((local_length, width), jnp.float32)
    hidden = []

    def prepared(k, *first):
        late = far_crossed[k]
        if first:
            late = [after(part, *first) for part in late]
        parts = [near_planes[k], far_planes[k]]
        for pair in zip(near_crossed[k], late):
            parts += pair
        normed, *own = normed_rows(parts, k == last, *([] if k else [hidden_shape]))
        hidden.extend(own)
        return [normed, over_seq(normed, 1)]

    def expert(tokens, *others):
        if others:
            tokens = lax.optimization_barrier((*tokens, *others))[: len(tokens)]
        return run_expert(at, tokens, gate_weight, up_weight, down_weight)

    def combine(k, *before):
        came = over_seq(after(send[k], *before) if before else send[k], 1)
        sums = []
        for n in range(len(across_steps)):
            chunk = slice((n + 1) * local_length, (n + 2) * local_length)
            sums.append(added([keep[k][chunk], came[chunk]]).astype(jnp.bfloat16))
        return [keep[k][:local_length], came[:local_length]], sums

    def pass_on(k):
        passed[k] = [over_seq(part, j) for part, j in zip(leaving[k], across_steps)]
        slots[k] += passed[k]

    ready = {far_plane: prepared(far_plane, far_planes[final], *far_crossed[final])}
    ready[final] = prepared(final)
    keep[far_plane], send[far_plane] = expert(ready[far_plane], ready[final][0])
    ready |= {k: prepared(k, keep[far_plane]) for k in (last, 0)}
    slots[far_plane], leaving[far_plane] = combine(far_plane)
    leaving[far_plane] = [after(part, ready[last][0], ready[0][0]) for part in leaving[far_plane]]
    pass_on(far_plane)
    keep[last], send[last] = expert(ready[last], keep[far_plane], *leaving[far_plane])
    slots[last], leaving[last] = combine(last)
    leaving[last] = [after(part, *passed[far_plane]) for part in leaving[last]]
    pass_on(last)
    keep[final], send[final] = expert(ready[final], keep[last])
    slots[far_plane] = [added(slots[far_plane]).astype(jnp.bfloat16)]
    slots[final], leaving[final] = combine(final, *passed[far_plane])
    leaving[final] = [after(part, *leaving[last]) for part in leaving[final]]
    pass_on(final)
    keep[0], send[0] = expert(ready[0], keep[final], *leaving[last])
    slots[0], leaving[0] = combine(0, *passed[last])
    leaving[0] = [after(part, *leaving[final]) for part in leaving[0]]
    pass_on(0)
    for bit in role_bits:
        for k in [k for k in sorted(slots, reverse=True) if k & bit]:
            going = added(slots.pop(k)).astype(jnp.bfloat16)
            if k == last:
                going = after(going, *leaving[final])
            slots[k ^ bit].append(over_role(going, bit))
    return added(hidden + slots[0]).astype(jnp.bfloat16).reshape(residual.shape)


def solution(mesh):
    placed = (
        P("groups", "seq", "role"),
        P("groups", ("seq", "role"), None),
        P("groups", ("seq", "role"), None),
        P("role", "seq"),
        P(("groups", "role"), "seq", None),
        P(),
        P(("groups", "role"), "seq", None),
        P(("groups", "role"), "seq", None),
        P(("seq", "role"), None, None),
        P(("seq", "role"), None, None),
        P(("seq", "role"), None, None),
    )
    experts = mesh.shape["seq"] * mesh.shape["role"]
    return jax.shard_map(
        gathered_shards if experts <= 2 * TOPK else routed_shards,
        mesh=mesh,
        in_specs=placed,
        out_specs=P(("groups", "role"), "seq", None),
        check_vma=False,
    )
```

```python
from functools import partial

import jax
import jax.numpy as jnp
from jax import lax
from jax.experimental import pallas as pl
from jax.experimental.pallas import tpu as pltpu
from jax.sharding import PartitionSpec as P

D = 2048
QUERY_HEADS = 32
KEY_VALUE_HEADS = 4
HEAD_WIDTH = 128
TOPK = 8


epsilon = 1e-06
masked_score = -1e30
EXPERT_VMEM = 16 * 2**20
SMALL_VMEM = 12 * 2**20
COPY_VMEM = 4 * 2**20
GATE_COLUMNS = 128
NOTHING = pl.CostEstimate(flops=1, bytes_accessed=1, transcendentals=0)
SHORT = pl.CostEstimate(flops=2 * 10**9, bytes_accessed=4 * 2**20, transcendentals=0)
LONG = pl.CostEstimate(flops=10**10, bytes_accessed=1, transcendentals=0)


def score_block(queries, every_key, query_position, block_start, block_width, score_scale):
    keys_part = lax.slice_in_dim(every_key, block_start, block_start + block_width, axis=0)
    raw_scores = (
        jnp.einsum("qhd,kd->hqk", queries, keys_part, preferred_element_type=jnp.float32)
        * score_scale
    )
    key_position = block_start + jnp.arange(block_width, dtype=jnp.int32)
    return jnp.where(
        key_position[None, None, :] <= query_position[None, :, None], raw_scores, masked_score
    )


def value_block(rounded, every_value, block_start, block_width):
    prob_block = lax.slice_in_dim(rounded, block_start, block_start + block_width, axis=2)
    values_part = lax.slice_in_dim(every_value, block_start, block_start + block_width, axis=0)
    return jnp.einsum("hqk,kd->qhd", prob_block, values_part, preferred_element_type=jnp.float32)


def routed_shards(
    query_rows,
    encoded_key_rows,
    value_matrix_rows,
    output_weight,
    residual,
    norm_gain,
    route_experts,
    route_gates,
    gate_weight,
    up_weight,
    down_weight,
):
    seq_count = lax.axis_size("seq")
    role_count = lax.axis_size("role")
    seq_index = lax.axis_index("seq")
    role_index = lax.axis_index("role")
    batch_count = query_rows.shape[0]
    local_length = query_rows.shape[1]
    local_heads = query_rows.shape[2] // HEAD_WIDTH
    full_length = local_length * seq_count
    query_group_width = QUERY_HEADS // KEY_VALUE_HEADS
    head_pick = role_index * local_heads // query_group_width
    role_keys, role_values = (
        lax.all_gather(encoded_key_rows, "role", axis=1, tiled=True),
        lax.all_gather(value_matrix_rows, "role", axis=1, tiled=True),
    )
    head_keys = lax.dynamic_slice_in_dim(role_keys, head_pick * HEAD_WIDTH, HEAD_WIDTH, 2)
    head_values = lax.dynamic_slice_in_dim(role_values, head_pick * HEAD_WIDTH, HEAD_WIDTH, 2)
    whole_keys, whole_values, whole_proj = (
        lax.all_gather(head_keys, "seq", axis=1, tiled=True),
        lax.all_gather(head_values, "seq", axis=1, tiled=True),
        lax.all_gather(output_weight, "seq", axis=1, tiled=True),
    )
    key_width = full_length // 8
    score_scale = HEAD_WIDTH ** (-0.5)
    query_position = seq_index * local_length + jnp.arange(local_length, dtype=jnp.int32)
    last_needed = (seq_index + 1) * local_length

    def one_sequence(operands):
        own_queries, every_key, every_value = operands
        queries = own_queries.reshape(local_length, local_heads, HEAD_WIDTH)
        pieces = []
        for number in range(8):
            block_start = number * key_width
            compute = partial(
                score_block, queries, every_key, query_position, block_start, key_width, score_scale
            )
            skipped = partial(
                jnp.full, (local_heads, local_length, key_width), masked_score, jnp.float32
            )
            pieces.append(lax.cond(block_start < last_needed, compute, skipped))
        scores = jnp.concatenate(pieces, axis=2)
        row_peak = jnp.max(scores, axis=2, keepdims=True)
        weights = jnp.exp(scores - row_peak)
        totals = jnp.sum(weights, axis=2, keepdims=True)
        rounded = weights.astype(jnp.bfloat16)
        mixed_rows = jnp.zeros((local_length, local_heads, HEAD_WIDTH), jnp.float32)
        for number in range(8):
            block_start = number * key_width
            product = partial(value_block, rounded, every_value, block_start, key_width)
            nothing = partial(jnp.zeros, (local_length, local_heads, HEAD_WIDTH), jnp.float32)
            mixed_rows = mixed_rows + lax.cond(block_start < last_needed, product, nothing)
        attended = (mixed_rows / totals.transpose(1, 0, 2)).astype(jnp.bfloat16)
        return attended.reshape(local_length, local_heads * HEAD_WIDTH)

    attended = lax.map(one_sequence, (query_rows, whole_keys, whole_values))
    flat_attended = attended.reshape(batch_count * local_length, local_heads * HEAD_WIDTH)
    projected = lax.psum_scatter(
        jnp.dot(flat_attended, whole_proj, preferred_element_type=jnp.float32).astype(jnp.bfloat16),
        "role",
        scatter_dimension=0,
        tiled=True,
    ).astype(jnp.float32)
    hidden = residual[0].astype(jnp.float32) + projected
    variance = jnp.mean(hidden * hidden, axis=-1, keepdims=True)
    normed = (hidden * lax.rsqrt(variance + epsilon) * norm_gain).astype(jnp.bfloat16)
    expert_ids = route_experts.reshape(-1)
    gate_values = route_gates.reshape(-1)
    experts_local = gate_weight.shape[0]
    device_count = seq_count * role_count
    expert_count = experts_local * device_count
    assign = expert_ids.shape[0]
    capacity = assign // expert_count + 1
    onehot = (expert_ids[:, None] == jnp.arange(expert_count, dtype=jnp.int32)[None, :]).astype(
        jnp.int32
    )
    earlier = jnp.cumsum(onehot, axis=0) - onehot
    slot_rank = jnp.sum(earlier * onehot, axis=1)
    slot_index = expert_ids * capacity + slot_rank
    source_token = jnp.arange(assign, dtype=jnp.int32) // TOPK
    slot_token = jnp.zeros((expert_count * capacity,), jnp.int32).at[slot_index].set(source_token)
    slot_used = jnp.zeros((expert_count * capacity,), jnp.bfloat16).at[slot_index].set(1.0)
    outgoing = (normed[slot_token] * slot_used[:, None]).reshape(
        device_count, experts_local, capacity, D
    )
    incoming = lax.all_to_all(outgoing, ("seq", "role"), split_axis=0, concat_axis=0, tiled=True)
    gate_hidden = jnp.einsum(
        "sjcd,jdf->sjcf", incoming, gate_weight, preferred_element_type=jnp.float32
    )
    up_hidden = jnp.einsum(
        "sjcd,jdf->sjcf", incoming, up_weight, preferred_element_type=jnp.float32
    )
    activated = (jax.nn.silu(gate_hidden) * up_hidden).astype(jnp.bfloat16)
    returned = lax.all_to_all(
        jnp.einsum(
            "sjcf,jfd->sjcd", activated, down_weight, preferred_element_type=jnp.float32
        ).astype(jnp.bfloat16),
        ("seq", "role"),
        split_axis=0,
        concat_axis=0,
        tiled=True,
    )
    gathered = returned.reshape(expert_count * capacity, D)[slot_index]
    weighted = gathered.astype(jnp.float32) * gate_values[:, None]
    expert_sum = jnp.sum(weighted.reshape(-1, TOPK, D), axis=1)
    return (hidden + expert_sum).astype(jnp.bfloat16).reshape(residual.shape)


def in_hbm(*arrays):
    return [pltpu.with_memory_space_constraint(array, pltpu.HBM) for array in arrays]


def hbm_specs(count):
    return [pl.BlockSpec(memory_space=pltpu.HBM)] * count


def fetch_scratch(*arrays):
    return [pltpu.VMEM(array.shape, array.dtype) for array in arrays] + [
        pltpu.SemaphoreType.DMA((len(arrays),))
    ]


def start_fetch(from_refs, scratch):
    *buffers, sems = scratch
    copies = [
        pltpu.make_async_copy(from_ref, buffer, sems.at[n])
        for n, (from_ref, buffer) in enumerate(zip(from_refs, buffers))
    ]
    for copy in copies:
        copy.start()
    return copies, buffers


def in_vmem(count):
    return [pl.BlockSpec(memory_space=pltpu.VMEM)] * count


def attend_kernel(seq_count, role_count, slots, groups, at_ref, *refs):
    last_block, proj_ref, *refs = refs
    count = seq_count
    attended_ref, *partial_refs = refs[count : count + 1 + len(groups)]
    copies, (query_ref, *buffers) = start_fetch(refs[:count], refs[count + 1 + len(groups) :])
    blocks = buffers + [last_block]
    seq_index, role_index = at_ref[0], at_ref[1]
    local_length = query_ref.shape[1]
    local_heads = query_ref.shape[2] // HEAD_WIDTH
    per_role = local_length // role_count
    heads = max(n for n in range(1, local_heads + 1) if local_heads % n == 0 and n * local_length <= 128)
    rows = heads * local_length
    keys_all = seq_count * local_length
    slot = lax.broadcasted_iota(jnp.int32, (rows, keys_all), 1)
    block_number, within = slot // local_length, slot % local_length
    key_position = (
        (seq_index ^ block_number) * local_length
        + (role_index ^ (within // per_role)) * per_role
        + within % per_role
    )
    query_position = (
        seq_index * local_length
        + lax.broadcasted_iota(jnp.int32, (rows, keys_all), 0) % local_length
    )
    seen = key_position <= query_position
    scale = HEAD_WIDTH ** (-0.5)
    for copy in copies:
        copy.wait()
    for n, k in enumerate(slots):
        b = role_index ^ k
        own = query_ref[b]
        key_value = jnp.concatenate([block[b] for block in blocks], axis=0)
        keys, values = key_value[:, :HEAD_WIDTH], key_value[:, HEAD_WIDTH:]
        for first in range(0, local_heads, heads):
            chosen = range(first, first + heads)
            queries = jnp.concatenate(
                [own[:, h * HEAD_WIDTH : (h + 1) * HEAD_WIDTH] for h in chosen], axis=0
            )
            scores = lax.dot_general(
                queries, keys, (((1,), (1,)), ((), ())), preferred_element_type=jnp.float32
            )
            scores = jnp.where(seen, scores * scale, masked_score)
            weights = jnp.exp(scores - jnp.max(scores, axis=1, keepdims=True))
            totals = jnp.sum(weights, axis=1, keepdims=True)
            mixed = jnp.dot(
                weights.astype(jnp.bfloat16), values, preferred_element_type=jnp.float32
            )
            attended = (mixed / totals).astype(jnp.bfloat16)
            for i, h in enumerate(chosen):
                attended_ref[
                    n * local_length : (n + 1) * local_length,
                    h * HEAD_WIDTH : (h + 1) * HEAD_WIDTH,
                ] = attended[i * local_length : (i + 1) * local_length]
    project_into(slots, groups, attended_ref, proj_ref, partial_refs)


def columns_kernel(*refs):
    *from_refs, to_ref, sems = refs
    copies, at = [], 0
    for n, ref in enumerate(from_refs):
        width = ref.shape[1]
        copies.append(pltpu.make_async_copy(ref, to_ref.at[:, at : at + width], sems.at[n]))
        copies[-1].start()
        at += width
    for copy in copies:
        copy.wait()


def join_kernel(*refs):
    *piece_refs, out_ref = refs
    at = 0
    for ref in piece_refs:
        size = ref.shape[1]
        out_ref[:, at : at + size, :] = ref[...]
        at += size


def role_groups(role_count):
    last = role_count // 2
    bits = [1 << n for n in range(last.bit_length() - 1)]
    return [[k for k in range(role_count) if k & -k == bit] for bit in bits] + [[0, last]]


def project_into(slots, groups, attended_ref, proj_ref, partial_refs):
    slots = list(slots)
    rows = attended_ref.shape[0] // len(slots)
    width = 512 if proj_ref.shape[1] % 512 == 0 else proj_ref.shape[1]
    for at in range(0, proj_ref.shape[1], width):
        product = jnp.dot(
            attended_ref[...], proj_ref[:, at : at + width], preferred_element_type=jnp.float32
        ).astype(jnp.bfloat16)
        for group, partial_ref in zip(groups, partial_refs):
            for n, k in enumerate(group):
                start = slots.index(k) * rows
                partial_ref[n * rows : (n + 1) * rows, at : at + width] = product[
                    start : start + rows
                ]


def project_kernel(slots, groups, attended_ref, proj_ref, order_ref, *partial_refs):
    project_into(slots, groups, attended_ref, proj_ref, partial_refs)


def partial_shapes(groups, rows, width):
    return [jax.ShapeDtypeStruct((rows * len(group), width), jnp.bfloat16) for group in groups]


def near_sum_kernel(route_ref, other_route_ref, came_ref, sent_any, *refs):
    out_refs, both_ref = refs[:2], refs[2]
    copies, (sent,) = start_fetch([sent_any], refs[3:])
    rows, width = sent.shape[0] // 2, sent.shape[1]
    lane = lax.broadcasted_iota(jnp.int32, (rows, GATE_COLUMNS), 1)
    half = GATE_COLUMNS // 2
    expert = (lane % half).astype(jnp.float32)
    for p, routes in enumerate((route_ref, other_route_ref)):
        shares = jnp.zeros((rows, GATE_COLUMNS), jnp.float32)
        routed = routes.shape[1] // 2
        for k in range(routed):
            named, weight = routes[:, k : k + 1], routes[:, routed + k : routed + k + 1]
            shares = shares + jnp.where(expert == named, weight, 0.0)
        first = shares.astype(jnp.bfloat16).astype(jnp.float32)
        terms = jnp.where(lane < half, first, shares - first).astype(jnp.bfloat16)
        out_refs[p][:, width:] = terms
        both_ref[p * rows : (p + 1) * rows, width:] = terms
    copies[0].wait()
    for p in range(2):
        total = sent[p * rows : (p + 1) * rows].astype(jnp.float32)
        total = total + came_ref[(1 - p) * rows : (2 - p) * rows].astype(jnp.float32)
        out_refs[p][:, :width] = total.astype(jnp.bfloat16)
        both_ref[p * rows : (p + 1) * rows, :width] = total.astype(jnp.bfloat16)


def far_sum_kernel(rows, order_count, *refs):
    refs = refs[order_count:]
    chips = (len(refs) - 4) // 3
    came_refs, sent_any = refs[:chips], refs[chips : 2 * chips]
    own_ref, other_ref, both_ref = refs[2 * chips : 2 * chips + 3]
    copies, sent_refs = start_fetch(sent_any, refs[2 * chips + 3 :])
    for copy in copies:
        copy.wait()
    size = chips * rows
    for n, (sent, came) in enumerate(zip(sent_refs, came_refs)):
        to = slice(n * rows, (n + 1) * rows)
        for p, out_ref in enumerate((own_ref, other_ref)):
            total = sent[p * rows : (p + 1) * rows].astype(jnp.float32)
            total = total + came[(1 - p) * rows : (2 - p) * rows].astype(jnp.float32)
            out_ref[to] = total.astype(jnp.bfloat16)
            both_ref[p * size + n * rows : p * size + (n + 1) * rows] = total.astype(jnp.bfloat16)


def norm_kernel(chips, near_row, far_row, at_ref, gain_ref, *refs):
    parts, (normed_ref, *hidden_refs, whole_ref) = refs[: 2 * chips], refs[2 * chips :]
    seq_index = at_ref[0]
    features = whole_ref.shape[1]
    rows = whole_ref.shape[0] // chips
    width = features // chips // 2
    for n in range(chips):
        near, far = parts[2 * n : 2 * n + 2]
        for m in range(chips):
            part = far if m else near
            first = ((far_row if m else near_row) if n else 0) + (m - 1 if m else 0) * rows
            to = slice((n ^ m) * rows, ((n ^ m) + 1) * rows)
            for j in range(2):
                start = pl.multiple_of((seq_index ^ (2 * n + j)) * width, width)
                whole_ref[to, pl.ds(start, width)] = part[
                    first : first + rows, j * width : (j + 1) * width
                ].astype(jnp.float32)
        first = near_row if n else 0
        normed_ref[n * rows : (n + 1) * rows, features:] = near[first : first + rows, 2 * width :]
    hidden = whole_ref[...]
    variance = jnp.mean(hidden * hidden, axis=1, keepdims=True)
    normed = hidden * lax.rsqrt(variance + epsilon) * gain_ref[...]
    normed_ref[:, :features] = normed.astype(jnp.bfloat16)
    for hidden_ref in hidden_refs:
        hidden_ref[...] = hidden[:rows]


def expert_kernel(token_count, at_ref, *refs):
    token_refs = refs[:token_count]
    gate_ref, up_ref, down_ref, keep_ref, send_ref, activated_ref = refs[token_count:]
    features, units = gate_ref.shape[1:]
    tokens = jnp.concatenate([ref[:, :features] for ref in token_refs], axis=0)
    gates = jnp.concatenate([ref[:, features:] for ref in token_refs], axis=0)
    lane = lax.broadcasted_iota(jnp.int32, gates.shape, 1)
    mine = lane % (GATE_COLUMNS // 2) == at_ref[2]
    share = jnp.sum(jnp.where(mine, gates.astype(jnp.float32), 0.0), axis=1, keepdims=True)
    block = 256 if units % 256 == 0 else units
    for f in range(0, units, block):
        gate_hidden = jnp.dot(
            tokens, gate_ref[0, :, f : f + block], preferred_element_type=jnp.float32
        )
        up_hidden = jnp.dot(tokens, up_ref[0, :, f : f + block], preferred_element_type=jnp.float32)
        activated_ref[:, f : f + block] = (
            gate_hidden / (1.0 + jnp.exp(-gate_hidden)) * up_hidden
        ).astype(jnp.bfloat16)
    kept = keep_ref.shape[0]
    block = 512 if features % 512 == 0 else features
    for c in range(0, features, block):
        product = jnp.dot(
            activated_ref[...], down_ref[0, :, c : c + block], preferred_element_type=jnp.float32
        )
        product = (product * share).astype(jnp.bfloat16)
        keep_ref[:, c : c + block] = product[:kept]
        send_ref[:, c : c + block] = product[kept:]


def run_expert(at, tokens, gate_weight, up_weight, down_weight):
    units = gate_weight.shape[2]
    width = gate_weight.shape[1]
    rows = sum(part.shape[0] for part in tokens)
    half = jax.ShapeDtypeStruct((rows // 2, width), jnp.bfloat16)
    return pl.pallas_call(
        partial(expert_kernel, len(tokens)),
        in_specs=[pl.BlockSpec(memory_space=pltpu.SMEM)] + in_vmem(len(tokens) + 3),
        out_specs=in_vmem(2),
        out_shape=[half, half],
        scratch_shapes=[pltpu.VMEM((rows, units), jnp.bfloat16)],
        compiler_params=pltpu.CompilerParams(vmem_limit_bytes=EXPERT_VMEM),
        cost_estimate=NOTHING,
    )(at, *tokens, gate_weight, up_weight, down_weight)


def after(array, *others):
    return lax.optimization_barrier((array, *others))[0]


def added(terms):
    total = terms[0].astype(jnp.float32)
    for term in terms[1:]:
        total = total + term.astype(jnp.float32)
    return total


def gathered_shards(
    query_rows,
    encoded_key_rows,
    value_matrix_rows,
    output_weight,
    residual,
    norm_gain,
    route_experts,
    route_gates,
    gate_weight,
    up_weight,
    down_weight,
):
    seq_count = lax.axis_size("seq")
    role_count = lax.axis_size("role")
    seq_index = lax.axis_index("seq")
    role_index = lax.axis_index("role")
    batch_count, local_length, query_width = query_rows.shape
    local_heads = query_width // HEAD_WIDTH
    group_width = QUERY_HEADS // KEY_VALUE_HEADS
    role_bits = [1 << n for n in range(role_count.bit_length() - 1)]
    at = jnp.stack([seq_index, role_index, seq_index * role_count + role_index]).astype(jnp.int32)

    def over_role(array, k):
        return lax.ppermute(array, "role", [(i, i ^ k) for i in range(role_count)])

    def over_seq(array, j):
        return lax.ppermute(array, "seq", [(i, i ^ j) for i in range(seq_count)])

    beside_proj = over_seq(output_weight, 1)
    block_width = output_weight.shape[1]
    across_steps = range(2, seq_count, 2)

    pieces = []
    for k in range(role_count):
        head = ((role_index ^ k) * local_heads // group_width) * HEAD_WIDTH
        piece = jnp.concatenate(
            [
                lax.dynamic_slice_in_dim(encoded_key_rows, head, HEAD_WIDTH, 2),
                lax.dynamic_slice_in_dim(value_matrix_rows, head, HEAD_WIDTH, 2),
            ],
            axis=2,
        )
        pieces.append(piece)
    near_proj = pl.pallas_call(
        columns_kernel,
        in_specs=hbm_specs(1) + in_vmem(1),
        out_specs=pl.BlockSpec(memory_space=pltpu.VMEM),
        out_shape=jax.ShapeDtypeStruct((query_width, 2 * block_width), jnp.bfloat16),
        scratch_shapes=[pltpu.SemaphoreType.DMA((2,))],
        compiler_params=pltpu.CompilerParams(vmem_limit_bytes=COPY_VMEM),
        cost_estimate=NOTHING,
    )(*in_hbm(output_weight), beside_proj)
    pieces[1] = after(pieces[1], near_proj)
    pieces = [piece if k == 0 else over_role(piece, k) for k, piece in enumerate(pieces)]
    block = pl.pallas_call(
        join_kernel,
        in_specs=in_vmem(len(pieces)),
        out_specs=pl.BlockSpec(memory_space=pltpu.VMEM),
        out_shape=jax.ShapeDtypeStruct(
            (batch_count, local_length, 2 * HEAD_WIDTH), jnp.bfloat16
        ),
        compiler_params=pltpu.CompilerParams(vmem_limit_bytes=COPY_VMEM),
        cost_estimate=SHORT,
    )(*pieces)
    same_core = [block] + [over_seq(block, j) for j in across_steps]
    blocks = []
    for part in same_core:
        blocks += [part, over_seq(part, 1)]
    last = role_count // 2
    routes = jnp.concatenate([route_experts[0].astype(jnp.float32), route_gates[0]], axis=1)
    residual_blocks = [
        lax.dynamic_slice_in_dim(residual[0], (seq_index ^ j) * block_width, block_width, 1)
        for j in range(seq_count)
    ]
    residuals = [
        jnp.concatenate(residual_blocks[j : j + 2], axis=1) for j in range(0, seq_count, 2)
    ]

    rows = batch_count * local_length
    near_width = 2 * output_weight.shape[1]
    groups = role_groups(role_count)
    attend_args = in_hbm(query_rows, *blocks[:-1])
    slot_sets = [(range(1, role_count, 2), groups[:1]), (range(0, role_count, 2), groups[1:])]
    attended, near = [], []
    for slots, parts in slot_sets:
        half_rows = jax.ShapeDtypeStruct((rows // 2, query_width), jnp.bfloat16)
        half, *partials = pl.pallas_call(
            partial(attend_kernel, seq_count, role_count, slots, parts),
            in_specs=[pl.BlockSpec(memory_space=pltpu.SMEM)]
            + in_vmem(2)
            + hbm_specs(len(attend_args)),
            out_specs=in_vmem(1 + len(parts)),
            out_shape=[half_rows] + partial_shapes(parts, local_length, near_width),
            scratch_shapes=fetch_scratch(*attend_args),
            compiler_params=pltpu.CompilerParams(vmem_limit_bytes=SMALL_VMEM),
            cost_estimate=SHORT,
        )(at, blocks[-1], near_proj, *attend_args)
        attended.append(half)
        near += partials

    for j in across_steps:
        residuals[j // 2] = over_seq(after(residuals[j // 2], attended[1]), j)
    other_routes = over_role(routes, last)

    def summed_over_role(parts, extra, *before):
        terms = [[part] for part in parts]
        for n, group in enumerate(groups[:-1]):
            bit = 1 << n
            leaving = terms[n][0] if len(terms[n]) == 1 else added(terms[n]).astype(jnp.bfloat16)
            came = over_role(leaving, bit)
            for m in range(n + 1, len(groups)):
                at_rows = [group.index(k ^ bit) for k in groups[m]]
                if at_rows == list(range(len(group))):
                    terms[m].append(came)
                else:
                    split = [came[i * local_length : (i + 1) * local_length] for i in at_rows]
                    terms[m].append(jnp.concatenate(split, axis=0))
        extra = jnp.pad(after(extra, *before) if before else extra, ((0, local_length), (0, 0)))
        sent = added(terms[-1] + [extra]).astype(jnp.bfloat16)
        return sent

    near_sent = summed_over_role(near, residuals[0])
    near_came = over_role(near_sent, last)
    near_args = in_hbm(near_sent)
    own_shape, both_shape = [
        jax.ShapeDtypeStruct((size, near_width + GATE_COLUMNS), jnp.bfloat16)
        for size in (local_length, 2 * local_length)
    ]
    near_halves = pl.pallas_call(
        near_sum_kernel,
        in_specs=in_vmem(3) + hbm_specs(1),
        out_specs=in_vmem(3),
        out_shape=[own_shape, own_shape, both_shape],
        scratch_shapes=fetch_scratch(*near_args),
        compiler_params=pltpu.CompilerParams(vmem_limit_bytes=SMALL_VMEM),
        cost_estimate=LONG,
    )(routes, other_routes, near_came, *near_args)

    def walk(k, bits):
        found = [k]
        for n, bit in enumerate(bits):
            found += walk(k | bit, bits[n + 1 :])
        return found

    lower_bits = role_bits[:-1][::-1]
    order = walk(last, lower_bits) + walk(0, lower_bits)
    far_plane, final = order[1], order[-1]

    def across(part):
        return [over_seq(part, j) for j in across_steps]

    def spread(own, other, both, ordered):
        planes, crossed = {0: own, last: other}, {}
        both_across = across(both)
        size = own.shape[0]
        for k in order:
            if k not in planes:
                bit = k & -k
                held = planes[k ^ bit]
                wait = ordered and k < last
                planes[k] = over_role(after(held, planes[far_plane]) if wait else held, bit)
            if k in (0, last):
                crossed[k] = both_across
            elif k < last:
                source = k ^ (k & -k)
                came = [part[:size] for part in crossed[source]] if source == 0 else crossed[source]
                crossed[k] = [over_role(part, k & -k) for part in came]
            else:
                crossed[k] = across(after(planes[k], *both_across))
        return planes, crossed

    near_planes, near_crossed = spread(*near_halves, False)

    sent, came = [], []
    for n, j in enumerate(across_steps, 1):
        far = []
        for half, (slots, parts) in zip(attended, slot_sets):
            far += pl.pallas_call(
                partial(project_kernel, slots, parts),
                in_specs=in_vmem(2) + [pl.BlockSpec(memory_space=pl.ANY)],
                out_specs=in_vmem(len(parts)),
                out_shape=partial_shapes(parts, local_length, near_width),
                compiler_params=pltpu.CompilerParams(vmem_limit_bytes=SMALL_VMEM),
                cost_estimate=SHORT,
            )(over_seq(half, j), near_proj, other_routes)
        sent.append(summed_over_role(far, residuals[n], near_halves[0]))
        came.append(over_role(sent[-1], last))

    chips = 1 + len(across_steps)
    far_args = in_hbm(*sent)
    far_rows = (chips - 1) * local_length
    far_shape, far_both_shape = [
        jax.ShapeDtypeStruct((size, near_width), jnp.bfloat16) for size in (far_rows, 2 * far_rows)
    ]
    first_come = [*near_crossed[0], near_planes[far_plane], *near_crossed[far_plane]]
    first_come.append(near_planes[final])
    far_halves = pl.pallas_call(
        partial(far_sum_kernel, local_length, len(first_come)),
        in_specs=[pl.BlockSpec(memory_space=pl.ANY)] * len(first_come)
        + in_vmem(len(came))
        + hbm_specs(len(far_args)),
        out_specs=in_vmem(3),
        out_shape=[far_shape, far_shape, far_both_shape],
        scratch_shapes=fetch_scratch(*far_args),
        compiler_params=pltpu.CompilerParams(vmem_limit_bytes=SMALL_VMEM),
        cost_estimate=SHORT,
    )(*first_come, *came, *far_args)
    far_own, far_other, far_both = far_halves
    far_other = after(far_other, *near_crossed[final])
    far_planes, far_crossed = spread(far_own, far_other, far_both, True)

    width = residual.shape[2]
    gain = norm_gain.reshape(1, width)

    def normed_rows(parts, second, *hidden_shape):
        rows = chips * local_length
        firsts = (local_length, far_rows) if second else (0, 0)
        return pl.pallas_call(
            partial(norm_kernel, chips, *firsts),
            in_specs=[pl.BlockSpec(memory_space=pltpu.SMEM)] + in_vmem(1 + 2 * chips),
            out_specs=in_vmem(1 + len(hidden_shape)),
            out_shape=[
                jax.ShapeDtypeStruct((rows, width + GATE_COLUMNS), jnp.bfloat16),
                *hidden_shape,
            ],
            scratch_shapes=[pltpu.VMEM((rows, width), jnp.float32)],
            compiler_params=pltpu.CompilerParams(vmem_limit_bytes=SMALL_VMEM),
            cost_estimate=NOTHING,
        )(at, gain, *parts)

    keep, send, slots, leaving, passed = {}, {}, {}, {}, {}

    hidden_shape = jax.ShapeDtypeStruct((local_length, width), jnp.float32)
    hidden = []

    hidden_shape = jax.ShapeDtypeStruct((local_length, width), jnp.float32)
    hidden = []

    def prepared(k, *first):
        late = far_crossed[k]
        if first:
            late = [after(part, *first) for part in late]
        parts = [near_planes[k], far_planes[k]]
        for pair in zip(near_crossed[k], late):
            parts += pair
        normed, *own = normed_rows(parts, k == last, *([] if k else [hidden_shape]))
        hidden.extend(own)
        return [normed, over_seq(normed, 1)]

    def expert(tokens, *others):
        if others:
            tokens = lax.optimization_barrier((*tokens, *others))[: len(tokens)]
        return run_expert(at, tokens, gate_weight, up_weight, down_weight)

    def combine(k, *before):
        came = over_seq(after(send[k], *before) if before else send[k], 1)
        sums = []
        for n in range(len(across_steps)):
            chunk = slice((n + 1) * local_length, (n + 2) * local_length)
            sums.append(added([keep[k][chunk], came[chunk]]).astype(jnp.bfloat16))
        return [keep[k][:local_length], came[:local_length]], sums

    def pass_on(k):
        passed[k] = [over_seq(part, j) for part, j in zip(leaving[k], across_steps)]
        slots[k] += passed[k]

    ready = {far_plane: prepared(far_plane, far_planes[final], *far_crossed[final])}
    ready[final] = prepared(final)
    keep[far_plane], send[far_plane] = expert(ready[far_plane], ready[final][0])
    ready |= {k: prepared(k, keep[far_plane]) for k in (last, 0)}
    slots[far_plane], leaving[far_plane] = combine(far_plane)
    leaving[far_plane] = [after(part, ready[last][0], ready[0][0]) for part in leaving[far_plane]]
    pass_on(far_plane)
    keep[last], send[last] = expert(ready[last], keep[far_plane], *leaving[far_plane])
    slots[last], leaving[last] = combine(last)
    leaving[last] = [after(part, *passed[far_plane]) for part in leaving[last]]
    pass_on(last)
    keep[final], send[final] = expert(ready[final], keep[last])
    slots[far_plane] = [added(slots[far_plane]).astype(jnp.bfloat16)]
    slots[final], leaving[final] = combine(final, *passed[far_plane])
    leaving[final] = [after(part, *leaving[last]) for part in leaving[final]]
    pass_on(final)
    keep[0], send[0] = expert(ready[0], keep[final], *leaving[last])
    slots[0], leaving[0] = combine(0, *passed[last])
    leaving[0] = [after(part, *leaving[final]) for part in leaving[0]]
    pass_on(0)
    for bit in role_bits:
        for k in [k for k in sorted(slots, reverse=True) if k & bit]:
            going = added(slots.pop(k)).astype(jnp.bfloat16)
            if k == last:
                going = after(going, *leaving[final])
            slots[k ^ bit].append(over_role(going, bit))
    return added(hidden + slots[0]).astype(jnp.bfloat16).reshape(residual.shape)


def solution(mesh):
    placed = (
        P("groups", "seq", "role"),
        P("groups", ("seq", "role"), None),
        P("groups", ("seq", "role"), None),
        P("role", "seq"),
        P(("groups", "role"), "seq", None),
        P(),
        P(("groups", "role"), "seq", None),
        P(("groups", "role"), "seq", None),
        P(("seq", "role"), None, None),
        P(("seq", "role"), None, None),
        P(("seq", "role"), None, None),
    )
    experts = mesh.shape["seq"] * mesh.shape["role"]
    return jax.shard_map(
        gathered_shards if experts <= 2 * TOPK else routed_shards,
        mesh=mesh,
        in_specs=placed,
        out_specs=P(("groups", "role"), "seq", None),
        check_vma=False,
    )
```

```python
from functools import partial

import jax
import jax.numpy as jnp
from jax import lax
from jax.experimental import pallas as pl
from jax.experimental.pallas import tpu as pltpu
from jax.sharding import PartitionSpec as P

D = 2048
QUERY_HEADS = 32
KEY_VALUE_HEADS = 4
HEAD_WIDTH = 128
TOPK = 8


epsilon = 1e-06
masked_score = -1e30
EXPERT_VMEM = 16 * 2**20
SMALL_VMEM = 12 * 2**20
COPY_VMEM = 4 * 2**20
GATE_COLUMNS = 128
LOG2_E = 1.4426950408889634
NOTHING = pl.CostEstimate(flops=1, bytes_accessed=1, transcendentals=0)
SHORT = pl.CostEstimate(flops=2 * 10**9, bytes_accessed=4 * 2**20, transcendentals=0)
LONG = pl.CostEstimate(flops=10**10, bytes_accessed=1, transcendentals=0)


def score_block(queries, every_key, query_position, block_start, block_width, score_scale):
    keys_part = lax.slice_in_dim(every_key, block_start, block_start + block_width, axis=0)
    raw_scores = (
        jnp.einsum("qhd,kd->hqk", queries, keys_part, preferred_element_type=jnp.float32)
        * score_scale
    )
    key_position = block_start + jnp.arange(block_width, dtype=jnp.int32)
    return jnp.where(
        key_position[None, None, :] <= query_position[None, :, None], raw_scores, masked_score
    )


def value_block(rounded, every_value, block_start, block_width):
    prob_block = lax.slice_in_dim(rounded, block_start, block_start + block_width, axis=2)
    values_part = lax.slice_in_dim(every_value, block_start, block_start + block_width, axis=0)
    return jnp.einsum("hqk,kd->qhd", prob_block, values_part, preferred_element_type=jnp.float32)


def routed_shards(
    query_rows,
    encoded_key_rows,
    value_matrix_rows,
    output_weight,
    residual,
    norm_gain,
    route_experts,
    route_gates,
    gate_weight,
    up_weight,
    down_weight,
):
    seq_count = lax.axis_size("seq")
    role_count = lax.axis_size("role")
    seq_index = lax.axis_index("seq")
    role_index = lax.axis_index("role")
    batch_count = query_rows.shape[0]
    local_length = query_rows.shape[1]
    local_heads = query_rows.shape[2] // HEAD_WIDTH
    full_length = local_length * seq_count
    query_group_width = QUERY_HEADS // KEY_VALUE_HEADS
    head_pick = role_index * local_heads // query_group_width
    role_keys, role_values = (
        lax.all_gather(encoded_key_rows, "role", axis=1, tiled=True),
        lax.all_gather(value_matrix_rows, "role", axis=1, tiled=True),
    )
    head_keys = lax.dynamic_slice_in_dim(role_keys, head_pick * HEAD_WIDTH, HEAD_WIDTH, 2)
    head_values = lax.dynamic_slice_in_dim(role_values, head_pick * HEAD_WIDTH, HEAD_WIDTH, 2)
    whole_keys, whole_values, whole_proj = (
        lax.all_gather(head_keys, "seq", axis=1, tiled=True),
        lax.all_gather(head_values, "seq", axis=1, tiled=True),
        lax.all_gather(output_weight, "seq", axis=1, tiled=True),
    )
    key_width = full_length // 8
    score_scale = HEAD_WIDTH ** (-0.5)
    query_position = seq_index * local_length + jnp.arange(local_length, dtype=jnp.int32)
    last_needed = (seq_index + 1) * local_length

    def one_sequence(operands):
        own_queries, every_key, every_value = operands
        queries = own_queries.reshape(local_length, local_heads, HEAD_WIDTH)
        pieces = []
        for number in range(8):
            block_start = number * key_width
            compute = partial(
                score_block, queries, every_key, query_position, block_start, key_width, score_scale
            )
            skipped = partial(
                jnp.full, (local_heads, local_length, key_width), masked_score, jnp.float32
            )
            pieces.append(lax.cond(block_start < last_needed, compute, skipped))
        scores = jnp.concatenate(pieces, axis=2)
        row_peak = jnp.max(scores, axis=2, keepdims=True)
        weights = jnp.exp(scores - row_peak)
        totals = jnp.sum(weights, axis=2, keepdims=True)
        rounded = weights.astype(jnp.bfloat16)
        mixed_rows = jnp.zeros((local_length, local_heads, HEAD_WIDTH), jnp.float32)
        for number in range(8):
            block_start = number * key_width
            product = partial(value_block, rounded, every_value, block_start, key_width)
            nothing = partial(jnp.zeros, (local_length, local_heads, HEAD_WIDTH), jnp.float32)
            mixed_rows = mixed_rows + lax.cond(block_start < last_needed, product, nothing)
        attended = (mixed_rows / totals.transpose(1, 0, 2)).astype(jnp.bfloat16)
        return attended.reshape(local_length, local_heads * HEAD_WIDTH)

    attended = lax.map(one_sequence, (query_rows, whole_keys, whole_values))
    flat_attended = attended.reshape(batch_count * local_length, local_heads * HEAD_WIDTH)
    projected = lax.psum_scatter(
        jnp.dot(flat_attended, whole_proj, preferred_element_type=jnp.float32).astype(jnp.bfloat16),
        "role",
        scatter_dimension=0,
        tiled=True,
    ).astype(jnp.float32)
    hidden = residual[0].astype(jnp.float32) + projected
    variance = jnp.mean(hidden * hidden, axis=-1, keepdims=True)
    normed = (hidden * lax.rsqrt(variance + epsilon) * norm_gain).astype(jnp.bfloat16)
    expert_ids = route_experts.reshape(-1)
    gate_values = route_gates.reshape(-1)
    experts_local = gate_weight.shape[0]
    device_count = seq_count * role_count
    expert_count = experts_local * device_count
    assign = expert_ids.shape[0]
    capacity = assign // expert_count + 1
    onehot = (expert_ids[:, None] == jnp.arange(expert_count, dtype=jnp.int32)[None, :]).astype(
        jnp.int32
    )
    earlier = jnp.cumsum(onehot, axis=0) - onehot
    slot_rank = jnp.sum(earlier * onehot, axis=1)
    slot_index = expert_ids * capacity + slot_rank
    source_token = jnp.arange(assign, dtype=jnp.int32) // TOPK
    slot_token = jnp.zeros((expert_count * capacity,), jnp.int32).at[slot_index].set(source_token)
    slot_used = jnp.zeros((expert_count * capacity,), jnp.bfloat16).at[slot_index].set(1.0)
    outgoing = (normed[slot_token] * slot_used[:, None]).reshape(
        device_count, experts_local, capacity, D
    )
    incoming = lax.all_to_all(outgoing, ("seq", "role"), split_axis=0, concat_axis=0, tiled=True)
    gate_hidden = jnp.einsum(
        "sjcd,jdf->sjcf", incoming, gate_weight, preferred_element_type=jnp.float32
    )
    up_hidden = jnp.einsum(
        "sjcd,jdf->sjcf", incoming, up_weight, preferred_element_type=jnp.float32
    )
    activated = (jax.nn.silu(gate_hidden) * up_hidden).astype(jnp.bfloat16)
    returned = lax.all_to_all(
        jnp.einsum(
            "sjcf,jfd->sjcd", activated, down_weight, preferred_element_type=jnp.float32
        ).astype(jnp.bfloat16),
        ("seq", "role"),
        split_axis=0,
        concat_axis=0,
        tiled=True,
    )
    gathered = returned.reshape(expert_count * capacity, D)[slot_index]
    weighted = gathered.astype(jnp.float32) * gate_values[:, None]
    expert_sum = jnp.sum(weighted.reshape(-1, TOPK, D), axis=1)
    return (hidden + expert_sum).astype(jnp.bfloat16).reshape(residual.shape)


def in_hbm(*arrays):
    return [pltpu.with_memory_space_constraint(array, pltpu.HBM) for array in arrays]


def hbm_specs(count):
    return [pl.BlockSpec(memory_space=pltpu.HBM)] * count


def fetch_scratch(*arrays):
    return [pltpu.VMEM(array.shape, array.dtype) for array in arrays] + [
        pltpu.SemaphoreType.DMA((len(arrays),))
    ]


def start_fetch(from_refs, scratch):
    *buffers, sems = scratch
    copies = [
        pltpu.make_async_copy(from_ref, buffer, sems.at[n])
        for n, (from_ref, buffer) in enumerate(zip(from_refs, buffers))
    ]
    for copy in copies:
        copy.start()
    return copies, buffers


def in_vmem(count):
    return [pl.BlockSpec(memory_space=pltpu.VMEM)] * count


def attend_kernel(seq_count, role_count, slots, groups, at_ref, *refs):
    last_block, *refs = refs
    count = seq_count + 2
    attended_ref, *partial_refs = refs[count : count + 1 + len(groups)]
    copies, (query_ref, *buffers) = start_fetch(refs[:count], refs[count + 1 + len(groups) :])
    blocks, proj_refs = buffers[: seq_count - 1] + [last_block], buffers[seq_count - 1 :]
    seq_index, role_index = at_ref[0], at_ref[1]
    local_length = query_ref.shape[1]
    local_heads = query_ref.shape[2] // HEAD_WIDTH
    per_role = local_length // role_count
    rows = local_heads * local_length
    keys_all = seq_count * local_length
    slot = lax.broadcasted_iota(jnp.int32, (rows, keys_all), 1)
    block_number, within = slot // local_length, slot % local_length
    key_position = (
        (seq_index ^ block_number) * local_length
        + (role_index ^ (within // per_role)) * per_role
        + within % per_role
    )
    query_position = (
        seq_index * local_length
        + lax.broadcasted_iota(jnp.int32, (rows, keys_all), 0) % local_length
    )
    seen = key_position <= query_position
    scale = HEAD_WIDTH ** (-0.5) * LOG2_E
    for copy in copies[:seq_count]:
        copy.wait()
    for n, k in enumerate(slots):
        b = role_index ^ k
        own = query_ref[b]
        queries = jnp.concatenate(
            [own[:, h * HEAD_WIDTH : (h + 1) * HEAD_WIDTH] for h in range(local_heads)], axis=0
        )
        key_value = jnp.concatenate([block[b] for block in blocks], axis=0)
        keys, values = key_value[:, :HEAD_WIDTH], key_value[:, HEAD_WIDTH:]
        scores = lax.dot_general(
            queries, keys, (((1,), (1,)), ((), ())), preferred_element_type=jnp.float32
        )
        scores = jnp.where(seen, scores * scale, masked_score)
        weights = jnp.exp2(scores - jnp.max(scores, axis=1, keepdims=True))
        totals = jnp.sum(weights, axis=1, keepdims=True)
        mixed = jnp.dot(weights.astype(jnp.bfloat16), values, preferred_element_type=jnp.float32)
        attended = (mixed * (1.0 / totals)).astype(jnp.bfloat16)
        for h in range(local_heads):
            attended_ref[
                n * local_length : (n + 1) * local_length, h * HEAD_WIDTH : (h + 1) * HEAD_WIDTH
            ] = attended[h * local_length : (h + 1) * local_length]
    for copy in copies[seq_count:]:
        copy.wait()
    project_into(slots, groups, attended_ref, proj_refs, partial_refs)


def join_kernel(*refs):
    *piece_refs, out_ref = refs
    at = 0
    for ref in piece_refs:
        size = ref.shape[1]
        out_ref[:, at : at + size, :] = ref[...]
        at += size


def role_groups(role_count):
    last = role_count // 2
    bits = [1 << n for n in range(last.bit_length() - 1)]
    return [[k for k in range(role_count) if k & -k == bit] for bit in bits] + [[0, last]]


def project_into(slots, groups, attended_ref, proj_refs, partial_refs):
    slots = list(slots)
    rows = attended_ref.shape[0] // len(slots)
    at = 0
    for proj_ref in proj_refs:
        width = proj_ref.shape[1]
        product = jnp.dot(
            attended_ref[...], proj_ref[...], preferred_element_type=jnp.float32
        ).astype(jnp.bfloat16)
        for group, partial_ref in zip(groups, partial_refs):
            for n, k in enumerate(group):
                start = slots.index(k) * rows
                partial_ref[n * rows : (n + 1) * rows, at : at + width] = product[
                    start : start + rows
                ]
        at += width


def project_kernel(slots, groups, attended_ref, order_ref, *refs):
    count = (len(refs) - len(groups) - 1) // 2
    copies, proj_refs = start_fetch(refs[:count], refs[count + len(groups) :])
    for copy in copies:
        copy.wait()
    project_into(slots, groups, attended_ref, proj_refs, refs[count : count + len(groups)])


def partial_shapes(groups, rows, width):
    return [jax.ShapeDtypeStruct((rows * len(group), width), jnp.bfloat16) for group in groups]


def near_sum_kernel(route_ref, other_route_ref, came_ref, sent_any, *refs):
    out_refs, both_ref = refs[:2], refs[2]
    copies, (sent,) = start_fetch([sent_any], refs[3:])
    rows, width = sent.shape[0] // 2, sent.shape[1]
    lane = lax.broadcasted_iota(jnp.int32, (rows, GATE_COLUMNS), 1)
    half = GATE_COLUMNS // 2
    expert = (lane % half).astype(jnp.float32)
    for p, routes in enumerate((route_ref, other_route_ref)):
        shares = jnp.zeros((rows, GATE_COLUMNS), jnp.float32)
        routed = routes.shape[1] // 2
        for k in range(routed):
            named, weight = routes[:, k : k + 1], routes[:, routed + k : routed + k + 1]
            shares = shares + jnp.where(expert == named, weight, 0.0)
        first = shares.astype(jnp.bfloat16).astype(jnp.float32)
        terms = jnp.where(lane < half, first, shares - first).astype(jnp.bfloat16)
        out_refs[p][:, width:] = terms
        both_ref[p * rows : (p + 1) * rows, width:] = terms
    copies[0].wait()
    for p in range(2):
        total = sent[p * rows : (p + 1) * rows].astype(jnp.float32)
        total = total + came_ref[(1 - p) * rows : (2 - p) * rows].astype(jnp.float32)
        out_refs[p][:, :width] = total.astype(jnp.bfloat16)
        both_ref[p * rows : (p + 1) * rows, :width] = total.astype(jnp.bfloat16)


def far_sum_kernel(rows, order_count, *refs):
    refs = refs[order_count:]
    chips = (len(refs) - 4) // 3
    came_refs, sent_any = refs[:chips], refs[chips : 2 * chips]
    own_ref, other_ref, both_ref = refs[2 * chips : 2 * chips + 3]
    copies, sent_refs = start_fetch(sent_any, refs[2 * chips + 3 :])
    for copy in copies:
        copy.wait()
    size = chips * rows
    for n, (sent, came) in enumerate(zip(sent_refs, came_refs)):
        to = slice(n * rows, (n + 1) * rows)
        for p, out_ref in enumerate((own_ref, other_ref)):
            total = sent[p * rows : (p + 1) * rows].astype(jnp.float32)
            total = total + came[(1 - p) * rows : (2 - p) * rows].astype(jnp.float32)
            out_ref[to] = total.astype(jnp.bfloat16)
            both_ref[p * size + n * rows : p * size + (n + 1) * rows] = total.astype(jnp.bfloat16)


def norm_kernel(chips, near_row, far_row, at_ref, gain_ref, *refs):
    parts, (normed_ref, *hidden_refs, whole_ref) = refs[: 2 * chips], refs[2 * chips :]
    seq_index = at_ref[0]
    features = whole_ref.shape[1]
    rows = whole_ref.shape[0] // chips
    width = features // chips // 2
    for n in range(chips):
        near, far = parts[2 * n : 2 * n + 2]
        for m in range(chips):
            part = far if m else near
            first = ((far_row if m else near_row) if n else 0) + (m - 1 if m else 0) * rows
            to = slice((n ^ m) * rows, ((n ^ m) + 1) * rows)
            for j in range(2):
                start = pl.multiple_of((seq_index ^ (2 * n + j)) * width, width)
                whole_ref[to, pl.ds(start, width)] = part[
                    first : first + rows, j * width : (j + 1) * width
                ].astype(jnp.float32)
        first = near_row if n else 0
        normed_ref[n * rows : (n + 1) * rows, features:] = near[first : first + rows, 2 * width :]
    hidden = whole_ref[...]
    variance = jnp.mean(hidden * hidden, axis=1, keepdims=True)
    normed = hidden * lax.rsqrt(variance + epsilon) * gain_ref[...]
    normed_ref[:, :features] = normed.astype(jnp.bfloat16)
    for hidden_ref in hidden_refs:
        hidden_ref[...] = hidden[:rows]


def expert_kernel(token_count, at_ref, *refs):
    token_refs = refs[:token_count]
    gate_ref, up_ref, down_ref, keep_ref, send_ref, activated_ref = refs[token_count:]
    features, units = gate_ref.shape[1:]
    tokens = jnp.concatenate([ref[:, :features] for ref in token_refs], axis=0)
    gates = jnp.concatenate([ref[:, features:] for ref in token_refs], axis=0)
    lane = lax.broadcasted_iota(jnp.int32, gates.shape, 1)
    mine = lane % (GATE_COLUMNS // 2) == at_ref[2]
    share = jnp.sum(jnp.where(mine, gates.astype(jnp.float32), 0.0), axis=1, keepdims=True)
    block = units
    for f in range(0, units, block):
        gate_hidden = jnp.dot(
            tokens, gate_ref[0, :, f : f + block], preferred_element_type=jnp.float32
        )
        up_hidden = jnp.dot(tokens, up_ref[0, :, f : f + block], preferred_element_type=jnp.float32)
        activated_ref[:, f : f + block] = (
            gate_hidden / (1.0 + jnp.exp(-gate_hidden)) * up_hidden
        ).astype(jnp.bfloat16)
    kept = keep_ref.shape[0]
    block = 1024 if features % 1024 == 0 else features
    for c in range(0, features, block):
        product = jnp.dot(
            activated_ref[...], down_ref[0, :, c : c + block], preferred_element_type=jnp.float32
        )
        product = (product * share).astype(jnp.bfloat16)
        keep_ref[:, c : c + block] = product[:kept]
        send_ref[:, c : c + block] = product[kept:]


def run_expert(at, tokens, gate_weight, up_weight, down_weight):
    units = gate_weight.shape[2]
    width = gate_weight.shape[1]
    rows = sum(part.shape[0] for part in tokens)
    half = jax.ShapeDtypeStruct((rows // 2, width), jnp.bfloat16)
    return pl.pallas_call(
        partial(expert_kernel, len(tokens)),
        in_specs=[pl.BlockSpec(memory_space=pltpu.SMEM)] + in_vmem(len(tokens) + 3),
        out_specs=in_vmem(2),
        out_shape=[half, half],
        scratch_shapes=[pltpu.VMEM((rows, units), jnp.bfloat16)],
        compiler_params=pltpu.CompilerParams(vmem_limit_bytes=EXPERT_VMEM),
        cost_estimate=NOTHING,
    )(at, *tokens, gate_weight, up_weight, down_weight)


def after(array, *others):
    return lax.optimization_barrier((array, *others))[0]


def added(terms):
    total = terms[0].astype(jnp.float32)
    for term in terms[1:]:
        total = total + term.astype(jnp.float32)
    return total


def gathered_shards(
    query_rows,
    encoded_key_rows,
    value_matrix_rows,
    output_weight,
    residual,
    norm_gain,
    route_experts,
    route_gates,
    gate_weight,
    up_weight,
    down_weight,
):
    seq_count = lax.axis_size("seq")
    role_count = lax.axis_size("role")
    seq_index = lax.axis_index("seq")
    role_index = lax.axis_index("role")
    batch_count, local_length, query_width = query_rows.shape
    local_heads = query_width // HEAD_WIDTH
    group_width = QUERY_HEADS // KEY_VALUE_HEADS
    role_bits = [1 << n for n in range(role_count.bit_length() - 1)]
    at = jnp.stack([seq_index, role_index, seq_index * role_count + role_index]).astype(jnp.int32)

    def over_role(array, k):
        return lax.ppermute(array, "role", [(i, i ^ k) for i in range(role_count)])

    def over_seq(array, j):
        return lax.ppermute(array, "seq", [(i, i ^ j) for i in range(seq_count)])

    beside_proj = over_seq(output_weight, 1)
    block_width = output_weight.shape[1]
    across_steps = range(2, seq_count, 2)

    pieces = []
    for k in range(role_count):
        head = ((role_index ^ k) * local_heads // group_width) * HEAD_WIDTH
        piece = jnp.concatenate(
            [
                lax.dynamic_slice_in_dim(encoded_key_rows, head, HEAD_WIDTH, 2),
                lax.dynamic_slice_in_dim(value_matrix_rows, head, HEAD_WIDTH, 2),
            ],
            axis=2,
        )
        pieces.append(piece)
    pieces[1] = after(pieces[1], beside_proj)
    pieces = [piece if k == 0 else over_role(piece, k) for k, piece in enumerate(pieces)]
    block = pl.pallas_call(
        join_kernel,
        in_specs=in_vmem(len(pieces)),
        out_specs=pl.BlockSpec(memory_space=pltpu.VMEM),
        out_shape=jax.ShapeDtypeStruct(
            (batch_count, local_length, 2 * HEAD_WIDTH), jnp.bfloat16
        ),
        compiler_params=pltpu.CompilerParams(vmem_limit_bytes=COPY_VMEM),
        cost_estimate=SHORT,
    )(*pieces)
    same_core = [block] + [over_seq(block, j) for j in across_steps]
    blocks = []
    for part in same_core:
        blocks += [part, over_seq(part, 1)]
    last = role_count // 2
    routes = jnp.concatenate([route_experts[0].astype(jnp.float32), route_gates[0]], axis=1)
    residual_blocks = [
        lax.dynamic_slice_in_dim(residual[0], (seq_index ^ j) * block_width, block_width, 1)
        for j in range(seq_count)
    ]
    residuals = [
        jnp.concatenate(residual_blocks[j : j + 2], axis=1) for j in range(0, seq_count, 2)
    ]

    rows = batch_count * local_length
    near_width = 2 * output_weight.shape[1]
    groups = role_groups(role_count)
    attend_args = in_hbm(query_rows, *blocks[:-1], output_weight, beside_proj)
    slot_sets = [(range(1, role_count, 2), groups[:1]), (range(0, role_count, 2), groups[1:])]
    attended, near = [], []
    for slots, parts in slot_sets:
        half_rows = jax.ShapeDtypeStruct((rows // 2, query_width), jnp.bfloat16)
        half, *partials = pl.pallas_call(
            partial(attend_kernel, seq_count, role_count, slots, parts),
            in_specs=[pl.BlockSpec(memory_space=pltpu.SMEM)]
            + in_vmem(1)
            + hbm_specs(len(attend_args)),
            out_specs=in_vmem(1 + len(parts)),
            out_shape=[half_rows] + partial_shapes(parts, local_length, near_width),
            scratch_shapes=fetch_scratch(*attend_args),
            compiler_params=pltpu.CompilerParams(vmem_limit_bytes=SMALL_VMEM),
            cost_estimate=SHORT,
        )(at, blocks[-1], *attend_args)
        attended.append(half)
        near += partials

    for j in across_steps:
        residuals[j // 2] = over_seq(after(residuals[j // 2], attended[1]), j)
    other_routes = over_role(routes, last)

    def summed_over_role(parts, extra, *before):
        terms = [[part] for part in parts]
        for n, group in enumerate(groups[:-1]):
            bit = 1 << n
            leaving = terms[n][0] if len(terms[n]) == 1 else added(terms[n]).astype(jnp.bfloat16)
            came = over_role(leaving, bit)
            for m in range(n + 1, len(groups)):
                at_rows = [group.index(k ^ bit) for k in groups[m]]
                if at_rows == list(range(len(group))):
                    terms[m].append(came)
                else:
                    split = [came[i * local_length : (i + 1) * local_length] for i in at_rows]
                    terms[m].append(jnp.concatenate(split, axis=0))
        extra = jnp.pad(after(extra, *before) if before else extra, ((0, local_length), (0, 0)))
        sent = added(terms[-1] + [extra]).astype(jnp.bfloat16)
        return sent

    near_sent = summed_over_role(near, residuals[0])
    near_came = over_role(near_sent, last)
    near_args = in_hbm(near_sent)
    own_shape, both_shape = [
        jax.ShapeDtypeStruct((size, near_width + GATE_COLUMNS), jnp.bfloat16)
        for size in (local_length, 2 * local_length)
    ]
    near_halves = pl.pallas_call(
        near_sum_kernel,
        in_specs=in_vmem(3) + hbm_specs(1),
        out_specs=in_vmem(3),
        out_shape=[own_shape, own_shape, both_shape],
        scratch_shapes=fetch_scratch(*near_args),
        compiler_params=pltpu.CompilerParams(vmem_limit_bytes=SMALL_VMEM),
        cost_estimate=LONG,
    )(routes, other_routes, near_came, *near_args)

    def walk(k, bits):
        found = [k]
        for n, bit in enumerate(bits):
            found += walk(k | bit, bits[n + 1 :])
        return found

    lower_bits = role_bits[:-1][::-1]
    order = walk(last, lower_bits) + walk(0, lower_bits)
    far_plane, final = order[1], order[-1]

    def across(part):
        return [over_seq(part, j) for j in across_steps]

    def spread(own, other, both, ordered):
        planes, crossed = {0: own, last: other}, {}
        both_across = across(both)
        size = own.shape[0]
        for k in order:
            if k not in planes:
                bit = k & -k
                held = planes[k ^ bit]
                wait = ordered and k < last
                planes[k] = over_role(after(held, planes[far_plane]) if wait else held, bit)
            if k in (0, last):
                crossed[k] = both_across
            elif k < last:
                source = k ^ (k & -k)
                came = [part[:size] for part in crossed[source]] if source == 0 else crossed[source]
                crossed[k] = [over_role(part, k & -k) for part in came]
            else:
                crossed[k] = across(after(planes[k], *both_across))
        return planes, crossed

    near_planes, near_crossed = spread(*near_halves, False)

    sent, came = [], []
    for n, j in enumerate(across_steps, 1):
        far = []
        for half, (slots, parts) in zip(attended, slot_sets):
            far += pl.pallas_call(
                partial(project_kernel, slots, parts),
                in_specs=in_vmem(1) + [pl.BlockSpec(memory_space=pl.ANY)] + hbm_specs(2),
                out_specs=in_vmem(len(parts)),
                out_shape=partial_shapes(parts, local_length, near_width),
                scratch_shapes=fetch_scratch(output_weight, beside_proj),
                compiler_params=pltpu.CompilerParams(vmem_limit_bytes=SMALL_VMEM),
                cost_estimate=SHORT,
            )(over_seq(half, j), other_routes, *in_hbm(output_weight, beside_proj))
        sent.append(summed_over_role(far, residuals[n], near_halves[0]))
        came.append(over_role(sent[-1], last))

    chips = 1 + len(across_steps)
    far_args = in_hbm(*sent)
    far_rows = (chips - 1) * local_length
    far_shape, far_both_shape = [
        jax.ShapeDtypeStruct((size, near_width), jnp.bfloat16) for size in (far_rows, 2 * far_rows)
    ]
    first_come = [*near_crossed[0], near_planes[far_plane], *near_crossed[far_plane]]
    first_come.append(near_planes[final])
    far_halves = pl.pallas_call(
        partial(far_sum_kernel, local_length, len(first_come)),
        in_specs=[pl.BlockSpec(memory_space=pl.ANY)] * len(first_come)
        + in_vmem(len(came))
        + hbm_specs(len(far_args)),
        out_specs=in_vmem(3),
        out_shape=[far_shape, far_shape, far_both_shape],
        scratch_shapes=fetch_scratch(*far_args),
        compiler_params=pltpu.CompilerParams(vmem_limit_bytes=SMALL_VMEM),
        cost_estimate=SHORT,
    )(*first_come, *came, *far_args)
    far_own, far_other, far_both = far_halves
    far_other = after(far_other, *near_crossed[final])
    far_planes, far_crossed = spread(far_own, far_other, far_both, True)

    width = residual.shape[2]
    gain = norm_gain.reshape(1, width)

    def normed_rows(parts, second, *hidden_shape):
        rows = chips * local_length
        firsts = (local_length, far_rows) if second else (0, 0)
        return pl.pallas_call(
            partial(norm_kernel, chips, *firsts),
            in_specs=[pl.BlockSpec(memory_space=pltpu.SMEM)] + in_vmem(1 + 2 * chips),
            out_specs=in_vmem(1 + len(hidden_shape)),
            out_shape=[
                jax.ShapeDtypeStruct((rows, width + GATE_COLUMNS), jnp.bfloat16),
                *hidden_shape,
            ],
            scratch_shapes=[pltpu.VMEM((rows, width), jnp.float32)],
            compiler_params=pltpu.CompilerParams(vmem_limit_bytes=SMALL_VMEM),
            cost_estimate=NOTHING,
        )(at, gain, *parts)

    keep, send, slots, leaving, passed = {}, {}, {}, {}, {}

    hidden_shape = jax.ShapeDtypeStruct((local_length, width), jnp.float32)
    hidden = []

    hidden_shape = jax.ShapeDtypeStruct((local_length, width), jnp.float32)
    hidden = []

    def prepared(k, *first):
        late = far_crossed[k]
        if first:
            late = [after(part, *first) for part in late]
        parts = [near_planes[k], far_planes[k]]
        for pair in zip(near_crossed[k], late):
            parts += pair
        normed, *own = normed_rows(parts, k == last, *([] if k else [hidden_shape]))
        hidden.extend(own)
        return [normed, over_seq(normed, 1)]

    def expert(tokens, *others):
        if others:
            tokens = lax.optimization_barrier((*tokens, *others))[: len(tokens)]
        return run_expert(at, tokens, gate_weight, up_weight, down_weight)

    def combine(k, *before):
        came = over_seq(after(send[k], *before) if before else send[k], 1)
        sums = []
        for n in range(len(across_steps)):
            chunk = slice((n + 1) * local_length, (n + 2) * local_length)
            sums.append(added([keep[k][chunk], came[chunk]]).astype(jnp.bfloat16))
        return [keep[k][:local_length], came[:local_length]], sums

    def pass_on(k):
        passed[k] = [over_seq(part, j) for part, j in zip(leaving[k], across_steps)]
        slots[k] += passed[k]

    ready = {far_plane: prepared(far_plane, far_planes[final], *far_crossed[final])}
    ready[final] = prepared(final)
    keep[far_plane], send[far_plane] = expert(ready[far_plane], ready[final][0])
    ready |= {k: prepared(k, keep[far_plane]) for k in (last, 0)}
    slots[far_plane], leaving[far_plane] = combine(far_plane)
    leaving[far_plane] = [after(part, ready[last][0], ready[0][0]) for part in leaving[far_plane]]
    pass_on(far_plane)
    keep[last], send[last] = expert(ready[last], keep[far_plane], *leaving[far_plane])
    slots[last], leaving[last] = combine(last)
    leaving[last] = [after(part, *passed[far_plane]) for part in leaving[last]]
    pass_on(last)
    keep[final], send[final] = expert(ready[final], keep[last])
    slots[far_plane] = [added(slots[far_plane]).astype(jnp.bfloat16)]
    slots[final], leaving[final] = combine(final, *passed[far_plane])
    leaving[final] = [after(part, *leaving[last]) for part in leaving[final]]
    pass_on(final)
    keep[0], send[0] = expert(ready[0], keep[final], *leaving[last])
    slots[0], leaving[0] = combine(0, *passed[last])
    leaving[0] = [after(part, *leaving[final]) for part in leaving[0]]
    pass_on(0)
    for bit in role_bits:
        for k in [k for k in sorted(slots, reverse=True) if k & bit]:
            going = added(slots.pop(k)).astype(jnp.bfloat16)
            if k == last:
                going = after(going, *leaving[final])
            slots[k ^ bit].append(over_role(going, bit))
    return added(hidden + slots[0]).astype(jnp.bfloat16).reshape(residual.shape)


def solution(mesh):
    placed = (
        P("groups", "seq", "role"),
        P("groups", ("seq", "role"), None),
        P("groups", ("seq", "role"), None),
        P("role", "seq"),
        P(("groups", "role"), "seq", None),
        P(),
        P(("groups", "role"), "seq", None),
        P(("groups", "role"), "seq", None),
        P(("seq", "role"), None, None),
        P(("seq", "role"), None, None),
        P(("seq", "role"), None, None),
    )
    experts = mesh.shape["seq"] * mesh.shape["role"]
    return jax.shard_map(
        gathered_shards if experts <= 2 * TOPK else routed_shards,
        mesh=mesh,
        in_specs=placed,
        out_specs=P(("groups", "role"), "seq", None),
        check_vma=False,
    )
```

```python
from functools import partial

import jax
import jax.numpy as jnp
from jax import lax
from jax.experimental import pallas as pl
from jax.experimental.pallas import tpu as pltpu
from jax.sharding import PartitionSpec as P

D = 2048
QUERY_HEADS = 32
KEY_VALUE_HEADS = 4
HEAD_WIDTH = 128
TOPK = 8


epsilon = 1e-06
masked_score = -1e30
EXPERT_VMEM = 16 * 2**20
SMALL_VMEM = 12 * 2**20
COPY_VMEM = 4 * 2**20
GATE_COLUMNS = 128
LOG2_E = 1.4426950408889634
NOTHING = pl.CostEstimate(flops=1, bytes_accessed=1, transcendentals=0)
SHORT = pl.CostEstimate(flops=2 * 10**9, bytes_accessed=4 * 2**20, transcendentals=0)
LONG = pl.CostEstimate(flops=10**10, bytes_accessed=1, transcendentals=0)


def score_block(queries, every_key, query_position, block_start, block_width, score_scale):
    keys_part = lax.slice_in_dim(every_key, block_start, block_start + block_width, axis=0)
    raw_scores = (
        jnp.einsum("qhd,kd->hqk", queries, keys_part, preferred_element_type=jnp.float32)
        * score_scale
    )
    key_position = block_start + jnp.arange(block_width, dtype=jnp.int32)
    return jnp.where(
        key_position[None, None, :] <= query_position[None, :, None], raw_scores, masked_score
    )


def value_block(rounded, every_value, block_start, block_width):
    prob_block = lax.slice_in_dim(rounded, block_start, block_start + block_width, axis=2)
    values_part = lax.slice_in_dim(every_value, block_start, block_start + block_width, axis=0)
    return jnp.einsum("hqk,kd->qhd", prob_block, values_part, preferred_element_type=jnp.float32)


def routed_shards(
    query_rows,
    encoded_key_rows,
    value_matrix_rows,
    output_weight,
    residual,
    norm_gain,
    route_experts,
    route_gates,
    gate_weight,
    up_weight,
    down_weight,
):
    seq_count = lax.axis_size("seq")
    role_count = lax.axis_size("role")
    seq_index = lax.axis_index("seq")
    role_index = lax.axis_index("role")
    batch_count = query_rows.shape[0]
    local_length = query_rows.shape[1]
    local_heads = query_rows.shape[2] // HEAD_WIDTH
    full_length = local_length * seq_count
    query_group_width = QUERY_HEADS // KEY_VALUE_HEADS
    head_pick = role_index * local_heads // query_group_width
    role_keys, role_values = (
        lax.all_gather(encoded_key_rows, "role", axis=1, tiled=True),
        lax.all_gather(value_matrix_rows, "role", axis=1, tiled=True),
    )
    head_keys = lax.dynamic_slice_in_dim(role_keys, head_pick * HEAD_WIDTH, HEAD_WIDTH, 2)
    head_values = lax.dynamic_slice_in_dim(role_values, head_pick * HEAD_WIDTH, HEAD_WIDTH, 2)
    whole_keys, whole_values, whole_proj = (
        lax.all_gather(head_keys, "seq", axis=1, tiled=True),
        lax.all_gather(head_values, "seq", axis=1, tiled=True),
        lax.all_gather(output_weight, "seq", axis=1, tiled=True),
    )
    key_width = full_length // 8
    score_scale = HEAD_WIDTH ** (-0.5)
    query_position = seq_index * local_length + jnp.arange(local_length, dtype=jnp.int32)
    last_needed = (seq_index + 1) * local_length

    def one_sequence(operands):
        own_queries, every_key, every_value = operands
        queries = own_queries.reshape(local_length, local_heads, HEAD_WIDTH)
        pieces = []
        for number in range(8):
            block_start = number * key_width
            compute = partial(
                score_block, queries, every_key, query_position, block_start, key_width, score_scale
            )
            skipped = partial(
                jnp.full, (local_heads, local_length, key_width), masked_score, jnp.float32
            )
            pieces.append(lax.cond(block_start < last_needed, compute, skipped))
        scores = jnp.concatenate(pieces, axis=2)
        row_peak = jnp.max(scores, axis=2, keepdims=True)
        weights = jnp.exp(scores - row_peak)
        totals = jnp.sum(weights, axis=2, keepdims=True)
        rounded = weights.astype(jnp.bfloat16)
        mixed_rows = jnp.zeros((local_length, local_heads, HEAD_WIDTH), jnp.float32)
        for number in range(8):
            block_start = number * key_width
            product = partial(value_block, rounded, every_value, block_start, key_width)
            nothing = partial(jnp.zeros, (local_length, local_heads, HEAD_WIDTH), jnp.float32)
            mixed_rows = mixed_rows + lax.cond(block_start < last_needed, product, nothing)
        attended = (mixed_rows / totals.transpose(1, 0, 2)).astype(jnp.bfloat16)
        return attended.reshape(local_length, local_heads * HEAD_WIDTH)

    attended = lax.map(one_sequence, (query_rows, whole_keys, whole_values))
    flat_attended = attended.reshape(batch_count * local_length, local_heads * HEAD_WIDTH)
    projected = lax.psum_scatter(
        jnp.dot(flat_attended, whole_proj, preferred_element_type=jnp.float32).astype(jnp.bfloat16),
        "role",
        scatter_dimension=0,
        tiled=True,
    ).astype(jnp.float32)
    hidden = residual[0].astype(jnp.float32) + projected
    variance = jnp.mean(hidden * hidden, axis=-1, keepdims=True)
    normed = (hidden * lax.rsqrt(variance + epsilon) * norm_gain).astype(jnp.bfloat16)
    expert_ids = route_experts.reshape(-1)
    gate_values = route_gates.reshape(-1)
    experts_local = gate_weight.shape[0]
    device_count = seq_count * role_count
    expert_count = experts_local * device_count
    assign = expert_ids.shape[0]
    capacity = assign // expert_count + 1
    onehot = (expert_ids[:, None] == jnp.arange(expert_count, dtype=jnp.int32)[None, :]).astype(
        jnp.int32
    )
    earlier = jnp.cumsum(onehot, axis=0) - onehot
    slot_rank = jnp.sum(earlier * onehot, axis=1)
    slot_index = expert_ids * capacity + slot_rank
    source_token = jnp.arange(assign, dtype=jnp.int32) // TOPK
    slot_token = jnp.zeros((expert_count * capacity,), jnp.int32).at[slot_index].set(source_token)
    slot_used = jnp.zeros((expert_count * capacity,), jnp.bfloat16).at[slot_index].set(1.0)
    outgoing = (normed[slot_token] * slot_used[:, None]).reshape(
        device_count, experts_local, capacity, D
    )
    incoming = lax.all_to_all(outgoing, ("seq", "role"), split_axis=0, concat_axis=0, tiled=True)
    gate_hidden = jnp.einsum(
        "sjcd,jdf->sjcf", incoming, gate_weight, preferred_element_type=jnp.float32
    )
    up_hidden = jnp.einsum(
        "sjcd,jdf->sjcf", incoming, up_weight, preferred_element_type=jnp.float32
    )
    activated = (jax.nn.silu(gate_hidden) * up_hidden).astype(jnp.bfloat16)
    returned = lax.all_to_all(
        jnp.einsum(
            "sjcf,jfd->sjcd", activated, down_weight, preferred_element_type=jnp.float32
        ).astype(jnp.bfloat16),
        ("seq", "role"),
        split_axis=0,
        concat_axis=0,
        tiled=True,
    )
    gathered = returned.reshape(expert_count * capacity, D)[slot_index]
    weighted = gathered.astype(jnp.float32) * gate_values[:, None]
    expert_sum = jnp.sum(weighted.reshape(-1, TOPK, D), axis=1)
    return (hidden + expert_sum).astype(jnp.bfloat16).reshape(residual.shape)


def in_hbm(*arrays):
    return [pltpu.with_memory_space_constraint(array, pltpu.HBM) for array in arrays]


def hbm_specs(count):
    return [pl.BlockSpec(memory_space=pltpu.HBM)] * count


def fetch_scratch(*arrays):
    return [pltpu.VMEM(array.shape, array.dtype) for array in arrays] + [
        pltpu.SemaphoreType.DMA((len(arrays),))
    ]


def start_fetch(from_refs, scratch):
    *buffers, sems = scratch
    copies = [
        pltpu.make_async_copy(from_ref, buffer, sems.at[n])
        for n, (from_ref, buffer) in enumerate(zip(from_refs, buffers))
    ]
    for copy in copies:
        copy.start()
    return copies, buffers


def in_vmem(count):
    return [pl.BlockSpec(memory_space=pltpu.VMEM)] * count


def attend_kernel(seq_count, role_count, slots, groups, at_ref, *refs):
    last_block, *refs = refs
    count = seq_count + 2
    attended_ref, *partial_refs = refs[count : count + 1 + len(groups)]
    copies, (query_ref, *buffers) = start_fetch(refs[:count], refs[count + 1 + len(groups) :])
    blocks, proj_refs = buffers[: seq_count - 1] + [last_block], buffers[seq_count - 1 :]
    seq_index, role_index = at_ref[0], at_ref[1]
    local_length = query_ref.shape[1]
    local_heads = query_ref.shape[2] // HEAD_WIDTH
    per_role = local_length // role_count
    rows = local_heads * local_length
    keys_all = seq_count * local_length
    slot = lax.broadcasted_iota(jnp.int32, (rows, keys_all), 1)
    block_number, within = slot // local_length, slot % local_length
    key_position = (
        (seq_index ^ block_number) * local_length
        + (role_index ^ (within // per_role)) * per_role
        + within % per_role
    )
    query_position = (
        seq_index * local_length
        + lax.broadcasted_iota(jnp.int32, (rows, keys_all), 0) % local_length
    )
    seen = key_position <= query_position
    scale = HEAD_WIDTH ** (-0.5) * LOG2_E
    for copy in copies[:seq_count]:
        copy.wait()
    for n, k in enumerate(slots):
        b = role_index ^ k
        own = query_ref[b]
        queries = jnp.concatenate(
            [own[:, h * HEAD_WIDTH : (h + 1) * HEAD_WIDTH] for h in range(local_heads)], axis=0
        )
        key_value = jnp.concatenate([block[b] for block in blocks], axis=0)
        keys, values = key_value[:, :HEAD_WIDTH], key_value[:, HEAD_WIDTH:]
        scores = lax.dot_general(
            queries, keys, (((1,), (1,)), ((), ())), preferred_element_type=jnp.float32
        )
        scores = jnp.where(seen, scores * scale, masked_score)
        weights = jnp.exp2(scores - jnp.max(scores, axis=1, keepdims=True))
        totals = jnp.sum(weights, axis=1, keepdims=True)
        mixed = jnp.dot(weights.astype(jnp.bfloat16), values, preferred_element_type=jnp.float32)
        attended = (mixed * (1.0 / totals)).astype(jnp.bfloat16)
        for h in range(local_heads):
            attended_ref[
                n * local_length : (n + 1) * local_length, h * HEAD_WIDTH : (h + 1) * HEAD_WIDTH
            ] = attended[h * local_length : (h + 1) * local_length]
    for copy in copies[seq_count:]:
        copy.wait()
    project_into(slots, groups, attended_ref, proj_refs, partial_refs)


def join_kernel(*refs):
    *piece_refs, out_ref = refs
    at = 0
    for ref in piece_refs:
        size = ref.shape[1]
        out_ref[:, at : at + size, :] = ref[...]
        at += size


def role_groups(role_count):
    last = role_count // 2
    bits = [1 << n for n in range(last.bit_length() - 1)]
    return [[k for k in range(role_count) if k & -k == bit] for bit in bits] + [[0, last]]


def project_into(slots, groups, attended_ref, proj_refs, partial_refs):
    slots = list(slots)
    rows = attended_ref.shape[0] // len(slots)
    at = 0
    for proj_ref in proj_refs:
        width = proj_ref.shape[1]
        product = jnp.dot(
            attended_ref[...], proj_ref[...], preferred_element_type=jnp.float32
        ).astype(jnp.bfloat16)
        for group, partial_ref in zip(groups, partial_refs):
            for n, k in enumerate(group):
                start = slots.index(k) * rows
                partial_ref[n * rows : (n + 1) * rows, at : at + width] = product[
                    start : start + rows
                ]
        at += width


def project_kernel(slots, groups, attended_ref, order_ref, *refs):
    count = (len(refs) - len(groups) - 1) // 2
    copies, proj_refs = start_fetch(refs[:count], refs[count + len(groups) :])
    for copy in copies:
        copy.wait()
    project_into(slots, groups, attended_ref, proj_refs, refs[count : count + len(groups)])


def partial_shapes(groups, rows, width):
    return [jax.ShapeDtypeStruct((rows * len(group), width), jnp.bfloat16) for group in groups]


def near_sum_kernel(route_ref, other_route_ref, came_ref, sent, *refs):
    out_refs, both_ref = refs[:2], refs[2]
    rows, width = sent.shape[0] // 2, sent.shape[1]
    lane = lax.broadcasted_iota(jnp.int32, (rows, GATE_COLUMNS), 1)
    half = GATE_COLUMNS // 2
    expert = (lane % half).astype(jnp.float32)
    for p, routes in enumerate((route_ref, other_route_ref)):
        shares = jnp.zeros((rows, GATE_COLUMNS), jnp.float32)
        routed = routes.shape[1] // 2
        for k in range(routed):
            named, weight = routes[:, k : k + 1], routes[:, routed + k : routed + k + 1]
            shares = shares + jnp.where(expert == named, weight, 0.0)
        first = shares.astype(jnp.bfloat16).astype(jnp.float32)
        terms = jnp.where(lane < half, first, shares - first).astype(jnp.bfloat16)
        out_refs[p][:, width:] = terms
        both_ref[p * rows : (p + 1) * rows, width:] = terms
    for p in range(2):
        total = sent[p * rows : (p + 1) * rows].astype(jnp.float32)
        total = total + came_ref[(1 - p) * rows : (2 - p) * rows].astype(jnp.float32)
        out_refs[p][:, :width] = total.astype(jnp.bfloat16)
        both_ref[p * rows : (p + 1) * rows, :width] = total.astype(jnp.bfloat16)


def far_sum_kernel(rows, order_count, *refs):
    refs = refs[order_count:]
    chips = (len(refs) - 3) // 2
    came_refs, sent_refs = refs[:chips], refs[chips : 2 * chips]
    own_ref, other_ref, both_ref = refs[2 * chips : 2 * chips + 3]
    size = chips * rows
    for n, (sent, came) in enumerate(zip(sent_refs, came_refs)):
        to = slice(n * rows, (n + 1) * rows)
        for p, out_ref in enumerate((own_ref, other_ref)):
            total = sent[p * rows : (p + 1) * rows].astype(jnp.float32)
            total = total + came[(1 - p) * rows : (2 - p) * rows].astype(jnp.float32)
            out_ref[to] = total.astype(jnp.bfloat16)
            both_ref[p * size + n * rows : p * size + (n + 1) * rows] = total.astype(jnp.bfloat16)


def norm_kernel(chips, near_row, far_row, at_ref, gain_ref, *refs):
    parts, (normed_ref, *hidden_refs) = refs[: 2 * chips], refs[2 * chips :]
    seq_index = at_ref[0]
    rows = normed_ref.shape[0] // chips
    features = gain_ref.shape[1]
    width = features // chips // 2

    def pieces(to):
        for n in range(chips):
            m = n ^ to
            part = parts[2 * n + (1 if m else 0)]
            first = ((far_row if m else near_row) if n else 0) + (m - 1 if m else 0) * rows
            for j in range(2):
                values = part[first : first + rows, j * width : (j + 1) * width]
                yield seq_index ^ (2 * n + j), values.astype(jnp.float32)

    for to in range(chips):
        squares = sum(
            jnp.sum(values * values, axis=1, keepdims=True) for _, values in pieces(to)
        )
        factor = lax.rsqrt(squares * (1.0 / features) + epsilon)
        to_rows = slice(to * rows, (to + 1) * rows)
        for block, values in pieces(to):
            columns = pl.ds(pl.multiple_of(block * width, width), width)
            normed_ref[to_rows, columns] = (values * factor * gain_ref[:, columns]).astype(
                jnp.bfloat16
            )
            if to == 0:
                for hidden_ref in hidden_refs:
                    hidden_ref[:, columns] = values
        near, first = parts[2 * to], near_row if to else 0
        normed_ref[to_rows, features:] = near[first : first + rows, 2 * width :]


def expert_kernel(token_count, at_ref, *refs):
    token_refs = refs[:token_count]
    gate_ref, up_ref, down_ref, keep_ref, send_ref, activated_ref = refs[token_count:]
    features, units = gate_ref.shape[1:]
    tokens = jnp.concatenate([ref[:, :features] for ref in token_refs], axis=0)
    gates = jnp.concatenate([ref[:, features:] for ref in token_refs], axis=0)
    lane = lax.broadcasted_iota(jnp.int32, gates.shape, 1)
    mine = lane % (GATE_COLUMNS // 2) == at_ref[2]
    share = jnp.sum(jnp.where(mine, gates.astype(jnp.float32), 0.0), axis=1, keepdims=True)
    block = units
    for f in range(0, units, block):
        gate_hidden = jnp.dot(
            tokens, gate_ref[0, :, f : f + block], preferred_element_type=jnp.float32
        )
        up_hidden = jnp.dot(tokens, up_ref[0, :, f : f + block], preferred_element_type=jnp.float32)
        activated_ref[:, f : f + block] = (
            gate_hidden / (1.0 + jnp.exp(-gate_hidden)) * up_hidden
        ).astype(jnp.bfloat16)
    kept = keep_ref.shape[0]
    block = 1024 if features % 1024 == 0 else features
    for c in range(0, features, block):
        product = jnp.dot(
            activated_ref[...], down_ref[0, :, c : c + block], preferred_element_type=jnp.float32
        )
        product = (product * share).astype(jnp.bfloat16)
        keep_ref[:, c : c + block] = product[:kept]
        send_ref[:, c : c + block] = product[kept:]


def run_expert(at, tokens, gate_weight, up_weight, down_weight):
    units = gate_weight.shape[2]
    width = gate_weight.shape[1]
    rows = sum(part.shape[0] for part in tokens)
    half = jax.ShapeDtypeStruct((rows // 2, width), jnp.bfloat16)
    return pl.pallas_call(
        partial(expert_kernel, len(tokens)),
        in_specs=[pl.BlockSpec(memory_space=pltpu.SMEM)] + in_vmem(len(tokens) + 3),
        out_specs=in_vmem(2),
        out_shape=[half, half],
        scratch_shapes=[pltpu.VMEM((rows, units), jnp.bfloat16)],
        compiler_params=pltpu.CompilerParams(vmem_limit_bytes=EXPERT_VMEM),
        cost_estimate=NOTHING,
    )(at, *tokens, gate_weight, up_weight, down_weight)


def after(array, *others):
    return lax.optimization_barrier((array, *others))[0]


def added(terms):
    total = terms[0].astype(jnp.float32)
    for term in terms[1:]:
        total = total + term.astype(jnp.float32)
    return total


def gathered_shards(
    query_rows,
    encoded_key_rows,
    value_matrix_rows,
    output_weight,
    residual,
    norm_gain,
    route_experts,
    route_gates,
    gate_weight,
    up_weight,
    down_weight,
):
    seq_count = lax.axis_size("seq")
    role_count = lax.axis_size("role")
    seq_index = lax.axis_index("seq")
    role_index = lax.axis_index("role")
    batch_count, local_length, query_width = query_rows.shape
    local_heads = query_width // HEAD_WIDTH
    group_width = QUERY_HEADS // KEY_VALUE_HEADS
    role_bits = [1 << n for n in range(role_count.bit_length() - 1)]
    at = jnp.stack([seq_index, role_index, seq_index * role_count + role_index]).astype(jnp.int32)

    def over_role(array, k):
        return lax.ppermute(array, "role", [(i, i ^ k) for i in range(role_count)])

    def over_seq(array, j):
        return lax.ppermute(array, "seq", [(i, i ^ j) for i in range(seq_count)])

    beside_proj = over_seq(output_weight, 1)
    block_width = output_weight.shape[1]
    across_steps = range(2, seq_count, 2)

    pieces = []
    for k in range(role_count):
        head = ((role_index ^ k) * local_heads // group_width) * HEAD_WIDTH
        piece = jnp.concatenate(
            [
                lax.dynamic_slice_in_dim(encoded_key_rows, head, HEAD_WIDTH, 2),
                lax.dynamic_slice_in_dim(value_matrix_rows, head, HEAD_WIDTH, 2),
            ],
            axis=2,
        )
        pieces.append(piece)
    pieces[1] = after(pieces[1], beside_proj)
    pieces = [piece if k == 0 else over_role(piece, k) for k, piece in enumerate(pieces)]
    block = pl.pallas_call(
        join_kernel,
        in_specs=in_vmem(len(pieces)),
        out_specs=pl.BlockSpec(memory_space=pltpu.VMEM),
        out_shape=jax.ShapeDtypeStruct(
            (batch_count, local_length, 2 * HEAD_WIDTH), jnp.bfloat16
        ),
        compiler_params=pltpu.CompilerParams(vmem_limit_bytes=COPY_VMEM),
        cost_estimate=SHORT,
    )(*pieces)
    same_core = [block] + [over_seq(block, j) for j in across_steps]
    blocks = []
    for part in same_core:
        blocks += [part, over_seq(part, 1)]
    last = role_count // 2
    routes = jnp.concatenate([route_experts[0].astype(jnp.float32), route_gates[0]], axis=1)
    residual_blocks = [
        lax.dynamic_slice_in_dim(residual[0], (seq_index ^ j) * block_width, block_width, 1)
        for j in range(seq_count)
    ]
    residuals = [
        jnp.concatenate(residual_blocks[j : j + 2], axis=1) for j in range(0, seq_count, 2)
    ]

    rows = batch_count * local_length
    near_width = 2 * output_weight.shape[1]
    groups = role_groups(role_count)
    attend_args = in_hbm(query_rows, *blocks[:-1], output_weight, beside_proj)
    slot_sets = [(range(1, role_count, 2), groups[:1]), (range(0, role_count, 2), groups[1:])]
    attended, near = [], []
    for slots, parts in slot_sets:
        half_rows = jax.ShapeDtypeStruct((rows // 2, query_width), jnp.bfloat16)
        half, *partials = pl.pallas_call(
            partial(attend_kernel, seq_count, role_count, slots, parts),
            in_specs=[pl.BlockSpec(memory_space=pltpu.SMEM)]
            + in_vmem(1)
            + hbm_specs(len(attend_args)),
            out_specs=in_vmem(1 + len(parts)),
            out_shape=[half_rows] + partial_shapes(parts, local_length, near_width),
            scratch_shapes=fetch_scratch(*attend_args),
            compiler_params=pltpu.CompilerParams(vmem_limit_bytes=SMALL_VMEM),
            cost_estimate=SHORT,
        )(at, blocks[-1], *attend_args)
        attended.append(half)
        near += partials

    for j in across_steps:
        residuals[j // 2] = over_seq(after(residuals[j // 2], attended[1]), j)
    other_routes = over_role(routes, last)

    def summed_over_role(parts, extra, *before):
        terms = [[part] for part in parts]
        for n, group in enumerate(groups[:-1]):
            bit = 1 << n
            leaving = terms[n][0] if len(terms[n]) == 1 else added(terms[n]).astype(jnp.bfloat16)
            came = over_role(leaving, bit)
            for m in range(n + 1, len(groups)):
                at_rows = [group.index(k ^ bit) for k in groups[m]]
                if at_rows == list(range(len(group))):
                    terms[m].append(came)
                else:
                    split = [came[i * local_length : (i + 1) * local_length] for i in at_rows]
                    terms[m].append(jnp.concatenate(split, axis=0))
        extra = jnp.pad(after(extra, *before) if before else extra, ((0, local_length), (0, 0)))
        sent = added(terms[-1] + [extra]).astype(jnp.bfloat16)
        return sent

    near_sent = summed_over_role(near, residuals[0])
    near_came = over_role(near_sent, last)
    own_shape, both_shape = [
        jax.ShapeDtypeStruct((size, near_width + GATE_COLUMNS), jnp.bfloat16)
        for size in (local_length, 2 * local_length)
    ]
    near_halves = pl.pallas_call(
        near_sum_kernel,
        in_specs=in_vmem(4),
        out_specs=in_vmem(3),
        out_shape=[own_shape, own_shape, both_shape],
        compiler_params=pltpu.CompilerParams(vmem_limit_bytes=SMALL_VMEM),
        cost_estimate=LONG,
    )(routes, other_routes, near_came, near_sent)

    def walk(k, bits):
        found = [k]
        for n, bit in enumerate(bits):
            found += walk(k | bit, bits[n + 1 :])
        return found

    lower_bits = role_bits[:-1][::-1]
    order = walk(last, lower_bits) + walk(0, lower_bits)
    far_plane, final = order[1], order[-1]

    def across(part):
        return [over_seq(part, j) for j in across_steps]

    def spread(own, other, both, ordered):
        planes, crossed = {0: own, last: other}, {}
        both_across = across(both)
        size = own.shape[0]
        for k in order:
            if k not in planes:
                bit = k & -k
                held = planes[k ^ bit]
                wait = ordered and k < last
                planes[k] = over_role(after(held, planes[far_plane]) if wait else held, bit)
            if k in (0, last):
                crossed[k] = both_across
            elif k < last:
                source = k ^ (k & -k)
                came = [part[:size] for part in crossed[source]] if source == 0 else crossed[source]
                crossed[k] = [over_role(part, k & -k) for part in came]
            else:
                crossed[k] = across(after(planes[k], *both_across))
        return planes, crossed

    near_planes, near_crossed = spread(*near_halves, False)

    sent, came = [], []
    for n, j in enumerate(across_steps, 1):
        far = []
        for half, (slots, parts) in zip(attended, slot_sets):
            far += pl.pallas_call(
                partial(project_kernel, slots, parts),
                in_specs=in_vmem(1) + [pl.BlockSpec(memory_space=pl.ANY)] + hbm_specs(2),
                out_specs=in_vmem(len(parts)),
                out_shape=partial_shapes(parts, local_length, near_width),
                scratch_shapes=fetch_scratch(output_weight, beside_proj),
                compiler_params=pltpu.CompilerParams(vmem_limit_bytes=SMALL_VMEM),
                cost_estimate=SHORT,
            )(over_seq(half, j), other_routes, *in_hbm(output_weight, beside_proj))
        sent.append(summed_over_role(far, residuals[n], near_halves[0]))
        came.append(over_role(sent[-1], last))

    chips = 1 + len(across_steps)
    far_rows = (chips - 1) * local_length
    far_shape, far_both_shape = [
        jax.ShapeDtypeStruct((size, near_width), jnp.bfloat16) for size in (far_rows, 2 * far_rows)
    ]
    first_come = [*near_crossed[0], near_planes[far_plane], *near_crossed[far_plane]]
    first_come.append(near_planes[final])
    far_halves = pl.pallas_call(
        partial(far_sum_kernel, local_length, len(first_come)),
        in_specs=[pl.BlockSpec(memory_space=pl.ANY)] * len(first_come)
        + in_vmem(len(came) + len(sent)),
        out_specs=in_vmem(3),
        out_shape=[far_shape, far_shape, far_both_shape],
        compiler_params=pltpu.CompilerParams(vmem_limit_bytes=SMALL_VMEM),
        cost_estimate=SHORT,
    )(*first_come, *came, *sent)
    far_own, far_other, far_both = far_halves
    far_other = after(far_other, *near_crossed[final])
    far_planes, far_crossed = spread(far_own, far_other, far_both, True)

    width = residual.shape[2]
    gain = norm_gain.reshape(1, width)

    def normed_rows(parts, second, *hidden_shape):
        rows = chips * local_length
        firsts = (local_length, far_rows) if second else (0, 0)
        return pl.pallas_call(
            partial(norm_kernel, chips, *firsts),
            in_specs=[pl.BlockSpec(memory_space=pltpu.SMEM)] + in_vmem(1 + 2 * chips),
            out_specs=in_vmem(1 + len(hidden_shape)),
            out_shape=[
                jax.ShapeDtypeStruct((rows, width + GATE_COLUMNS), jnp.bfloat16),
                *hidden_shape,
            ],
            compiler_params=pltpu.CompilerParams(vmem_limit_bytes=SMALL_VMEM),
            cost_estimate=NOTHING,
        )(at, gain, *parts)

    keep, send, slots, leaving, passed = {}, {}, {}, {}, {}

    hidden_shape = jax.ShapeDtypeStruct((local_length, width), jnp.float32)
    hidden = []

    hidden_shape = jax.ShapeDtypeStruct((local_length, width), jnp.float32)
    hidden = []

    def prepared(k, *first):
        late = far_crossed[k]
        if first:
            late = [after(part, *first) for part in late]
        parts = [near_planes[k], far_planes[k]]
        for pair in zip(near_crossed[k], late):
            parts += pair
        normed, *own = normed_rows(parts, k == last, *([] if k else [hidden_shape]))
        hidden.extend(own)
        return [normed, over_seq(normed, 1)]

    def expert(tokens, *others):
        if others:
            tokens = lax.optimization_barrier((*tokens, *others))[: len(tokens)]
        return run_expert(at, tokens, gate_weight, up_weight, down_weight)

    def combine(k, *before):
        came = over_seq(after(send[k], *before) if before else send[k], 1)
        sums = []
        for n in range(len(across_steps)):
            chunk = slice((n + 1) * local_length, (n + 2) * local_length)
            sums.append(added([keep[k][chunk], came[chunk]]).astype(jnp.bfloat16))
        return [keep[k][:local_length], came[:local_length]], sums

    def pass_on(k):
        passed[k] = [over_seq(part, j) for part, j in zip(leaving[k], across_steps)]
        slots[k] += passed[k]

    ready = {far_plane: prepared(far_plane, far_planes[final], *far_crossed[final])}
    ready[final] = prepared(final)
    keep[far_plane], send[far_plane] = expert(ready[far_plane], ready[final][0])
    ready |= {k: prepared(k, keep[far_plane]) for k in (last, 0)}
    slots[far_plane], leaving[far_plane] = combine(far_plane)
    leaving[far_plane] = [after(part, ready[last][0], ready[0][0]) for part in leaving[far_plane]]
    pass_on(far_plane)
    keep[last], send[last] = expert(ready[last], keep[far_plane], *leaving[far_plane])
    slots[last], leaving[last] = combine(last)
    leaving[last] = [after(part, *passed[far_plane]) for part in leaving[last]]
    pass_on(last)
    keep[final], send[final] = expert(ready[final], keep[last])
    slots[far_plane] = [added(slots[far_plane]).astype(jnp.bfloat16)]
    slots[final], leaving[final] = combine(final, *passed[far_plane])
    leaving[final] = [after(part, *leaving[last]) for part in leaving[final]]
    pass_on(final)
    keep[0], send[0] = expert(ready[0], keep[final], *leaving[last])
    slots[0], leaving[0] = combine(0, *passed[last])
    leaving[0] = [after(part, *leaving[final]) for part in leaving[0]]
    pass_on(0)
    for bit in role_bits:
        for k in [k for k in sorted(slots, reverse=True) if k & bit]:
            going = added(slots.pop(k)).astype(jnp.bfloat16)
            if k == last:
                going = after(going, *leaving[final])
            slots[k ^ bit].append(over_role(going, bit))
    return added(hidden + slots[0]).astype(jnp.bfloat16).reshape(residual.shape)


def solution(mesh):
    placed = (
        P("groups", "seq", "role"),
        P("groups", ("seq", "role"), None),
        P("groups", ("seq", "role"), None),
        P("role", "seq"),
        P(("groups", "role"), "seq", None),
        P(),
        P(("groups", "role"), "seq", None),
        P(("groups", "role"), "seq", None),
        P(("seq", "role"), None, None),
        P(("seq", "role"), None, None),
        P(("seq", "role"), None, None),
    )
    experts = mesh.shape["seq"] * mesh.shape["role"]
    return jax.shard_map(
        gathered_shards if experts <= 2 * TOPK else routed_shards,
        mesh=mesh,
        in_specs=placed,
        out_specs=P(("groups", "role"), "seq", None),
        check_vma=False,
    )
```

```python
from functools import partial

import jax
import jax.numpy as jnp
from jax import lax
from jax.experimental import pallas as pl
from jax.experimental.pallas import tpu as pltpu
from jax.sharding import PartitionSpec as P

D = 2048
QUERY_HEADS = 32
KEY_VALUE_HEADS = 4
HEAD_WIDTH = 128
TOPK = 8


epsilon = 1e-06
masked_score = -1e30
EXPERT_VMEM = 16 * 2**20
SMALL_VMEM = 12 * 2**20
COPY_VMEM = 4 * 2**20
GATE_COLUMNS = 128
LOG2_E = 1.4426950408889634
NOTHING = pl.CostEstimate(flops=1, bytes_accessed=1, transcendentals=0)
SHORT = pl.CostEstimate(flops=2 * 10**9, bytes_accessed=4 * 2**20, transcendentals=0)
LONG = pl.CostEstimate(flops=10**10, bytes_accessed=1, transcendentals=0)


def score_block(queries, every_key, query_position, block_start, block_width, score_scale):
    keys_part = lax.slice_in_dim(every_key, block_start, block_start + block_width, axis=0)
    raw_scores = (
        jnp.einsum("qhd,kd->hqk", queries, keys_part, preferred_element_type=jnp.float32)
        * score_scale
    )
    key_position = block_start + jnp.arange(block_width, dtype=jnp.int32)
    return jnp.where(
        key_position[None, None, :] <= query_position[None, :, None], raw_scores, masked_score
    )


def value_block(rounded, every_value, block_start, block_width):
    prob_block = lax.slice_in_dim(rounded, block_start, block_start + block_width, axis=2)
    values_part = lax.slice_in_dim(every_value, block_start, block_start + block_width, axis=0)
    return jnp.einsum("hqk,kd->qhd", prob_block, values_part, preferred_element_type=jnp.float32)


def routed_shards(
    query_rows,
    encoded_key_rows,
    value_matrix_rows,
    output_weight,
    residual,
    norm_gain,
    route_experts,
    route_gates,
    gate_weight,
    up_weight,
    down_weight,
):
    seq_count = lax.axis_size("seq")
    role_count = lax.axis_size("role")
    seq_index = lax.axis_index("seq")
    role_index = lax.axis_index("role")
    batch_count = query_rows.shape[0]
    local_length = query_rows.shape[1]
    local_heads = query_rows.shape[2] // HEAD_WIDTH
    full_length = local_length * seq_count
    query_group_width = QUERY_HEADS // KEY_VALUE_HEADS
    head_pick = role_index * local_heads // query_group_width
    role_keys, role_values = (
        lax.all_gather(encoded_key_rows, "role", axis=1, tiled=True),
        lax.all_gather(value_matrix_rows, "role", axis=1, tiled=True),
    )
    head_keys = lax.dynamic_slice_in_dim(role_keys, head_pick * HEAD_WIDTH, HEAD_WIDTH, 2)
    head_values = lax.dynamic_slice_in_dim(role_values, head_pick * HEAD_WIDTH, HEAD_WIDTH, 2)
    whole_keys, whole_values, whole_proj = (
        lax.all_gather(head_keys, "seq", axis=1, tiled=True),
        lax.all_gather(head_values, "seq", axis=1, tiled=True),
        lax.all_gather(output_weight, "seq", axis=1, tiled=True),
    )
    key_width = full_length // 8
    score_scale = HEAD_WIDTH ** (-0.5)
    query_position = seq_index * local_length + jnp.arange(local_length, dtype=jnp.int32)
    last_needed = (seq_index + 1) * local_length

    def one_sequence(operands):
        own_queries, every_key, every_value = operands
        queries = own_queries.reshape(local_length, local_heads, HEAD_WIDTH)
        pieces = []
        for number in range(8):
            block_start = number * key_width
            compute = partial(
                score_block, queries, every_key, query_position, block_start, key_width, score_scale
            )
            skipped = partial(
                jnp.full, (local_heads, local_length, key_width), masked_score, jnp.float32
            )
            pieces.append(lax.cond(block_start < last_needed, compute, skipped))
        scores = jnp.concatenate(pieces, axis=2)
        row_peak = jnp.max(scores, axis=2, keepdims=True)
        weights = jnp.exp(scores - row_peak)
        totals = jnp.sum(weights, axis=2, keepdims=True)
        rounded = weights.astype(jnp.bfloat16)
        mixed_rows = jnp.zeros((local_length, local_heads, HEAD_WIDTH), jnp.float32)
        for number in range(8):
            block_start = number * key_width
            product = partial(value_block, rounded, every_value, block_start, key_width)
            nothing = partial(jnp.zeros, (local_length, local_heads, HEAD_WIDTH), jnp.float32)
            mixed_rows = mixed_rows + lax.cond(block_start < last_needed, product, nothing)
        attended = (mixed_rows / totals.transpose(1, 0, 2)).astype(jnp.bfloat16)
        return attended.reshape(local_length, local_heads * HEAD_WIDTH)

    attended = lax.map(one_sequence, (query_rows, whole_keys, whole_values))
    flat_attended = attended.reshape(batch_count * local_length, local_heads * HEAD_WIDTH)
    projected = lax.psum_scatter(
        jnp.dot(flat_attended, whole_proj, preferred_element_type=jnp.float32).astype(jnp.bfloat16),
        "role",
        scatter_dimension=0,
        tiled=True,
    ).astype(jnp.float32)
    hidden = residual[0].astype(jnp.float32) + projected
    variance = jnp.mean(hidden * hidden, axis=-1, keepdims=True)
    normed = (hidden * lax.rsqrt(variance + epsilon) * norm_gain).astype(jnp.bfloat16)
    expert_ids = route_experts.reshape(-1)
    gate_values = route_gates.reshape(-1)
    experts_local = gate_weight.shape[0]
    device_count = seq_count * role_count
    expert_count = experts_local * device_count
    assign = expert_ids.shape[0]
    capacity = assign // expert_count + 1
    onehot = (expert_ids[:, None] == jnp.arange(expert_count, dtype=jnp.int32)[None, :]).astype(
        jnp.int32
    )
    earlier = jnp.cumsum(onehot, axis=0) - onehot
    slot_rank = jnp.sum(earlier * onehot, axis=1)
    slot_index = expert_ids * capacity + slot_rank
    source_token = jnp.arange(assign, dtype=jnp.int32) // TOPK
    slot_token = jnp.zeros((expert_count * capacity,), jnp.int32).at[slot_index].set(source_token)
    slot_used = jnp.zeros((expert_count * capacity,), jnp.bfloat16).at[slot_index].set(1.0)
    outgoing = (normed[slot_token] * slot_used[:, None]).reshape(
        device_count, experts_local, capacity, D
    )
    incoming = lax.all_to_all(outgoing, ("seq", "role"), split_axis=0, concat_axis=0, tiled=True)
    gate_hidden = jnp.einsum(
        "sjcd,jdf->sjcf", incoming, gate_weight, preferred_element_type=jnp.float32
    )
    up_hidden = jnp.einsum(
        "sjcd,jdf->sjcf", incoming, up_weight, preferred_element_type=jnp.float32
    )
    activated = (jax.nn.silu(gate_hidden) * up_hidden).astype(jnp.bfloat16)
    returned = lax.all_to_all(
        jnp.einsum(
            "sjcf,jfd->sjcd", activated, down_weight, preferred_element_type=jnp.float32
        ).astype(jnp.bfloat16),
        ("seq", "role"),
        split_axis=0,
        concat_axis=0,
        tiled=True,
    )
    gathered = returned.reshape(expert_count * capacity, D)[slot_index]
    weighted = gathered.astype(jnp.float32) * gate_values[:, None]
    expert_sum = jnp.sum(weighted.reshape(-1, TOPK, D), axis=1)
    return (hidden + expert_sum).astype(jnp.bfloat16).reshape(residual.shape)


def in_hbm(*arrays):
    return [pltpu.with_memory_space_constraint(array, pltpu.HBM) for array in arrays]


def hbm_specs(count):
    return [pl.BlockSpec(memory_space=pltpu.HBM)] * count


def fetch_scratch(*arrays):
    return [pltpu.VMEM(array.shape, array.dtype) for array in arrays] + [
        pltpu.SemaphoreType.DMA((len(arrays),))
    ]


def start_fetch(from_refs, scratch):
    *buffers, sems = scratch
    copies = [
        pltpu.make_async_copy(from_ref, buffer, sems.at[n])
        for n, (from_ref, buffer) in enumerate(zip(from_refs, buffers))
    ]
    for copy in copies:
        copy.start()
    return copies, buffers


def in_vmem(count):
    return [pl.BlockSpec(memory_space=pltpu.VMEM)] * count


def attend_kernel(seq_count, role_count, slots, groups, at_ref, *refs):
    last_block, *refs = refs
    count = seq_count + 2
    attended_ref, *partial_refs = refs[count : count + 1 + len(groups)]
    copies, (query_ref, *buffers) = start_fetch(refs[:count], refs[count + 1 + len(groups) :])
    blocks, proj_refs = buffers[: seq_count - 1] + [last_block], buffers[seq_count - 1 :]
    seq_index, role_index = at_ref[0], at_ref[1]
    local_length = query_ref.shape[1]
    local_heads = query_ref.shape[2] // HEAD_WIDTH
    per_role = local_length // role_count
    rows = local_heads * local_length
    keys_all = seq_count * local_length
    slot = lax.broadcasted_iota(jnp.int32, (rows, keys_all), 1)
    block_number, within = slot // local_length, slot % local_length
    key_position = (
        (seq_index ^ block_number) * local_length
        + (role_index ^ (within // per_role)) * per_role
        + within % per_role
    )
    query_position = (
        seq_index * local_length
        + lax.broadcasted_iota(jnp.int32, (rows, keys_all), 0) % local_length
    )
    seen = key_position <= query_position
    scale = HEAD_WIDTH ** (-0.5) * LOG2_E
    for copy in copies[:seq_count]:
        copy.wait()
    for n, k in enumerate(slots):
        b = role_index ^ k
        own = query_ref[b]
        queries = jnp.concatenate(
            [own[:, h * HEAD_WIDTH : (h + 1) * HEAD_WIDTH] for h in range(local_heads)], axis=0
        )
        key_value = jnp.concatenate([block[b] for block in blocks], axis=0)
        keys, values = key_value[:, :HEAD_WIDTH], key_value[:, HEAD_WIDTH:]
        scores = lax.dot_general(
            queries, keys, (((1,), (1,)), ((), ())), preferred_element_type=jnp.float32
        )
        scores = jnp.where(seen, scores * scale, masked_score)
        weights = jnp.exp2(scores - jnp.max(scores, axis=1, keepdims=True))
        totals = jnp.sum(weights, axis=1, keepdims=True)
        mixed = jnp.dot(weights.astype(jnp.bfloat16), values, preferred_element_type=jnp.float32)
        attended = (mixed * (1.0 / totals)).astype(jnp.bfloat16)
        for h in range(local_heads):
            attended_ref[
                n * local_length : (n + 1) * local_length, h * HEAD_WIDTH : (h + 1) * HEAD_WIDTH
            ] = attended[h * local_length : (h + 1) * local_length]
    for copy in copies[seq_count:]:
        copy.wait()
    project_into(slots, groups, attended_ref, proj_refs, partial_refs)


def join_kernel(*refs):
    *piece_refs, out_ref = refs
    at = 0
    for ref in piece_refs:
        size = ref.shape[1]
        out_ref[:, at : at + size, :] = ref[...]
        at += size


def role_groups(role_count):
    last = role_count // 2
    bits = [1 << n for n in range(last.bit_length() - 1)]
    return [[k for k in range(role_count) if k & -k == bit] for bit in bits] + [[0, last]]


def project_into(slots, groups, attended_ref, proj_refs, partial_refs):
    slots = list(slots)
    rows = attended_ref.shape[0] // len(slots)
    at = 0
    for proj_ref in proj_refs:
        width = proj_ref.shape[1]
        product = jnp.dot(
            attended_ref[...], proj_ref[...], preferred_element_type=jnp.float32
        ).astype(jnp.bfloat16)
        for group, partial_ref in zip(groups, partial_refs):
            for n, k in enumerate(group):
                start = slots.index(k) * rows
                partial_ref[n * rows : (n + 1) * rows, at : at + width] = product[
                    start : start + rows
                ]
        at += width


def project_kernel(slots, groups, attended_ref, order_ref, *refs):
    count = (len(refs) - len(groups) - 1) // 2
    copies, proj_refs = start_fetch(refs[:count], refs[count + len(groups) :])
    for copy in copies:
        copy.wait()
    project_into(slots, groups, attended_ref, proj_refs, refs[count : count + len(groups)])


def partial_shapes(groups, rows, width):
    return [jax.ShapeDtypeStruct((rows * len(group), width), jnp.bfloat16) for group in groups]


def near_sum_kernel(route_ref, other_route_ref, came_ref, sent, *refs):
    out_refs, both_ref = refs[:2], refs[2]
    rows, width = sent.shape[0] // 2, sent.shape[1]
    lane = lax.broadcasted_iota(jnp.int32, (rows, GATE_COLUMNS), 1)
    half = GATE_COLUMNS // 2
    expert = (lane % half).astype(jnp.float32)
    for p, routes in enumerate((route_ref, other_route_ref)):
        shares = jnp.zeros((rows, GATE_COLUMNS), jnp.float32)
        routed = routes.shape[1] // 2
        for k in range(routed):
            named, weight = routes[:, k : k + 1], routes[:, routed + k : routed + k + 1]
            shares = shares + jnp.where(expert == named, weight, 0.0)
        first = shares.astype(jnp.bfloat16).astype(jnp.float32)
        terms = jnp.where(lane < half, first, shares - first).astype(jnp.bfloat16)
        out_refs[p][:, width:] = terms
        both_ref[p * rows : (p + 1) * rows, width:] = terms
    for p in range(2):
        total = sent[p * rows : (p + 1) * rows].astype(jnp.float32)
        total = total + came_ref[(1 - p) * rows : (2 - p) * rows].astype(jnp.float32)
        out_refs[p][:, :width] = total.astype(jnp.bfloat16)
        both_ref[p * rows : (p + 1) * rows, :width] = total.astype(jnp.bfloat16)


def far_sum_kernel(rows, order_count, *refs):
    refs = refs[order_count:]
    chips = (len(refs) - 3) // 2
    came_refs, sent_refs = refs[:chips], refs[chips : 2 * chips]
    own_ref, other_ref, both_ref = refs[2 * chips : 2 * chips + 3]
    size = chips * rows
    for n, (sent, came) in enumerate(zip(sent_refs, came_refs)):
        to = slice(n * rows, (n + 1) * rows)
        for p, out_ref in enumerate((own_ref, other_ref)):
            total = sent[p * rows : (p + 1) * rows].astype(jnp.float32)
            total = total + came[(1 - p) * rows : (2 - p) * rows].astype(jnp.float32)
            out_ref[to] = total.astype(jnp.bfloat16)
            both_ref[p * size + n * rows : p * size + (n + 1) * rows] = total.astype(jnp.bfloat16)


def norm_kernel(chips, near_row, far_row, at_ref, gain_ref, *refs):
    parts, (normed_ref, *hidden_refs) = refs[: 2 * chips], refs[2 * chips :]
    seq_index = at_ref[0]
    rows = normed_ref.shape[0] // chips
    features = gain_ref.shape[1]
    width = features // chips // 2

    def pieces(to):
        for n in range(chips):
            m = n ^ to
            part = parts[2 * n + (1 if m else 0)]
            first = ((far_row if m else near_row) if n else 0) + (m - 1 if m else 0) * rows
            for j in range(2):
                values = part[first : first + rows, j * width : (j + 1) * width]
                yield seq_index ^ (2 * n + j), values.astype(jnp.float32)

    for to in range(chips):
        squares = sum(
            jnp.sum(values * values, axis=1, keepdims=True) for _, values in pieces(to)
        )
        factor = lax.rsqrt(squares * (1.0 / features) + epsilon)
        to_rows = slice(to * rows, (to + 1) * rows)
        for block, values in pieces(to):
            columns = pl.ds(pl.multiple_of(block * width, width), width)
            normed_ref[to_rows, columns] = (values * factor * gain_ref[:, columns]).astype(
                jnp.bfloat16
            )
            if to == 0:
                for hidden_ref in hidden_refs:
                    hidden_ref[:, columns] = values
        near, first = parts[2 * to], near_row if to else 0
        normed_ref[to_rows, features:] = near[first : first + rows, 2 * width :]


def expert_kernel(token_count, at_ref, *refs):
    token_refs = refs[:token_count]
    gate_ref, up_ref, down_ref, keep_ref, send_ref, activated_ref = refs[token_count:]
    features, units = gate_ref.shape[1:]
    tokens = jnp.concatenate([ref[:, :features] for ref in token_refs], axis=0)
    gates = jnp.concatenate([ref[:, features:] for ref in token_refs], axis=0)
    lane = lax.broadcasted_iota(jnp.int32, gates.shape, 1)
    mine = lane % (GATE_COLUMNS // 2) == at_ref[2]
    share = jnp.sum(jnp.where(mine, gates.astype(jnp.float32), 0.0), axis=1, keepdims=True)
    block = units
    for f in range(0, units, block):
        gate_hidden = jnp.dot(
            tokens, gate_ref[0, :, f : f + block], preferred_element_type=jnp.float32
        )
        up_hidden = jnp.dot(tokens, up_ref[0, :, f : f + block], preferred_element_type=jnp.float32)
        activated_ref[:, f : f + block] = (
            gate_hidden / (1.0 + jnp.exp(-gate_hidden)) * up_hidden
        ).astype(jnp.bfloat16)
    kept = keep_ref.shape[0]
    block = 1024 if features % 1024 == 0 else features
    for c in range(0, features, block):
        product = jnp.dot(
            activated_ref[...], down_ref[0, :, c : c + block], preferred_element_type=jnp.float32
        )
        product = (product * share).astype(jnp.bfloat16)
        keep_ref[:, c : c + block] = product[:kept]
        send_ref[:, c : c + block] = product[kept:]


def run_expert(at, tokens, gate_weight, up_weight, down_weight):
    units = gate_weight.shape[2]
    width = gate_weight.shape[1]
    rows = sum(part.shape[0] for part in tokens)
    half = jax.ShapeDtypeStruct((rows // 2, width), jnp.bfloat16)
    return pl.pallas_call(
        partial(expert_kernel, len(tokens)),
        in_specs=[pl.BlockSpec(memory_space=pltpu.SMEM)] + in_vmem(len(tokens) + 3),
        out_specs=in_vmem(2),
        out_shape=[half, half],
        scratch_shapes=[pltpu.VMEM((rows, units), jnp.bfloat16)],
        compiler_params=pltpu.CompilerParams(vmem_limit_bytes=EXPERT_VMEM),
        cost_estimate=NOTHING,
    )(at, *tokens, gate_weight, up_weight, down_weight)


def after(array, *others):
    return lax.optimization_barrier((array, *others))[0]


def added(terms):
    total = terms[0].astype(jnp.float32)
    for term in terms[1:]:
        total = total + term.astype(jnp.float32)
    return total


def gathered_shards(
    query_rows,
    encoded_key_rows,
    value_matrix_rows,
    output_weight,
    residual,
    norm_gain,
    route_experts,
    route_gates,
    gate_weight,
    up_weight,
    down_weight,
):
    seq_count = lax.axis_size("seq")
    role_count = lax.axis_size("role")
    seq_index = lax.axis_index("seq")
    role_index = lax.axis_index("role")
    batch_count, local_length, query_width = query_rows.shape
    local_heads = query_width // HEAD_WIDTH
    group_width = QUERY_HEADS // KEY_VALUE_HEADS
    role_bits = [1 << n for n in range(role_count.bit_length() - 1)]
    at = jnp.stack([seq_index, role_index, seq_index * role_count + role_index]).astype(jnp.int32)

    def over_role(array, k):
        return lax.ppermute(array, "role", [(i, i ^ k) for i in range(role_count)])

    def over_seq(array, j):
        return lax.ppermute(array, "seq", [(i, i ^ j) for i in range(seq_count)])

    beside_proj = over_seq(output_weight, 1)
    block_width = output_weight.shape[1]
    across_steps = range(2, seq_count, 2)

    pieces = []
    for k in range(role_count):
        head = ((role_index ^ k) * local_heads // group_width) * HEAD_WIDTH
        piece = jnp.concatenate(
            [
                lax.dynamic_slice_in_dim(encoded_key_rows, head, HEAD_WIDTH, 2),
                lax.dynamic_slice_in_dim(value_matrix_rows, head, HEAD_WIDTH, 2),
            ],
            axis=2,
        )
        pieces.append(piece)
    pieces[1] = after(pieces[1], beside_proj)
    pieces = [piece if k == 0 else over_role(piece, k) for k, piece in enumerate(pieces)]
    block = pl.pallas_call(
        join_kernel,
        in_specs=in_vmem(len(pieces)),
        out_specs=pl.BlockSpec(memory_space=pltpu.VMEM),
        out_shape=jax.ShapeDtypeStruct(
            (batch_count, local_length, 2 * HEAD_WIDTH), jnp.bfloat16
        ),
        compiler_params=pltpu.CompilerParams(vmem_limit_bytes=COPY_VMEM),
        cost_estimate=SHORT,
    )(*pieces)
    same_core = [block] + [over_seq(block, j) for j in across_steps]
    blocks = []
    for part in same_core:
        blocks += [part, over_seq(part, 1)]
    last = role_count // 2
    routes = jnp.concatenate([route_experts[0].astype(jnp.float32), route_gates[0]], axis=1)
    residual_blocks = [
        lax.dynamic_slice_in_dim(residual[0], (seq_index ^ j) * block_width, block_width, 1)
        for j in range(seq_count)
    ]
    residuals = [
        jnp.concatenate(residual_blocks[j : j + 2], axis=1) for j in range(0, seq_count, 2)
    ]

    rows = batch_count * local_length
    near_width = 2 * output_weight.shape[1]
    groups = role_groups(role_count)
    attend_args = in_hbm(query_rows, *blocks[:-1], output_weight, beside_proj)
    slot_sets = [(range(1, role_count, 2), groups[:1]), (range(0, role_count, 2), groups[1:])]
    attended, near = [], []
    for slots, parts in slot_sets:
        half_rows = jax.ShapeDtypeStruct((rows // 2, query_width), jnp.bfloat16)
        half, *partials = pl.pallas_call(
            partial(attend_kernel, seq_count, role_count, slots, parts),
            in_specs=[pl.BlockSpec(memory_space=pltpu.SMEM)]
            + in_vmem(1)
            + hbm_specs(len(attend_args)),
            out_specs=in_vmem(1 + len(parts)),
            out_shape=[half_rows] + partial_shapes(parts, local_length, near_width),
            scratch_shapes=fetch_scratch(*attend_args),
            compiler_params=pltpu.CompilerParams(vmem_limit_bytes=SMALL_VMEM),
            cost_estimate=SHORT,
        )(at, blocks[-1], *attend_args)
        attended.append(half)
        near += partials

    for j in across_steps:
        residuals[j // 2] = over_seq(after(residuals[j // 2], attended[1]), j)
    other_routes = over_role(routes, last)

    def summed_over_role(parts, extra, *before):
        terms = [[part] for part in parts]
        for n, group in enumerate(groups[:-1]):
            bit = 1 << n
            leaving = terms[n][0] if len(terms[n]) == 1 else added(terms[n]).astype(jnp.bfloat16)
            came = over_role(leaving, bit)
            for m in range(n + 1, len(groups)):
                at_rows = [group.index(k ^ bit) for k in groups[m]]
                if at_rows == list(range(len(group))):
                    terms[m].append(came)
                else:
                    split = [came[i * local_length : (i + 1) * local_length] for i in at_rows]
                    terms[m].append(jnp.concatenate(split, axis=0))
        extra = jnp.pad(after(extra, *before) if before else extra, ((0, local_length), (0, 0)))
        sent = added(terms[-1] + [extra]).astype(jnp.bfloat16)
        return sent

    near_sent = summed_over_role(near, residuals[0])
    near_came = over_role(near_sent, last)
    own_shape, both_shape = [
        jax.ShapeDtypeStruct((size, near_width + GATE_COLUMNS), jnp.bfloat16)
        for size in (local_length, 2 * local_length)
    ]
    near_halves = pl.pallas_call(
        near_sum_kernel,
        in_specs=in_vmem(4),
        out_specs=in_vmem(3),
        out_shape=[own_shape, own_shape, both_shape],
        compiler_params=pltpu.CompilerParams(vmem_limit_bytes=SMALL_VMEM),
        cost_estimate=LONG,
    )(routes, other_routes, near_came, near_sent)

    def walk(k, bits):
        found = [k]
        for n, bit in enumerate(bits):
            found += walk(k | bit, bits[n + 1 :])
        return found

    lower_bits = role_bits[:-1][::-1]
    order = walk(last, lower_bits) + walk(0, lower_bits)
    far_plane, final = order[1], order[-1]

    def across(part):
        return [over_seq(part, j) for j in across_steps]

    def spread(own, other, both, ordered):
        planes, crossed = {0: own, last: other}, {}
        both_across = across(both)
        size = own.shape[0]
        for k in order:
            if k not in planes:
                bit = k & -k
                held = planes[k ^ bit]
                wait = ordered and k < last
                planes[k] = over_role(after(held, planes[far_plane]) if wait else held, bit)
            if k in (0, last):
                crossed[k] = both_across
            elif k < last:
                source = k ^ (k & -k)
                came = [part[:size] for part in crossed[source]] if source == 0 else crossed[source]
                crossed[k] = [over_role(part, k & -k) for part in came]
            else:
                crossed[k] = across(after(planes[k], *both_across))
        return planes, crossed

    near_planes, near_crossed = spread(*near_halves, False)

    sent, came = [], []
    for n, j in enumerate(across_steps, 1):
        far = []
        for half, (slots, parts) in zip(attended, slot_sets):
            far += pl.pallas_call(
                partial(project_kernel, slots, parts),
                in_specs=in_vmem(1) + [pl.BlockSpec(memory_space=pl.ANY)] + hbm_specs(2),
                out_specs=in_vmem(len(parts)),
                out_shape=partial_shapes(parts, local_length, near_width),
                scratch_shapes=fetch_scratch(output_weight, beside_proj),
                compiler_params=pltpu.CompilerParams(vmem_limit_bytes=SMALL_VMEM),
                cost_estimate=SHORT,
            )(over_seq(half, j), other_routes, *in_hbm(output_weight, beside_proj))
        sent.append(summed_over_role(far, residuals[n], near_halves[0]))
        came.append(over_role(sent[-1], last))

    chips = 1 + len(across_steps)
    far_rows = (chips - 1) * local_length
    far_shape, far_both_shape = [
        jax.ShapeDtypeStruct((size, near_width), jnp.bfloat16) for size in (far_rows, 2 * far_rows)
    ]
    first_come = [*near_crossed[0], near_planes[far_plane], *near_crossed[far_plane]]
    first_come += [near_planes[final], gate_weight, up_weight, down_weight]
    far_halves = pl.pallas_call(
        partial(far_sum_kernel, local_length, len(first_come)),
        in_specs=[pl.BlockSpec(memory_space=pl.ANY)] * len(first_come)
        + in_vmem(len(came) + len(sent)),
        out_specs=in_vmem(3),
        out_shape=[far_shape, far_shape, far_both_shape],
        compiler_params=pltpu.CompilerParams(vmem_limit_bytes=SMALL_VMEM),
        cost_estimate=SHORT,
    )(*first_come, *came, *sent)
    far_own, far_other, far_both = far_halves
    far_other = after(far_other, *near_crossed[final])
    far_planes, far_crossed = spread(far_own, far_other, far_both, True)

    width = residual.shape[2]
    gain = norm_gain.reshape(1, width)

    def normed_rows(parts, second, cost, *hidden_shape):
        rows = chips * local_length
        firsts = (local_length, far_rows) if second else (0, 0)
        return pl.pallas_call(
            partial(norm_kernel, chips, *firsts),
            in_specs=[pl.BlockSpec(memory_space=pltpu.SMEM)] + in_vmem(1 + 2 * chips),
            out_specs=in_vmem(1 + len(hidden_shape)),
            out_shape=[
                jax.ShapeDtypeStruct((rows, width + GATE_COLUMNS), jnp.bfloat16),
                *hidden_shape,
            ],
            compiler_params=pltpu.CompilerParams(vmem_limit_bytes=SMALL_VMEM),
            cost_estimate=cost,
        )(at, gain, *parts)

    keep, send, slots, leaving, passed = {}, {}, {}, {}, {}

    hidden_shape = jax.ShapeDtypeStruct((local_length, width), jnp.float32)
    hidden = []

    hidden_shape = jax.ShapeDtypeStruct((local_length, width), jnp.float32)
    hidden = []

    def prepared(k, *first):
        late = far_crossed[k]
        if first:
            late = [after(part, *first) for part in late]
        parts = [near_planes[k], far_planes[k]]
        for pair in zip(near_crossed[k], late):
            parts += pair
        normed, *own = normed_rows(parts, k == last, LONG if k == final else NOTHING, *([] if k else [hidden_shape]))
        hidden.extend(own)
        return [normed, over_seq(normed, 1)]

    def expert(tokens, *others):
        if others:
            tokens = lax.optimization_barrier((*tokens, *others))[: len(tokens)]
        return run_expert(at, tokens, gate_weight, up_weight, down_weight)

    def combine(k, *before):
        came = over_seq(after(send[k], *before) if before else send[k], 1)
        sums = []
        for n in range(len(across_steps)):
            chunk = slice((n + 1) * local_length, (n + 2) * local_length)
            sums.append(added([keep[k][chunk], came[chunk]]).astype(jnp.bfloat16))
        return [keep[k][:local_length], came[:local_length]], sums

    def pass_on(k):
        passed[k] = [over_seq(part, j) for part, j in zip(leaving[k], across_steps)]
        slots[k] += passed[k]

    ready = {far_plane: prepared(far_plane, far_planes[final])}
    ready[final] = prepared(final)
    keep[far_plane], send[far_plane] = expert(ready[far_plane], ready[final][0])
    ready |= {k: prepared(k, keep[far_plane]) for k in (last, 0)}
    slots[far_plane], leaving[far_plane] = combine(far_plane)
    leaving[far_plane] = [after(part, ready[last][0], ready[0][0]) for part in leaving[far_plane]]
    pass_on(far_plane)
    keep[last], send[last] = expert(ready[last], keep[far_plane], *leaving[far_plane])
    slots[last], leaving[last] = combine(last)
    leaving[last] = [after(part, *passed[far_plane]) for part in leaving[last]]
    pass_on(last)
    keep[final], send[final] = expert(ready[final], keep[last])
    slots[far_plane] = [added(slots[far_plane]).astype(jnp.bfloat16)]
    slots[final], leaving[final] = combine(final, *passed[far_plane])
    leaving[final] = [after(part, *leaving[last]) for part in leaving[final]]
    pass_on(final)
    keep[0], send[0] = expert(ready[0], keep[final], *leaving[last])
    slots[0], leaving[0] = combine(0, *passed[last])
    leaving[0] = [after(part, *leaving[final]) for part in leaving[0]]
    pass_on(0)
    for bit in role_bits:
        for k in [k for k in sorted(slots, reverse=True) if k & bit]:
            going = added(slots.pop(k)).astype(jnp.bfloat16)
            if k == last:
                going = after(going, *leaving[final])
            slots[k ^ bit].append(over_role(going, bit))
    return added(hidden + slots[0]).astype(jnp.bfloat16).reshape(residual.shape)


def solution(mesh):
    placed = (
        P("groups", "seq", "role"),
        P("groups", ("seq", "role"), None),
        P("groups", ("seq", "role"), None),
        P("role", "seq"),
        P(("groups", "role"), "seq", None),
        P(),
        P(("groups", "role"), "seq", None),
        P(("groups", "role"), "seq", None),
        P(("seq", "role"), None, None),
        P(("seq", "role"), None, None),
        P(("seq", "role"), None, None),
    )
    experts = mesh.shape["seq"] * mesh.shape["role"]
    return jax.shard_map(
        gathered_shards if experts <= 2 * TOPK else routed_shards,
        mesh=mesh,
        in_specs=placed,
        out_specs=P(("groups", "role"), "seq", None),
        check_vma=False,
    )
```

```python
from functools import partial

import jax
import jax.numpy as jnp
from jax import lax
from jax.experimental import pallas as pl
from jax.experimental.pallas import tpu as pltpu
from jax.sharding import PartitionSpec as P

D = 2048
QUERY_HEADS = 32
KEY_VALUE_HEADS = 4
HEAD_WIDTH = 128
TOPK = 8


epsilon = 1e-06
masked_score = -1e30
EXPERT_VMEM = 16 * 2**20
SMALL_VMEM = 12 * 2**20
COPY_VMEM = 4 * 2**20
GATE_COLUMNS = 128
LOG2_E = 1.4426950408889634
NOTHING = pl.CostEstimate(flops=1, bytes_accessed=1, transcendentals=0)
SHORT = pl.CostEstimate(flops=2 * 10**9, bytes_accessed=4 * 2**20, transcendentals=0)
LONG = pl.CostEstimate(flops=10**10, bytes_accessed=1, transcendentals=0)


def score_block(queries, every_key, query_position, block_start, block_width, score_scale):
    keys_part = lax.slice_in_dim(every_key, block_start, block_start + block_width, axis=0)
    raw_scores = (
        jnp.einsum("qhd,kd->hqk", queries, keys_part, preferred_element_type=jnp.float32)
        * score_scale
    )
    key_position = block_start + jnp.arange(block_width, dtype=jnp.int32)
    return jnp.where(
        key_position[None, None, :] <= query_position[None, :, None], raw_scores, masked_score
    )


def value_block(rounded, every_value, block_start, block_width):
    prob_block = lax.slice_in_dim(rounded, block_start, block_start + block_width, axis=2)
    values_part = lax.slice_in_dim(every_value, block_start, block_start + block_width, axis=0)
    return jnp.einsum("hqk,kd->qhd", prob_block, values_part, preferred_element_type=jnp.float32)


def routed_shards(
    query_rows,
    encoded_key_rows,
    value_matrix_rows,
    output_weight,
    residual,
    norm_gain,
    route_experts,
    route_gates,
    gate_weight,
    up_weight,
    down_weight,
):
    seq_count = lax.axis_size("seq")
    role_count = lax.axis_size("role")
    seq_index = lax.axis_index("seq")
    role_index = lax.axis_index("role")
    batch_count = query_rows.shape[0]
    local_length = query_rows.shape[1]
    local_heads = query_rows.shape[2] // HEAD_WIDTH
    full_length = local_length * seq_count
    query_group_width = QUERY_HEADS // KEY_VALUE_HEADS
    head_pick = role_index * local_heads // query_group_width
    role_keys, role_values = (
        lax.all_gather(encoded_key_rows, "role", axis=1, tiled=True),
        lax.all_gather(value_matrix_rows, "role", axis=1, tiled=True),
    )
    head_keys = lax.dynamic_slice_in_dim(role_keys, head_pick * HEAD_WIDTH, HEAD_WIDTH, 2)
    head_values = lax.dynamic_slice_in_dim(role_values, head_pick * HEAD_WIDTH, HEAD_WIDTH, 2)
    whole_keys, whole_values, whole_proj = (
        lax.all_gather(head_keys, "seq", axis=1, tiled=True),
        lax.all_gather(head_values, "seq", axis=1, tiled=True),
        lax.all_gather(output_weight, "seq", axis=1, tiled=True),
    )
    key_width = full_length // 8
    score_scale = HEAD_WIDTH ** (-0.5)
    query_position = seq_index * local_length + jnp.arange(local_length, dtype=jnp.int32)
    last_needed = (seq_index + 1) * local_length

    def one_sequence(operands):
        own_queries, every_key, every_value = operands
        queries = own_queries.reshape(local_length, local_heads, HEAD_WIDTH)
        pieces = []
        for number in range(8):
            block_start = number * key_width
            compute = partial(
                score_block, queries, every_key, query_position, block_start, key_width, score_scale
            )
            skipped = partial(
                jnp.full, (local_heads, local_length, key_width), masked_score, jnp.float32
            )
            pieces.append(lax.cond(block_start < last_needed, compute, skipped))
        scores = jnp.concatenate(pieces, axis=2)
        row_peak = jnp.max(scores, axis=2, keepdims=True)
        weights = jnp.exp(scores - row_peak)
        totals = jnp.sum(weights, axis=2, keepdims=True)
        rounded = weights.astype(jnp.bfloat16)
        mixed_rows = jnp.zeros((local_length, local_heads, HEAD_WIDTH), jnp.float32)
        for number in range(8):
            block_start = number * key_width
            product = partial(value_block, rounded, every_value, block_start, key_width)
            nothing = partial(jnp.zeros, (local_length, local_heads, HEAD_WIDTH), jnp.float32)
            mixed_rows = mixed_rows + lax.cond(block_start < last_needed, product, nothing)
        attended = (mixed_rows / totals.transpose(1, 0, 2)).astype(jnp.bfloat16)
        return attended.reshape(local_length, local_heads * HEAD_WIDTH)

    attended = lax.map(one_sequence, (query_rows, whole_keys, whole_values))
    flat_attended = attended.reshape(batch_count * local_length, local_heads * HEAD_WIDTH)
    projected = lax.psum_scatter(
        jnp.dot(flat_attended, whole_proj, preferred_element_type=jnp.float32).astype(jnp.bfloat16),
        "role",
        scatter_dimension=0,
        tiled=True,
    ).astype(jnp.float32)
    hidden = residual[0].astype(jnp.float32) + projected
    variance = jnp.mean(hidden * hidden, axis=-1, keepdims=True)
    normed = (hidden * lax.rsqrt(variance + epsilon) * norm_gain).astype(jnp.bfloat16)
    expert_ids = route_experts.reshape(-1)
    gate_values = route_gates.reshape(-1)
    experts_local = gate_weight.shape[0]
    device_count = seq_count * role_count
    expert_count = experts_local * device_count
    assign = expert_ids.shape[0]
    capacity = assign // expert_count + 1
    onehot = (expert_ids[:, None] == jnp.arange(expert_count, dtype=jnp.int32)[None, :]).astype(
        jnp.int32
    )
    earlier = jnp.cumsum(onehot, axis=0) - onehot
    slot_rank = jnp.sum(earlier * onehot, axis=1)
    slot_index = expert_ids * capacity + slot_rank
    source_token = jnp.arange(assign, dtype=jnp.int32) // TOPK
    slot_token = jnp.zeros((expert_count * capacity,), jnp.int32).at[slot_index].set(source_token)
    slot_used = jnp.zeros((expert_count * capacity,), jnp.bfloat16).at[slot_index].set(1.0)
    outgoing = (normed[slot_token] * slot_used[:, None]).reshape(
        device_count, experts_local, capacity, D
    )
    incoming = lax.all_to_all(outgoing, ("seq", "role"), split_axis=0, concat_axis=0, tiled=True)
    gate_hidden = jnp.einsum(
        "sjcd,jdf->sjcf", incoming, gate_weight, preferred_element_type=jnp.float32
    )
    up_hidden = jnp.einsum(
        "sjcd,jdf->sjcf", incoming, up_weight, preferred_element_type=jnp.float32
    )
    activated = (jax.nn.silu(gate_hidden) * up_hidden).astype(jnp.bfloat16)
    returned = lax.all_to_all(
        jnp.einsum(
            "sjcf,jfd->sjcd", activated, down_weight, preferred_element_type=jnp.float32
        ).astype(jnp.bfloat16),
        ("seq", "role"),
        split_axis=0,
        concat_axis=0,
        tiled=True,
    )
    gathered = returned.reshape(expert_count * capacity, D)[slot_index]
    weighted = gathered.astype(jnp.float32) * gate_values[:, None]
    expert_sum = jnp.sum(weighted.reshape(-1, TOPK, D), axis=1)
    return (hidden + expert_sum).astype(jnp.bfloat16).reshape(residual.shape)


def in_hbm(*arrays):
    return [pltpu.with_memory_space_constraint(array, pltpu.HBM) for array in arrays]


def hbm_specs(count):
    return [pl.BlockSpec(memory_space=pltpu.HBM)] * count


def fetch_scratch(*arrays):
    return [pltpu.VMEM(array.shape, array.dtype) for array in arrays] + [
        pltpu.SemaphoreType.DMA((len(arrays),))
    ]


def start_fetch(from_refs, scratch):
    *buffers, sems = scratch
    copies = [
        pltpu.make_async_copy(from_ref, buffer, sems.at[n])
        for n, (from_ref, buffer) in enumerate(zip(from_refs, buffers))
    ]
    for copy in copies:
        copy.start()
    return copies, buffers


def in_vmem(count):
    return [pl.BlockSpec(memory_space=pltpu.VMEM)] * count


def attend_kernel(seq_count, role_count, slots, groups, at_ref, *refs):
    last_block, proj_ref, *refs = refs
    count = seq_count
    attended_ref, *partial_refs = refs[count : count + 1 + len(groups)]
    copies, (query_ref, *buffers) = start_fetch(refs[:count], refs[count + 1 + len(groups) :])
    blocks = buffers + [last_block]
    seq_index, role_index = at_ref[0], at_ref[1]
    local_length = query_ref.shape[1]
    local_heads = query_ref.shape[2] // HEAD_WIDTH
    per_role = local_length // role_count
    rows = local_heads * local_length
    keys_all = seq_count * local_length
    slot = lax.broadcasted_iota(jnp.int32, (rows, keys_all), 1)
    block_number, within = slot // local_length, slot % local_length
    key_position = (
        (seq_index ^ block_number) * local_length
        + (role_index ^ (within // per_role)) * per_role
        + within % per_role
    )
    query_position = (
        seq_index * local_length
        + lax.broadcasted_iota(jnp.int32, (rows, keys_all), 0) % local_length
    )
    seen = key_position <= query_position
    scale = HEAD_WIDTH ** (-0.5) * LOG2_E
    for copy in copies:
        copy.wait()
    for n, k in enumerate(slots):
        b = role_index ^ k
        own = query_ref[b]
        queries = jnp.concatenate(
            [own[:, h * HEAD_WIDTH : (h + 1) * HEAD_WIDTH] for h in range(local_heads)], axis=0
        )
        key_value = jnp.concatenate([block[b] for block in blocks], axis=0)
        keys, values = key_value[:, :HEAD_WIDTH], key_value[:, HEAD_WIDTH:]
        scores = lax.dot_general(
            queries, keys, (((1,), (1,)), ((), ())), preferred_element_type=jnp.float32
        )
        scores = jnp.where(seen, scores * scale, masked_score)
        weights = jnp.exp2(scores - jnp.max(scores, axis=1, keepdims=True))
        totals = jnp.sum(weights, axis=1, keepdims=True)
        mixed = jnp.dot(weights.astype(jnp.bfloat16), values, preferred_element_type=jnp.float32)
        attended = (mixed * (1.0 / totals)).astype(jnp.bfloat16)
        for h in range(local_heads):
            attended_ref[
                n * local_length : (n + 1) * local_length, h * HEAD_WIDTH : (h + 1) * HEAD_WIDTH
            ] = attended[h * local_length : (h + 1) * local_length]
    project_into(slots, groups, attended_ref, proj_ref, partial_refs)


def columns_kernel(*refs):
    *from_refs, to_ref, sems = refs
    copies, at = [], 0
    for n, ref in enumerate(from_refs):
        width = ref.shape[1]
        copies.append(pltpu.make_async_copy(ref, to_ref.at[:, at : at + width], sems.at[n]))
        copies[-1].start()
        at += width
    for copy in copies:
        copy.wait()


def join_kernel(*refs):
    *piece_refs, _, out_ref = refs
    at = 0
    for ref in piece_refs:
        size = ref.shape[1]
        out_ref[:, at : at + size, :] = ref[...]
        at += size


def role_groups(role_count):
    last = role_count // 2
    bits = [1 << n for n in range(last.bit_length() - 1)]
    return [[k for k in range(role_count) if k & -k == bit] for bit in bits] + [[0, last]]


def project_into(slots, groups, attended_ref, proj_ref, partial_refs):
    slots = list(slots)
    rows = attended_ref.shape[0] // len(slots)
    width = 512 if proj_ref.shape[1] % 512 == 0 else proj_ref.shape[1]
    for at in range(0, proj_ref.shape[1], width):
        product = jnp.dot(
            attended_ref[...], proj_ref[:, at : at + width], preferred_element_type=jnp.float32
        ).astype(jnp.bfloat16)
        for group, partial_ref in zip(groups, partial_refs):
            for n, k in enumerate(group):
                start = slots.index(k) * rows
                partial_ref[n * rows : (n + 1) * rows, at : at + width] = product[
                    start : start + rows
                ]


def project_kernel(slots, groups, attended_ref, proj_ref, order_ref, *partial_refs):
    project_into(slots, groups, attended_ref, proj_ref, partial_refs)


def partial_shapes(groups, rows, width):
    return [jax.ShapeDtypeStruct((rows * len(group), width), jnp.bfloat16) for group in groups]


def near_sum_kernel(route_ref, other_route_ref, came_ref, sent, *refs):
    out_refs, both_ref = refs[:2], refs[2]
    rows, width = sent.shape[0] // 2, sent.shape[1]
    lane = lax.broadcasted_iota(jnp.int32, (rows, GATE_COLUMNS), 1)
    half = GATE_COLUMNS // 2
    expert = (lane % half).astype(jnp.float32)
    for p, routes in enumerate((route_ref, other_route_ref)):
        shares = jnp.zeros((rows, GATE_COLUMNS), jnp.float32)
        routed = routes.shape[1] // 2
        for k in range(routed):
            named, weight = routes[:, k : k + 1], routes[:, routed + k : routed + k + 1]
            shares = shares + jnp.where(expert == named, weight, 0.0)
        first = shares.astype(jnp.bfloat16).astype(jnp.float32)
        terms = jnp.where(lane < half, first, shares - first).astype(jnp.bfloat16)
        out_refs[p][:, width:] = terms
        both_ref[p * rows : (p + 1) * rows, width:] = terms
    for p in range(2):
        total = sent[p * rows : (p + 1) * rows].astype(jnp.float32)
        total = total + came_ref[(1 - p) * rows : (2 - p) * rows].astype(jnp.float32)
        out_refs[p][:, :width] = total.astype(jnp.bfloat16)
        both_ref[p * rows : (p + 1) * rows, :width] = total.astype(jnp.bfloat16)


def far_sum_kernel(rows, order_count, *refs):
    refs = refs[order_count:]
    chips = (len(refs) - 3) // 2
    came_refs, sent_refs = refs[:chips], refs[chips : 2 * chips]
    own_ref, other_ref, both_ref = refs[2 * chips : 2 * chips + 3]
    size = chips * rows
    for n, (sent, came) in enumerate(zip(sent_refs, came_refs)):
        to = slice(n * rows, (n + 1) * rows)
        for p, out_ref in enumerate((own_ref, other_ref)):
            total = sent[p * rows : (p + 1) * rows].astype(jnp.float32)
            total = total + came[(1 - p) * rows : (2 - p) * rows].astype(jnp.float32)
            out_ref[to] = total.astype(jnp.bfloat16)
            both_ref[p * size + n * rows : p * size + (n + 1) * rows] = total.astype(jnp.bfloat16)


def norm_kernel(chips, near_row, far_row, at_ref, gain_ref, *refs):
    parts, (normed_ref, *hidden_refs) = refs[: 2 * chips], refs[2 * chips :]
    seq_index = at_ref[0]
    rows = normed_ref.shape[0] // chips
    features = gain_ref.shape[1]
    width = features // chips // 2

    def pieces(to):
        for n in range(chips):
            m = n ^ to
            part = parts[2 * n + (1 if m else 0)]
            first = ((far_row if m else near_row) if n else 0) + (m - 1 if m else 0) * rows
            for j in range(2):
                values = part[first : first + rows, j * width : (j + 1) * width]
                yield seq_index ^ (2 * n + j), values.astype(jnp.float32)

    for to in range(chips):
        squares = sum(
            jnp.sum(values * values, axis=1, keepdims=True) for _, values in pieces(to)
        )
        factor = lax.rsqrt(squares * (1.0 / features) + epsilon)
        to_rows = slice(to * rows, (to + 1) * rows)
        for block, values in pieces(to):
            columns = pl.ds(pl.multiple_of(block * width, width), width)
            normed_ref[to_rows, columns] = (values * factor * gain_ref[:, columns]).astype(
                jnp.bfloat16
            )
            if to == 0:
                for hidden_ref in hidden_refs:
                    hidden_ref[:, columns] = values
        near, first = parts[2 * to], near_row if to else 0
        normed_ref[to_rows, features:] = near[first : first + rows, 2 * width :]


def expert_kernel(token_count, at_ref, *refs):
    token_refs = refs[:token_count]
    gate_ref, up_ref, down_ref, keep_ref, send_ref, activated_ref = refs[token_count:]
    features, units = gate_ref.shape[1:]
    tokens = jnp.concatenate([ref[:, :features] for ref in token_refs], axis=0)
    gates = jnp.concatenate([ref[:, features:] for ref in token_refs], axis=0)
    lane = lax.broadcasted_iota(jnp.int32, gates.shape, 1)
    mine = lane % (GATE_COLUMNS // 2) == at_ref[2]
    share = jnp.sum(jnp.where(mine, gates.astype(jnp.float32), 0.0), axis=1, keepdims=True)
    block = units
    for f in range(0, units, block):
        gate_hidden = jnp.dot(
            tokens, gate_ref[0, :, f : f + block], preferred_element_type=jnp.float32
        )
        up_hidden = jnp.dot(tokens, up_ref[0, :, f : f + block], preferred_element_type=jnp.float32)
        activated_ref[:, f : f + block] = (
            gate_hidden / (1.0 + jnp.exp(-gate_hidden)) * up_hidden
        ).astype(jnp.bfloat16)
    kept = keep_ref.shape[0]
    block = 1024 if features % 1024 == 0 else features
    for c in range(0, features, block):
        product = jnp.dot(
            activated_ref[...], down_ref[0, :, c : c + block], preferred_element_type=jnp.float32
        )
        product = (product * share).astype(jnp.bfloat16)
        keep_ref[:, c : c + block] = product[:kept]
        send_ref[:, c : c + block] = product[kept:]


def run_expert(at, tokens, gate_weight, up_weight, down_weight):
    units = gate_weight.shape[2]
    width = gate_weight.shape[1]
    rows = sum(part.shape[0] for part in tokens)
    half = jax.ShapeDtypeStruct((rows // 2, width), jnp.bfloat16)
    return pl.pallas_call(
        partial(expert_kernel, len(tokens)),
        in_specs=[pl.BlockSpec(memory_space=pltpu.SMEM)] + in_vmem(len(tokens) + 3),
        out_specs=in_vmem(2),
        out_shape=[half, half],
        scratch_shapes=[pltpu.VMEM((rows, units), jnp.bfloat16)],
        compiler_params=pltpu.CompilerParams(vmem_limit_bytes=EXPERT_VMEM),
        cost_estimate=NOTHING,
    )(at, *tokens, gate_weight, up_weight, down_weight)


def after(array, *others):
    return lax.optimization_barrier((array, *others))[0]


def added(terms):
    total = terms[0].astype(jnp.float32)
    for term in terms[1:]:
        total = total + term.astype(jnp.float32)
    return total


def gathered_shards(
    query_rows,
    encoded_key_rows,
    value_matrix_rows,
    output_weight,
    residual,
    norm_gain,
    route_experts,
    route_gates,
    gate_weight,
    up_weight,
    down_weight,
):
    seq_count = lax.axis_size("seq")
    role_count = lax.axis_size("role")
    seq_index = lax.axis_index("seq")
    role_index = lax.axis_index("role")
    batch_count, local_length, query_width = query_rows.shape
    local_heads = query_width // HEAD_WIDTH
    group_width = QUERY_HEADS // KEY_VALUE_HEADS
    role_bits = [1 << n for n in range(role_count.bit_length() - 1)]
    at = jnp.stack([seq_index, role_index, seq_index * role_count + role_index]).astype(jnp.int32)

    def over_role(array, k):
        return lax.ppermute(array, "role", [(i, i ^ k) for i in range(role_count)])

    def over_seq(array, j):
        return lax.ppermute(array, "seq", [(i, i ^ j) for i in range(seq_count)])

    beside_proj = over_seq(output_weight, 1)
    block_width = output_weight.shape[1]
    across_steps = range(2, seq_count, 2)

    pieces = []
    for k in range(role_count):
        head = ((role_index ^ k) * local_heads // group_width) * HEAD_WIDTH
        piece = jnp.concatenate(
            [
                lax.dynamic_slice_in_dim(encoded_key_rows, head, HEAD_WIDTH, 2),
                lax.dynamic_slice_in_dim(value_matrix_rows, head, HEAD_WIDTH, 2),
            ],
            axis=2,
        )
        pieces.append(piece)
    near_proj = pl.pallas_call(
        columns_kernel,
        in_specs=hbm_specs(1) + in_vmem(1),
        out_specs=pl.BlockSpec(memory_space=pltpu.VMEM),
        out_shape=jax.ShapeDtypeStruct((query_width, 2 * block_width), jnp.bfloat16),
        scratch_shapes=[pltpu.SemaphoreType.DMA((2,))],
        compiler_params=pltpu.CompilerParams(vmem_limit_bytes=COPY_VMEM),
        cost_estimate=NOTHING,
    )(*in_hbm(output_weight), beside_proj)
    pieces[1] = after(pieces[1], beside_proj)
    pieces = [piece if k == 0 else over_role(piece, k) for k, piece in enumerate(pieces)]
    block = pl.pallas_call(
        join_kernel,
        in_specs=in_vmem(len(pieces)) + [pl.BlockSpec(memory_space=pl.ANY)],
        out_specs=pl.BlockSpec(memory_space=pltpu.VMEM),
        out_shape=jax.ShapeDtypeStruct(
            (batch_count, local_length, 2 * HEAD_WIDTH), jnp.bfloat16
        ),
        compiler_params=pltpu.CompilerParams(vmem_limit_bytes=COPY_VMEM),
        cost_estimate=SHORT,
    )(*pieces, near_proj)
    same_core = [block] + [over_seq(block, j) for j in across_steps]
    blocks = []
    for part in same_core:
        blocks += [part, over_seq(part, 1)]
    last = role_count // 2
    routes = jnp.concatenate([route_experts[0].astype(jnp.float32), route_gates[0]], axis=1)
    residual_blocks = [
        lax.dynamic_slice_in_dim(residual[0], (seq_index ^ j) * block_width, block_width, 1)
        for j in range(seq_count)
    ]
    residuals = [
        jnp.concatenate(residual_blocks[j : j + 2], axis=1) for j in range(0, seq_count, 2)
    ]

    rows = batch_count * local_length
    near_width = 2 * output_weight.shape[1]
    groups = role_groups(role_count)
    attend_args = in_hbm(query_rows, *blocks[:-1])
    slot_sets = [(range(1, role_count, 2), groups[:1]), (range(0, role_count, 2), groups[1:])]
    attended, near = [], []
    for slots, parts in slot_sets:
        half_rows = jax.ShapeDtypeStruct((rows // 2, query_width), jnp.bfloat16)
        half, *partials = pl.pallas_call(
            partial(attend_kernel, seq_count, role_count, slots, parts),
            in_specs=[pl.BlockSpec(memory_space=pltpu.SMEM)]
            + in_vmem(2)
            + hbm_specs(len(attend_args)),
            out_specs=in_vmem(1 + len(parts)),
            out_shape=[half_rows] + partial_shapes(parts, local_length, near_width),
            scratch_shapes=fetch_scratch(*attend_args),
            compiler_params=pltpu.CompilerParams(vmem_limit_bytes=SMALL_VMEM),
            cost_estimate=SHORT,
        )(at, blocks[-1], near_proj, *attend_args)
        attended.append(half)
        near += partials

    for j in across_steps:
        residuals[j // 2] = over_seq(after(residuals[j // 2], attended[1]), j)
    other_routes = over_role(routes, last)

    def summed_over_role(parts, extra, *before):
        terms = [[part] for part in parts]
        for n, group in enumerate(groups[:-1]):
            bit = 1 << n
            leaving = terms[n][0] if len(terms[n]) == 1 else added(terms[n]).astype(jnp.bfloat16)
            came = over_role(leaving, bit)
            for m in range(n + 1, len(groups)):
                at_rows = [group.index(k ^ bit) for k in groups[m]]
                if at_rows == list(range(len(group))):
                    terms[m].append(came)
                else:
                    split = [came[i * local_length : (i + 1) * local_length] for i in at_rows]
                    terms[m].append(jnp.concatenate(split, axis=0))
        extra = jnp.pad(after(extra, *before) if before else extra, ((0, local_length), (0, 0)))
        sent = added(terms[-1] + [extra]).astype(jnp.bfloat16)
        return sent

    near_sent = summed_over_role(near, residuals[0])
    near_came = over_role(near_sent, last)
    own_shape, both_shape = [
        jax.ShapeDtypeStruct((size, near_width + GATE_COLUMNS), jnp.bfloat16)
        for size in (local_length, 2 * local_length)
    ]
    near_halves = pl.pallas_call(
        near_sum_kernel,
        in_specs=in_vmem(4),
        out_specs=in_vmem(3),
        out_shape=[own_shape, own_shape, both_shape],
        compiler_params=pltpu.CompilerParams(vmem_limit_bytes=SMALL_VMEM),
        cost_estimate=LONG,
    )(routes, other_routes, near_came, near_sent)

    def walk(k, bits):
        found = [k]
        for n, bit in enumerate(bits):
            found += walk(k | bit, bits[n + 1 :])
        return found

    lower_bits = role_bits[:-1][::-1]
    order = walk(last, lower_bits) + walk(0, lower_bits)
    far_plane, final = order[1], order[-1]

    def across(part):
        return [over_seq(part, j) for j in across_steps]

    def spread(own, other, both, ordered):
        planes, crossed = {0: own, last: other}, {}
        both_across = across(both)
        size = own.shape[0]
        for k in order:
            if k not in planes:
                bit = k & -k
                held = planes[k ^ bit]
                wait = ordered and k < last
                planes[k] = over_role(after(held, planes[far_plane]) if wait else held, bit)
            if k in (0, last):
                crossed[k] = both_across
            elif k < last:
                source = k ^ (k & -k)
                came = [part[:size] for part in crossed[source]] if source == 0 else crossed[source]
                crossed[k] = [over_role(part, k & -k) for part in came]
            else:
                crossed[k] = across(after(planes[k], *both_across))
        return planes, crossed

    near_planes, near_crossed = spread(*near_halves, False)

    sent, came = [], []
    for n, j in enumerate(across_steps, 1):
        far = []
        for half, (slots, parts) in zip(attended, slot_sets):
            far += pl.pallas_call(
                partial(project_kernel, slots, parts),
                in_specs=in_vmem(2) + [pl.BlockSpec(memory_space=pl.ANY)],
                out_specs=in_vmem(len(parts)),
                out_shape=partial_shapes(parts, local_length, near_width),
                compiler_params=pltpu.CompilerParams(vmem_limit_bytes=SMALL_VMEM),
                cost_estimate=SHORT,
            )(over_seq(half, j), near_proj, other_routes)
        sent.append(summed_over_role(far, residuals[n], near_halves[0]))
        came.append(over_role(sent[-1], last))

    chips = 1 + len(across_steps)
    far_rows = (chips - 1) * local_length
    far_shape, far_both_shape = [
        jax.ShapeDtypeStruct((size, near_width), jnp.bfloat16) for size in (far_rows, 2 * far_rows)
    ]
    first_come = [*near_crossed[0], near_planes[far_plane], *near_crossed[far_plane]]
    first_come += [near_planes[final], gate_weight, up_weight, down_weight]
    far_halves = pl.pallas_call(
        partial(far_sum_kernel, local_length, len(first_come)),
        in_specs=[pl.BlockSpec(memory_space=pl.ANY)] * len(first_come)
        + in_vmem(len(came) + len(sent)),
        out_specs=in_vmem(3),
        out_shape=[far_shape, far_shape, far_both_shape],
        compiler_params=pltpu.CompilerParams(vmem_limit_bytes=SMALL_VMEM),
        cost_estimate=SHORT,
    )(*first_come, *came, *sent)
    far_own, far_other, far_both = far_halves
    far_other = after(far_other, *near_crossed[final])
    far_planes, far_crossed = spread(far_own, far_other, far_both, True)

    width = residual.shape[2]
    gain = norm_gain.reshape(1, width)

    def normed_rows(parts, second, cost, *hidden_shape):
        rows = chips * local_length
        firsts = (local_length, far_rows) if second else (0, 0)
        return pl.pallas_call(
            partial(norm_kernel, chips, *firsts),
            in_specs=[pl.BlockSpec(memory_space=pltpu.SMEM)] + in_vmem(1 + 2 * chips),
            out_specs=in_vmem(1 + len(hidden_shape)),
            out_shape=[
                jax.ShapeDtypeStruct((rows, width + GATE_COLUMNS), jnp.bfloat16),
                *hidden_shape,
            ],
            compiler_params=pltpu.CompilerParams(vmem_limit_bytes=SMALL_VMEM),
            cost_estimate=cost,
        )(at, gain, *parts)

    keep, send, slots, leaving, passed = {}, {}, {}, {}, {}

    hidden_shape = jax.ShapeDtypeStruct((local_length, width), jnp.float32)
    hidden = []

    hidden_shape = jax.ShapeDtypeStruct((local_length, width), jnp.float32)
    hidden = []

    def prepared(k, *first):
        late = far_crossed[k]
        if first:
            late = [after(part, *first) for part in late]
        parts = [near_planes[k], far_planes[k]]
        for pair in zip(near_crossed[k], late):
            parts += pair
        normed, *own = normed_rows(parts, k == last, LONG if k == final else NOTHING, *([] if k else [hidden_shape]))
        hidden.extend(own)
        return [normed, over_seq(normed, 1)]

    def expert(tokens, *others):
        if others:
            tokens = lax.optimization_barrier((*tokens, *others))[: len(tokens)]
        return run_expert(at, tokens, gate_weight, up_weight, down_weight)

    def combine(k, *before):
        came = over_seq(after(send[k], *before) if before else send[k], 1)
        sums = []
        for n in range(len(across_steps)):
            chunk = slice((n + 1) * local_length, (n + 2) * local_length)
            sums.append(added([keep[k][chunk], came[chunk]]).astype(jnp.bfloat16))
        return [keep[k][:local_length], came[:local_length]], sums

    def pass_on(k):
        passed[k] = [over_seq(part, j) for part, j in zip(leaving[k], across_steps)]
        slots[k] += passed[k]

    ready = {far_plane: prepared(far_plane, far_planes[final])}
    ready[final] = prepared(final)
    keep[far_plane], send[far_plane] = expert(ready[far_plane], ready[final][0])
    ready |= {k: prepared(k, keep[far_plane]) for k in (last, 0)}
    slots[far_plane], leaving[far_plane] = combine(far_plane)
    leaving[far_plane] = [after(part, ready[last][0], ready[0][0]) for part in leaving[far_plane]]
    pass_on(far_plane)
    keep[last], send[last] = expert(ready[last], keep[far_plane], *leaving[far_plane])
    slots[last], leaving[last] = combine(last)
    leaving[last] = [after(part, *passed[far_plane]) for part in leaving[last]]
    pass_on(last)
    keep[final], send[final] = expert(ready[final], keep[last])
    slots[far_plane] = [added(slots[far_plane]).astype(jnp.bfloat16)]
    slots[final], leaving[final] = combine(final, *passed[far_plane])
    leaving[final] = [after(part, *leaving[last]) for part in leaving[final]]
    pass_on(final)
    keep[0], send[0] = expert(ready[0], keep[final], *leaving[last])
    slots[0], leaving[0] = combine(0, *passed[last])
    leaving[0] = [after(part, *leaving[final]) for part in leaving[0]]
    pass_on(0)
    for bit in role_bits:
        for k in [k for k in sorted(slots, reverse=True) if k & bit]:
            going = added(slots.pop(k)).astype(jnp.bfloat16)
            if k == last:
                going = after(going, *leaving[final])
            slots[k ^ bit].append(over_role(going, bit))
    return added(hidden + slots[0]).astype(jnp.bfloat16).reshape(residual.shape)


def solution(mesh):
    placed = (
        P("groups", "seq", "role"),
        P("groups", ("seq", "role"), None),
        P("groups", ("seq", "role"), None),
        P("role", "seq"),
        P(("groups", "role"), "seq", None),
        P(),
        P(("groups", "role"), "seq", None),
        P(("groups", "role"), "seq", None),
        P(("seq", "role"), None, None),
        P(("seq", "role"), None, None),
        P(("seq", "role"), None, None),
    )
    experts = mesh.shape["seq"] * mesh.shape["role"]
    return jax.shard_map(
        gathered_shards if experts <= 2 * TOPK else routed_shards,
        mesh=mesh,
        in_specs=placed,
        out_specs=P(("groups", "role"), "seq", None),
        check_vma=False,
    )
```

```python
from functools import partial

import jax
import jax.numpy as jnp
from jax import lax
from jax.experimental import pallas as pl
from jax.experimental.pallas import tpu as pltpu
from jax.sharding import PartitionSpec as P

D = 2048
QUERY_HEADS = 32
KEY_VALUE_HEADS = 4
HEAD_WIDTH = 128
TOPK = 8


epsilon = 1e-06
masked_score = -1e30
EXPERT_VMEM = 16 * 2**20
SMALL_VMEM = 12 * 2**20
COPY_VMEM = 4 * 2**20
GATE_COLUMNS = 128
LOG2_E = 1.4426950408889634
NOTHING = pl.CostEstimate(flops=1, bytes_accessed=1, transcendentals=0)
SHORT = pl.CostEstimate(flops=2 * 10**9, bytes_accessed=4 * 2**20, transcendentals=0)
LONG = pl.CostEstimate(flops=10**10, bytes_accessed=1, transcendentals=0)


def score_block(queries, every_key, query_position, block_start, block_width, score_scale):
    keys_part = lax.slice_in_dim(every_key, block_start, block_start + block_width, axis=0)
    raw_scores = (
        jnp.einsum("qhd,kd->hqk", queries, keys_part, preferred_element_type=jnp.float32)
        * score_scale
    )
    key_position = block_start + jnp.arange(block_width, dtype=jnp.int32)
    return jnp.where(
        key_position[None, None, :] <= query_position[None, :, None], raw_scores, masked_score
    )


def value_block(rounded, every_value, block_start, block_width):
    prob_block = lax.slice_in_dim(rounded, block_start, block_start + block_width, axis=2)
    values_part = lax.slice_in_dim(every_value, block_start, block_start + block_width, axis=0)
    return jnp.einsum("hqk,kd->qhd", prob_block, values_part, preferred_element_type=jnp.float32)


def routed_shards(
    query_rows,
    encoded_key_rows,
    value_matrix_rows,
    output_weight,
    residual,
    norm_gain,
    route_experts,
    route_gates,
    gate_weight,
    up_weight,
    down_weight,
):
    seq_count = lax.axis_size("seq")
    role_count = lax.axis_size("role")
    seq_index = lax.axis_index("seq")
    role_index = lax.axis_index("role")
    batch_count = query_rows.shape[0]
    local_length = query_rows.shape[1]
    local_heads = query_rows.shape[2] // HEAD_WIDTH
    full_length = local_length * seq_count
    query_group_width = QUERY_HEADS // KEY_VALUE_HEADS
    head_pick = role_index * local_heads // query_group_width
    role_keys, role_values = (
        lax.all_gather(encoded_key_rows, "role", axis=1, tiled=True),
        lax.all_gather(value_matrix_rows, "role", axis=1, tiled=True),
    )
    head_keys = lax.dynamic_slice_in_dim(role_keys, head_pick * HEAD_WIDTH, HEAD_WIDTH, 2)
    head_values = lax.dynamic_slice_in_dim(role_values, head_pick * HEAD_WIDTH, HEAD_WIDTH, 2)
    whole_keys, whole_values, whole_proj = (
        lax.all_gather(head_keys, "seq", axis=1, tiled=True),
        lax.all_gather(head_values, "seq", axis=1, tiled=True),
        lax.all_gather(output_weight, "seq", axis=1, tiled=True),
    )
    key_width = full_length // 8
    score_scale = HEAD_WIDTH ** (-0.5)
    query_position = seq_index * local_length + jnp.arange(local_length, dtype=jnp.int32)
    last_needed = (seq_index + 1) * local_length

    def one_sequence(operands):
        own_queries, every_key, every_value = operands
        queries = own_queries.reshape(local_length, local_heads, HEAD_WIDTH)
        pieces = []
        for number in range(8):
            block_start = number * key_width
            compute = partial(
                score_block, queries, every_key, query_position, block_start, key_width, score_scale
            )
            skipped = partial(
                jnp.full, (local_heads, local_length, key_width), masked_score, jnp.float32
            )
            pieces.append(lax.cond(block_start < last_needed, compute, skipped))
        scores = jnp.concatenate(pieces, axis=2)
        row_peak = jnp.max(scores, axis=2, keepdims=True)
        weights = jnp.exp(scores - row_peak)
        totals = jnp.sum(weights, axis=2, keepdims=True)
        rounded = weights.astype(jnp.bfloat16)
        mixed_rows = jnp.zeros((local_length, local_heads, HEAD_WIDTH), jnp.float32)
        for number in range(8):
            block_start = number * key_width
            product = partial(value_block, rounded, every_value, block_start, key_width)
            nothing = partial(jnp.zeros, (local_length, local_heads, HEAD_WIDTH), jnp.float32)
            mixed_rows = mixed_rows + lax.cond(block_start < last_needed, product, nothing)
        attended = (mixed_rows / totals.transpose(1, 0, 2)).astype(jnp.bfloat16)
        return attended.reshape(local_length, local_heads * HEAD_WIDTH)

    attended = lax.map(one_sequence, (query_rows, whole_keys, whole_values))
    flat_attended = attended.reshape(batch_count * local_length, local_heads * HEAD_WIDTH)
    projected = lax.psum_scatter(
        jnp.dot(flat_attended, whole_proj, preferred_element_type=jnp.float32).astype(jnp.bfloat16),
        "role",
        scatter_dimension=0,
        tiled=True,
    ).astype(jnp.float32)
    hidden = residual[0].astype(jnp.float32) + projected
    variance = jnp.mean(hidden * hidden, axis=-1, keepdims=True)
    normed = (hidden * lax.rsqrt(variance + epsilon) * norm_gain).astype(jnp.bfloat16)
    expert_ids = route_experts.reshape(-1)
    gate_values = route_gates.reshape(-1)
    experts_local = gate_weight.shape[0]
    device_count = seq_count * role_count
    expert_count = experts_local * device_count
    assign = expert_ids.shape[0]
    capacity = assign // expert_count + 1
    onehot = (expert_ids[:, None] == jnp.arange(expert_count, dtype=jnp.int32)[None, :]).astype(
        jnp.int32
    )
    earlier = jnp.cumsum(onehot, axis=0) - onehot
    slot_rank = jnp.sum(earlier * onehot, axis=1)
    slot_index = expert_ids * capacity + slot_rank
    source_token = jnp.arange(assign, dtype=jnp.int32) // TOPK
    slot_token = jnp.zeros((expert_count * capacity,), jnp.int32).at[slot_index].set(source_token)
    slot_used = jnp.zeros((expert_count * capacity,), jnp.bfloat16).at[slot_index].set(1.0)
    outgoing = (normed[slot_token] * slot_used[:, None]).reshape(
        device_count, experts_local, capacity, D
    )
    incoming = lax.all_to_all(outgoing, ("seq", "role"), split_axis=0, concat_axis=0, tiled=True)
    gate_hidden = jnp.einsum(
        "sjcd,jdf->sjcf", incoming, gate_weight, preferred_element_type=jnp.float32
    )
    up_hidden = jnp.einsum(
        "sjcd,jdf->sjcf", incoming, up_weight, preferred_element_type=jnp.float32
    )
    activated = (jax.nn.silu(gate_hidden) * up_hidden).astype(jnp.bfloat16)
    returned = lax.all_to_all(
        jnp.einsum(
            "sjcf,jfd->sjcd", activated, down_weight, preferred_element_type=jnp.float32
        ).astype(jnp.bfloat16),
        ("seq", "role"),
        split_axis=0,
        concat_axis=0,
        tiled=True,
    )
    gathered = returned.reshape(expert_count * capacity, D)[slot_index]
    weighted = gathered.astype(jnp.float32) * gate_values[:, None]
    expert_sum = jnp.sum(weighted.reshape(-1, TOPK, D), axis=1)
    return (hidden + expert_sum).astype(jnp.bfloat16).reshape(residual.shape)


def in_hbm(*arrays):
    return [pltpu.with_memory_space_constraint(array, pltpu.HBM) for array in arrays]


def hbm_specs(count):
    return [pl.BlockSpec(memory_space=pltpu.HBM)] * count


def fetch_scratch(*arrays):
    return [pltpu.VMEM(array.shape, array.dtype) for array in arrays] + [
        pltpu.SemaphoreType.DMA((len(arrays),))
    ]


def start_fetch(from_refs, scratch):
    *buffers, sems = scratch
    copies = [
        pltpu.make_async_copy(from_ref, buffer, sems.at[n])
        for n, (from_ref, buffer) in enumerate(zip(from_refs, buffers))
    ]
    for copy in copies:
        copy.start()
    return copies, buffers


def in_vmem(count):
    return [pl.BlockSpec(memory_space=pltpu.VMEM)] * count


def attend_kernel(seq_count, role_count, slots, groups, at_ref, *refs):
    last_block, proj_ref, *refs = refs
    count = seq_count
    attended_ref, *partial_refs = refs[count : count + 1 + len(groups)]
    copies, (query_ref, *buffers) = start_fetch(refs[:count], refs[count + 1 + len(groups) :])
    blocks = buffers + [last_block]
    seq_index, role_index = at_ref[0], at_ref[1]
    local_length = query_ref.shape[1]
    local_heads = query_ref.shape[2] // HEAD_WIDTH
    per_role = local_length // role_count
    rows = local_heads * local_length
    keys_all = seq_count * local_length
    slot = lax.broadcasted_iota(jnp.int32, (rows, keys_all), 1)
    block_number, within = slot // local_length, slot % local_length
    key_position = (
        (seq_index ^ block_number) * local_length
        + (role_index ^ (within // per_role)) * per_role
        + within % per_role
    )
    query_position = (
        seq_index * local_length
        + lax.broadcasted_iota(jnp.int32, (rows, keys_all), 0) % local_length
    )
    seen = key_position <= query_position
    scale = HEAD_WIDTH ** (-0.5) * LOG2_E
    for copy in copies:
        copy.wait()
    for n, k in enumerate(slots):
        b = role_index ^ k
        own = query_ref[b]
        queries = jnp.concatenate(
            [own[:, h * HEAD_WIDTH : (h + 1) * HEAD_WIDTH] for h in range(local_heads)], axis=0
        )
        key_value = jnp.concatenate([block[b] for block in blocks], axis=0)
        keys, values = key_value[:, :HEAD_WIDTH], key_value[:, HEAD_WIDTH:]
        scores = lax.dot_general(
            queries, keys, (((1,), (1,)), ((), ())), preferred_element_type=jnp.float32
        )
        scores = jnp.where(seen, scores * scale, masked_score)
        weights = jnp.exp2(scores - jnp.max(scores, axis=1, keepdims=True))
        totals = jnp.sum(weights, axis=1, keepdims=True)
        mixed = jnp.dot(weights.astype(jnp.bfloat16), values, preferred_element_type=jnp.float32)
        attended = (mixed * (1.0 / totals)).astype(jnp.bfloat16)
        for h in range(local_heads):
            attended_ref[
                n * local_length : (n + 1) * local_length, h * HEAD_WIDTH : (h + 1) * HEAD_WIDTH
            ] = attended[h * local_length : (h + 1) * local_length]
    project_into(slots, groups, attended_ref, proj_ref, partial_refs)


def columns_kernel(*refs):
    *from_refs, to_ref, sems = refs
    copies, at = [], 0
    for n, ref in enumerate(from_refs):
        width = ref.shape[1]
        copies.append(pltpu.make_async_copy(ref, to_ref.at[:, at : at + width], sems.at[n]))
        copies[-1].start()
        at += width
    for copy in copies:
        copy.wait()


def join_kernel(*refs):
    *piece_refs, _, out_ref = refs
    at = 0
    for ref in piece_refs:
        size = ref.shape[1]
        out_ref[:, at : at + size, :] = ref[...]
        at += size


def role_groups(role_count):
    last = role_count // 2
    bits = [1 << n for n in range(last.bit_length() - 1)]
    return [[k for k in range(role_count) if k & -k == bit] for bit in bits] + [[0, last]]


def project_into(slots, groups, attended_ref, proj_ref, partial_refs):
    slots = list(slots)
    rows = attended_ref.shape[0] // len(slots)
    width = 512 if proj_ref.shape[1] % 512 == 0 else proj_ref.shape[1]
    for at in range(0, proj_ref.shape[1], width):
        product = jnp.dot(
            attended_ref[...], proj_ref[:, at : at + width], preferred_element_type=jnp.float32
        ).astype(jnp.bfloat16)
        for group, partial_ref in zip(groups, partial_refs):
            for n, k in enumerate(group):
                start = slots.index(k) * rows
                partial_ref[n * rows : (n + 1) * rows, at : at + width] = product[
                    start : start + rows
                ]


def project_kernel(slots, groups, attended_ref, proj_ref, order_ref, *partial_refs):
    project_into(slots, groups, attended_ref, proj_ref, partial_refs)


def partial_shapes(groups, rows, width):
    return [jax.ShapeDtypeStruct((rows * len(group), width), jnp.bfloat16) for group in groups]


def near_sum_kernel(route_ref, other_route_ref, came_ref, sent, *refs):
    out_refs, both_ref = refs[:2], refs[2]
    rows, width = sent.shape[0] // 2, sent.shape[1]
    lane = lax.broadcasted_iota(jnp.int32, (rows, GATE_COLUMNS), 1)
    half = GATE_COLUMNS // 2
    expert = (lane % half).astype(jnp.float32)
    for p, routes in enumerate((route_ref, other_route_ref)):
        shares = jnp.zeros((rows, GATE_COLUMNS), jnp.float32)
        routed = routes.shape[1] // 2
        for k in range(routed):
            named, weight = routes[:, k : k + 1], routes[:, routed + k : routed + k + 1]
            shares = shares + jnp.where(expert == named, weight, 0.0)
        first = shares.astype(jnp.bfloat16).astype(jnp.float32)
        terms = jnp.where(lane < half, first, shares - first).astype(jnp.bfloat16)
        out_refs[p][:, width:] = terms
        both_ref[p * rows : (p + 1) * rows, width:] = terms
    for p in range(2):
        total = sent[p * rows : (p + 1) * rows].astype(jnp.float32)
        total = total + came_ref[(1 - p) * rows : (2 - p) * rows].astype(jnp.float32)
        out_refs[p][:, :width] = total.astype(jnp.bfloat16)
        both_ref[p * rows : (p + 1) * rows, :width] = total.astype(jnp.bfloat16)


def far_sum_kernel(rows, order_count, *refs):
    refs = refs[order_count:]
    chips = (len(refs) - 3) // 2
    came_refs, sent_refs = refs[:chips], refs[chips : 2 * chips]
    own_ref, other_ref, both_ref = refs[2 * chips : 2 * chips + 3]
    size = chips * rows
    for n, (sent, came) in enumerate(zip(sent_refs, came_refs)):
        to = slice(n * rows, (n + 1) * rows)
        for p, out_ref in enumerate((own_ref, other_ref)):
            total = sent[p * rows : (p + 1) * rows].astype(jnp.float32)
            total = total + came[(1 - p) * rows : (2 - p) * rows].astype(jnp.float32)
            out_ref[to] = total.astype(jnp.bfloat16)
            both_ref[p * size + n * rows : p * size + (n + 1) * rows] = total.astype(jnp.bfloat16)


def norm_kernel(chips, near_row, far_row, at_ref, gain_ref, *refs):
    parts, (normed_ref, *hidden_refs) = refs[: 2 * chips], refs[2 * chips :]
    seq_index = at_ref[0]
    rows = normed_ref.shape[0] // chips
    features = gain_ref.shape[1]
    width = features // chips // 2

    def pieces(to):
        for n in range(chips):
            m = n ^ to
            part = parts[2 * n + (1 if m else 0)]
            first = ((far_row if m else near_row) if n else 0) + (m - 1 if m else 0) * rows
            for j in range(2):
                values = part[first : first + rows, j * width : (j + 1) * width]
                yield seq_index ^ (2 * n + j), values.astype(jnp.float32)

    for to in range(chips):
        squares = sum(
            jnp.sum(values * values, axis=1, keepdims=True) for _, values in pieces(to)
        )
        factor = lax.rsqrt(squares * (1.0 / features) + epsilon)
        to_rows = slice(to * rows, (to + 1) * rows)
        for block, values in pieces(to):
            columns = pl.ds(pl.multiple_of(block * width, width), width)
            normed_ref[to_rows, columns] = (values * factor * gain_ref[:, columns]).astype(
                jnp.bfloat16
            )
            if to == 0:
                for hidden_ref in hidden_refs:
                    hidden_ref[:, columns] = values
        near, first = parts[2 * to], near_row if to else 0
        normed_ref[to_rows, features:] = near[first : first + rows, 2 * width :]


def expert_kernel(token_count, at_ref, *refs):
    token_refs = refs[:token_count]
    gate_ref, up_ref, down_ref, keep_ref, send_ref, activated_ref = refs[token_count:]
    features, units = gate_ref.shape[1:]
    tokens = jnp.concatenate([ref[:, :features] for ref in token_refs], axis=0)
    gates = jnp.concatenate([ref[:, features:] for ref in token_refs], axis=0)
    lane = lax.broadcasted_iota(jnp.int32, gates.shape, 1)
    mine = lane % (GATE_COLUMNS // 2) == at_ref[2]
    share = jnp.sum(jnp.where(mine, gates.astype(jnp.float32), 0.0), axis=1, keepdims=True)
    block = units
    for f in range(0, units, block):
        gate_hidden = jnp.dot(
            tokens, gate_ref[0, :, f : f + block], preferred_element_type=jnp.float32
        )
        up_hidden = jnp.dot(tokens, up_ref[0, :, f : f + block], preferred_element_type=jnp.float32)
        activated_ref[:, f : f + block] = (
            gate_hidden / (1.0 + jnp.exp(-gate_hidden)) * up_hidden
        ).astype(jnp.bfloat16)
    kept = keep_ref.shape[0]
    block = 1024 if features % 1024 == 0 else features
    for c in range(0, features, block):
        product = jnp.dot(
            activated_ref[...], down_ref[0, :, c : c + block], preferred_element_type=jnp.float32
        )
        product = (product * share).astype(jnp.bfloat16)
        keep_ref[:, c : c + block] = product[:kept]
        send_ref[:, c : c + block] = product[kept:]


def run_expert(at, tokens, gate_weight, up_weight, down_weight):
    units = gate_weight.shape[2]
    width = gate_weight.shape[1]
    rows = sum(part.shape[0] for part in tokens)
    half = jax.ShapeDtypeStruct((rows // 2, width), jnp.bfloat16)
    return pl.pallas_call(
        partial(expert_kernel, len(tokens)),
        in_specs=[pl.BlockSpec(memory_space=pltpu.SMEM)] + in_vmem(len(tokens) + 3),
        out_specs=in_vmem(2),
        out_shape=[half, half],
        scratch_shapes=[pltpu.VMEM((rows, units), jnp.bfloat16)],
        compiler_params=pltpu.CompilerParams(vmem_limit_bytes=EXPERT_VMEM),
        cost_estimate=NOTHING,
    )(at, *tokens, gate_weight, up_weight, down_weight)


def after(array, *others):
    return lax.optimization_barrier((array, *others))[0]


def added(terms):
    total = terms[0].astype(jnp.float32)
    for term in terms[1:]:
        total = total + term.astype(jnp.float32)
    return total


def gathered_shards(
    query_rows,
    encoded_key_rows,
    value_matrix_rows,
    output_weight,
    residual,
    norm_gain,
    route_experts,
    route_gates,
    gate_weight,
    up_weight,
    down_weight,
):
    seq_count = lax.axis_size("seq")
    role_count = lax.axis_size("role")
    seq_index = lax.axis_index("seq")
    role_index = lax.axis_index("role")
    batch_count, local_length, query_width = query_rows.shape
    local_heads = query_width // HEAD_WIDTH
    group_width = QUERY_HEADS // KEY_VALUE_HEADS
    role_bits = [1 << n for n in range(role_count.bit_length() - 1)]
    at = jnp.stack([seq_index, role_index, seq_index * role_count + role_index]).astype(jnp.int32)

    def over_role(array, k):
        return lax.ppermute(array, "role", [(i, i ^ k) for i in range(role_count)])

    def over_seq(array, j):
        return lax.ppermute(array, "seq", [(i, i ^ j) for i in range(seq_count)])

    beside_proj = over_seq(output_weight, 1)
    block_width = output_weight.shape[1]
    across_steps = range(2, seq_count, 2)

    pieces = []
    for k in range(role_count):
        head = ((role_index ^ k) * local_heads // group_width) * HEAD_WIDTH
        piece = jnp.concatenate(
            [
                lax.dynamic_slice_in_dim(encoded_key_rows, head, HEAD_WIDTH, 2),
                lax.dynamic_slice_in_dim(value_matrix_rows, head, HEAD_WIDTH, 2),
            ],
            axis=2,
        )
        pieces.append(piece)
    near_proj = pl.pallas_call(
        columns_kernel,
        in_specs=hbm_specs(1) + in_vmem(1),
        out_specs=pl.BlockSpec(memory_space=pltpu.VMEM),
        out_shape=jax.ShapeDtypeStruct((query_width, 2 * block_width), jnp.bfloat16),
        scratch_shapes=[pltpu.SemaphoreType.DMA((2,))],
        compiler_params=pltpu.CompilerParams(vmem_limit_bytes=COPY_VMEM),
        cost_estimate=NOTHING,
    )(*in_hbm(output_weight), beside_proj)
    pieces[1] = after(pieces[1], beside_proj)
    pieces = [piece if k == 0 else over_role(piece, k) for k, piece in enumerate(pieces)]
    block = pl.pallas_call(
        join_kernel,
        in_specs=in_vmem(len(pieces)) + [pl.BlockSpec(memory_space=pl.ANY)],
        out_specs=pl.BlockSpec(memory_space=pltpu.VMEM),
        out_shape=jax.ShapeDtypeStruct(
            (batch_count, local_length, 2 * HEAD_WIDTH), jnp.bfloat16
        ),
        compiler_params=pltpu.CompilerParams(vmem_limit_bytes=COPY_VMEM),
        cost_estimate=SHORT,
    )(*pieces, near_proj)
    same_core = [block] + [over_seq(block, j) for j in across_steps]
    blocks = []
    for part in same_core:
        blocks += [part, over_seq(part, 1)]
    last = role_count // 2
    routes = jnp.concatenate([route_experts[0].astype(jnp.float32), route_gates[0]], axis=1)
    residual_blocks = [
        lax.dynamic_slice_in_dim(residual[0], (seq_index ^ j) * block_width, block_width, 1)
        for j in range(seq_count)
    ]
    residuals = [
        jnp.concatenate(residual_blocks[j : j + 2], axis=1) for j in range(0, seq_count, 2)
    ]

    rows = batch_count * local_length
    near_width = 2 * output_weight.shape[1]
    groups = role_groups(role_count)
    attend_args = in_hbm(query_rows, *blocks[:-1])
    slot_sets = [(range(1, role_count, 2), groups[:1]), (range(0, role_count, 2), groups[1:])]
    attended, near = [], []
    for slots, parts in slot_sets:
        half_rows = jax.ShapeDtypeStruct((rows // 2, query_width), jnp.bfloat16)
        half, *partials = pl.pallas_call(
            partial(attend_kernel, seq_count, role_count, slots, parts),
            in_specs=[pl.BlockSpec(memory_space=pltpu.SMEM)]
            + in_vmem(2)
            + hbm_specs(len(attend_args)),
            out_specs=in_vmem(1 + len(parts)),
            out_shape=[half_rows] + partial_shapes(parts, local_length, near_width),
            scratch_shapes=fetch_scratch(*attend_args),
            compiler_params=pltpu.CompilerParams(vmem_limit_bytes=SMALL_VMEM),
            cost_estimate=SHORT,
        )(at, blocks[-1], near_proj, *attend_args)
        attended.append(half)
        near += partials

    for j in across_steps:
        residuals[j // 2] = over_seq(after(residuals[j // 2], attended[1]), j)
    other_routes = over_role(routes, last)

    def summed_over_role(parts, extra, *before):
        terms = [[part] for part in parts]
        for n, group in enumerate(groups[:-1]):
            bit = 1 << n
            leaving = terms[n][0] if len(terms[n]) == 1 else added(terms[n]).astype(jnp.bfloat16)
            came = over_role(leaving, bit)
            for m in range(n + 1, len(groups)):
                at_rows = [group.index(k ^ bit) for k in groups[m]]
                if at_rows == list(range(len(group))):
                    terms[m].append(came)
                else:
                    split = [came[i * local_length : (i + 1) * local_length] for i in at_rows]
                    terms[m].append(jnp.concatenate(split, axis=0))
        extra = jnp.pad(after(extra, *before) if before else extra, ((0, local_length), (0, 0)))
        sent = added(terms[-1] + [extra]).astype(jnp.bfloat16)
        return sent

    near_sent = summed_over_role(near, residuals[0])
    near_came = over_role(near_sent, last)
    own_shape, both_shape = [
        jax.ShapeDtypeStruct((size, near_width + GATE_COLUMNS), jnp.bfloat16)
        for size in (local_length, 2 * local_length)
    ]
    near_halves = pl.pallas_call(
        near_sum_kernel,
        in_specs=in_vmem(4),
        out_specs=in_vmem(3),
        out_shape=[own_shape, own_shape, both_shape],
        compiler_params=pltpu.CompilerParams(vmem_limit_bytes=SMALL_VMEM),
        cost_estimate=LONG,
    )(routes, other_routes, near_came, near_sent)

    def walk(k, bits):
        found = [k]
        for n, bit in enumerate(bits):
            found += walk(k | bit, bits[n + 1 :])
        return found

    lower_bits = role_bits[:-1][::-1]
    order = walk(last, lower_bits) + walk(0, lower_bits)
    far_plane, final = order[1], order[-1]

    def across(part):
        return [over_seq(part, j) for j in across_steps]

    def spread(own, other, both, ordered):
        planes, crossed = {0: own, last: other}, {}
        both_across = across(both)
        size = own.shape[0]
        for k in order:
            if k not in planes:
                bit = k & -k
                held = planes[k ^ bit]
                wait = ordered and k < last
                planes[k] = over_role(after(held, planes[far_plane]) if wait else held, bit)
            if k in (0, last):
                crossed[k] = both_across
            elif k < last:
                source = k ^ (k & -k)
                came = [part[:size] for part in crossed[source]] if source == 0 else crossed[source]
                crossed[k] = [over_role(part, k & -k) for part in came]
            else:
                crossed[k] = across(after(planes[k], *both_across))
        return planes, crossed

    near_planes, near_crossed = spread(*near_halves, False)

    sent, came = [], []
    for n, j in enumerate(across_steps, 1):
        far = []
        for half, (slots, parts) in zip(attended, slot_sets):
            far += pl.pallas_call(
                partial(project_kernel, slots, parts),
                in_specs=in_vmem(2) + [pl.BlockSpec(memory_space=pl.ANY)],
                out_specs=in_vmem(len(parts)),
                out_shape=partial_shapes(parts, local_length, near_width),
                compiler_params=pltpu.CompilerParams(vmem_limit_bytes=SMALL_VMEM),
                cost_estimate=SHORT,
            )(over_seq(half, j), near_proj, other_routes)
        sent.append(summed_over_role(far, residuals[n], near_halves[0]))
        came.append(over_role(sent[-1], last))

    chips = 1 + len(across_steps)
    far_rows = (chips - 1) * local_length
    far_shape, far_both_shape = [
        jax.ShapeDtypeStruct((size, near_width), jnp.bfloat16) for size in (far_rows, 2 * far_rows)
    ]
    first_come = [*near_crossed[0], near_planes[far_plane], *near_crossed[far_plane]]
    first_come += [near_planes[final], gate_weight, up_weight, down_weight]
    far_halves = pl.pallas_call(
        partial(far_sum_kernel, local_length, len(first_come)),
        in_specs=[pl.BlockSpec(memory_space=pl.ANY)] * len(first_come)
        + in_vmem(len(came) + len(sent)),
        out_specs=in_vmem(3),
        out_shape=[far_shape, far_shape, far_both_shape],
        compiler_params=pltpu.CompilerParams(vmem_limit_bytes=SMALL_VMEM),
        cost_estimate=SHORT,
    )(*first_come, *came, *sent)
    far_own, far_other, far_both = far_halves
    far_other = after(far_other, *near_crossed[final])
    far_planes, far_crossed = spread(far_own, far_other, far_both, True)

    width = residual.shape[2]
    gain = norm_gain.reshape(1, width)

    def normed_rows(parts, second, cost, *hidden_shape):
        rows = chips * local_length
        firsts = (local_length, far_rows) if second else (0, 0)
        return pl.pallas_call(
            partial(norm_kernel, chips, *firsts),
            in_specs=[pl.BlockSpec(memory_space=pltpu.SMEM)] + in_vmem(1 + 2 * chips),
            out_specs=in_vmem(1 + len(hidden_shape)),
            out_shape=[
                jax.ShapeDtypeStruct((rows, width + GATE_COLUMNS), jnp.bfloat16),
                *hidden_shape,
            ],
            compiler_params=pltpu.CompilerParams(vmem_limit_bytes=SMALL_VMEM),
            cost_estimate=cost,
        )(at, gain, *parts)

    keep, send, slots, leaving, passed = {}, {}, {}, {}, {}

    hidden_shape = jax.ShapeDtypeStruct((local_length, width), jnp.float32)
    hidden = []

    hidden_shape = jax.ShapeDtypeStruct((local_length, width), jnp.float32)
    hidden = []

    def prepared(k, *first):
        late = far_crossed[k]
        if first:
            late = [after(part, *first) for part in late]
        parts = [near_planes[k], far_planes[k]]
        for pair in zip(near_crossed[k], late):
            parts += pair
        normed, *own = normed_rows(parts, k == last, LONG if k == final else NOTHING, *([] if k else [hidden_shape]))
        hidden.extend(own)
        return [normed, over_seq(normed, 1)]

    def expert(tokens, *others):
        if others:
            tokens = lax.optimization_barrier((*tokens, *others))[: len(tokens)]
        return run_expert(at, tokens, gate_weight, up_weight, down_weight)

    def combine(k, *before):
        came = over_seq(after(send[k], *before) if before else send[k], 1)
        sums = []
        for n in range(len(across_steps)):
            chunk = slice((n + 1) * local_length, (n + 2) * local_length)
            sums.append(added([keep[k][chunk], came[chunk]]).astype(jnp.bfloat16))
        return [keep[k][:local_length], came[:local_length]], sums

    def pass_on(k):
        passed[k] = [over_seq(part, j) for part, j in zip(leaving[k], across_steps)]
        slots[k] += passed[k]

    ready = {far_plane: prepared(far_plane, far_planes[final])}
    ready[final] = prepared(final)
    keep[far_plane], send[far_plane] = expert(ready[far_plane], ready[final][0])
    ready |= {k: prepared(k, keep[far_plane]) for k in (last, 0)}
    slots[far_plane], leaving[far_plane] = combine(far_plane)
    leaving[far_plane] = [after(part, ready[last][0], ready[0][0]) for part in leaving[far_plane]]
    pass_on(far_plane)
    keep[last], send[last] = expert(ready[last], keep[far_plane], *leaving[far_plane])
    slots[last], leaving[last] = combine(last)
    leaving[last] = [after(part, *passed[far_plane]) for part in leaving[last]]
    pass_on(last)
    keep[final], send[final] = expert(ready[final], keep[last])
    slots[far_plane] = [added(slots[far_plane]).astype(jnp.bfloat16)]
    slots[final], leaving[final] = combine(final)
    leaving[final] = [after(part, *leaving[last]) for part in leaving[final]]
    pass_on(final)
    keep[0], send[0] = expert(ready[0], keep[final], *leaving[last])
    slots[0], leaving[0] = combine(0, *passed[last])
    leaving[0] = [after(part, *leaving[final]) for part in leaving[0]]
    pass_on(0)
    for bit in role_bits:
        for k in [k for k in sorted(slots, reverse=True) if k & bit]:
            going = added(slots.pop(k)).astype(jnp.bfloat16)
            if k == last:
                going = after(going, *leaving[final])
            slots[k ^ bit].append(over_role(going, bit))
    return added(hidden + slots[0]).astype(jnp.bfloat16).reshape(residual.shape)


def solution(mesh):
    placed = (
        P("groups", "seq", "role"),
        P("groups", ("seq", "role"), None),
        P("groups", ("seq", "role"), None),
        P("role", "seq"),
        P(("groups", "role"), "seq", None),
        P(),
        P(("groups", "role"), "seq", None),
        P(("groups", "role"), "seq", None),
        P(("seq", "role"), None, None),
        P(("seq", "role"), None, None),
        P(("seq", "role"), None, None),
    )
    experts = mesh.shape["seq"] * mesh.shape["role"]
    return jax.shard_map(
        gathered_shards if experts <= 2 * TOPK else routed_shards,
        mesh=mesh,
        in_specs=placed,
        out_specs=P(("groups", "role"), "seq", None),
        check_vma=False,
    )
```
